32 devices in a mesh: groups: 2 (over y), tile: 4 (over z), chan: 2 (over x), tm: 2 (over core).
Axes of the slice: x: 2, y: 2, z: 4, core: 2. Of those that a mesh axis runs over, the one named last changes fastest.
Arguments:
- latents: bfloat16 [8, 32, 576], P('tm', 'groups', 'tile'), parts along dimension 1, may hold values from -6 to 6
- tile_order: int32 [8], P('groups'), parts along dimension 0, may hold values from 0 to 3, each once
- w_in: bfloat16 [27, 16, 512], P(None, None, 'chan'), may hold values from -0.3125 to 0.3125
- gain_in: float32 [512], P('chan'), may hold values from 0.25 to 1.75
- shift_in: float32 [512], P('chan'), may hold values from -3 to 3
- w_mid: bfloat16 [27, 512, 512], P(None, None, 'chan'), may hold values from -0.0546875 to 0.0546875
- gain_mid: float32 [512], P('chan'), may hold values from 0.25 to 1.75
- shift_mid: float32 [512], P('chan'), may hold values from -3 to 3
- w_out: bfloat16 [3, 512], P(None, 'chan'), may hold values from -0.25 to 0.25
- blend_weight: float32 [8, 256], P('groups'), parts along dimension 0, may hold values from 0.25 to 4
Outputs:
- decoded: float32 [8, 6, 576], P('tm', 'groups', 'tile'), parts along dimension 1
The draws below stay inside these ranges and needn't reach their ends.
There are 2 independent parts, one for each index of `groups`. The reference program is written for one: setup_inputs(seed, part) draws one part's arguments, and reference() takes and returns one part's arrays. A program takes and returns all parts, laid end to end along the dimension named above; an argument that names none is the same for every part. Nothing has to cross between parts.
Inputs may be any that keep to these rules, and one draw needn't show every extreme that they name: `tile_order`: each image block is held by exactly one latent block.
All inputs are finite; a program needn't handle non-finite values.
Results may differ from the reference program's by a relative error of at most 0.0037.
Values may be sent and summed in bfloat16 or wider, within the bound.
No kernel may reach another device: no remote copies, remote signals or barrier semaphores. Data moves between devices by JAX's collectives and lax.ppermute only.
A program may use at most 64 MiB of HBM per device.

```python
import math
import jax
import jax.numpy as jnp
from jax import lax

CH = 512
LATENT_CH = 16
GROUPS = 32
TSIDE = 16
STRIDE = 12
GRID_X = 4
FRAMES = 8
TILES = 4
PIXELS = 256
NPIX = 576


def level_of(own_key, shape, shards, least, high):
    factor_of = 1.0
    for dim, blocks in shards:
        draws = jax.random.uniform(jax.random.fold_in(jax.random.fold_in(own_key, 6), dim), (blocks,), jnp.float32, least / len(shards), high / len(shards))
        factor_of = factor_of * jnp.repeat(jnp.exp(draws), shape[dim] // blocks).reshape((-1,) + (1,) * (len(shape) - 1 - dim))
    return factor_of


def scatter_about(key, extent, scale, bound, pieces=(), kind=jnp.bfloat16):
    level = level_of(key, extent, pieces, -0.22, 0.18) if pieces else 1.0
    values = jax.random.normal(key, extent, jnp.float32) * scale * level
    return jnp.minimum(jnp.maximum(values, -bound), bound).astype(kind)


def setup_inputs(seed: int = 0, part: int = 0) -> dict:
    streams_of = jax.random.split(jax.random.key(seed), 11)
    own_keys = jax.random.split(jax.random.fold_in(streams_of[10], part), 11)
    latents = scatter_about(own_keys[0], (FRAMES, LATENT_CH, NPIX), 1.0, 6.0, ((0, 2), (2, 4)))
    tile_order = jax.random.permutation(own_keys[1], TILES).astype(jnp.int32)
    w_in = scatter_about(streams_of[2], (27, LATENT_CH, CH), (27 * LATENT_CH) ** -0.5, 0.3125, ((2, 2),))
    gain_in = jnp.clip(1.0 + 0.15 * jax.random.normal(streams_of[3], (CH,), jnp.float32), 0.25, 1.75)
    shift_in = scatter_about(streams_of[4], (CH,), 0.5, 3.0, ((0, 2),), jnp.float32)
    w_mid = scatter_about(streams_of[5], (27, CH, CH), (27 * CH) ** -0.5, 0.0546875, ((2, 2),))
    gain_mid = jnp.clip(1.0 + 0.15 * jax.random.normal(streams_of[6], (CH,), jnp.float32), 0.25, 1.75)
    shift_mid = scatter_about(streams_of[7], (CH,), 0.5, 3.0, ((0, 2),), jnp.float32)
    w_out = scatter_about(streams_of[8], (3, CH), CH ** -0.5, 0.25, ((1, 2),))
    blend_weight = jnp.clip(jnp.exp(jax.random.uniform(own_keys[9], (TILES, PIXELS), jnp.float32, math.log(0.25), math.log(4.0))), 0.25, 4.0)
    return {"latents": latents, "tile_order": tile_order, "w_in": w_in, "gain_in": gain_in, "shift_in": shift_in, "w_mid": w_mid, "gain_mid": gain_mid, "shift_mid": shift_mid, "w_out": w_out, "blend_weight": blend_weight}


EPSILON = 1e-06

def window_index(tile_id, tiles):
    slots = jnp.arange(TSIDE * TSIDE, dtype=jnp.int32)
    row = tile_id // GRID_X * STRIDE + slots // TSIDE
    col = tile_id % GRID_X * STRIDE + slots % TSIDE
    valid = (row < tiles // GRID_X * STRIDE) & (col < GRID_X * STRIDE)
    block = row // STRIDE * GRID_X + col // STRIDE
    index = block * (STRIDE * STRIDE) + row % STRIDE * STRIDE + col % STRIDE
    return (jnp.where(valid, index, 0).astype(jnp.int32), valid)

def causal_conv(values, weights, frames, side):
    pixels = side * side
    rows = jnp.arange(pixels, dtype=jnp.int32) // side
    cols = jnp.arange(pixels, dtype=jnp.int32) % side
    padded = jnp.concatenate([jnp.zeros((2,) + values.shape[1:], values.dtype), values], axis=0).astype(jnp.float32)
    weights = weights.astype(jnp.float32)
    total = jnp.zeros((frames, weights.shape[2], pixels), jnp.float32)
    for depth in range(3):
        window = padded[depth:depth + frames]
        for down in range(3):
            for across in range(3):
                offset = (down - 1) * side + (across - 1)
                inside = (rows + down - 1 >= 0) & (rows + down - 1 < side) & (cols + across - 1 >= 0) & (cols + across - 1 < side)
                moved = jnp.roll(window, -offset, axis=2)
                moved = jnp.where(inside[None, None, :], moved, jnp.zeros_like(moved))
                total = total + jnp.einsum('fcp,co->fop', moved, weights[9 * depth + 3 * down + across])
    return total

def normalize(values, gain, shift):
    frames, chans, pixels = values.shape
    width = CH // GROUPS
    grouped = values.reshape(frames, chans // width, width, pixels)
    count = frames * width * pixels
    mean = lax.optimization_barrier(jnp.sum(grouped, axis=(0, 2, 3))) / count
    variance = lax.optimization_barrier(jnp.sum(grouped * grouped, axis=(0, 2, 3))) / count - mean * mean
    scale = lax.rsqrt(variance + EPSILON)
    normed = (grouped - mean[None, :, None, None]) * scale[None, :, None, None]
    normed = normed.reshape(frames, chans, pixels) * gain[None, :, None] + shift[None, :, None]
    return jax.nn.silu(normed).astype(jnp.bfloat16)

def reference(latents, tile_order, w_in, gain_in, shift_in, w_mid, gain_mid, shift_mid, w_out, blend_weight):
    own = STRIDE * STRIDE
    blocks = latents.reshape(FRAMES, LATENT_CH, TILES, own)
    image = jnp.zeros_like(blocks).at[:, :, tile_order.astype(jnp.int32)].set(blocks)
    image = image.reshape(FRAMES, LATENT_CH, TILES * own)

    def accumulate(carry, tile_id):
        numer, denom = carry
        index, valid = window_index(tile_id, TILES)
        window = jnp.where(valid[None, None, :], jnp.take(image, index, axis=2), jnp.zeros((), jnp.bfloat16))
        first = causal_conv(window, w_in, FRAMES, TSIDE)
        hidden = normalize(first, gain_in, shift_in)
        second = causal_conv(hidden, w_mid, FRAMES, TSIDE)
        upper = normalize(second, gain_mid, shift_mid)
        color = jnp.einsum('oc,fcp->fop', w_out.astype(jnp.float32), upper.astype(jnp.float32))
        weight = jnp.where(valid, blend_weight[tile_id], jnp.float32(0.0))
        numer = numer.at[:, :, index].add(color * weight[None, None, :])
        denom = denom.at[index].add(weight)
        return ((numer, denom), None)
    start = (jnp.zeros((FRAMES, 3, TILES * own), jnp.float32), jnp.zeros((TILES * own,), jnp.float32))
    (numer, denom), _ = lax.scan(accumulate, start, jnp.arange(TILES, dtype=jnp.int32))
    return numer / denom[None, None, :]
```

```python
import jax
import jax.numpy as jnp
from jax import lax
from jax.experimental import pallas as pl
from jax.experimental.pallas import tpu as pltpu
from jax.sharding import PartitionSpec as P

CH = 512
GROUPS = 32
TSIDE = 16
STRIDE = 12
GRID_X = 4

EPSILON = 1e-06
LANES = 128


def shifted(value, axis, steps):
    count = lax.axis_size(axis)
    leading, last = (max(0, -steps), min(count, count - steps))
    return lax.ppermute(value, axis, [(source, source + steps) for source in range(leading, last)])


def window_index(tile_id, tiles):
    slots = jnp.arange(TSIDE * TSIDE, dtype=jnp.int32)
    row = tile_id // GRID_X * STRIDE + slots // TSIDE
    col = tile_id % GRID_X * STRIDE + slots % TSIDE
    valid = (row < tiles // GRID_X * STRIDE) & (col < GRID_X * STRIDE)
    block = row // STRIDE * GRID_X + col // STRIDE
    index = block * (STRIDE * STRIDE) + row % STRIDE * STRIDE + col % STRIDE
    return (jnp.where(valid, index, 0), valid)


def causal_conv(extended, weights, frames, side):
    pixels = side * side
    rows = jnp.arange(pixels, dtype=jnp.int32) // side
    cols = jnp.arange(pixels, dtype=jnp.int32) % side
    total = jnp.zeros((frames, weights.shape[2], pixels), jnp.float32)
    for depth in range(3):
        window = extended[depth : depth + frames]
        for down in range(3):
            for across in range(3):
                offset = (down - 1) * side + (across - 1)
                inside = (
                    (rows + down - 1 >= 0)
                    & (rows + down - 1 < side)
                    & (cols + across - 1 >= 0)
                    & (cols + across - 1 < side)
                )
                moved = jnp.roll(window, -offset, axis=2)
                moved = jnp.where(inside[None, None, :], moved, jnp.zeros_like(moved))
                total = total + jnp.einsum(
                    "fcp,co->fop",
                    moved,
                    weights[9 * depth + 3 * down + across],
                    preferred_element_type=jnp.float32,
                )
    return total


def with_history(values):
    frames = values.shape[0]
    earlier = shifted(values[frames - 2 :], "tm", 1)
    return jnp.concatenate([earlier, values], axis=0)


def normalize(values, gain, shift, total_frames):
    frames, chans, pixels = values.shape
    width = CH // GROUPS
    grouped = values.reshape(frames, chans // width, width, pixels)
    sums = jnp.sum(grouped, axis=(0, 2, 3))
    squares = jnp.sum(grouped * grouped, axis=(0, 2, 3))
    sums, squares = lax.psum((sums, squares), "tm")
    count = total_frames * width * pixels
    mean = sums / count
    variance = squares / count - mean * mean
    scale = lax.rsqrt(variance + EPSILON)
    normed = (grouped - mean[None, :, None, None]) * scale[None, :, None, None]
    normed = normed.reshape(frames, chans, pixels) * gain[None, :, None] + shift[None, :, None]
    return jax.nn.silu(normed).astype(jnp.bfloat16)


def spread(color, weight, index, total_pixels):
    numer = (
        jnp.zeros((color.shape[0], 3, total_pixels), jnp.float32)
        .at[:, :, index]
        .add(color * weight[None, None, :])
    )
    denom = jnp.zeros((total_pixels,), jnp.float32).at[index].add(weight)
    return (numer, denom)


def route_owned(numer, denom, tile_id, own):
    frames = numer.shape[0]
    margin = (GRID_X + 1) * own
    numer_wide = jnp.concatenate([numer, jnp.zeros((frames, 3, margin), jnp.float32)], axis=2)
    denom_wide = jnp.concatenate([denom, jnp.zeros((margin,), jnp.float32)], axis=0)
    first_pixel = tile_id * own

    def block_at(offset):
        start_pixel = first_pixel + offset * own
        return (
            lax.dynamic_slice_in_dim(numer_wide, start_pixel, own, 2),
            lax.dynamic_slice_in_dim(denom_wide, start_pixel, own, 0),
        )

    owned_numer, owned_denom = block_at(0)
    for offset in (1, GRID_X, GRID_X + 1):
        piece_numer, piece_denom = block_at(offset)
        got_numer, got_denom = shifted((piece_numer, piece_denom), "tile", offset)
        owned_numer = owned_numer + got_numer
        owned_denom = owned_denom + got_denom
    return (owned_numer, owned_denom)


def general_body(
    latents, tile_order, w_in, gain_in, shift_in, w_mid, gain_mid, shift_mid, w_out, blend_weight
):
    frames = latents.shape[0]
    total_frames = frames * lax.axis_size("tm")
    tiles = tile_order.shape[0]
    own = STRIDE * STRIDE
    total_pixels = tiles * own
    tile_id = lax.axis_index("tile")
    index, valid = window_index(tile_id, tiles)
    whole = lax.all_gather(latents, "tile", axis=2, tiled=True)
    blocks = whole.reshape(frames, whole.shape[1], tiles, own)
    image = (
        jnp.zeros_like(blocks)
        .at[:, :, tile_order]
        .set(blocks)
        .reshape(frames, whole.shape[1], total_pixels)
    )
    window = jnp.where(
        valid[None, None, :], jnp.take(image, index, axis=2), jnp.zeros((), jnp.bfloat16)
    )
    first = causal_conv(with_history(window), w_in, frames, TSIDE)
    hidden = normalize(first, gain_in, shift_in, total_frames)
    second = causal_conv(
        lax.all_gather(with_history(hidden), "chan", axis=1, tiled=True), w_mid, frames, TSIDE
    )
    upper = normalize(second, gain_mid, shift_mid, total_frames)
    color = jnp.einsum("oc,fcp->fop", w_out, upper, preferred_element_type=jnp.float32)
    weight = jnp.where(valid, blend_weight[tile_id], jnp.float32(0.0))
    numer, denom = spread(color, weight, index, total_pixels)
    numer, denom = route_owned(numer, denom, tile_id, own)
    numer = lax.psum(numer, "chan")
    return numer / denom[None, None, :]


def block_cases(tiles):
    downs = (0, 1) if tiles // GRID_X > 1 else (0,)
    return [(down, across) for down in downs for across in (0, 1)]


def group_affine(sums, squares, gain, shift, count):
    lanes = sums.shape[1]
    width = CH // GROUPS
    same = lax.broadcasted_iota(jnp.int32, (lanes, lanes), 0) // width == (
        lax.broadcasted_iota(jnp.int32, (lanes, lanes), 1) // width
    )
    total = jnp.dot(
        jnp.concatenate([sums, squares], axis=0),
        jnp.where(same, 1.0, 0.0).astype(jnp.float32),
        precision=lax.Precision.HIGHEST,
        preferred_element_type=jnp.float32,
    )
    mean = jnp.sum(total[:8], axis=0, keepdims=True) / count
    variance = jnp.sum(total[8:], axis=0, keepdims=True) / count - mean * mean
    scale = gain * lax.rsqrt(variance + EPSILON)
    return 0.5 * scale, 0.5 * (shift - mean * scale)


def silu_of_half(half):
    return half + half * jnp.tanh(half)


def fold(values):
    rows, lanes = values.shape
    return jnp.sum(values.reshape(rows // 8, 8, lanes), axis=0)


def decode_kernel(
    order_ref,
    blocks_ref,
    w_in_ref,
    affine_in_ref,
    w_mid_ref,
    gain_mid_ref,
    shift_mid_ref,
    w_out_ref,
    blend_ref,
    pieces_ref,
    denom_ref,
    taps,
    first,
    hidden,
    weights,
    partial,
    sems,
):
    tiles, rows_in, own = blocks_ref.shape
    shares, depth_in, wide = w_in_ref.shape
    frames = first.shape[0]
    pixels = TSIDE * TSIDE
    latent = rows_in // frames
    lanes = partial.shape[3]
    spans = frames // pieces_ref.shape[2]
    tile_id = lax.axis_index("tile")
    mine = lax.axis_index("tm")
    cases = block_cases(tiles)

    copies = []
    for a in range(3):
        for b in range(3):
            for e in range(3):
                tap = 9 * a + 3 * b + e
                copy = pltpu.make_async_copy(
                    w_mid_ref.at[tap, :, pl.ds(pl.multiple_of(mine * lanes, LANES), lanes)],
                    weights.at[pl.ds(b * CH, CH), pl.ds((3 * a + e) * lanes, lanes)],
                    sems.at[tap],
                )
                copy.start()
                copies.append(copy)

    tile_row, tile_col = tile_id // GRID_X, tile_id % GRID_X
    chosen = []
    for down, across in cases:
        inside = (tile_row + down < tiles // GRID_X) & (tile_col + across < GRID_X)
        wanted = tile_id + down * GRID_X + across
        place = jnp.int32(0)
        for d in range(tiles):
            place = place + jnp.where(order_ref[d] == wanted, jnp.int32(d), jnp.int32(0))
        block = blocks_ref[place]
        chosen.append(jnp.where(inside, block, jnp.zeros_like(block)))
    taps[0:2] = jnp.zeros((2,) + taps.shape[1:], taps.dtype)
    slot = lax.broadcasted_iota(jnp.int32, (1, pixels), 1)
    source = lax.broadcasted_iota(jnp.int32, (own, pixels), 0)
    for b in range(3):
        for e in range(3):
            up, along = slot // TSIDE + b - 1, slot % TSIDE + e - 1
            window = jnp.zeros((rows_in, pixels), jnp.float32)
            for (down, across), block in zip(cases, chosen):
                u, v = up - down * STRIDE, along - across * STRIDE
                high = STRIDE if down == 0 else TSIDE - STRIDE
                far = STRIDE if across == 0 else TSIDE - STRIDE
                good = (u >= 0) & (u < high) & (v >= 0) & (v < far)
                pick = source == jnp.where(good, u * STRIDE + v, -1)
                window = window + jnp.dot(
                    block,
                    jnp.where(pick, 1.0, 0.0).astype(jnp.bfloat16),
                    preferred_element_type=jnp.float32,
                )
            taps[2:, 3 * b + e] = window.astype(jnp.bfloat16).reshape(frames, latent, pixels)

    sums = [jnp.zeros((8, wide), jnp.float32) for _ in range(shares)]
    squares = [jnp.zeros((8, wide), jnp.float32) for _ in range(shares)]
    for f in range(frames):
        patch = taps[f : f + 3].reshape(depth_in, pixels)
        for s in range(shares):
            value = lax.dot_general(
                patch, w_in_ref[s], (((0,), (0,)), ((), ())), preferred_element_type=jnp.float32
            )
            first[f, :, s * wide : (s + 1) * wide] = value
            sums[s] = sums[s] + fold(value)
            squares[s] = squares[s] + fold(value * value)
    count = frames * (CH // GROUPS) * pixels
    affine = [
        group_affine(
            sums[s], squares[s], affine_in_ref[s, 0:1, :], affine_in_ref[s, 1:2, :], count
        )
        for s in range(shares)
    ]

    edge = jnp.zeros((TSIDE, CH), jnp.bfloat16)
    for f in range(frames):
        hidden[f, 0:TSIDE] = edge
        hidden[f, TSIDE + pixels : 2 * TSIDE + pixels] = edge
        for s in range(shares):
            scale, bias = affine[s]
            value = first[f, :, s * wide : (s + 1) * wide] * scale + bias
            hidden[f, TSIDE : TSIDE + pixels, s * wide : (s + 1) * wide] = silu_of_half(
                value
            ).astype(jnp.bfloat16)

    for copy in copies:
        copy.wait()

    partial[...] = jnp.zeros_like(partial)

    def convolve(start, several, depth_taps):
        lhs = jnp.concatenate(
            [
                hidden[pl.ds(start, several), b * TSIDE : b * TSIDE + pixels].reshape(
                    several * pixels, CH
                )
                for b in range(3)
            ],
            axis=1,
        )
        low = depth_taps[0] * 3 * lanes
        product = jnp.dot(lhs, weights[:, low:], preferred_element_type=jnp.float32)
        for a in depth_taps:
            for e in range(3):
                at = (3 * a + e) * lanes - low
                target = pl.ds(start + 2 - a, several)
                partial[e, target] += product[:, at : at + lanes].reshape(several, pixels, lanes)

    together = 2
    full = (frames - 2) // together

    def step(index, carry):
        convolve(index * together, together, (0, 1, 2))
        return carry

    lax.fori_loop(0, full, step, 0)
    for f in range(full * together, frames):
        convolve(f, 1, tuple(a for a in range(3) if f + 2 - a < frames))

    column = lax.broadcasted_iota(jnp.int32, (pixels, lanes), 0) % TSIDE
    total = jnp.zeros((8, lanes), jnp.float32)
    total_squares = jnp.zeros((8, lanes), jnp.float32)
    for f in range(frames):
        left = jnp.where(column == 0, 0.0, pltpu.roll(partial[0, f], 1, 0))
        right = jnp.where(column == TSIDE - 1, 0.0, pltpu.roll(partial[2, f], pixels - 1, 0))
        value = partial[1, f] + left + right
        partial[1, f] = value
        total = total + fold(value)
        total_squares = total_squares + fold(value * value)
    part = pl.ds(pl.multiple_of(mine * lanes, LANES), lanes)
    scale, bias = group_affine(
        total, total_squares, gain_mid_ref[:, part], shift_mid_ref[:, part], count
    )
    blend = blend_ref[pl.ds(tile_id, 1), :]
    blend = jnp.where(
        (tile_row * STRIDE + slot // TSIDE < tiles // GRID_X * STRIDE)
        & (tile_col * STRIDE + slot % TSIDE < GRID_X * STRIDE),
        blend,
        0.0,
    )
    colors = []
    for f in range(frames):
        upper = silu_of_half(partial[1, f] * scale + bias).astype(jnp.bfloat16)
        color = lax.dot_general(
            w_out_ref[:, part],
            upper,
            (((1,), (1,)), ((), ())),
            preferred_element_type=jnp.float32,
        )
        colors.append(color * blend)
    colors = jnp.concatenate(colors, axis=0)

    slot_in = lax.broadcasted_iota(jnp.int32, (pixels, own), 0)
    pixel = lax.broadcasted_iota(jnp.int32, (pixels, own), 1)
    denom = jnp.zeros((8, own), jnp.float32)
    for number, (down, across) in enumerate(cases):
        u, v = slot_in // TSIDE - down * STRIDE, slot_in % TSIDE - across * STRIDE
        good = (u >= 0) & (u < STRIDE) & (v >= 0) & (v < STRIDE) & (u * STRIDE + v == pixel)
        pick = jnp.where(good, 1.0, 0.0).astype(jnp.float32)
        piece = jnp.dot(
            colors, pick, precision=lax.Precision.HIGHEST, preferred_element_type=jnp.float32
        )
        piece = piece.reshape(spans, frames // spans, 8, own)
        for dest in range(pieces_ref.shape[0]):
            pieces_ref[dest, number] = piece[dest % spans]
        inside = (tile_row >= down) & (tile_col >= across)
        other = jnp.maximum(tile_id - down * GRID_X - across, 0)
        weight = jnp.where(inside, blend_ref[pl.ds(other, 1), :], 0.0)
        denom = denom + jnp.dot(
            jnp.broadcast_to(weight, (8, pixels)),
            pick,
            precision=lax.Precision.HIGHEST,
            preferred_element_type=jnp.float32,
        )
    denom_ref[...] = denom


def exchange_weights(w_in, gain_in, shift_in):
    shares = lax.axis_size("chan")
    taps, latent, wide = w_in.shape
    table = jnp.stack([gain_in, shift_in])
    high = lax.reduce_precision(table, 8, 7)
    low = lax.reduce_precision(table - high, 8, 7)
    message = jnp.concatenate(
        [
            w_in.reshape(taps * latent, wide),
            high.astype(jnp.bfloat16),
            low.astype(jnp.bfloat16),
        ],
        axis=0,
    )
    got = [message]
    for turn in range(1, shares):
        got.append(
            lax.ppermute(message, "chan", [((d + turn) % shares, d) for d in range(shares)])
        )
    mine = lax.axis_index("chan")
    whole = jnp.stack(got)
    whole = jnp.roll(whole, mine, axis=0) if shares > 2 else jnp.where(mine == 0, whole, whole[::-1])
    depth = taps * latent
    table = whole[:, depth : depth + 2].astype(jnp.float32) + whole[:, depth + 2 :].astype(
        jnp.float32
    )
    return whole[:, :depth], table


def lanes_body(
    latents, tile_order, w_in, gain_in, shift_in, w_mid, gain_mid, shift_mid, w_out, blend_weight
):
    own_frames, latent, own = latents.shape
    spans = lax.axis_size("tm")
    shares = lax.axis_size("chan")
    frames = own_frames * spans
    tiles = tile_order.shape[0]
    wide = w_in.shape[2]
    lanes = wide // spans
    pixels = TSIDE * TSIDE
    cases = block_cases(tiles)

    sent = jnp.broadcast_to(
        latents.reshape(1, own_frames * latent, own), (tiles * spans, own_frames * latent, own)
    )
    blocks = lax.all_to_all(sent, ("tile", "tm"), 0, 0, tiled=True)
    blocks = blocks.reshape(tiles, frames * latent, own)
    w_in_all, affine_in = exchange_weights(w_in, gain_in, shift_in)

    vmem = pl.BlockSpec(memory_space=pltpu.VMEM)
    pieces, denom = pl.pallas_call(
        decode_kernel,
        out_shape=(
            jax.ShapeDtypeStruct((shares * spans, len(cases), own_frames, 8, own), jnp.float32),
            jax.ShapeDtypeStruct((8, own), jnp.float32),
        ),
        in_specs=[
            pl.BlockSpec(memory_space=pltpu.SMEM),
            vmem,
            vmem,
            vmem,
            pl.BlockSpec(memory_space=pl.ANY),
            vmem,
            vmem,
            vmem,
            vmem,
        ],
        out_specs=(vmem, vmem),
        scratch_shapes=[
            pltpu.VMEM((frames + 2, 9, latent, pixels), jnp.bfloat16),
            pltpu.VMEM((frames, pixels, CH), jnp.float32),
            pltpu.VMEM((frames, pixels + 2 * TSIDE, CH), jnp.bfloat16),
            pltpu.VMEM((3 * CH, 9 * lanes), jnp.bfloat16),
            pltpu.VMEM((3, frames, pixels, lanes), jnp.float32),
            pltpu.SemaphoreType.DMA((27,)),
        ],
        compiler_params=pltpu.CompilerParams(vmem_limit_bytes=48 * 1024 * 1024),
        cost_estimate=pl.CostEstimate(
            flops=2 * frames * pixels * 27 * CH * lanes, bytes_accessed=8_000_000, transcendentals=0
        ),
    )(
        tile_order,
        blocks,
        w_in_all,
        affine_in,
        w_mid,
        gain_mid.reshape(1, wide),
        shift_mid.reshape(1, wide),
        jnp.pad(w_out, ((0, 5), (0, 0))),
        blend_weight,
    )
    got = jnp.sum(lax.all_to_all(pieces, ("chan", "tm"), 0, 0, tiled=True), axis=0)
    numer = got[0]
    for number, (down, across) in enumerate(cases):
        steps = down * GRID_X + across
        if steps and steps < tiles:
            numer = numer + shifted(got[number], "tile", steps)
    return numer[:, :3] / denom[0][None, None, :]


def solution(mesh):
    placed = (
        P("tm", "groups", "tile"),
        P("groups"),
        P(None, None, "chan"),
        P("chan"),
        P("chan"),
        P(None, None, "chan"),
        P("chan"),
        P("chan"),
        P(None, "chan"),
        P("groups", None),
    )
    whole_lanes = CH % (mesh.shape["chan"] * mesh.shape["tm"] * LANES) == 0
    return jax.shard_map(
        lanes_body if whole_lanes else general_body,
        mesh=mesh,
        in_specs=placed,
        out_specs=P("tm", "groups", "tile"),
        check_vma=False,
    )
```

```python
import functools

import jax
import jax.numpy as jnp
from jax import lax
from jax.experimental import pallas as pl
from jax.experimental.pallas import tpu as pltpu
from jax.sharding import PartitionSpec as P

CH = 512
GROUPS = 32
TSIDE = 16
STRIDE = 12
GRID_X = 4

EPSILON = 1e-06
LANES = 128
PACKED = 16

W_OUT_ROW = 0
GAIN_ROW = 8
SHIFT_ROW = 9
ORDER_ROW = 10
LATENT_ROW = 16


def shifted(value, axis, steps):
    count = lax.axis_size(axis)
    leading, last = (max(0, -steps), min(count, count - steps))
    return lax.ppermute(value, axis, [(source, source + steps) for source in range(leading, last)])


def window_index(tile_id, tiles):
    slots = jnp.arange(TSIDE * TSIDE, dtype=jnp.int32)
    row = tile_id // GRID_X * STRIDE + slots // TSIDE
    col = tile_id % GRID_X * STRIDE + slots % TSIDE
    valid = (row < tiles // GRID_X * STRIDE) & (col < GRID_X * STRIDE)
    block = row // STRIDE * GRID_X + col // STRIDE
    index = block * (STRIDE * STRIDE) + row % STRIDE * STRIDE + col % STRIDE
    return (jnp.where(valid, index, 0), valid)


def causal_conv(extended, weights, frames, side):
    pixels = side * side
    rows = jnp.arange(pixels, dtype=jnp.int32) // side
    cols = jnp.arange(pixels, dtype=jnp.int32) % side
    total = jnp.zeros((frames, weights.shape[2], pixels), jnp.float32)
    for depth in range(3):
        window = extended[depth : depth + frames]
        for down in range(3):
            for across in range(3):
                offset = (down - 1) * side + (across - 1)
                inside = (
                    (rows + down - 1 >= 0)
                    & (rows + down - 1 < side)
                    & (cols + across - 1 >= 0)
                    & (cols + across - 1 < side)
                )
                moved = jnp.roll(window, -offset, axis=2)
                moved = jnp.where(inside[None, None, :], moved, jnp.zeros_like(moved))
                total = total + jnp.einsum(
                    "fcp,co->fop",
                    moved,
                    weights[9 * depth + 3 * down + across],
                    preferred_element_type=jnp.float32,
                )
    return total


def with_history(values):
    frames = values.shape[0]
    earlier = shifted(values[frames - 2 :], "tm", 1)
    return jnp.concatenate([earlier, values], axis=0)


def normalize(values, gain, shift, total_frames):
    frames, chans, pixels = values.shape
    width = CH // GROUPS
    grouped = values.reshape(frames, chans // width, width, pixels)
    sums = jnp.sum(grouped, axis=(0, 2, 3))
    squares = jnp.sum(grouped * grouped, axis=(0, 2, 3))
    sums, squares = lax.psum((sums, squares), "tm")
    count = total_frames * width * pixels
    mean = sums / count
    variance = squares / count - mean * mean
    scale = lax.rsqrt(variance + EPSILON)
    normed = (grouped - mean[None, :, None, None]) * scale[None, :, None, None]
    normed = normed.reshape(frames, chans, pixels) * gain[None, :, None] + shift[None, :, None]
    return jax.nn.silu(normed).astype(jnp.bfloat16)


def spread(color, weight, index, total_pixels):
    numer = (
        jnp.zeros((color.shape[0], 3, total_pixels), jnp.float32)
        .at[:, :, index]
        .add(color * weight[None, None, :])
    )
    denom = jnp.zeros((total_pixels,), jnp.float32).at[index].add(weight)
    return (numer, denom)


def route_owned(numer, denom, tile_id, own):
    frames = numer.shape[0]
    margin = (GRID_X + 1) * own
    numer_wide = jnp.concatenate([numer, jnp.zeros((frames, 3, margin), jnp.float32)], axis=2)
    denom_wide = jnp.concatenate([denom, jnp.zeros((margin,), jnp.float32)], axis=0)
    first_pixel = tile_id * own

    def block_at(offset):
        start_pixel = first_pixel + offset * own
        return (
            lax.dynamic_slice_in_dim(numer_wide, start_pixel, own, 2),
            lax.dynamic_slice_in_dim(denom_wide, start_pixel, own, 0),
        )

    owned_numer, owned_denom = block_at(0)
    for offset in (1, GRID_X, GRID_X + 1):
        piece_numer, piece_denom = block_at(offset)
        got_numer, got_denom = shifted((piece_numer, piece_denom), "tile", offset)
        owned_numer = owned_numer + got_numer
        owned_denom = owned_denom + got_denom
    return (owned_numer, owned_denom)


def general_body(
    latents, tile_order, w_in, gain_in, shift_in, w_mid, gain_mid, shift_mid, w_out, blend_weight
):
    frames = latents.shape[0]
    total_frames = frames * lax.axis_size("tm")
    tiles = tile_order.shape[0]
    own = STRIDE * STRIDE
    total_pixels = tiles * own
    tile_id = lax.axis_index("tile")
    index, valid = window_index(tile_id, tiles)
    whole = lax.all_gather(latents, "tile", axis=2, tiled=True)
    blocks = whole.reshape(frames, whole.shape[1], tiles, own)
    image = (
        jnp.zeros_like(blocks)
        .at[:, :, tile_order]
        .set(blocks)
        .reshape(frames, whole.shape[1], total_pixels)
    )
    window = jnp.where(
        valid[None, None, :], jnp.take(image, index, axis=2), jnp.zeros((), jnp.bfloat16)
    )
    first = causal_conv(with_history(window), w_in, frames, TSIDE)
    hidden = normalize(first, gain_in, shift_in, total_frames)
    second = causal_conv(
        lax.all_gather(with_history(hidden), "chan", axis=1, tiled=True), w_mid, frames, TSIDE
    )
    upper = normalize(second, gain_mid, shift_mid, total_frames)
    color = jnp.einsum("oc,fcp->fop", w_out, upper, preferred_element_type=jnp.float32)
    weight = jnp.where(valid, blend_weight[tile_id], jnp.float32(0.0))
    numer, denom = spread(color, weight, index, total_pixels)
    numer, denom = route_owned(numer, denom, tile_id, own)
    numer = lax.psum(numer, "chan")
    return numer / denom[None, None, :]


def block_cases(tiles):
    downs = (0, 1) if tiles // GRID_X > 1 else (0,)
    return [(down, across) for down in downs for across in (0, 1)]


def group_affine(sums, squares, gain, shift, count):
    lanes = sums.shape[1]
    width = CH // GROUPS
    same = lax.broadcasted_iota(jnp.int32, (lanes, lanes), 0) // width == (
        lax.broadcasted_iota(jnp.int32, (lanes, lanes), 1) // width
    )
    total = jnp.dot(
        jnp.concatenate([sums, squares], axis=0),
        jnp.where(same, 1.0, 0.0).astype(jnp.float32),
        precision=lax.Precision.HIGHEST,
        preferred_element_type=jnp.float32,
    )
    mean = jnp.sum(total[:8], axis=0, keepdims=True) / count
    variance = jnp.sum(total[8:], axis=0, keepdims=True) / count - mean * mean
    scale = gain * lax.rsqrt(variance + EPSILON)
    return 0.5 * scale, 0.5 * (shift - mean * scale)


def silu_of_half(half):
    return half + half * jnp.tanh(half)


def fold(values):
    rows, lanes = values.shape
    return jnp.sum(values.reshape(rows // 8, 8, lanes), axis=0)


def decode_kernel(
    tiles,
    spans,
    shares,
    *refs,
):
    cases = block_cases(tiles)
    refs = list(refs)

    def take(number):
        taken = refs[:number]
        del refs[:number]
        return taken

    w_mid_ref, table_ref = take(2)
    latent_refs = take(tiles * spans - 1)
    w_in_refs = take(shares)
    piece_refs = take(spans * len(cases))
    (denom_ref,) = take(1)
    chosen, taps, first, hidden, weights, partial, sems = take(7)

    rows_own, own = latent_refs[0].shape
    rows_in = rows_own * spans
    wide = w_in_refs[0].shape[1]
    depth_in = w_in_refs[0].shape[0] - PACKED
    frames = first.shape[1]
    own_frames = frames // spans
    pixels = TSIDE * TSIDE
    latent = rows_in // frames
    lanes = partial.shape[3]
    tile_id = lax.axis_index("tile")
    mine = lax.axis_index("tm")
    chan_id = lax.axis_index("chan")

    copies = []
    for a in range(3):
        for b in range(3):
            for e in range(3):
                tap = 9 * a + 3 * b + e
                copy = pltpu.make_async_copy(
                    w_mid_ref.at[tap, :, pl.ds(pl.multiple_of(mine * lanes, LANES), lanes)],
                    weights.at[pl.ds(b * CH, CH), pl.ds((3 * a + e) * lanes, lanes)],
                    sems.at[tap],
                )
                copy.start()
                copies.append(copy)

    tile_row, tile_col = tile_id // GRID_X, tile_id % GRID_X
    taps[0:2] = jnp.zeros((2,) + taps.shape[1:], taps.dtype)
    order = table_ref[ORDER_ROW : ORDER_ROW + 1, :]
    block_number = lax.broadcasted_iota(jnp.int32, order.shape, 1)
    for number, (down, across) in enumerate(cases):
        inside = (tile_row + down < tiles // GRID_X) & (tile_col + across < GRID_X)
        wanted = tile_id + down * GRID_X + across
        found = (order == wanted.astype(jnp.float32)) & (block_number < tiles)
        place = jnp.sum(jnp.where(found, block_number.astype(jnp.float32), 0.0))
        turn = (tile_id - place.astype(jnp.int32) + tiles) % tiles
        for steps in range(tiles):

            @pl.when(inside & (turn == steps))
            def _():
                for swap in range(spans):
                    if steps or swap:
                        block = latent_refs[steps * spans + swap - 1][...]
                    else:
                        block = table_ref[LATENT_ROW : LATENT_ROW + rows_own, :own]
                    chosen[number, (mine + swap) % spans] = block.astype(jnp.bfloat16)

        @pl.when(jnp.logical_not(inside))
        def _():
            chosen[number] = jnp.zeros(chosen.shape[1:], chosen.dtype)

    slot = lax.broadcasted_iota(jnp.int32, (1, pixels), 1)
    source = lax.broadcasted_iota(jnp.int32, (own, pixels), 0)
    for b in range(3):
        for e in range(3):
            up, along = slot // TSIDE + b - 1, slot % TSIDE + e - 1
            window = jnp.zeros((rows_in, pixels), jnp.float32)
            for number, (down, across) in enumerate(cases):
                block = chosen[number].reshape(rows_in, own)
                u, v = up - down * STRIDE, along - across * STRIDE
                high = STRIDE if down == 0 else TSIDE - STRIDE
                far = STRIDE if across == 0 else TSIDE - STRIDE
                good = (u >= 0) & (u < high) & (v >= 0) & (v < far)
                pick = source == jnp.where(good, u * STRIDE + v, -1)
                window = window + jnp.dot(
                    block,
                    jnp.where(pick, 1.0, 0.0).astype(jnp.bfloat16),
                    preferred_element_type=jnp.float32,
                )
            taps[2:, 3 * b + e] = window.astype(jnp.bfloat16).reshape(frames, latent, pixels)

    sums = [jnp.zeros((8, wide), jnp.float32) for _ in range(shares)]
    squares = [jnp.zeros((8, wide), jnp.float32) for _ in range(shares)]
    for f in range(frames):
        patch = taps[f : f + 3].reshape(depth_in, pixels)
        for s in range(shares):
            value = lax.dot_general(
                patch,
                w_in_refs[s][:depth_in],
                (((0,), (0,)), ((), ())),
                preferred_element_type=jnp.float32,
            )
            first[s, f] = value
            sums[s] = sums[s] + fold(value)
            squares[s] = squares[s] + fold(value * value)
    count = frames * (CH // GROUPS) * pixels
    affine = []
    for s in range(shares):
        table = w_in_refs[s][depth_in : depth_in + PACKED].astype(jnp.float32)
        table = table[0:2] + table[2:4]
        affine.append(group_affine(sums[s], squares[s], table[0:1], table[1:2], count))

    edge = jnp.zeros((TSIDE, CH), jnp.bfloat16)
    for f in range(frames):
        hidden[f, 0:TSIDE] = edge
        hidden[f, TSIDE + pixels : 2 * TSIDE + pixels] = edge
        for s in range(shares):
            scale, bias = affine[s]
            value = silu_of_half(first[s, f] * scale + bias).astype(jnp.bfloat16)
            channels = pl.ds(pl.multiple_of((chan_id + s) % shares * wide, LANES), wide)
            hidden[f, TSIDE : TSIDE + pixels, channels] = value

    for copy in copies:
        copy.wait()

    partial[...] = jnp.zeros_like(partial)

    def convolve(start, several, depth_taps):
        lhs = jnp.concatenate(
            [
                hidden[pl.ds(start, several), b * TSIDE : b * TSIDE + pixels].reshape(
                    several * pixels, CH
                )
                for b in range(3)
            ],
            axis=1,
        )
        low = depth_taps[0] * 3 * lanes
        product = jnp.dot(lhs, weights[:, low:], preferred_element_type=jnp.float32)
        for a in depth_taps:
            for e in range(3):
                at = (3 * a + e) * lanes - low
                target = pl.ds(start + 2 - a, several)
                partial[e, target] += product[:, at : at + lanes].reshape(several, pixels, lanes)

    together = 2
    full = (frames - 2) // together

    def step(index, carry):
        convolve(index * together, together, (0, 1, 2))
        return carry

    lax.fori_loop(0, full, step, 0)
    for f in range(full * together, frames):
        convolve(f, 1, tuple(a for a in range(3) if f + 2 - a < frames))

    column = lax.broadcasted_iota(jnp.int32, (pixels, lanes), 0) % TSIDE
    total = jnp.zeros((8, lanes), jnp.float32)
    total_squares = jnp.zeros((8, lanes), jnp.float32)
    for f in range(frames):
        left = jnp.where(column == 0, 0.0, pltpu.roll(partial[0, f], 1, 0))
        right = jnp.where(column == TSIDE - 1, 0.0, pltpu.roll(partial[2, f], pixels - 1, 0))
        value = partial[1, f] + left + right
        partial[1, f] = value
        total = total + fold(value)
        total_squares = total_squares + fold(value * value)
    part = pl.ds(pl.multiple_of(mine * lanes, LANES), lanes)
    scale, bias = group_affine(
        total, total_squares, table_ref[GAIN_ROW : GAIN_ROW + 1, part], table_ref[SHIFT_ROW : SHIFT_ROW + 1, part], count
    )
    blend_row = LATENT_ROW + rows_own
    blend = table_ref[pl.ds(blend_row + tile_id, 1), :]
    blend = jnp.where(
        (tile_row * STRIDE + slot // TSIDE < tiles // GRID_X * STRIDE)
        & (tile_col * STRIDE + slot % TSIDE < GRID_X * STRIDE),
        blend,
        0.0,
    )
    w_out = table_ref[W_OUT_ROW : W_OUT_ROW + 8, part].astype(jnp.bfloat16)
    colors = []
    for f in range(frames):
        upper = silu_of_half(partial[1, f] * scale + bias).astype(jnp.bfloat16)
        color = lax.dot_general(
            w_out,
            upper,
            (((1,), (1,)), ((), ())),
            preferred_element_type=jnp.float32,
        )
        colors.append(color * blend)
    colors = jnp.concatenate(colors, axis=0)

    slot_in = lax.broadcasted_iota(jnp.int32, (pixels, own), 0)
    pixel = lax.broadcasted_iota(jnp.int32, (pixels, own), 1)
    denom = jnp.zeros((8, own), jnp.float32)
    for number, (down, across) in enumerate(cases):
        u, v = slot_in // TSIDE - down * STRIDE, slot_in % TSIDE - across * STRIDE
        good = (u >= 0) & (u < STRIDE) & (v >= 0) & (v < STRIDE) & (u * STRIDE + v == pixel)
        pick = jnp.where(good, 1.0, 0.0).astype(jnp.float32)
        piece = jnp.dot(
            colors, pick, precision=lax.Precision.HIGHEST, preferred_element_type=jnp.float32
        )
        for f in range(frames):
            for swap in range(spans):

                @pl.when((mine + swap) % spans == f // own_frames)
                def _():
                    for o in range(3):
                        piece_refs[swap * len(cases) + number][
                            o, f % own_frames : f % own_frames + 1, :
                        ] = piece[8 * f + o : 8 * f + o + 1]

        inside = (tile_row >= down) & (tile_col >= across)
        other = jnp.maximum(tile_id - down * GRID_X - across, 0)
        weight = jnp.where(inside, table_ref[pl.ds(blend_row + other, 1), :], 0.0)
        denom = denom + jnp.dot(
            jnp.broadcast_to(weight, (8, pixels)),
            pick,
            precision=lax.Precision.HIGHEST,
            preferred_element_type=jnp.float32,
        )
    denom_ref[...] = denom


def exchange_weights(w_in, gain_in, shift_in):
    shares = lax.axis_size("chan")
    taps, latent, wide = w_in.shape
    table = jnp.stack([gain_in, shift_in])
    high = lax.reduce_precision(table, 8, 7)
    low = lax.reduce_precision(table - high, 8, 7)
    message = jnp.concatenate(
        [
            w_in.reshape(taps * latent, wide),
            high.astype(jnp.bfloat16),
            low.astype(jnp.bfloat16),
            jnp.zeros((PACKED - 4, wide), jnp.bfloat16),
        ],
        axis=0,
    )
    return [message] + [
        lax.ppermute(message, "chan", [((d + turn) % shares, d) for d in range(shares)])
        for turn in range(1, shares)
    ]


def exchange_latents(latents):
    tiles, spans = lax.axis_size("tile"), lax.axis_size("tm")
    got = []
    for steps in range(tiles):
        for swap in range(spans):
            pairs = [
                (t * spans + m, (t + steps) % tiles * spans + (m - swap) % spans)
                for t in range(tiles)
                for m in range(spans)
            ]
            moved = steps or swap
            got.append(lax.ppermute(latents, ("tile", "tm"), pairs) if moved else latents)
    return got


def collect(pieces, cases):
    tiles, shares, spans = (lax.axis_size(name) for name in ("tile", "chan", "tm"))
    numer = pieces[0]
    for number, (down, across) in enumerate(cases):
        steps = down * GRID_X + across
        for turn in range(shares):
            for swap in range(spans):
                if steps >= tiles or not (steps or turn or swap):
                    continue
                pairs = [
                    (
                        (t * shares + c) * spans + m,
                        ((t + steps) * shares + (c + turn) % shares) * spans + (m + swap) % spans,
                    )
                    for t in range(tiles - steps)
                    for c in range(shares)
                    for m in range(spans)
                ]
                numer = numer + lax.ppermute(
                    pieces[swap * len(cases) + number], ("tile", "chan", "tm"), pairs
                )
    return numer


def small_table(latents, tile_order, gain_mid, shift_mid, w_out, blend_weight):
    lanes = gain_mid.shape[0]

    def rows(value, count):
        value = value.astype(jnp.float32)
        value = value.reshape(-1, value.shape[-1])
        return jnp.pad(value, ((0, count - value.shape[0]), (0, lanes - value.shape[1])))

    tiles = tile_order.shape[0]
    return jnp.concatenate(
        [
            rows(w_out, GAIN_ROW - W_OUT_ROW),
            rows(gain_mid, 1),
            rows(shift_mid, 1),
            rows(tile_order, LATENT_ROW - ORDER_ROW),
            rows(latents, latents.shape[0]),
            rows(blend_weight, (tiles + 7) // 8 * 8),
        ],
        axis=0,
    )


def lanes_body(
    latents, tile_order, w_in, gain_in, shift_in, w_mid, gain_mid, shift_mid, w_out, blend_weight
):
    own_frames, latent, own = latents.shape
    spans = lax.axis_size("tm")
    shares = lax.axis_size("chan")
    frames = own_frames * spans
    tiles = tile_order.shape[0]
    wide = w_in.shape[2]
    lanes = wide // spans
    pixels = TSIDE * TSIDE
    cases = block_cases(tiles)

    latents = latents.reshape(own_frames * latent, own)
    w_in_all = exchange_weights(w_in, gain_in, shift_in)
    latents_all = exchange_latents(latents)
    table = small_table(latents, tile_order, gain_mid, shift_mid, w_out, blend_weight)

    vmem = pl.BlockSpec(memory_space=pltpu.VMEM)
    *pieces, denom = pl.pallas_call(
        functools.partial(decode_kernel, tiles, spans, shares),
        out_shape=[jax.ShapeDtypeStruct((3, own_frames, own), jnp.float32)] * (spans * len(cases))
        + [jax.ShapeDtypeStruct((8, own), jnp.float32)],
        in_specs=[pl.BlockSpec(memory_space=pl.ANY)] + [vmem] * (tiles * spans + shares),
        out_specs=[vmem] * (spans * len(cases) + 1),
        scratch_shapes=[
            pltpu.VMEM((len(cases), spans, own_frames * latent, own), jnp.bfloat16),
            pltpu.VMEM((frames + 2, 9, latent, pixels), jnp.bfloat16),
            pltpu.VMEM((shares, frames, pixels, wide), jnp.float32),
            pltpu.VMEM((frames, pixels + 2 * TSIDE, CH), jnp.bfloat16),
            pltpu.VMEM((3 * CH, 9 * lanes), jnp.bfloat16),
            pltpu.VMEM((3, frames, pixels, lanes), jnp.float32),
            pltpu.SemaphoreType.DMA((27,)),
        ],
        compiler_params=pltpu.CompilerParams(vmem_limit_bytes=48 * 1024 * 1024),
        cost_estimate=pl.CostEstimate(
            flops=2 * frames * pixels * 27 * CH * lanes, bytes_accessed=8_000_000, transcendentals=0
        ),
    )(w_mid, table, *latents_all[1:], *w_in_all)
    return jnp.transpose(collect(pieces, cases) / denom[0][None, None, :], (1, 0, 2))


def solution(mesh):
    placed = (
        P("tm", "groups", "tile"),
        P("groups"),
        P(None, None, "chan"),
        P("chan"),
        P("chan"),
        P(None, None, "chan"),
        P("chan"),
        P("chan"),
        P(None, "chan"),
        P("groups", None),
    )
    whole_lanes = CH % (mesh.shape["chan"] * mesh.shape["tm"] * LANES) == 0
    return jax.shard_map(
        lanes_body if whole_lanes else general_body,
        mesh=mesh,
        in_specs=placed,
        out_specs=P("tm", "groups", "tile"),
        check_vma=False,
    )
```

```python
import functools

import jax
import jax.numpy as jnp
from jax import lax
from jax.experimental import pallas as pl
from jax.experimental.pallas import tpu as pltpu
from jax.sharding import PartitionSpec as P

CH = 512
GROUPS = 32
TSIDE = 16
STRIDE = 12
GRID_X = 4

EPSILON = 1e-06
LANES = 128
PACKED = 16
VMEM_BYTES = 60 * 1024 * 1024


def shifted(value, axis, steps):
    count = lax.axis_size(axis)
    leading, last = (max(0, -steps), min(count, count - steps))
    return lax.ppermute(value, axis, [(source, source + steps) for source in range(leading, last)])


def window_index(tile_id, tiles):
    slots = jnp.arange(TSIDE * TSIDE, dtype=jnp.int32)
    row = tile_id // GRID_X * STRIDE + slots // TSIDE
    col = tile_id % GRID_X * STRIDE + slots % TSIDE
    valid = (row < tiles // GRID_X * STRIDE) & (col < GRID_X * STRIDE)
    block = row // STRIDE * GRID_X + col // STRIDE
    index = block * (STRIDE * STRIDE) + row % STRIDE * STRIDE + col % STRIDE
    return (jnp.where(valid, index, 0), valid)


def causal_conv(extended, weights, frames, side):
    pixels = side * side
    rows = jnp.arange(pixels, dtype=jnp.int32) // side
    cols = jnp.arange(pixels, dtype=jnp.int32) % side
    total = jnp.zeros((frames, weights.shape[2], pixels), jnp.float32)
    for depth in range(3):
        window = extended[depth : depth + frames]
        for down in range(3):
            for across in range(3):
                offset = (down - 1) * side + (across - 1)
                inside = (
                    (rows + down - 1 >= 0)
                    & (rows + down - 1 < side)
                    & (cols + across - 1 >= 0)
                    & (cols + across - 1 < side)
                )
                moved = jnp.roll(window, -offset, axis=2)
                moved = jnp.where(inside[None, None, :], moved, jnp.zeros_like(moved))
                total = total + jnp.einsum(
                    "fcp,co->fop",
                    moved,
                    weights[9 * depth + 3 * down + across],
                    preferred_element_type=jnp.float32,
                )
    return total


def with_history(values):
    frames = values.shape[0]
    earlier = shifted(values[frames - 2 :], "tm", 1)
    return jnp.concatenate([earlier, values], axis=0)


def normalize(values, gain, shift, total_frames):
    frames, chans, pixels = values.shape
    width = CH // GROUPS
    grouped = values.reshape(frames, chans // width, width, pixels)
    sums = jnp.sum(grouped, axis=(0, 2, 3))
    squares = jnp.sum(grouped * grouped, axis=(0, 2, 3))
    sums, squares = lax.psum((sums, squares), "tm")
    count = total_frames * width * pixels
    mean = sums / count
    variance = squares / count - mean * mean
    scale = lax.rsqrt(variance + EPSILON)
    normed = (grouped - mean[None, :, None, None]) * scale[None, :, None, None]
    normed = normed.reshape(frames, chans, pixels) * gain[None, :, None] + shift[None, :, None]
    return jax.nn.silu(normed).astype(jnp.bfloat16)


def spread(color, weight, index, total_pixels):
    numer = (
        jnp.zeros((color.shape[0], 3, total_pixels), jnp.float32)
        .at[:, :, index]
        .add(color * weight[None, None, :])
    )
    denom = jnp.zeros((total_pixels,), jnp.float32).at[index].add(weight)
    return (numer, denom)


def route_owned(numer, denom, tile_id, own):
    frames = numer.shape[0]
    margin = (GRID_X + 1) * own
    numer_wide = jnp.concatenate([numer, jnp.zeros((frames, 3, margin), jnp.float32)], axis=2)
    denom_wide = jnp.concatenate([denom, jnp.zeros((margin,), jnp.float32)], axis=0)
    first_pixel = tile_id * own

    def block_at(offset):
        start_pixel = first_pixel + offset * own
        return (
            lax.dynamic_slice_in_dim(numer_wide, start_pixel, own, 2),
            lax.dynamic_slice_in_dim(denom_wide, start_pixel, own, 0),
        )

    owned_numer, owned_denom = block_at(0)
    for offset in (1, GRID_X, GRID_X + 1):
        piece_numer, piece_denom = block_at(offset)
        got_numer, got_denom = shifted((piece_numer, piece_denom), "tile", offset)
        owned_numer = owned_numer + got_numer
        owned_denom = owned_denom + got_denom
    return (owned_numer, owned_denom)


def general_body(
    latents, tile_order, w_in, gain_in, shift_in, w_mid, gain_mid, shift_mid, w_out, blend_weight
):
    frames = latents.shape[0]
    total_frames = frames * lax.axis_size("tm")
    tiles = tile_order.shape[0]
    own = STRIDE * STRIDE
    total_pixels = tiles * own
    tile_id = lax.axis_index("tile")
    index, valid = window_index(tile_id, tiles)
    whole = lax.all_gather(latents, "tile", axis=2, tiled=True)
    blocks = whole.reshape(frames, whole.shape[1], tiles, own)
    image = (
        jnp.zeros_like(blocks)
        .at[:, :, tile_order]
        .set(blocks)
        .reshape(frames, whole.shape[1], total_pixels)
    )
    window = jnp.where(
        valid[None, None, :], jnp.take(image, index, axis=2), jnp.zeros((), jnp.bfloat16)
    )
    first = causal_conv(with_history(window), w_in, frames, TSIDE)
    hidden = normalize(first, gain_in, shift_in, total_frames)
    second = causal_conv(
        lax.all_gather(with_history(hidden), "chan", axis=1, tiled=True), w_mid, frames, TSIDE
    )
    upper = normalize(second, gain_mid, shift_mid, total_frames)
    color = jnp.einsum("oc,fcp->fop", w_out, upper, preferred_element_type=jnp.float32)
    weight = jnp.where(valid, blend_weight[tile_id], jnp.float32(0.0))
    numer, denom = spread(color, weight, index, total_pixels)
    numer, denom = route_owned(numer, denom, tile_id, own)
    numer = lax.psum(numer, "chan")
    return numer / denom[None, None, :]


def block_cases(tiles):
    downs = (0, 1) if tiles // GRID_X > 1 else (0,)
    return [(down, across) for down in downs for across in (0, 1)]


def group_affine(sums, squares, gain, shift, count):
    lanes = sums.shape[1]
    width = CH // GROUPS
    same = lax.broadcasted_iota(jnp.int32, (lanes, lanes), 0) // width == (
        lax.broadcasted_iota(jnp.int32, (lanes, lanes), 1) // width
    )
    total = jnp.dot(
        jnp.concatenate([sums, squares], axis=0),
        jnp.where(same, 1.0, 0.0).astype(jnp.float32),
        precision=lax.Precision.HIGHEST,
        preferred_element_type=jnp.float32,
    )
    mean = jnp.sum(total[:8], axis=0, keepdims=True) / count
    variance = jnp.sum(total[8:], axis=0, keepdims=True) / count - mean * mean
    scale = gain * lax.rsqrt(variance + EPSILON)
    return 0.5 * scale, 0.5 * (shift - mean * scale)


def silu_of_half(half):
    return half + half * jnp.tanh(half)


def fold(values):
    rows, lanes = values.shape
    return jnp.sum(values.reshape(rows // 8, 8, lanes), axis=0)


def decode_kernel(
    tiles,
    spans,
    shares,
    *refs,
):
    cases = block_cases(tiles)
    refs = list(refs)

    def take(number):
        taken = refs[:number]
        del refs[:number]
        return taken

    w_mid_ref, order_hbm = take(2)
    plain_hbm = take(4 + tiles + shares)
    keep_ref, send_ref, denom_ref = take(3)
    order_ref = take(1)[0]
    plain_refs = take(4 + tiles + shares)
    gain_mid_ref, shift_mid_ref, w_out_ref, blend_ref = plain_refs[:4]
    latent_refs, w_in_refs = plain_refs[4 : 4 + tiles], plain_refs[4 + tiles :]
    chosen, taps, first, hidden, weights, partial, sems, small_sems = take(8)

    own = denom_ref.shape[1]
    own_frames = keep_ref.shape[2]
    frames = own_frames * spans
    latent, wide = w_in_refs[0].shape[1:]
    rows_in = frames * latent
    depth_in = w_in_refs[0].shape[0] * latent
    pixels = TSIDE * TSIDE
    lanes = partial.shape[3]
    tile_id = lax.axis_index("tile")
    mine = lax.axis_index("tm")
    chan_id = lax.axis_index("chan")

    small = []
    for number, (source_ref, target_ref) in enumerate(
        zip([order_hbm] + plain_hbm, [order_ref] + plain_refs)
    ):
        copy = pltpu.make_async_copy(source_ref, target_ref, small_sems.at[number])
        copy.start()
        small.append(copy)
    copies = []
    for a in range(3):
        for b in range(3):
            for e in range(3):
                tap = 9 * a + 3 * b + e
                copy = pltpu.make_async_copy(
                    w_mid_ref.at[tap, :, pl.ds(pl.multiple_of(mine * lanes, LANES), lanes)],
                    weights.at[pl.ds(b * CH, CH), pl.ds((3 * a + e) * lanes, lanes)],
                    sems.at[tap],
                )
                copy.start()
                copies.append(copy)

    tile_row, tile_col = tile_id // GRID_X, tile_id % GRID_X
    taps[0:2] = jnp.zeros((2,) + taps.shape[1:], taps.dtype)
    for copy in small:
        copy.wait()
    for number, (down, across) in enumerate(cases):
        inside = (tile_row + down < tiles // GRID_X) & (tile_col + across < GRID_X)
        wanted = tile_id + down * GRID_X + across
        place = jnp.int32(0)
        for d in range(tiles):
            place = place + jnp.where(order_ref[0, d] == wanted, jnp.int32(d), jnp.int32(0))
        turn = (tile_id - place + tiles) % tiles
        for steps in range(tiles):

            @pl.when(inside & (turn == steps))
            def _():
                for swap in range(spans):
                    chosen[number, (mine + swap) % spans] = latent_refs[steps][
                        swap * latent * own_frames : (swap + 1) * latent * own_frames, :own
                    ]

        @pl.when(jnp.logical_not(inside))
        def _():
            chosen[number] = jnp.zeros(chosen.shape[1:], chosen.dtype)

    slot = lax.broadcasted_iota(jnp.int32, (1, pixels), 1)
    source = lax.broadcasted_iota(jnp.int32, (own, pixels), 0)
    for b in range(3):
        for e in range(3):
            up, along = slot // TSIDE + b - 1, slot % TSIDE + e - 1
            window = jnp.zeros((rows_in, pixels), jnp.float32)
            for number, (down, across) in enumerate(cases):
                block = chosen[number].reshape(rows_in, own)
                u, v = up - down * STRIDE, along - across * STRIDE
                high = STRIDE if down == 0 else TSIDE - STRIDE
                far = STRIDE if across == 0 else TSIDE - STRIDE
                good = (u >= 0) & (u < high) & (v >= 0) & (v < far)
                pick = source == jnp.where(good, u * STRIDE + v, -1)
                window = window + jnp.dot(
                    block,
                    jnp.where(pick, 1.0, 0.0).astype(jnp.bfloat16),
                    preferred_element_type=jnp.float32,
                )
            taps[2:, 3 * b + e] = window.astype(jnp.bfloat16).reshape(frames, latent, pixels)

    sums = [jnp.zeros((8, wide), jnp.float32) for _ in range(shares)]
    squares = [jnp.zeros((8, wide), jnp.float32) for _ in range(shares)]
    for f in range(frames):
        patch = taps[f : f + 3].reshape(depth_in, pixels)
        for s in range(shares):
            value = lax.dot_general(
                patch,
                w_in_refs[s][...].reshape(depth_in, wide),
                (((0,), (0,)), ((), ())),
                preferred_element_type=jnp.float32,
            )
            first[s, f] = value
            sums[s] = sums[s] + fold(value)
            squares[s] = squares[s] + fold(value * value)
    count = frames * (CH // GROUPS) * pixels
    affine = []
    for s in range(shares):
        table = latent_refs[s][rows_in : rows_in + PACKED].astype(jnp.float32)
        table = table[0:2] + table[2:4]
        affine.append(group_affine(sums[s], squares[s], table[0:1], table[1:2], count))

    edge = jnp.zeros((TSIDE, CH), jnp.bfloat16)
    for f in range(frames):
        hidden[f, 0:TSIDE] = edge
        hidden[f, TSIDE + pixels : 2 * TSIDE + pixels] = edge
        for s in range(shares):
            scale, bias = affine[s]
            value = silu_of_half(first[s, f] * scale + bias).astype(jnp.bfloat16)
            channels = pl.ds(pl.multiple_of((chan_id + s) % shares * wide, LANES), wide)
            hidden[f, TSIDE : TSIDE + pixels, channels] = value

    for copy in copies:
        copy.wait()

    partial[...] = jnp.zeros_like(partial)

    def convolve(start, several, depth_taps):
        lhs = jnp.concatenate(
            [
                hidden[pl.ds(start, several), b * TSIDE : b * TSIDE + pixels].reshape(
                    several * pixels, CH
                )
                for b in range(3)
            ],
            axis=1,
        )
        low = depth_taps[0] * 3 * lanes
        product = jnp.dot(lhs, weights[:, low:], preferred_element_type=jnp.float32)
        for a in depth_taps:
            for e in range(3):
                at = (3 * a + e) * lanes - low
                target = pl.ds(start + 2 - a, several)
                partial[e, target] += product[:, at : at + lanes].reshape(several, pixels, lanes)

    together = 2
    full = (frames - 2) // together

    def step(index, carry):
        convolve(index * together, together, (0, 1, 2))
        return carry

    lax.fori_loop(0, full, step, 0)
    for f in range(full * together, frames):
        convolve(f, 1, tuple(a for a in range(3) if f + 2 - a < frames))

    column = lax.broadcasted_iota(jnp.int32, (pixels, lanes), 0) % TSIDE
    total = jnp.zeros((8, lanes), jnp.float32)
    total_squares = jnp.zeros((8, lanes), jnp.float32)
    for f in range(frames):
        left = jnp.where(column == 0, 0.0, pltpu.roll(partial[0, f], 1, 0))
        right = jnp.where(column == TSIDE - 1, 0.0, pltpu.roll(partial[2, f], pixels - 1, 0))
        value = partial[1, f] + left + right
        partial[1, f] = value
        total = total + fold(value)
        total_squares = total_squares + fold(value * value)
    part = pl.ds(pl.multiple_of(mine * lanes, LANES), lanes)
    scale, bias = group_affine(
        total, total_squares, gain_mid_ref[:, part], shift_mid_ref[:, part], count
    )
    blend = blend_ref[pl.ds(tile_id, 1), :]
    blend = jnp.where(
        (tile_row * STRIDE + slot // TSIDE < tiles // GRID_X * STRIDE)
        & (tile_col * STRIDE + slot % TSIDE < GRID_X * STRIDE),
        blend,
        0.0,
    )
    w_out = jnp.concatenate(
        [w_out_ref[:, part].astype(jnp.float32), jnp.zeros((5, lanes), jnp.float32)], axis=0
    ).astype(jnp.bfloat16)
    colors = []
    for f in range(frames):
        upper = silu_of_half(partial[1, f] * scale + bias).astype(jnp.bfloat16)
        color = lax.dot_general(
            w_out,
            upper,
            (((1,), (1,)), ((), ())),
            preferred_element_type=jnp.float32,
        )
        colors.append(color * blend)
    colors = jnp.concatenate(colors, axis=0)

    slot_in = lax.broadcasted_iota(jnp.int32, (pixels, own), 0)
    pixel = lax.broadcasted_iota(jnp.int32, (pixels, own), 1)
    denom = jnp.zeros((8, own), jnp.float32)
    for number, (down, across) in enumerate(cases):
        u, v = slot_in // TSIDE - down * STRIDE, slot_in % TSIDE - across * STRIDE
        good = (u >= 0) & (u < STRIDE) & (v >= 0) & (v < STRIDE) & (u * STRIDE + v == pixel)
        pick = jnp.where(good, 1.0, 0.0).astype(jnp.float32)
        piece = jnp.dot(
            colors, pick, precision=lax.Precision.HIGHEST, preferred_element_type=jnp.float32
        )
        for f in range(frames):
            span, at = f // own_frames, f % own_frames

            @pl.when(mine == span)
            def _():
                for o in range(3):
                    keep_ref[number, o, at : at + 1, :] = piece[8 * f + o : 8 * f + o + 1]

            @pl.when(mine != span)
            def _():
                for o in range(3):
                    send_ref[(span - mine + spans) % spans - 1, number, o, at : at + 1, :] = piece[
                        8 * f + o : 8 * f + o + 1
                    ]

        inside = (tile_row >= down) & (tile_col >= across)
        other = jnp.maximum(tile_id - down * GRID_X - across, 0)
        weight = jnp.where(inside, blend_ref[pl.ds(other, 1), :], 0.0)
        denom = denom + jnp.dot(
            jnp.broadcast_to(weight, (8, pixels)),
            pick,
            precision=lax.Precision.HIGHEST,
            preferred_element_type=jnp.float32,
        )
    denom_ref[...] = denom


def exchange_weights(w_in):
    shares = lax.axis_size("chan")
    return [w_in] + [
        lax.ppermute(w_in, "chan", [((d + turn) % shares, d) for d in range(shares)])
        for turn in range(1, shares)
    ]


def exchange_latents(latents, gain_in, shift_in):
    tiles, shares, spans = (lax.axis_size(name) for name in ("tile", "chan", "tm"))
    parts = [latents] + [
        lax.ppermute(latents, "tm", [((d + swap) % spans, d) for d in range(spans)])
        for swap in range(1, spans)
    ]
    wide = gain_in.shape[0]
    table = jnp.stack([gain_in, shift_in])
    high = lax.reduce_precision(table, 8, 7)
    low = lax.reduce_precision(table - high, 8, 7)
    table = jnp.concatenate([high, low], axis=0).astype(jnp.bfloat16)
    message = jnp.concatenate(
        [jnp.pad(part, ((0, 0), (0, wide - part.shape[1]))) for part in parts]
        + [jnp.pad(table, ((0, PACKED - table.shape[0]), (0, 0)))],
        axis=0,
    )
    got = [message]
    for steps in range(1, tiles):
        turn = steps if steps < shares else 0
        pairs = [
            (t * shares + (c + turn) % shares, (t + steps) % tiles * shares + c)
            for t in range(tiles)
            for c in range(shares)
        ]
        got.append(lax.ppermute(message, ("tile", "chan"), pairs))
    return got


def ring_sum(kept, sent, axis):
    count = lax.axis_size(axis)
    for turn in range(1, count):
        kept = kept + lax.ppermute(
            sent[turn - 1], axis, [(d, (d + turn) % count) for d in range(count)]
        )
    return kept


def lanes_body(
    latents, tile_order, w_in, gain_in, shift_in, w_mid, gain_mid, shift_mid, w_out, blend_weight
):
    own_frames, latent, own = latents.shape
    spans = lax.axis_size("tm")
    shares = lax.axis_size("chan")
    frames = own_frames * spans
    tiles = tile_order.shape[0]
    wide = w_in.shape[2]
    lanes = wide // spans
    pixels = TSIDE * TSIDE
    cases = block_cases(tiles)

    w_in_all = exchange_weights(w_in)
    latents_all = exchange_latents(
        latents.reshape(own_frames * latent, own), gain_in, shift_in
    )
    plain = [
        gain_mid.reshape(1, wide),
        shift_mid.reshape(1, wide),
        w_out,
        blend_weight,
        *latents_all,
        *w_in_all,
    ]

    vmem = pl.BlockSpec(memory_space=pltpu.VMEM)
    piece = (len(cases), 3, own_frames, own)
    kept, sent, denom = pl.pallas_call(
        functools.partial(decode_kernel, tiles, spans, shares),
        out_shape=[
            jax.ShapeDtypeStruct(piece, jnp.float32),
            jax.ShapeDtypeStruct((max(spans - 1, 1),) + piece, jnp.float32),
            jax.ShapeDtypeStruct((8, own), jnp.float32),
        ],
        in_specs=[pl.BlockSpec(memory_space=pl.ANY)] * (2 + len(plain)),
        out_specs=[vmem] * 3,
        scratch_shapes=[pltpu.SMEM((1, tiles), jnp.int32)]
        + [pltpu.VMEM(value.shape, value.dtype) for value in plain]
        + [
            pltpu.VMEM((len(cases), spans, own_frames * latent, own), jnp.bfloat16),
            pltpu.VMEM((frames + 2, 9, latent, pixels), jnp.bfloat16),
            pltpu.VMEM((shares, frames, pixels, wide), jnp.float32),
            pltpu.VMEM((frames, pixels + 2 * TSIDE, CH), jnp.bfloat16),
            pltpu.VMEM((3 * CH, 9 * lanes), jnp.bfloat16),
            pltpu.VMEM((3, frames, pixels, lanes), jnp.float32),
            pltpu.SemaphoreType.DMA((27,)),
            pltpu.SemaphoreType.DMA((1 + len(plain),)),
        ],
        compiler_params=pltpu.CompilerParams(vmem_limit_bytes=VMEM_BYTES),
        cost_estimate=pl.CostEstimate(
            flops=2 * frames * pixels * 27 * CH * lanes, bytes_accessed=8_000_000, transcendentals=0
        ),
    )(w_mid, tile_order.reshape(1, tiles), *plain)
    total = ring_sum(kept, sent, "tm")
    total = ring_sum(total, [total] * (shares - 1), "chan")
    numer = total[0]
    for number, (down, across) in enumerate(cases):
        steps = down * GRID_X + across
        if steps and steps < tiles:
            numer = numer + shifted(total[number], "tile", steps)
    return jnp.transpose(numer / denom[0][None, None, :], (1, 0, 2))


def solution(mesh):
    placed = (
        P("tm", "groups", "tile"),
        P("groups"),
        P(None, None, "chan"),
        P("chan"),
        P("chan"),
        P(None, None, "chan"),
        P("chan"),
        P("chan"),
        P(None, "chan"),
        P("groups", None),
    )
    whole_lanes = (
        CH % (mesh.shape["chan"] * mesh.shape["tm"] * LANES) == 0
        and mesh.shape["chan"] <= mesh.shape["tile"]
    )
    return jax.shard_map(
        lanes_body if whole_lanes else general_body,
        mesh=mesh,
        in_specs=placed,
        out_specs=P("tm", "groups", "tile"),
        check_vma=False,
    )
```

```python
import functools

import jax
import jax.numpy as jnp
from jax import lax
from jax.experimental import pallas as pl
from jax.experimental.pallas import tpu as pltpu
from jax.sharding import PartitionSpec as P

CH = 512
GROUPS = 32
TSIDE = 16
STRIDE = 12
GRID_X = 4

EPSILON = 1e-06
LANES = 128
PACKED = 16

GAIN_ROW = 0
SHIFT_ROW = 1
W_OUT_ROW = 2
ORDER_ROW = 5
BLEND_ROW = 6
VMEM_BYTES = 48 * 1024 * 1024


def shifted(value, axis, steps):
    count = lax.axis_size(axis)
    leading, last = (max(0, -steps), min(count, count - steps))
    return lax.ppermute(value, axis, [(source, source + steps) for source in range(leading, last)])


def window_index(tile_id, tiles):
    slots = jnp.arange(TSIDE * TSIDE, dtype=jnp.int32)
    row = tile_id // GRID_X * STRIDE + slots // TSIDE
    col = tile_id % GRID_X * STRIDE + slots % TSIDE
    valid = (row < tiles // GRID_X * STRIDE) & (col < GRID_X * STRIDE)
    block = row // STRIDE * GRID_X + col // STRIDE
    index = block * (STRIDE * STRIDE) + row % STRIDE * STRIDE + col % STRIDE
    return (jnp.where(valid, index, 0), valid)


def causal_conv(extended, weights, frames, side):
    pixels = side * side
    rows = jnp.arange(pixels, dtype=jnp.int32) // side
    cols = jnp.arange(pixels, dtype=jnp.int32) % side
    total = jnp.zeros((frames, weights.shape[2], pixels), jnp.float32)
    for depth in range(3):
        window = extended[depth : depth + frames]
        for down in range(3):
            for across in range(3):
                offset = (down - 1) * side + (across - 1)
                inside = (
                    (rows + down - 1 >= 0)
                    & (rows + down - 1 < side)
                    & (cols + across - 1 >= 0)
                    & (cols + across - 1 < side)
                )
                moved = jnp.roll(window, -offset, axis=2)
                moved = jnp.where(inside[None, None, :], moved, jnp.zeros_like(moved))
                total = total + jnp.einsum(
                    "fcp,co->fop",
                    moved,
                    weights[9 * depth + 3 * down + across],
                    preferred_element_type=jnp.float32,
                )
    return total


def with_history(values):
    frames = values.shape[0]
    earlier = shifted(values[frames - 2 :], "tm", 1)
    return jnp.concatenate([earlier, values], axis=0)


def normalize(values, gain, shift, total_frames):
    frames, chans, pixels = values.shape
    width = CH // GROUPS
    grouped = values.reshape(frames, chans // width, width, pixels)
    sums = jnp.sum(grouped, axis=(0, 2, 3))
    squares = jnp.sum(grouped * grouped, axis=(0, 2, 3))
    sums, squares = lax.psum((sums, squares), "tm")
    count = total_frames * width * pixels
    mean = sums / count
    variance = squares / count - mean * mean
    scale = lax.rsqrt(variance + EPSILON)
    normed = (grouped - mean[None, :, None, None]) * scale[None, :, None, None]
    normed = normed.reshape(frames, chans, pixels) * gain[None, :, None] + shift[None, :, None]
    return jax.nn.silu(normed).astype(jnp.bfloat16)


def spread(color, weight, index, total_pixels):
    numer = (
        jnp.zeros((color.shape[0], 3, total_pixels), jnp.float32)
        .at[:, :, index]
        .add(color * weight[None, None, :])
    )
    denom = jnp.zeros((total_pixels,), jnp.float32).at[index].add(weight)
    return (numer, denom)


def route_owned(numer, denom, tile_id, own):
    frames = numer.shape[0]
    margin = (GRID_X + 1) * own
    numer_wide = jnp.concatenate([numer, jnp.zeros((frames, 3, margin), jnp.float32)], axis=2)
    denom_wide = jnp.concatenate([denom, jnp.zeros((margin,), jnp.float32)], axis=0)
    first_pixel = tile_id * own

    def block_at(offset):
        start_pixel = first_pixel + offset * own
        return (
            lax.dynamic_slice_in_dim(numer_wide, start_pixel, own, 2),
            lax.dynamic_slice_in_dim(denom_wide, start_pixel, own, 0),
        )

    owned_numer, owned_denom = block_at(0)
    for offset in (1, GRID_X, GRID_X + 1):
        piece_numer, piece_denom = block_at(offset)
        got_numer, got_denom = shifted((piece_numer, piece_denom), "tile", offset)
        owned_numer = owned_numer + got_numer
        owned_denom = owned_denom + got_denom
    return (owned_numer, owned_denom)


def general_body(
    latents, tile_order, w_in, gain_in, shift_in, w_mid, gain_mid, shift_mid, w_out, blend_weight
):
    frames = latents.shape[0]
    total_frames = frames * lax.axis_size("tm")
    tiles = tile_order.shape[0]
    own = STRIDE * STRIDE
    total_pixels = tiles * own
    tile_id = lax.axis_index("tile")
    index, valid = window_index(tile_id, tiles)
    whole = lax.all_gather(latents, "tile", axis=2, tiled=True)
    blocks = whole.reshape(frames, whole.shape[1], tiles, own)
    image = (
        jnp.zeros_like(blocks)
        .at[:, :, tile_order]
        .set(blocks)
        .reshape(frames, whole.shape[1], total_pixels)
    )
    window = jnp.where(
        valid[None, None, :], jnp.take(image, index, axis=2), jnp.zeros((), jnp.bfloat16)
    )
    first = causal_conv(with_history(window), w_in, frames, TSIDE)
    hidden = normalize(first, gain_in, shift_in, total_frames)
    second = causal_conv(
        lax.all_gather(with_history(hidden), "chan", axis=1, tiled=True), w_mid, frames, TSIDE
    )
    upper = normalize(second, gain_mid, shift_mid, total_frames)
    color = jnp.einsum("oc,fcp->fop", w_out, upper, preferred_element_type=jnp.float32)
    weight = jnp.where(valid, blend_weight[tile_id], jnp.float32(0.0))
    numer, denom = spread(color, weight, index, total_pixels)
    numer, denom = route_owned(numer, denom, tile_id, own)
    numer = lax.psum(numer, "chan")
    return numer / denom[None, None, :]


def block_cases(tiles):
    downs = (0, 1) if tiles // GRID_X > 1 else (0,)
    return [(down, across) for down in downs for across in (0, 1)]


def group_affine(sums, squares, gain, shift, count):
    lanes = sums.shape[1]
    width = CH // GROUPS
    same = lax.broadcasted_iota(jnp.int32, (lanes, lanes), 0) // width == (
        lax.broadcasted_iota(jnp.int32, (lanes, lanes), 1) // width
    )
    total = jnp.dot(
        jnp.concatenate([sums, squares], axis=0),
        jnp.where(same, 1.0, 0.0).astype(jnp.float32),
        precision=lax.Precision.HIGHEST,
        preferred_element_type=jnp.float32,
    )
    mean = jnp.sum(total[:8], axis=0, keepdims=True) / count
    variance = jnp.sum(total[8:], axis=0, keepdims=True) / count - mean * mean
    scale = gain * lax.rsqrt(variance + EPSILON)
    return 0.5 * scale, 0.5 * (shift - mean * scale)


def silu_of_half(half):
    return half + half * jnp.tanh(half)


def fold(values):
    rows, lanes = values.shape
    return jnp.sum(values.reshape(rows // 8, 8, lanes), axis=0)


def decode_kernel(
    tiles,
    spans,
    shares,
    *refs,
):
    cases = block_cases(tiles)
    refs = list(refs)

    def take(number):
        taken = refs[:number]
        del refs[:number]
        return taken

    w_mid_ref, table_ref = take(2)
    latent_refs, w_in_refs = take(tiles), take(shares)
    keep_refs = take(len(cases))
    send_ref, denom_ref = take(2)
    chosen, taps, first, hidden, weights, partial, sems = take(7)

    own = denom_ref.shape[1]
    own_frames = keep_refs[0].shape[1]
    frames = own_frames * spans
    latent, wide = w_in_refs[0].shape[1:]
    rows_in = frames * latent
    depth_in = 27 * latent
    pixels = TSIDE * TSIDE
    lanes = partial.shape[3]
    tile_id = lax.axis_index("tile")
    mine = lax.axis_index("tm")
    chan_id = lax.axis_index("chan")

    copies = []
    for a in range(3):
        for b in range(3):
            for e in range(3):
                tap = 9 * a + 3 * b + e
                copy = pltpu.make_async_copy(
                    w_mid_ref.at[tap, :, pl.ds(pl.multiple_of(mine * lanes, LANES), lanes)],
                    weights.at[pl.ds(b * CH, CH), pl.ds((3 * a + e) * lanes, lanes)],
                    sems.at[tap],
                )
                copy.start()
                copies.append(copy)

    tile_row, tile_col = tile_id // GRID_X, tile_id % GRID_X
    taps[0:2] = jnp.zeros((2,) + taps.shape[1:], taps.dtype)
    order = table_ref[ORDER_ROW : ORDER_ROW + 1, :]
    number_of = lax.broadcasted_iota(jnp.int32, order.shape, 1)
    for number, (down, across) in enumerate(cases):
        inside = (tile_row + down < tiles // GRID_X) & (tile_col + across < GRID_X)
        wanted = tile_id + down * GRID_X + across
        found = (order == wanted.astype(jnp.float32)) & (number_of < tiles)
        place = jnp.sum(jnp.where(found, number_of.astype(jnp.float32), 0.0))
        turn = (tile_id - place.astype(jnp.int32) + tiles) % tiles
        for steps in range(tiles):

            @pl.when(inside & (turn == steps))
            def _():
                for swap in range(spans):
                    chosen[number, (mine + swap) % spans] = latent_refs[steps][
                        swap * latent * own_frames : (swap + 1) * latent * own_frames, :own
                    ]

        @pl.when(jnp.logical_not(inside))
        def _():
            chosen[number] = jnp.zeros(chosen.shape[1:], chosen.dtype)

    slot = lax.broadcasted_iota(jnp.int32, (1, pixels), 1)
    source = lax.broadcasted_iota(jnp.int32, (own, pixels), 0)
    for b in range(3):
        for e in range(3):
            up, along = slot // TSIDE + b - 1, slot % TSIDE + e - 1
            window = jnp.zeros((rows_in, pixels), jnp.float32)
            for number, (down, across) in enumerate(cases):
                block = chosen[number].reshape(rows_in, own)
                u, v = up - down * STRIDE, along - across * STRIDE
                high = STRIDE if down == 0 else TSIDE - STRIDE
                far = STRIDE if across == 0 else TSIDE - STRIDE
                good = (u >= 0) & (u < high) & (v >= 0) & (v < far)
                pick = source == jnp.where(good, u * STRIDE + v, -1)
                window = window + jnp.dot(
                    block,
                    jnp.where(pick, 1.0, 0.0).astype(jnp.bfloat16),
                    preferred_element_type=jnp.float32,
                )
            taps[2:, 3 * b + e] = window.astype(jnp.bfloat16).reshape(frames, latent, pixels)

    sums = [jnp.zeros((8, wide), jnp.float32) for _ in range(shares)]
    squares = [jnp.zeros((8, wide), jnp.float32) for _ in range(shares)]
    for f in range(frames):
        patch = taps[f : f + 3].reshape(depth_in, pixels)
        for s in range(shares):
            value = lax.dot_general(
                patch,
                w_in_refs[s][:27].reshape(depth_in, wide),
                (((0,), (0,)), ((), ())),
                preferred_element_type=jnp.float32,
            )
            first[s, f] = value
            sums[s] = sums[s] + fold(value)
            squares[s] = squares[s] + fold(value * value)
    count = frames * (CH // GROUPS) * pixels
    affine = []
    for s in range(shares):
        table = latent_refs[s][rows_in : rows_in + PACKED].astype(jnp.float32)
        table = table[0:2] + table[2:4]
        affine.append(group_affine(sums[s], squares[s], table[0:1], table[1:2], count))

    edge = jnp.zeros((TSIDE, CH), jnp.bfloat16)
    for f in range(frames):
        hidden[f, 0:TSIDE] = edge
        hidden[f, TSIDE + pixels : 2 * TSIDE + pixels] = edge
        for s in range(shares):
            scale, bias = affine[s]
            value = silu_of_half(first[s, f] * scale + bias).astype(jnp.bfloat16)
            channels = pl.ds(pl.multiple_of((chan_id + s) % shares * wide, LANES), wide)
            hidden[f, TSIDE : TSIDE + pixels, channels] = value

    for copy in copies:
        copy.wait()

    partial[...] = jnp.zeros_like(partial)

    def convolve(start, several, depth_taps):
        lhs = jnp.concatenate(
            [
                hidden[pl.ds(start, several), b * TSIDE : b * TSIDE + pixels].reshape(
                    several * pixels, CH
                )
                for b in range(3)
            ],
            axis=1,
        )
        low = depth_taps[0] * 3 * lanes
        product = jnp.dot(lhs, weights[:, low:], preferred_element_type=jnp.float32)
        for a in depth_taps:
            for e in range(3):
                at = (3 * a + e) * lanes - low
                target = pl.ds(start + 2 - a, several)
                partial[e, target] += product[:, at : at + lanes].reshape(several, pixels, lanes)

    together = 2
    full = (frames - 2) // together

    def step(index, carry):
        convolve(index * together, together, (0, 1, 2))
        return carry

    lax.fori_loop(0, full, step, 0)
    for f in range(full * together, frames):
        convolve(f, 1, tuple(a for a in range(3) if f + 2 - a < frames))

    column = lax.broadcasted_iota(jnp.int32, (pixels, lanes), 0) % TSIDE
    total = jnp.zeros((8, lanes), jnp.float32)
    total_squares = jnp.zeros((8, lanes), jnp.float32)
    for f in range(frames):
        left = jnp.where(column == 0, 0.0, pltpu.roll(partial[0, f], 1, 0))
        right = jnp.where(column == TSIDE - 1, 0.0, pltpu.roll(partial[2, f], pixels - 1, 0))
        value = partial[1, f] + left + right
        partial[1, f] = value
        total = total + fold(value)
        total_squares = total_squares + fold(value * value)
    part = pl.ds(pl.multiple_of(mine * lanes, LANES), lanes)
    scale, bias = group_affine(
        total, total_squares, table_ref[GAIN_ROW : GAIN_ROW + 1, part], table_ref[SHIFT_ROW : SHIFT_ROW + 1, part], count
    )
    blend = table_ref[pl.ds(BLEND_ROW + tile_id, 1), :]
    blend = jnp.where(
        (tile_row * STRIDE + slot // TSIDE < tiles // GRID_X * STRIDE)
        & (tile_col * STRIDE + slot % TSIDE < GRID_X * STRIDE),
        blend,
        0.0,
    )
    w_out = jnp.concatenate(
        [table_ref[W_OUT_ROW : W_OUT_ROW + 3, part], jnp.zeros((5, lanes), jnp.float32)], axis=0
    ).astype(jnp.bfloat16)
    colors = []
    for f in range(frames):
        upper = silu_of_half(partial[1, f] * scale + bias).astype(jnp.bfloat16)
        color = lax.dot_general(
            w_out,
            upper,
            (((1,), (1,)), ((), ())),
            preferred_element_type=jnp.float32,
        )
        colors.append(color * blend)
    colors = jnp.concatenate(colors, axis=0)

    slot_in = lax.broadcasted_iota(jnp.int32, (pixels, own), 0)
    pixel = lax.broadcasted_iota(jnp.int32, (pixels, own), 1)
    denom = jnp.zeros((8, own), jnp.float32)
    for number, (down, across) in enumerate(cases):
        u, v = slot_in // TSIDE - down * STRIDE, slot_in % TSIDE - across * STRIDE
        good = (u >= 0) & (u < STRIDE) & (v >= 0) & (v < STRIDE) & (u * STRIDE + v == pixel)
        pick = jnp.where(good, 1.0, 0.0).astype(jnp.float32)
        piece = jnp.dot(
            colors, pick, precision=lax.Precision.HIGHEST, preferred_element_type=jnp.float32
        )
        for f in range(frames):
            span, at = f // own_frames, f % own_frames

            @pl.when(mine == span)
            def _():
                for o in range(3):
                    keep_refs[number][o, at : at + 1, :] = piece[8 * f + o : 8 * f + o + 1]

            @pl.when(mine != span)
            def _():
                for o in range(3):
                    send_ref[(span - mine + spans) % spans - 1, number, o, at : at + 1, :] = piece[
                        8 * f + o : 8 * f + o + 1
                    ]

        inside = (tile_row >= down) & (tile_col >= across)
        other = jnp.maximum(tile_id - down * GRID_X - across, 0)
        weight = jnp.where(inside, table_ref[pl.ds(BLEND_ROW + other, 1), :], 0.0)
        denom = denom + jnp.dot(
            jnp.broadcast_to(weight, (8, pixels)),
            pick,
            precision=lax.Precision.HIGHEST,
            preferred_element_type=jnp.float32,
        )
    denom_ref[...] = denom


def exchange_weights(w_in):
    shares = lax.axis_size("chan")
    return [w_in] + [
        lax.ppermute(w_in, "chan", [((d + turn) % shares, d) for d in range(shares)])
        for turn in range(1, shares)
    ]


def exchange_latents(latents, gain_in, shift_in):
    tiles, shares, spans = (lax.axis_size(name) for name in ("tile", "chan", "tm"))
    parts = [latents] + [
        lax.ppermute(latents, "tm", [((d + swap) % spans, d) for d in range(spans)])
        for swap in range(1, spans)
    ]
    wide = gain_in.shape[0]
    table = jnp.stack([gain_in, shift_in])
    high = lax.reduce_precision(table, 8, 7)
    low = lax.reduce_precision(table - high, 8, 7)
    table = jnp.concatenate([high.astype(jnp.bfloat16), low.astype(jnp.bfloat16)], axis=0)
    message = jnp.concatenate(
        [jnp.pad(part, ((0, 0), (0, wide - part.shape[1]))) for part in parts]
        + [jnp.pad(table, ((0, PACKED - table.shape[0]), (0, 0)))],
        axis=0,
    )
    got = [message]
    for steps in range(1, tiles):
        turn = steps if steps < shares else 0
        pairs = [
            (t * shares + (c + turn) % shares, (t + steps) % tiles * shares + c)
            for t in range(tiles)
            for c in range(shares)
        ]
        got.append(lax.ppermute(message, ("tile", "chan"), pairs))
    return got


def lanes_body(
    latents, tile_order, w_in, gain_in, shift_in, w_mid, gain_mid, shift_mid, w_out, blend_weight
):
    own_frames, latent, own = latents.shape
    spans = lax.axis_size("tm")
    shares = lax.axis_size("chan")
    frames = own_frames * spans
    tiles = tile_order.shape[0]
    wide = w_in.shape[2]
    lanes = wide // spans
    pixels = TSIDE * TSIDE
    cases = block_cases(tiles)

    w_in_all = exchange_weights(w_in)
    w_in_all[0] = jnp.pad(w_in, ((0, 1), (0, 0), (0, 0)))
    latents_all = exchange_latents(
        latents.reshape(own_frames * latent, own), gain_in, shift_in
    )
    order = jnp.pad(tile_order.astype(jnp.float32)[None, :], ((0, 0), (0, wide - tiles)))
    table = jnp.concatenate(
        [
            gain_mid.reshape(1, wide),
            shift_mid.reshape(1, wide),
            w_out.astype(jnp.float32),
            order,
            blend_weight,
        ],
        axis=0,
    )

    vmem = pl.BlockSpec(memory_space=pltpu.VMEM)
    piece = (3, own_frames, own)
    *kept, sent, denom = pl.pallas_call(
        functools.partial(decode_kernel, tiles, spans, shares),
        out_shape=[
            *[jax.ShapeDtypeStruct(piece, jnp.float32)] * len(cases),
            jax.ShapeDtypeStruct((max(spans - 1, 1), len(cases)) + piece, jnp.float32),
            jax.ShapeDtypeStruct((8, own), jnp.float32),
        ],
        in_specs=[pl.BlockSpec(memory_space=pl.ANY)] + [vmem] * (1 + tiles + shares),
        out_specs=[vmem] * (len(cases) + 2),
        scratch_shapes=[
            pltpu.VMEM((len(cases), spans, own_frames * latent, own), jnp.bfloat16),
            pltpu.VMEM((frames + 2, 9, latent, pixels), jnp.bfloat16),
            pltpu.VMEM((shares, frames, pixels, wide), jnp.float32),
            pltpu.VMEM((frames, pixels + 2 * TSIDE, CH), jnp.bfloat16),
            pltpu.VMEM((3 * CH, 9 * lanes), jnp.bfloat16),
            pltpu.VMEM((3, frames, pixels, lanes), jnp.float32),
            pltpu.SemaphoreType.DMA((27,)),
        ],
        compiler_params=pltpu.CompilerParams(vmem_limit_bytes=VMEM_BYTES),
        cost_estimate=pl.CostEstimate(
            flops=2 * frames * pixels * 27 * CH * lanes, bytes_accessed=8_000_000, transcendentals=0
        ),
    )(w_mid, table, *latents_all, *w_in_all)
    total = list(kept)
    for swap in range(1, spans):
        got = lax.ppermute(
            sent[swap - 1], "tm", [(d, (d + swap) % spans) for d in range(spans)]
        )
        total = [value + got[number] for number, value in enumerate(total)]
    numer = total[0]
    for number, (down, across) in enumerate(cases):
        steps = down * GRID_X + across
        for turn in range(shares):
            if steps < tiles and (steps or turn):
                pairs = [
                    (t * shares + c, (t + steps) * shares + (c + turn) % shares)
                    for t in range(tiles - steps)
                    for c in range(shares)
                ]
                numer = numer + lax.ppermute(total[number], ("tile", "chan"), pairs)
    return jnp.transpose(numer / denom[0][None, None, :], (1, 0, 2))


def solution(mesh):
    placed = (
        P("tm", "groups", "tile"),
        P("groups"),
        P(None, None, "chan"),
        P("chan"),
        P("chan"),
        P(None, None, "chan"),
        P("chan"),
        P("chan"),
        P(None, "chan"),
        P("groups", None),
    )
    whole_lanes = (
        CH % (mesh.shape["chan"] * mesh.shape["tm"] * LANES) == 0
        and mesh.shape["chan"] <= mesh.shape["tile"] <= LANES
    )
    return jax.shard_map(
        lanes_body if whole_lanes else general_body,
        mesh=mesh,
        in_specs=placed,
        out_specs=P("tm", "groups", "tile"),
        check_vma=False,
    )
```

```python
import functools

import jax
import jax.numpy as jnp
from jax import lax
from jax.experimental import pallas as pl
from jax.experimental.pallas import tpu as pltpu
from jax.sharding import PartitionSpec as P

CH = 512
GROUPS = 32
TSIDE = 16
STRIDE = 12
GRID_X = 4

EPSILON = 1e-06
LANES = 128

GAIN_ROW = 0
SHIFT_ROW = 1
W_OUT_ROW = 2
ORDER_ROW = 5
BLEND_ROW = 6
VMEM_BYTES = 48 * 1024 * 1024


def shifted(value, axis, steps):
    count = lax.axis_size(axis)
    leading, last = (max(0, -steps), min(count, count - steps))
    return lax.ppermute(value, axis, [(source, source + steps) for source in range(leading, last)])


def window_index(tile_id, tiles):
    slots = jnp.arange(TSIDE * TSIDE, dtype=jnp.int32)
    row = tile_id // GRID_X * STRIDE + slots // TSIDE
    col = tile_id % GRID_X * STRIDE + slots % TSIDE
    valid = (row < tiles // GRID_X * STRIDE) & (col < GRID_X * STRIDE)
    block = row // STRIDE * GRID_X + col // STRIDE
    index = block * (STRIDE * STRIDE) + row % STRIDE * STRIDE + col % STRIDE
    return (jnp.where(valid, index, 0), valid)


def causal_conv(extended, weights, frames, side):
    pixels = side * side
    rows = jnp.arange(pixels, dtype=jnp.int32) // side
    cols = jnp.arange(pixels, dtype=jnp.int32) % side
    total = jnp.zeros((frames, weights.shape[2], pixels), jnp.float32)
    for depth in range(3):
        window = extended[depth : depth + frames]
        for down in range(3):
            for across in range(3):
                offset = (down - 1) * side + (across - 1)
                inside = (
                    (rows + down - 1 >= 0)
                    & (rows + down - 1 < side)
                    & (cols + across - 1 >= 0)
                    & (cols + across - 1 < side)
                )
                moved = jnp.roll(window, -offset, axis=2)
                moved = jnp.where(inside[None, None, :], moved, jnp.zeros_like(moved))
                total = total + jnp.einsum(
                    "fcp,co->fop",
                    moved,
                    weights[9 * depth + 3 * down + across],
                    preferred_element_type=jnp.float32,
                )
    return total


def with_history(values):
    frames = values.shape[0]
    earlier = shifted(values[frames - 2 :], "tm", 1)
    return jnp.concatenate([earlier, values], axis=0)


def normalize(values, gain, shift, total_frames):
    frames, chans, pixels = values.shape
    width = CH // GROUPS
    grouped = values.reshape(frames, chans // width, width, pixels)
    sums = jnp.sum(grouped, axis=(0, 2, 3))
    squares = jnp.sum(grouped * grouped, axis=(0, 2, 3))
    sums, squares = lax.psum((sums, squares), "tm")
    count = total_frames * width * pixels
    mean = sums / count
    variance = squares / count - mean * mean
    scale = lax.rsqrt(variance + EPSILON)
    normed = (grouped - mean[None, :, None, None]) * scale[None, :, None, None]
    normed = normed.reshape(frames, chans, pixels) * gain[None, :, None] + shift[None, :, None]
    return jax.nn.silu(normed).astype(jnp.bfloat16)


def spread(color, weight, index, total_pixels):
    numer = (
        jnp.zeros((color.shape[0], 3, total_pixels), jnp.float32)
        .at[:, :, index]
        .add(color * weight[None, None, :])
    )
    denom = jnp.zeros((total_pixels,), jnp.float32).at[index].add(weight)
    return (numer, denom)


def route_owned(numer, denom, tile_id, own):
    frames = numer.shape[0]
    margin = (GRID_X + 1) * own
    numer_wide = jnp.concatenate([numer, jnp.zeros((frames, 3, margin), jnp.float32)], axis=2)
    denom_wide = jnp.concatenate([denom, jnp.zeros((margin,), jnp.float32)], axis=0)
    first_pixel = tile_id * own

    def block_at(offset):
        start_pixel = first_pixel + offset * own
        return (
            lax.dynamic_slice_in_dim(numer_wide, start_pixel, own, 2),
            lax.dynamic_slice_in_dim(denom_wide, start_pixel, own, 0),
        )

    owned_numer, owned_denom = block_at(0)
    for offset in (1, GRID_X, GRID_X + 1):
        piece_numer, piece_denom = block_at(offset)
        got_numer, got_denom = shifted((piece_numer, piece_denom), "tile", offset)
        owned_numer = owned_numer + got_numer
        owned_denom = owned_denom + got_denom
    return (owned_numer, owned_denom)


def general_body(
    latents, tile_order, w_in, gain_in, shift_in, w_mid, gain_mid, shift_mid, w_out, blend_weight
):
    frames = latents.shape[0]
    total_frames = frames * lax.axis_size("tm")
    tiles = tile_order.shape[0]
    own = STRIDE * STRIDE
    total_pixels = tiles * own
    tile_id = lax.axis_index("tile")
    index, valid = window_index(tile_id, tiles)
    whole = lax.all_gather(latents, "tile", axis=2, tiled=True)
    blocks = whole.reshape(frames, whole.shape[1], tiles, own)
    image = (
        jnp.zeros_like(blocks)
        .at[:, :, tile_order]
        .set(blocks)
        .reshape(frames, whole.shape[1], total_pixels)
    )
    window = jnp.where(
        valid[None, None, :], jnp.take(image, index, axis=2), jnp.zeros((), jnp.bfloat16)
    )
    first = causal_conv(with_history(window), w_in, frames, TSIDE)
    hidden = normalize(first, gain_in, shift_in, total_frames)
    second = causal_conv(
        lax.all_gather(with_history(hidden), "chan", axis=1, tiled=True), w_mid, frames, TSIDE
    )
    upper = normalize(second, gain_mid, shift_mid, total_frames)
    color = jnp.einsum("oc,fcp->fop", w_out, upper, preferred_element_type=jnp.float32)
    weight = jnp.where(valid, blend_weight[tile_id], jnp.float32(0.0))
    numer, denom = spread(color, weight, index, total_pixels)
    numer, denom = route_owned(numer, denom, tile_id, own)
    numer = lax.psum(numer, "chan")
    return numer / denom[None, None, :]


def block_cases(tiles):
    downs = (0, 1) if tiles // GRID_X > 1 else (0,)
    return [(down, across) for down in downs for across in (0, 1)]


def group_affine(sums, squares, gain, shift, count):
    lanes = sums.shape[1]
    width = CH // GROUPS
    same = lax.broadcasted_iota(jnp.int32, (lanes, lanes), 0) // width == (
        lax.broadcasted_iota(jnp.int32, (lanes, lanes), 1) // width
    )
    total = jnp.dot(
        jnp.concatenate([sums, squares], axis=0),
        jnp.where(same, 1.0, 0.0).astype(jnp.float32),
        precision=lax.Precision.HIGHEST,
        preferred_element_type=jnp.float32,
    )
    mean = jnp.sum(total[:8], axis=0, keepdims=True) / count
    variance = jnp.sum(total[8:], axis=0, keepdims=True) / count - mean * mean
    scale = gain * lax.rsqrt(variance + EPSILON)
    return 0.5 * scale, 0.5 * (shift - mean * scale)


def silu_of_half(half):
    return half + half * jnp.tanh(half)


def fold(values):
    rows, lanes = values.shape
    return jnp.sum(values.reshape(rows // 8, 8, lanes), axis=0)


def decode_kernel(
    tiles,
    spans,
    shares,
    *refs,
):
    cases = block_cases(tiles)
    refs = list(refs)

    def take(number):
        taken = refs[:number]
        del refs[:number]
        return taken

    w_mid_ref, table_ref = take(2)
    latent_refs, w_in_refs = take(tiles), take(shares)
    keep_ref, send_ref, denom_ref = take(3)
    chosen, taps, first, hidden, weights, partial, sems = take(7)

    own = denom_ref.shape[1]
    own_frames = keep_ref.shape[2]
    frames = own_frames * spans
    latent, wide = w_in_refs[0].shape[1:]
    rows_in = frames * latent
    rows_own = rows_in // spans
    depth_in = 27 * latent
    pixels = TSIDE * TSIDE
    lanes = partial.shape[3]
    tile_id = lax.axis_index("tile")
    mine = lax.axis_index("tm")
    chan_id = lax.axis_index("chan")

    copies = []
    for a in range(3):
        for b in range(3):
            for e in range(3):
                tap = 9 * a + 3 * b + e
                copy = pltpu.make_async_copy(
                    w_mid_ref.at[tap, :, pl.ds(pl.multiple_of(mine * lanes, LANES), lanes)],
                    weights.at[pl.ds(b * CH, CH), pl.ds((3 * a + e) * lanes, lanes)],
                    sems.at[tap],
                )
                copy.start()
                copies.append(copy)

    tile_row, tile_col = tile_id // GRID_X, tile_id % GRID_X
    taps[0:2] = jnp.zeros((2,) + taps.shape[1:], taps.dtype)
    order = table_ref[ORDER_ROW : ORDER_ROW + 1, :]
    number_of = lax.broadcasted_iota(jnp.int32, order.shape, 1)
    for number, (down, across) in enumerate(cases):
        inside = (tile_row + down < tiles // GRID_X) & (tile_col + across < GRID_X)
        wanted = tile_id + down * GRID_X + across
        found = (order == wanted.astype(jnp.float32)) & (number_of < tiles)
        place = jnp.sum(jnp.where(found, number_of.astype(jnp.float32), 0.0))
        turn = (tile_id - place.astype(jnp.int32) + tiles) % tiles
        for steps in range(tiles):

            @pl.when(inside & (turn == steps))
            def _():
                chosen[number] = latent_refs[steps][: (spans + 1) * rows_own]

        @pl.when(jnp.logical_not(inside))
        def _():
            chosen[number] = jnp.zeros(chosen.shape[1:], chosen.dtype)

    slot = lax.broadcasted_iota(jnp.int32, (1, pixels), 1)
    source = lax.broadcasted_iota(jnp.int32, (LANES, pixels), 0)
    tail = own - LANES

    def pick(wanted):
        return jnp.where(source == wanted, 1.0, 0.0).astype(jnp.bfloat16)

    for b in range(3):
        for e in range(3):
            up, along = slot // TSIDE + b - 1, slot % TSIDE + e - 1
            window = jnp.zeros((rows_in, pixels), jnp.float32)
            ends = [jnp.zeros((rows_own, pixels), jnp.float32) for _ in range(spans)]
            for number, (down, across) in enumerate(cases):
                u, v = up - down * STRIDE, along - across * STRIDE
                high = STRIDE if down == 0 else TSIDE - STRIDE
                far = STRIDE if across == 0 else TSIDE - STRIDE
                good = (u >= 0) & (u < high) & (v >= 0) & (v < far)
                wanted = jnp.where(good, u * STRIDE + v, -1)
                window = window + jnp.dot(
                    chosen[number, :rows_in], pick(wanted), preferred_element_type=jnp.float32
                )
                for swap in range(spans):
                    late = jnp.where(wanted >= LANES, wanted - LANES + tail * swap, -1)
                    ends[swap] = ends[swap] + jnp.dot(
                        chosen[number, rows_in:], pick(late), preferred_element_type=jnp.float32
                    )
            for swap in range(spans):
                value = window[swap * rows_own : (swap + 1) * rows_own] + ends[swap]
                value = value.astype(jnp.bfloat16).reshape(own_frames, latent, pixels)
                span = pl.ds(2 + (mine + swap) % spans * own_frames, own_frames)
                taps[span, 3 * b + e] = value

    sums = [jnp.zeros((8, wide), jnp.float32) for _ in range(shares)]
    squares = [jnp.zeros((8, wide), jnp.float32) for _ in range(shares)]
    for f in range(frames):
        patch = taps[f : f + 3].reshape(depth_in, pixels)
        for s in range(shares):
            value = lax.dot_general(
                patch,
                w_in_refs[s][:27].reshape(depth_in, wide),
                (((0,), (0,)), ((), ())),
                preferred_element_type=jnp.float32,
            )
            first[s, f] = value
            sums[s] = sums[s] + fold(value)
            squares[s] = squares[s] + fold(value * value)
    count = frames * (CH // GROUPS) * pixels
    affine = []
    for s in range(shares):
        at = (spans + 1) * rows_own
        table = latent_refs[s][at : at + wide // LANES * 4].astype(jnp.float32)
        pieces = [table[4 * lane : 4 * lane + 4] for lane in range(wide // LANES)]
        table = jnp.concatenate([part[0:2] + part[2:4] for part in pieces], axis=1)
        affine.append(group_affine(sums[s], squares[s], table[0:1], table[1:2], count))

    edge = jnp.zeros((TSIDE, CH), jnp.bfloat16)
    for f in range(frames):
        hidden[f, 0:TSIDE] = edge
        hidden[f, TSIDE + pixels : 2 * TSIDE + pixels] = edge
        for s in range(shares):
            scale, bias = affine[s]
            value = silu_of_half(first[s, f] * scale + bias).astype(jnp.bfloat16)
            channels = pl.ds(pl.multiple_of((chan_id + s) % shares * wide, LANES), wide)
            hidden[f, TSIDE : TSIDE + pixels, channels] = value

    for copy in copies:
        copy.wait()

    partial[...] = jnp.zeros_like(partial)

    def convolve(start, several, depth_taps):
        lhs = jnp.concatenate(
            [
                hidden[pl.ds(start, several), b * TSIDE : b * TSIDE + pixels].reshape(
                    several * pixels, CH
                )
                for b in range(3)
            ],
            axis=1,
        )
        low = depth_taps[0] * 3 * lanes
        product = jnp.dot(lhs, weights[:, low:], preferred_element_type=jnp.float32)
        for a in depth_taps:
            for e in range(3):
                at = (3 * a + e) * lanes - low
                target = pl.ds(start + 2 - a, several)
                partial[e, target] += product[:, at : at + lanes].reshape(several, pixels, lanes)

    together = 2
    full = (frames - 2) // together

    def step(index, carry):
        convolve(index * together, together, (0, 1, 2))
        return carry

    lax.fori_loop(0, full, step, 0)
    for f in range(full * together, frames):
        convolve(f, 1, tuple(a for a in range(3) if f + 2 - a < frames))

    column = lax.broadcasted_iota(jnp.int32, (pixels, lanes), 0) % TSIDE
    total = jnp.zeros((8, lanes), jnp.float32)
    total_squares = jnp.zeros((8, lanes), jnp.float32)
    for f in range(frames):
        left = jnp.where(column == 0, 0.0, pltpu.roll(partial[0, f], 1, 0))
        right = jnp.where(column == TSIDE - 1, 0.0, pltpu.roll(partial[2, f], pixels - 1, 0))
        value = partial[1, f] + left + right
        partial[1, f] = value
        total = total + fold(value)
        total_squares = total_squares + fold(value * value)
    part = pl.ds(pl.multiple_of(mine * lanes, LANES), lanes)
    scale, bias = group_affine(
        total, total_squares, table_ref[GAIN_ROW : GAIN_ROW + 1, part], table_ref[SHIFT_ROW : SHIFT_ROW + 1, part], count
    )
    blend = table_ref[pl.ds(BLEND_ROW + tile_id, 1), :]
    blend = jnp.where(
        (tile_row * STRIDE + slot // TSIDE < tiles // GRID_X * STRIDE)
        & (tile_col * STRIDE + slot % TSIDE < GRID_X * STRIDE),
        blend,
        0.0,
    )
    w_out = jnp.concatenate(
        [table_ref[W_OUT_ROW : W_OUT_ROW + 3, part], jnp.zeros((5, lanes), jnp.float32)], axis=0
    ).astype(jnp.bfloat16)
    colors = []
    for f in range(frames):
        upper = silu_of_half(partial[1, f] * scale + bias).astype(jnp.bfloat16)
        color = lax.dot_general(
            w_out,
            upper,
            (((1,), (1,)), ((), ())),
            preferred_element_type=jnp.float32,
        )
        colors.append(color * blend)
    colors = jnp.concatenate(colors, axis=0)

    slot_in = lax.broadcasted_iota(jnp.int32, (pixels, own), 0)
    pixel = lax.broadcasted_iota(jnp.int32, (pixels, own), 1)
    denom = jnp.zeros((8, own), jnp.float32)
    for number, (down, across) in enumerate(cases):
        u, v = slot_in // TSIDE - down * STRIDE, slot_in % TSIDE - across * STRIDE
        good = (u >= 0) & (u < STRIDE) & (v >= 0) & (v < STRIDE) & (u * STRIDE + v == pixel)
        pick = jnp.where(good, 1.0, 0.0).astype(jnp.float32)
        piece = jnp.dot(
            colors, pick, precision=lax.Precision.HIGHEST, preferred_element_type=jnp.float32
        )
        for f in range(frames):
            span, at = f // own_frames, f % own_frames

            @pl.when(mine == span)
            def _():
                for o in range(3):
                    keep_ref[number, o, at : at + 1, :] = piece[8 * f + o : 8 * f + o + 1]

            @pl.when(mine != span)
            def _():
                for o in range(3):
                    send_ref[(span - mine + spans) % spans - 1, number, o, at : at + 1, :] = piece[
                        8 * f + o : 8 * f + o + 1
                    ]

        inside = (tile_row >= down) & (tile_col >= across)
        other = jnp.maximum(tile_id - down * GRID_X - across, 0)
        weight = jnp.where(inside, table_ref[pl.ds(BLEND_ROW + other, 1), :], 0.0)
        denom = denom + jnp.dot(
            jnp.broadcast_to(weight, (8, pixels)),
            pick,
            precision=lax.Precision.HIGHEST,
            preferred_element_type=jnp.float32,
        )
    denom_ref[...] = denom


def from_ring(value, axis):
    count = lax.axis_size(axis)
    return [
        lax.ppermute(value, axis, [((d + turn) % count, d) for d in range(count)])
        for turn in range(1, count)
    ]


def ring_sum(kept, sent, axis):
    count = lax.axis_size(axis)
    for turn in range(1, count):
        kept = kept + lax.ppermute(
            sent[turn - 1], axis, [(d, (d + turn) % count) for d in range(count)]
        )
    return kept


def exchange_latents(latents, gain_in, shift_in):
    tiles, shares, spans = (lax.axis_size(name) for name in ("tile", "chan", "tm"))
    tail = latents.shape[1] - LANES
    parts = [latents] + from_ring(latents, "tm")
    tails = sum(
        jnp.pad(part[:, LANES:], ((0, 0), (tail * at, LANES - tail * (at + 1))))
        for at, part in enumerate(parts)
    )
    table = jnp.stack([gain_in, shift_in])
    high = lax.reduce_precision(table, 8, 7)
    low = lax.reduce_precision(table - high, 8, 7)
    table = jnp.concatenate([high, low], axis=0).astype(jnp.bfloat16)
    rows = [table[:, at : at + LANES] for at in range(0, table.shape[1], LANES)]
    rows = jnp.concatenate(rows, axis=0)
    rows = jnp.pad(rows, ((0, -rows.shape[0] % 16), (0, 0)))
    message = jnp.concatenate([part[:, :LANES] for part in parts] + [tails, rows], axis=0)
    got = [message]
    for steps in range(1, tiles):
        turn = steps if steps < shares else 0
        pairs = [
            (t * shares + (c + turn) % shares, (t + steps) % tiles * shares + c)
            for t in range(tiles)
            for c in range(shares)
        ]
        got.append(lax.ppermute(message, ("tile", "chan"), pairs))
    return got


def small_table(gain_mid, shift_mid, w_out, tile_order, blend_weight):
    wide = gain_mid.shape[0]
    total = 0.0
    for row, value in (
        (GAIN_ROW, gain_mid),
        (SHIFT_ROW, shift_mid),
        (W_OUT_ROW, w_out),
        (ORDER_ROW, tile_order),
        (BLEND_ROW, blend_weight),
    ):
        value = value.astype(jnp.float32).reshape(-1, value.shape[-1])
        below = BLEND_ROW + blend_weight.shape[0] - row - value.shape[0]
        total = total + jnp.pad(value, ((row, below), (0, wide - value.shape[1])))
    return total


def lanes_body(
    latents, tile_order, w_in, gain_in, shift_in, w_mid, gain_mid, shift_mid, w_out, blend_weight
):
    own_frames, latent, own = latents.shape
    spans = lax.axis_size("tm")
    shares = lax.axis_size("chan")
    frames = own_frames * spans
    tiles = tile_order.shape[0]
    wide = w_in.shape[2]
    lanes = wide // spans
    pixels = TSIDE * TSIDE
    cases = block_cases(tiles)

    w_in_all = from_ring(w_in, "chan")
    latents_all = exchange_latents(
        latents.reshape(own_frames * latent, own), gain_in, shift_in
    )
    _, w_in, *small = lax.optimization_barrier(
        (latents_all[0], w_in, gain_mid, shift_mid, w_out, tile_order, blend_weight)
    )
    w_in_own = from_ring(w_in, "tm")[:1] or [w_in]
    table = small_table(*small)

    vmem = pl.BlockSpec(memory_space=pltpu.VMEM)
    piece = (len(cases), 3, own_frames, own)
    kept, sent, denom = pl.pallas_call(
        functools.partial(decode_kernel, tiles, spans, shares),
        out_shape=[
            jax.ShapeDtypeStruct(piece, jnp.float32),
            jax.ShapeDtypeStruct((max(spans - 1, 1),) + piece, jnp.float32),
            jax.ShapeDtypeStruct((8, own), jnp.float32),
        ],
        in_specs=[pl.BlockSpec(memory_space=pl.ANY)] + [vmem] * (1 + tiles + shares),
        out_specs=[vmem] * 3,
        scratch_shapes=[
            pltpu.VMEM((len(cases), (spans + 1) * own_frames * latent, LANES), jnp.bfloat16),
            pltpu.VMEM((frames + 2, 9, latent, pixels), jnp.bfloat16),
            pltpu.VMEM((shares, frames, pixels, wide), jnp.float32),
            pltpu.VMEM((frames, pixels + 2 * TSIDE, CH), jnp.bfloat16),
            pltpu.VMEM((3 * CH, 9 * lanes), jnp.bfloat16),
            pltpu.VMEM((3, frames, pixels, lanes), jnp.float32),
            pltpu.SemaphoreType.DMA((27,)),
        ],
        compiler_params=pltpu.CompilerParams(vmem_limit_bytes=VMEM_BYTES),
        cost_estimate=pl.CostEstimate(
            flops=2 * frames * pixels * 27 * CH * lanes, bytes_accessed=8_000_000, transcendentals=0
        ),
    )(w_mid, table, *latents_all, *w_in_own, *w_in_all)
    total = ring_sum(kept, sent, "tm")
    total = ring_sum(total, [total] * (shares - 1), "chan")
    numer = total[0]
    for number, (down, across) in enumerate(cases):
        steps = down * GRID_X + across
        if steps and steps < tiles:
            numer = numer + shifted(total[number], "tile", steps)
    return jnp.transpose(numer / denom[0][None, None, :], (1, 0, 2))


def solution(mesh):
    placed = (
        P("tm", "groups", "tile"),
        P("groups"),
        P(None, None, "chan"),
        P("chan"),
        P("chan"),
        P(None, None, "chan"),
        P("chan"),
        P("chan"),
        P(None, "chan"),
        P("groups", None),
    )
    whole_lanes = (
        CH % (mesh.shape["chan"] * mesh.shape["tm"] * LANES) == 0
        and mesh.shape["chan"] <= mesh.shape["tile"] <= LANES
        and mesh.shape["tm"] * (STRIDE * STRIDE - LANES) <= LANES
    )
    return jax.shard_map(
        lanes_body if whole_lanes else general_body,
        mesh=mesh,
        in_specs=placed,
        out_specs=P("tm", "groups", "tile"),
        check_vma=False,
    )
```

```python
import functools

import jax
import jax.numpy as jnp
from jax import lax
from jax.experimental import pallas as pl
from jax.experimental.pallas import tpu as pltpu
from jax.sharding import PartitionSpec as P

CH = 512
GROUPS = 32
TSIDE = 16
STRIDE = 12
GRID_X = 4

EPSILON = 1e-06
LANES = 128

GAIN_ROW = 0
SHIFT_ROW = 1
W_OUT_ROW = 2
ORDER_ROW = 5
BLEND_ROW = 6
VMEM_BYTES = 48 * 1024 * 1024


def shifted(value, axis, steps):
    count = lax.axis_size(axis)
    leading, last = (max(0, -steps), min(count, count - steps))
    return lax.ppermute(value, axis, [(source, source + steps) for source in range(leading, last)])


def window_index(tile_id, tiles):
    slots = jnp.arange(TSIDE * TSIDE, dtype=jnp.int32)
    row = tile_id // GRID_X * STRIDE + slots // TSIDE
    col = tile_id % GRID_X * STRIDE + slots % TSIDE
    valid = (row < tiles // GRID_X * STRIDE) & (col < GRID_X * STRIDE)
    block = row // STRIDE * GRID_X + col // STRIDE
    index = block * (STRIDE * STRIDE) + row % STRIDE * STRIDE + col % STRIDE
    return (jnp.where(valid, index, 0), valid)


def causal_conv(extended, weights, frames, side):
    pixels = side * side
    rows = jnp.arange(pixels, dtype=jnp.int32) // side
    cols = jnp.arange(pixels, dtype=jnp.int32) % side
    total = jnp.zeros((frames, weights.shape[2], pixels), jnp.float32)
    for depth in range(3):
        window = extended[depth : depth + frames]
        for down in range(3):
            for across in range(3):
                offset = (down - 1) * side + (across - 1)
                inside = (
                    (rows + down - 1 >= 0)
                    & (rows + down - 1 < side)
                    & (cols + across - 1 >= 0)
                    & (cols + across - 1 < side)
                )
                moved = jnp.roll(window, -offset, axis=2)
                moved = jnp.where(inside[None, None, :], moved, jnp.zeros_like(moved))
                total = total + jnp.einsum(
                    "fcp,co->fop",
                    moved,
                    weights[9 * depth + 3 * down + across],
                    preferred_element_type=jnp.float32,
                )
    return total


def with_history(values):
    frames = values.shape[0]
    earlier = shifted(values[frames - 2 :], "tm", 1)
    return jnp.concatenate([earlier, values], axis=0)


def normalize(values, gain, shift, total_frames):
    frames, chans, pixels = values.shape
    width = CH // GROUPS
    grouped = values.reshape(frames, chans // width, width, pixels)
    sums = jnp.sum(grouped, axis=(0, 2, 3))
    squares = jnp.sum(grouped * grouped, axis=(0, 2, 3))
    sums, squares = lax.psum((sums, squares), "tm")
    count = total_frames * width * pixels
    mean = sums / count
    variance = squares / count - mean * mean
    scale = lax.rsqrt(variance + EPSILON)
    normed = (grouped - mean[None, :, None, None]) * scale[None, :, None, None]
    normed = normed.reshape(frames, chans, pixels) * gain[None, :, None] + shift[None, :, None]
    return jax.nn.silu(normed).astype(jnp.bfloat16)


def spread(color, weight, index, total_pixels):
    numer = (
        jnp.zeros((color.shape[0], 3, total_pixels), jnp.float32)
        .at[:, :, index]
        .add(color * weight[None, None, :])
    )
    denom = jnp.zeros((total_pixels,), jnp.float32).at[index].add(weight)
    return (numer, denom)


def route_owned(numer, denom, tile_id, own):
    frames = numer.shape[0]
    margin = (GRID_X + 1) * own
    numer_wide = jnp.concatenate([numer, jnp.zeros((frames, 3, margin), jnp.float32)], axis=2)
    denom_wide = jnp.concatenate([denom, jnp.zeros((margin,), jnp.float32)], axis=0)
    first_pixel = tile_id * own

    def block_at(offset):
        start_pixel = first_pixel + offset * own
        return (
            lax.dynamic_slice_in_dim(numer_wide, start_pixel, own, 2),
            lax.dynamic_slice_in_dim(denom_wide, start_pixel, own, 0),
        )

    owned_numer, owned_denom = block_at(0)
    for offset in (1, GRID_X, GRID_X + 1):
        piece_numer, piece_denom = block_at(offset)
        got_numer, got_denom = shifted((piece_numer, piece_denom), "tile", offset)
        owned_numer = owned_numer + got_numer
        owned_denom = owned_denom + got_denom
    return (owned_numer, owned_denom)


def general_body(
    latents, tile_order, w_in, gain_in, shift_in, w_mid, gain_mid, shift_mid, w_out, blend_weight
):
    frames = latents.shape[0]
    total_frames = frames * lax.axis_size("tm")
    tiles = tile_order.shape[0]
    own = STRIDE * STRIDE
    total_pixels = tiles * own
    tile_id = lax.axis_index("tile")
    index, valid = window_index(tile_id, tiles)
    whole = lax.all_gather(latents, "tile", axis=2, tiled=True)
    blocks = whole.reshape(frames, whole.shape[1], tiles, own)
    image = (
        jnp.zeros_like(blocks)
        .at[:, :, tile_order]
        .set(blocks)
        .reshape(frames, whole.shape[1], total_pixels)
    )
    window = jnp.where(
        valid[None, None, :], jnp.take(image, index, axis=2), jnp.zeros((), jnp.bfloat16)
    )
    first = causal_conv(with_history(window), w_in, frames, TSIDE)
    hidden = normalize(first, gain_in, shift_in, total_frames)
    second = causal_conv(
        lax.all_gather(with_history(hidden), "chan", axis=1, tiled=True), w_mid, frames, TSIDE
    )
    upper = normalize(second, gain_mid, shift_mid, total_frames)
    color = jnp.einsum("oc,fcp->fop", w_out, upper, preferred_element_type=jnp.float32)
    weight = jnp.where(valid, blend_weight[tile_id], jnp.float32(0.0))
    numer, denom = spread(color, weight, index, total_pixels)
    numer, denom = route_owned(numer, denom, tile_id, own)
    numer = lax.psum(numer, "chan")
    return numer / denom[None, None, :]


def block_cases(tiles):
    downs = (0, 1) if tiles // GRID_X > 1 else (0,)
    return [(down, across) for down in downs for across in (0, 1)]


def group_affine(sums, squares, gain, shift, count):
    lanes = sums.shape[1]
    width = CH // GROUPS
    same = lax.broadcasted_iota(jnp.int32, (lanes, lanes), 0) // width == (
        lax.broadcasted_iota(jnp.int32, (lanes, lanes), 1) // width
    )
    total = jnp.dot(
        jnp.concatenate([sums, squares], axis=0),
        jnp.where(same, 1.0, 0.0).astype(jnp.float32),
        precision=lax.Precision.HIGHEST,
        preferred_element_type=jnp.float32,
    )
    mean = jnp.sum(total[:8], axis=0, keepdims=True) / count
    variance = jnp.sum(total[8:], axis=0, keepdims=True) / count - mean * mean
    scale = gain * lax.rsqrt(variance + EPSILON)
    return 0.5 * scale, 0.5 * (shift - mean * scale)


def silu_of_half(half):
    return half + half * jnp.tanh(half)


def fold(values):
    rows, lanes = values.shape
    return jnp.sum(values.reshape(rows // 8, 8, lanes), axis=0)


def decode_kernel(
    tiles,
    spans,
    shares,
    *refs,
):
    cases = block_cases(tiles)
    refs = list(refs)

    def take(number):
        taken = refs[:number]
        del refs[:number]
        return taken

    w_mid_ref, table_ref = take(2)
    latent_refs, w_in_refs = take(tiles), take(shares)
    keep_ref, send_ref, denom_ref = take(3)
    chosen, taps, first, hidden, weights, partial, shown_ref, sems = take(8)

    own = denom_ref.shape[1]
    own_frames = keep_ref.shape[2]
    frames = own_frames * spans
    latent, wide = w_in_refs[0].shape[1:]
    rows_in = frames * latent
    rows_own = rows_in // spans
    depth_in = 27 * latent
    pixels = TSIDE * TSIDE
    lanes = partial.shape[3]
    tile_id = lax.axis_index("tile")
    mine = lax.axis_index("tm")
    chan_id = lax.axis_index("chan")

    copies = []
    for a in range(3):
        for b in range(3):
            for e in range(3):
                tap = 9 * a + 3 * b + e
                copy = pltpu.make_async_copy(
                    w_mid_ref.at[tap, :, pl.ds(pl.multiple_of(mine * lanes, LANES), lanes)],
                    weights.at[pl.ds(b * CH, CH), pl.ds((3 * a + e) * lanes, lanes)],
                    sems.at[tap],
                )
                copy.start()
                copies.append(copy)

    tile_row, tile_col = tile_id // GRID_X, tile_id % GRID_X
    order = table_ref[ORDER_ROW : ORDER_ROW + 1, :]
    number_of = lax.broadcasted_iota(jnp.int32, order.shape, 1)
    rows_sent = (spans + 1) * rows_own
    for number, (down, across) in enumerate(cases):
        inside = (tile_row + down < tiles // GRID_X) & (tile_col + across < GRID_X)
        wanted = tile_id + down * GRID_X + across
        found = (order == wanted.astype(jnp.float32)) & (number_of < tiles)
        place = jnp.sum(jnp.where(found, number_of.astype(jnp.float32), 0.0))
        turn = (tile_id - place.astype(jnp.int32) + tiles) % tiles
        part = slice(number * LANES, (number + 1) * LANES)
        for steps in range(tiles):

            @pl.when(inside & (turn == steps))
            def _():
                chosen[:, part] = latent_refs[steps][:rows_sent]

        @pl.when(jnp.logical_not(inside))
        def _():
            chosen[:, part] = jnp.zeros((rows_sent, LANES), chosen.dtype)

    slot = lax.broadcasted_iota(jnp.int32, (1, pixels), 1)
    up, along = slot // TSIDE, slot % TSIDE
    source = lax.broadcasted_iota(jnp.int32, (LANES, pixels), 0)
    tail = own - LANES

    def pick(swap):
        parts = []
        for down, across in cases:
            u, v = up - down * STRIDE, along - across * STRIDE
            good = (u >= 0) & (u < STRIDE) & (v >= 0) & (v < STRIDE)
            wanted = jnp.where(good, u * STRIDE + v, -1)
            if swap is not None:
                wanted = jnp.where(wanted >= LANES, wanted - LANES + tail * swap, -1)
            parts.append(jnp.where(source == wanted, 1.0, 0.0).astype(jnp.bfloat16))
        return jnp.concatenate(parts, axis=0)

    window = jnp.dot(chosen[:rows_in], pick(None), preferred_element_type=jnp.float32)
    ends = [
        jnp.dot(chosen[rows_in:], pick(swap), preferred_element_type=jnp.float32)
        for swap in range(spans)
    ]
    window = window + jnp.concatenate(ends, axis=0)
    taps[0:2] = jnp.zeros((2,) + taps.shape[1:], taps.dtype)
    for b in range(3):
        for e in range(3):
            inside = (
                (up + b - 1 >= 0)
                & (up + b - 1 < TSIDE)
                & (along + e - 1 >= 0)
                & (along + e - 1 < TSIDE)
            )
            offset = (b - 1) * TSIDE + e - 1
            moved = pltpu.roll(window, (-offset) % pixels, 1) if offset else window
            moved = jnp.where(inside, moved, 0.0).astype(jnp.bfloat16)
            for swap in range(spans):
                value = moved[swap * rows_own : (swap + 1) * rows_own]
                span = pl.ds(2 + (mine + swap) % spans * own_frames, own_frames)
                taps[span, 3 * b + e] = value.reshape(own_frames, latent, pixels)

    joined = jnp.concatenate(
        [w_in_refs[s][:27].reshape(depth_in, wide) for s in range(shares)], axis=1
    )
    sums = jnp.zeros((8, CH), jnp.float32)
    squares = jnp.zeros((8, CH), jnp.float32)
    for f in range(frames):
        patch = taps[f : f + 3].reshape(depth_in, pixels)
        value = lax.dot_general(
            patch, joined, (((0,), (0,)), ((), ())), preferred_element_type=jnp.float32
        )
        first[f] = value
        sums = sums + fold(value)
        squares = squares + fold(value * value)
    count = frames * (CH // GROUPS) * pixels
    affine = []
    for s in range(shares):
        at = (spans + 1) * rows_own
        table = latent_refs[s][at : at + wide // LANES * 4].astype(jnp.float32)
        pieces = [table[4 * lane : 4 * lane + 4] for lane in range(wide // LANES)]
        table = jnp.concatenate([part[0:2] + part[2:4] for part in pieces], axis=1)
        part = slice(s * wide, (s + 1) * wide)
        affine.append(
            group_affine(sums[:, part], squares[:, part], table[0:1], table[1:2], count)
        )
    channels = [
        pl.ds(pl.multiple_of((chan_id + s) % shares * wide, LANES), wide) for s in range(shares)
    ]

    def hide(f):
        edge = jnp.zeros((TSIDE, CH), jnp.bfloat16)
        hidden[f, 0:TSIDE] = edge
        hidden[f, TSIDE + pixels : 2 * TSIDE + pixels] = edge
        for s in range(shares):
            scale, bias = affine[s]
            value = first[f, :, s * wide : (s + 1) * wide] * scale + bias
            hidden[f, TSIDE : TSIDE + pixels, channels[s]] = silu_of_half(value).astype(
                jnp.bfloat16
            )

    def convolve(start, several, depth_taps):
        lhs = jnp.concatenate(
            [
                hidden[start : start + several, b * TSIDE : b * TSIDE + pixels].reshape(
                    several * pixels, CH
                )
                for b in range(3)
            ],
            axis=1,
        )
        low = depth_taps[0] * 3 * lanes
        product = jnp.dot(lhs, weights[:, low:], preferred_element_type=jnp.float32)
        for a in depth_taps:
            for e in range(3):
                at = (3 * a + e) * lanes - low
                for f in range(several):
                    target = start + f + 2 - a
                    value = product[f * pixels : (f + 1) * pixels, at : at + lanes]
                    if start + f == max(target - 2, 0):
                        partial[e, target] = value
                    else:
                        partial[e, target] += value

    column = lax.broadcasted_iota(jnp.int32, (pixels, lanes), 0) % TSIDE
    total = [jnp.zeros((8, lanes), jnp.float32)] * 2

    def gather(f):
        left = jnp.where(column == 0, 0.0, pltpu.roll(partial[0, f], 1, 0))
        right = jnp.where(column == TSIDE - 1, 0.0, pltpu.roll(partial[2, f], pixels - 1, 0))
        value = partial[1, f] + left + right
        partial[1, f] = value
        total[0] = total[0] + fold(value)
        total[1] = total[1] + fold(value * value)

    together = 2
    groups = [range(f, f + together) for f in range(0, frames - 2, together)]
    groups += [range(f, f + 1) for f in range(groups[-1].stop, frames)]
    for copy in copies:
        copy.wait()
    for f in groups[0]:
        hide(f)
    for number, group in enumerate(groups):
        if number + 1 < len(groups):
            for f in groups[number + 1]:
                hide(f)
        convolve(
            group.start,
            len(group),
            tuple(a for a in range(3) if group.stop - 1 + 2 - a < frames),
        )
        if number:
            for f in groups[number - 1]:
                gather(f)
    for f in groups[-1]:
        gather(f)

    part = pl.ds(pl.multiple_of(mine * lanes, LANES), lanes)
    scale, bias = group_affine(
        total[0],
        total[1],
        table_ref[GAIN_ROW : GAIN_ROW + 1, part],
        table_ref[SHIFT_ROW : SHIFT_ROW + 1, part],
        count,
    )
    blend = table_ref[pl.ds(BLEND_ROW + tile_id, 1), :]
    blend = jnp.where(
        (tile_row * STRIDE + up < tiles // GRID_X * STRIDE)
        & (tile_col * STRIDE + along < GRID_X * STRIDE),
        blend,
        0.0,
    )
    w_out = jnp.concatenate(
        [table_ref[W_OUT_ROW : W_OUT_ROW + 3, part], jnp.zeros((5, lanes), jnp.float32)], axis=0
    ).astype(jnp.bfloat16)
    colors = []
    for f in range(frames):
        upper = silu_of_half(partial[1, f] * scale + bias).astype(jnp.bfloat16)
        color = lax.dot_general(
            w_out, upper, (((1,), (1,)), ((), ())), preferred_element_type=jnp.float32
        )
        colors.append(color * blend)
    colors = jnp.concatenate(colors, axis=0)

    slot_in = lax.broadcasted_iota(jnp.int32, (pixels, own), 0)
    pixel = lax.broadcasted_iota(jnp.int32, (pixels, own), 1)
    denom = jnp.zeros((8, own), jnp.float32)
    for number, (down, across) in enumerate(cases):
        u, v = slot_in // TSIDE - down * STRIDE, slot_in % TSIDE - across * STRIDE
        good = (u >= 0) & (u < STRIDE) & (v >= 0) & (v < STRIDE) & (u * STRIDE + v == pixel)
        shown = jnp.where(good, 1.0, 0.0).astype(jnp.float32)
        inside = (tile_row >= down) & (tile_col >= across)
        other = jnp.maximum(tile_id - down * GRID_X - across, 0)
        weight = jnp.where(inside, table_ref[pl.ds(BLEND_ROW + other, 1), :], 0.0)
        piece = jnp.dot(
            jnp.concatenate([colors, jnp.broadcast_to(weight, (8, pixels))], axis=0),
            shown,
            precision=lax.Precision.HIGHEST,
            preferred_element_type=jnp.float32,
        )
        denom = denom + piece[8 * frames :]
        shown_ref[...] = piece
        for swap in range(spans):
            target = keep_ref if swap == 0 else send_ref.at[swap - 1]
            base = (mine + swap) % spans * own_frames * 8
            for at in range(own_frames):
                for o in range(3):
                    target[number, o, at : at + 1, :] = shown_ref[pl.ds(base + 8 * at + o, 1), :]

    denom_ref[...] = denom


def from_ring(value, axis):
    count = lax.axis_size(axis)
    return [
        lax.ppermute(value, axis, [((d + turn) % count, d) for d in range(count)])
        for turn in range(1, count)
    ]


def ring_sum(kept, sent, axis):
    count = lax.axis_size(axis)
    for turn in range(1, count):
        kept = kept + lax.ppermute(
            sent[turn - 1], axis, [(d, (d + turn) % count) for d in range(count)]
        )
    return kept


def exchange_latents(latents, gain_in, shift_in):
    tiles, shares, spans = (lax.axis_size(name) for name in ("tile", "chan", "tm"))
    tail = latents.shape[1] - LANES
    parts = [latents] + from_ring(latents, "tm")
    tails = sum(
        jnp.pad(part[:, LANES:], ((0, 0), (tail * at, LANES - tail * (at + 1))))
        for at, part in enumerate(parts)
    )
    table = jnp.stack([gain_in, shift_in])
    high = lax.reduce_precision(table, 8, 7)
    low = lax.reduce_precision(table - high, 8, 7)
    table = jnp.concatenate([high, low], axis=0).astype(jnp.bfloat16)
    rows = [table[:, at : at + LANES] for at in range(0, table.shape[1], LANES)]
    rows = jnp.concatenate(rows, axis=0)
    rows = jnp.pad(rows, ((0, -rows.shape[0] % 16), (0, 0)))
    message = jnp.concatenate([part[:, :LANES] for part in parts] + [tails, rows], axis=0)
    got = [message]
    for steps in range(1, tiles):
        turn = steps if steps < shares else 0
        pairs = [
            (t * shares + (c + turn) % shares, (t + steps) % tiles * shares + c)
            for t in range(tiles)
            for c in range(shares)
        ]
        got.append(lax.ppermute(message, ("tile", "chan"), pairs))
    return got


def small_table(gain_mid, shift_mid, w_out, tile_order, blend_weight):
    wide = gain_mid.shape[0]
    total = 0.0
    for row, value in (
        (GAIN_ROW, gain_mid),
        (SHIFT_ROW, shift_mid),
        (W_OUT_ROW, w_out),
        (ORDER_ROW, tile_order),
        (BLEND_ROW, blend_weight),
    ):
        value = value.astype(jnp.float32).reshape(-1, value.shape[-1])
        below = BLEND_ROW + blend_weight.shape[0] - row - value.shape[0]
        total = total + jnp.pad(value, ((row, below), (0, wide - value.shape[1])))
    return total


def lanes_body(
    latents, tile_order, w_in, gain_in, shift_in, w_mid, gain_mid, shift_mid, w_out, blend_weight
):
    own_frames, latent, own = latents.shape
    spans = lax.axis_size("tm")
    shares = lax.axis_size("chan")
    frames = own_frames * spans
    tiles = tile_order.shape[0]
    wide = w_in.shape[2]
    lanes = wide // spans
    pixels = TSIDE * TSIDE
    cases = block_cases(tiles)

    w_in_all = from_ring(w_in, "chan")
    latents_all = exchange_latents(
        latents.reshape(own_frames * latent, own), gain_in, shift_in
    )
    _, w_in, *small = lax.optimization_barrier(
        (latents_all[0], w_in, gain_mid, shift_mid, w_out, tile_order, blend_weight)
    )
    w_in_own = from_ring(w_in, "tm")[:1] or [w_in]
    table = small_table(*small)

    vmem = pl.BlockSpec(memory_space=pltpu.VMEM)
    piece = (len(cases), 3, own_frames, own)
    kept, sent, denom = pl.pallas_call(
        functools.partial(decode_kernel, tiles, spans, shares),
        out_shape=[
            jax.ShapeDtypeStruct(piece, jnp.float32),
            jax.ShapeDtypeStruct((max(spans - 1, 1),) + piece, jnp.float32),
            jax.ShapeDtypeStruct((8, own), jnp.float32),
        ],
        in_specs=[pl.BlockSpec(memory_space=pl.ANY)] + [vmem] * (1 + tiles + shares),
        out_specs=[vmem] * 3,
        scratch_shapes=[
            pltpu.VMEM(
                ((spans + 1) * own_frames * latent, len(cases) * LANES), jnp.bfloat16
            ),
            pltpu.VMEM((frames + 2, 9, latent, pixels), jnp.bfloat16),
            pltpu.VMEM((frames, pixels, CH), jnp.float32),
            pltpu.VMEM((frames, pixels + 2 * TSIDE, CH), jnp.bfloat16),
            pltpu.VMEM((3 * CH, 9 * lanes), jnp.bfloat16),
            pltpu.VMEM((3, frames, pixels, lanes), jnp.float32),
            pltpu.VMEM((8 * (frames + 1), own), jnp.float32),
            pltpu.SemaphoreType.DMA((27,)),
        ],
        compiler_params=pltpu.CompilerParams(vmem_limit_bytes=VMEM_BYTES),
        cost_estimate=pl.CostEstimate(
            flops=2 * frames * pixels * 27 * CH * lanes, bytes_accessed=8_000_000, transcendentals=0
        ),
    )(w_mid, table, *latents_all, *w_in_own, *w_in_all)
    total = ring_sum(kept, sent, "tm")
    total = ring_sum(total, [total] * (shares - 1), "chan")
    numer = total[0]
    for number, (down, across) in enumerate(cases):
        steps = down * GRID_X + across
        if steps and steps < tiles:
            numer = numer + shifted(total[number], "tile", steps)
    return jnp.transpose(numer / denom[0][None, None, :], (1, 0, 2))


def solution(mesh):
    placed = (
        P("tm", "groups", "tile"),
        P("groups"),
        P(None, None, "chan"),
        P("chan"),
        P("chan"),
        P(None, None, "chan"),
        P("chan"),
        P("chan"),
        P(None, "chan"),
        P("groups", None),
    )
    whole_lanes = (
        CH % (mesh.shape["chan"] * mesh.shape["tm"] * LANES) == 0
        and mesh.shape["chan"] <= mesh.shape["tile"] <= LANES
        and mesh.shape["tm"] * (STRIDE * STRIDE - LANES) <= LANES
    )
    return jax.shard_map(
        lanes_body if whole_lanes else general_body,
        mesh=mesh,
        in_specs=placed,
        out_specs=P("tm", "groups", "tile"),
        check_vma=False,
    )
```

```python
import functools

import jax
import jax.numpy as jnp
from jax import lax
from jax.experimental import pallas as pl
from jax.experimental.pallas import tpu as pltpu
from jax.sharding import PartitionSpec as P

CH = 512
GROUPS = 32
TSIDE = 16
STRIDE = 12
GRID_X = 4

EPSILON = 1e-06
LANES = 128
VMEM_BYTES = 48 * 1024 * 1024


def shifted(value, axis, steps):
    count = lax.axis_size(axis)
    leading, last = (max(0, -steps), min(count, count - steps))
    return lax.ppermute(value, axis, [(source, source + steps) for source in range(leading, last)])


def window_index(tile_id, tiles):
    slots = jnp.arange(TSIDE * TSIDE, dtype=jnp.int32)
    row = tile_id // GRID_X * STRIDE + slots // TSIDE
    col = tile_id % GRID_X * STRIDE + slots % TSIDE
    valid = (row < tiles // GRID_X * STRIDE) & (col < GRID_X * STRIDE)
    block = row // STRIDE * GRID_X + col // STRIDE
    index = block * (STRIDE * STRIDE) + row % STRIDE * STRIDE + col % STRIDE
    return (jnp.where(valid, index, 0), valid)


def causal_conv(extended, weights, frames, side):
    pixels = side * side
    rows = jnp.arange(pixels, dtype=jnp.int32) // side
    cols = jnp.arange(pixels, dtype=jnp.int32) % side
    total = jnp.zeros((frames, weights.shape[2], pixels), jnp.float32)
    for depth in range(3):
        window = extended[depth : depth + frames]
        for down in range(3):
            for across in range(3):
                offset = (down - 1) * side + (across - 1)
                inside = (
                    (rows + down - 1 >= 0)
                    & (rows + down - 1 < side)
                    & (cols + across - 1 >= 0)
                    & (cols + across - 1 < side)
                )
                moved = jnp.roll(window, -offset, axis=2)
                moved = jnp.where(inside[None, None, :], moved, jnp.zeros_like(moved))
                total = total + jnp.einsum(
                    "fcp,co->fop",
                    moved,
                    weights[9 * depth + 3 * down + across],
                    preferred_element_type=jnp.float32,
                )
    return total


def with_history(values):
    frames = values.shape[0]
    earlier = shifted(values[frames - 2 :], "tm", 1)
    return jnp.concatenate([earlier, values], axis=0)


def normalize(values, gain, shift, total_frames):
    frames, chans, pixels = values.shape
    width = CH // GROUPS
    grouped = values.reshape(frames, chans // width, width, pixels)
    sums = jnp.sum(grouped, axis=(0, 2, 3))
    squares = jnp.sum(grouped * grouped, axis=(0, 2, 3))
    sums, squares = lax.psum((sums, squares), "tm")
    count = total_frames * width * pixels
    mean = sums / count
    variance = squares / count - mean * mean
    scale = lax.rsqrt(variance + EPSILON)
    normed = (grouped - mean[None, :, None, None]) * scale[None, :, None, None]
    normed = normed.reshape(frames, chans, pixels) * gain[None, :, None] + shift[None, :, None]
    return jax.nn.silu(normed).astype(jnp.bfloat16)


def spread(color, weight, index, total_pixels):
    numer = (
        jnp.zeros((color.shape[0], 3, total_pixels), jnp.float32)
        .at[:, :, index]
        .add(color * weight[None, None, :])
    )
    denom = jnp.zeros((total_pixels,), jnp.float32).at[index].add(weight)
    return (numer, denom)


def route_owned(numer, denom, tile_id, own):
    frames = numer.shape[0]
    margin = (GRID_X + 1) * own
    numer_wide = jnp.concatenate([numer, jnp.zeros((frames, 3, margin), jnp.float32)], axis=2)
    denom_wide = jnp.concatenate([denom, jnp.zeros((margin,), jnp.float32)], axis=0)
    first_pixel = tile_id * own

    def block_at(offset):
        start_pixel = first_pixel + offset * own
        return (
            lax.dynamic_slice_in_dim(numer_wide, start_pixel, own, 2),
            lax.dynamic_slice_in_dim(denom_wide, start_pixel, own, 0),
        )

    owned_numer, owned_denom = block_at(0)
    for offset in (1, GRID_X, GRID_X + 1):
        piece_numer, piece_denom = block_at(offset)
        got_numer, got_denom = shifted((piece_numer, piece_denom), "tile", offset)
        owned_numer = owned_numer + got_numer
        owned_denom = owned_denom + got_denom
    return (owned_numer, owned_denom)


def general_body(
    latents, tile_order, w_in, gain_in, shift_in, w_mid, gain_mid, shift_mid, w_out, blend_weight
):
    frames = latents.shape[0]
    total_frames = frames * lax.axis_size("tm")
    tiles = tile_order.shape[0]
    own = STRIDE * STRIDE
    total_pixels = tiles * own
    tile_id = lax.axis_index("tile")
    index, valid = window_index(tile_id, tiles)
    whole = lax.all_gather(latents, "tile", axis=2, tiled=True)
    blocks = whole.reshape(frames, whole.shape[1], tiles, own)
    image = (
        jnp.zeros_like(blocks)
        .at[:, :, tile_order]
        .set(blocks)
        .reshape(frames, whole.shape[1], total_pixels)
    )
    window = jnp.where(
        valid[None, None, :], jnp.take(image, index, axis=2), jnp.zeros((), jnp.bfloat16)
    )
    first = causal_conv(with_history(window), w_in, frames, TSIDE)
    hidden = normalize(first, gain_in, shift_in, total_frames)
    second = causal_conv(
        lax.all_gather(with_history(hidden), "chan", axis=1, tiled=True), w_mid, frames, TSIDE
    )
    upper = normalize(second, gain_mid, shift_mid, total_frames)
    color = jnp.einsum("oc,fcp->fop", w_out, upper, preferred_element_type=jnp.float32)
    weight = jnp.where(valid, blend_weight[tile_id], jnp.float32(0.0))
    numer, denom = spread(color, weight, index, total_pixels)
    numer, denom = route_owned(numer, denom, tile_id, own)
    numer = lax.psum(numer, "chan")
    return numer / denom[None, None, :]


def block_cases(tiles):
    downs = (0, 1) if tiles // GRID_X > 1 else (0,)
    return [(down, across) for down in downs for across in (0, 1)]


def group_affine(sums, squares, gain, shift, count):
    lanes = sums.shape[1]
    width = CH // GROUPS
    same = lax.broadcasted_iota(jnp.int32, (lanes, lanes), 0) // width == (
        lax.broadcasted_iota(jnp.int32, (lanes, lanes), 1) // width
    )
    total = jnp.dot(
        jnp.concatenate([sums, squares], axis=0),
        jnp.where(same, 1.0, 0.0).astype(jnp.float32),
        precision=lax.Precision.HIGHEST,
        preferred_element_type=jnp.float32,
    )
    mean = jnp.sum(total[:8], axis=0, keepdims=True) / count
    variance = jnp.sum(total[8:], axis=0, keepdims=True) / count - mean * mean
    scale = gain * lax.rsqrt(variance + EPSILON)
    return 0.5 * scale, 0.5 * (shift - mean * scale)


def silu_of_half(half):
    return half + half * jnp.tanh(half)


def fold(values):
    rows, lanes = values.shape
    return jnp.sum(values.reshape(rows // 8, 8, lanes), axis=0)


def decode_kernel(
    tiles,
    spans,
    shares,
    *refs,
):
    cases = block_cases(tiles)
    refs = list(refs)

    def take(number):
        taken = refs[:number]
        del refs[:number]
        return taken

    w_mid_ref, table_ref, order_ref = take(3)
    latent_refs, w_in_refs = take(tiles), take(shares)
    keep_ref, send_ref, denom_ref = take(3)
    chosen, taps, first, hidden, weights, partial, shown_ref, sems = take(8)

    own = denom_ref.shape[1]
    own_frames = keep_ref.shape[2]
    frames = own_frames * spans
    latent, wide = w_in_refs[0].shape[1:]
    rows_in = frames * latent
    rows_own = rows_in // spans
    depth_in = 27 * latent
    pixels = TSIDE * TSIDE
    lanes = partial.shape[3]
    tile_id = lax.axis_index("tile")
    mine = lax.axis_index("tm")
    chan_id = lax.axis_index("chan")

    copies = []
    for a in range(3):
        for b in range(3):
            for e in range(3):
                tap = 9 * a + 3 * b + e
                copy = pltpu.make_async_copy(
                    w_mid_ref.at[tap, :, pl.ds(pl.multiple_of(mine * lanes, LANES), lanes)],
                    weights.at[pl.ds(b * CH, CH), pl.ds((3 * a + e) * lanes, lanes)],
                    sems.at[tap],
                )
                copy.start()
                copies.append(copy)

    tile_row, tile_col = tile_id // GRID_X, tile_id % GRID_X
    gain_row = rows_own + 2
    w_out_row = gain_row + 2
    blend_row = w_out_row + 3
    order = order_ref[...]
    number_of = lax.broadcasted_iota(jnp.int32, order.shape, 0)
    lane_of = lax.broadcasted_iota(jnp.int32, order.shape, 1)
    rows_sent = rows_in + latent
    for number, (down, across) in enumerate(cases):
        inside = (tile_row + down < tiles // GRID_X) & (tile_col + across < GRID_X)
        wanted = tile_id + down * GRID_X + across
        found = (order == wanted.astype(jnp.float32)) & (lane_of == 0)
        place = jnp.sum(jnp.where(found, number_of.astype(jnp.float32), 0.0))
        turn = (tile_id - place.astype(jnp.int32) + tiles) % tiles
        part = slice(number * LANES, (number + 1) * LANES)
        for steps in range(tiles):

            @pl.when(inside & (turn == steps))
            def _():
                chosen[:, part] = latent_refs[steps][:rows_sent]

        @pl.when(jnp.logical_not(inside))
        def _():
            chosen[:, part] = jnp.zeros((rows_sent, LANES), chosen.dtype)

    slot = lax.broadcasted_iota(jnp.int32, (1, pixels), 1)
    up, along = slot // TSIDE, slot % TSIDE
    source = lax.broadcasted_iota(jnp.int32, (LANES, pixels), 0)
    tail = own - LANES

    def pick(swap):
        parts = []
        for down, across in cases:
            u, v = up - down * STRIDE, along - across * STRIDE
            good = (u >= 0) & (u < STRIDE) & (v >= 0) & (v < STRIDE)
            wanted = jnp.where(good, u * STRIDE + v, -1)
            if swap is not None:
                wanted = jnp.where(wanted >= LANES, wanted - LANES + tail * swap, -1)
            parts.append(jnp.where(source == wanted, 1.0, 0.0).astype(jnp.bfloat16))
        return jnp.concatenate(parts, axis=0)

    window = jnp.dot(chosen[:rows_in], pick(None), preferred_element_type=jnp.float32)
    tails = chosen[rows_in:].astype(jnp.float32)
    width = tails.shape[1]
    tails = jnp.concatenate(
        [
            pltpu.roll(tails, (-f * spans * tail) % width, 1) if f else tails
            for f in range(own_frames)
        ],
        axis=0,
    ).astype(jnp.bfloat16)
    ends = [
        jnp.dot(tails, pick(swap), preferred_element_type=jnp.float32) for swap in range(spans)
    ]
    window = window + jnp.concatenate(ends, axis=0)
    taps[0:2] = jnp.zeros((2,) + taps.shape[1:], taps.dtype)
    for b in range(3):
        for e in range(3):
            inside = (
                (up + b - 1 >= 0)
                & (up + b - 1 < TSIDE)
                & (along + e - 1 >= 0)
                & (along + e - 1 < TSIDE)
            )
            offset = (b - 1) * TSIDE + e - 1
            moved = pltpu.roll(window, (-offset) % pixels, 1) if offset else window
            moved = jnp.where(inside, moved, 0.0).astype(jnp.bfloat16)
            for swap in range(spans):
                value = moved[swap * rows_own : (swap + 1) * rows_own]
                span = pl.ds(2 + (mine + swap) % spans * own_frames, own_frames)
                taps[span, 3 * b + e] = value.reshape(own_frames, latent, pixels)

    joined = jnp.concatenate(
        [w_in_refs[s][:27].reshape(depth_in, wide) for s in range(shares)], axis=1
    )
    sums = jnp.zeros((8, CH), jnp.float32)
    squares = jnp.zeros((8, CH), jnp.float32)
    for f in range(frames):
        patch = taps[f : f + 3].reshape(depth_in, pixels)
        value = lax.dot_general(
            patch, joined, (((0,), (0,)), ((), ())), preferred_element_type=jnp.float32
        )
        first[f] = value
        sums = sums + fold(value)
        squares = squares + fold(value * value)
    count = frames * (CH // GROUPS) * pixels
    affine = []
    for s in range(shares):
        at = rows_sent
        table = latent_refs[s][at : at + wide // LANES * 4].astype(jnp.float32)
        pieces = [table[4 * lane : 4 * lane + 4] for lane in range(wide // LANES)]
        table = jnp.concatenate([part[0:2] + part[2:4] for part in pieces], axis=1)
        part = slice(s * wide, (s + 1) * wide)
        affine.append(
            group_affine(sums[:, part], squares[:, part], table[0:1], table[1:2], count)
        )
    channels = [
        pl.ds(pl.multiple_of((chan_id + s) % shares * wide, LANES), wide) for s in range(shares)
    ]

    def hide(f):
        edge = jnp.zeros((TSIDE, CH), jnp.bfloat16)
        hidden[f, 0:TSIDE] = edge
        hidden[f, TSIDE + pixels : 2 * TSIDE + pixels] = edge
        for s in range(shares):
            scale, bias = affine[s]
            value = first[f, :, s * wide : (s + 1) * wide] * scale + bias
            hidden[f, TSIDE : TSIDE + pixels, channels[s]] = silu_of_half(value).astype(
                jnp.bfloat16
            )

    def convolve(start, several, depth_taps):
        lhs = jnp.concatenate(
            [
                hidden[start : start + several, b * TSIDE : b * TSIDE + pixels].reshape(
                    several * pixels, CH
                )
                for b in range(3)
            ],
            axis=1,
        )
        low = depth_taps[0] * 3 * lanes
        product = jnp.dot(lhs, weights[:, low:], preferred_element_type=jnp.float32)
        for a in depth_taps:
            for e in range(3):
                at = (3 * a + e) * lanes - low
                for f in range(several):
                    target = start + f + 2 - a
                    value = product[f * pixels : (f + 1) * pixels, at : at + lanes]
                    if start + f == max(target - 2, 0):
                        partial[e, target] = value
                    else:
                        partial[e, target] += value

    column = lax.broadcasted_iota(jnp.int32, (pixels, lanes), 0) % TSIDE
    total = [jnp.zeros((8, lanes), jnp.float32)] * 2

    def gather(f):
        left = jnp.where(column == 0, 0.0, pltpu.roll(partial[0, f], 1, 0))
        right = jnp.where(column == TSIDE - 1, 0.0, pltpu.roll(partial[2, f], pixels - 1, 0))
        value = partial[1, f] + left + right
        partial[1, f] = value
        total[0] = total[0] + fold(value)
        total[1] = total[1] + fold(value * value)

    together = 2
    groups = [range(f, f + together) for f in range(0, frames - 2, together)]
    groups += [range(f, f + 1) for f in range(groups[-1].stop, frames)]
    for copy in copies:
        copy.wait()
    for f in groups[0]:
        hide(f)
    for number, group in enumerate(groups):
        if number + 1 < len(groups):
            for f in groups[number + 1]:
                hide(f)
        convolve(
            group.start,
            len(group),
            tuple(a for a in range(3) if group.stop - 1 + 2 - a < frames),
        )
        if number:
            for f in groups[number - 1]:
                gather(f)
    for f in groups[-1]:
        gather(f)

    part = pl.ds(pl.multiple_of(mine * lanes, LANES), lanes)
    scale, bias = group_affine(
        total[0],
        total[1],
        table_ref[gain_row : gain_row + 1, part],
        table_ref[gain_row + 1 : gain_row + 2, part],
        count,
    )
    blend = table_ref[pl.ds(blend_row + tile_id, 1), :]
    blend = jnp.where(
        (tile_row * STRIDE + up < tiles // GRID_X * STRIDE)
        & (tile_col * STRIDE + along < GRID_X * STRIDE),
        blend,
        0.0,
    )
    w_out = jnp.concatenate(
        [table_ref[w_out_row : w_out_row + 3, part], jnp.zeros((5, lanes), jnp.float32)], axis=0
    ).astype(jnp.bfloat16)
    colors = []
    for f in range(frames):
        upper = silu_of_half(partial[1, f] * scale + bias).astype(jnp.bfloat16)
        color = lax.dot_general(
            w_out, upper, (((1,), (1,)), ((), ())), preferred_element_type=jnp.float32
        )
        colors.append(color * blend)
    colors = jnp.concatenate(colors, axis=0)

    slot_in = lax.broadcasted_iota(jnp.int32, (pixels, own), 0)
    pixel = lax.broadcasted_iota(jnp.int32, (pixels, own), 1)
    denom = jnp.zeros((8, own), jnp.float32)
    for number, (down, across) in enumerate(cases):
        u, v = slot_in // TSIDE - down * STRIDE, slot_in % TSIDE - across * STRIDE
        good = (u >= 0) & (u < STRIDE) & (v >= 0) & (v < STRIDE) & (u * STRIDE + v == pixel)
        shown = jnp.where(good, 1.0, 0.0).astype(jnp.float32)
        inside = (tile_row >= down) & (tile_col >= across)
        other = jnp.maximum(tile_id - down * GRID_X - across, 0)
        weight = jnp.where(inside, table_ref[pl.ds(blend_row + other, 1), :], 0.0)
        piece = jnp.dot(
            jnp.concatenate([colors, jnp.broadcast_to(weight, (8, pixels))], axis=0),
            shown,
            precision=lax.Precision.HIGHEST,
            preferred_element_type=jnp.float32,
        )
        denom = denom + piece[8 * frames :]
        shown_ref[...] = piece
        for swap in range(spans):
            target = keep_ref if swap == 0 else send_ref.at[swap - 1]
            base = (mine + swap) % spans * own_frames * 8
            for at in range(own_frames):
                for o in range(3):
                    target[number, o, at : at + 1, :] = shown_ref[pl.ds(base + 8 * at + o, 1), :]

    denom_ref[...] = denom


def from_ring(value, axis):
    count = lax.axis_size(axis)
    return [
        lax.ppermute(value, axis, [((d + turn) % count, d) for d in range(count)])
        for turn in range(1, count)
    ]


def ring_sum(kept, sent, axis):
    count = lax.axis_size(axis)
    for turn in range(1, count):
        kept = kept + lax.ppermute(
            sent[turn - 1], axis, [(d, (d + turn) % count) for d in range(count)]
        )
    return kept


def small_table(*values):
    values = [value.reshape(-1, value.shape[-1]) for value in values]
    wide = max(value.shape[1] for value in values)
    height = sum(value.shape[0] for value in values)
    total, row = 0.0, 0
    for value in values:
        below = height - row - value.shape[0]
        value = jnp.pad(value.astype(jnp.float32), ((row, below), (0, wide - value.shape[1])))
        total = total + value
        row = height - below
    return total


def exchange_latents(latents, table):
    tiles, shares, spans = (lax.axis_size(name) for name in ("tile", "chan", "tm"))
    frames, latent, own = latents.shape
    tail = own - LANES
    height = frames * latent
    others = from_ring(latents.reshape(height, own), "tm")
    parts = [table[:height, :own].astype(jnp.bfloat16)] + others
    tails = sum(
        jnp.pad(
            part[f * latent : (f + 1) * latent, LANES:],
            ((0, 0), (tail * (f * spans + at), LANES - tail * (f * spans + at + 1))),
        )
        for at, part in enumerate(parts)
        for f in range(frames)
    )
    affine = table[height : height + 2]
    high = lax.reduce_precision(affine, 8, 7)
    low = lax.reduce_precision(affine - high, 8, 7)
    affine = jnp.concatenate([high, low], axis=0).astype(jnp.bfloat16)
    rows = [affine[:, at : at + LANES] for at in range(0, affine.shape[1], LANES)]
    rows = jnp.concatenate(rows, axis=0)
    rows = jnp.pad(rows, ((0, -rows.shape[0] % 16), (0, 0)))
    message = jnp.concatenate([part[:, :LANES] for part in parts] + [tails, rows], axis=0)
    got = [message]
    for steps in range(1, tiles):
        turn = steps if steps < shares else 0
        pairs = [
            (t * shares + (c + turn) % shares, (t + steps) % tiles * shares + c)
            for t in range(tiles)
            for c in range(shares)
        ]
        got.append(lax.ppermute(message, ("tile", "chan"), pairs))
    return got


def lanes_body(
    latents, tile_order, w_in, gain_in, shift_in, w_mid, gain_mid, shift_mid, w_out, blend_weight
):
    own_frames, latent, own = latents.shape
    spans = lax.axis_size("tm")
    shares = lax.axis_size("chan")
    frames = own_frames * spans
    tiles = tile_order.shape[0]
    wide = w_in.shape[2]
    lanes = wide // spans
    pixels = TSIDE * TSIDE
    cases = block_cases(tiles)

    w_in_all = from_ring(w_in, "chan")
    table = lax.optimization_barrier(
        small_table(
            latents.reshape(own_frames * latent, own),
            gain_in,
            shift_in,
            gain_mid,
            shift_mid,
            w_out,
            blend_weight,
        )
    )
    latents_all = exchange_latents(latents, table)
    _, w_in, tile_order = lax.optimization_barrier((latents_all[0], w_in, tile_order))
    order = jnp.broadcast_to(tile_order.astype(jnp.float32)[:, None], (tiles, LANES))
    w_in_own = from_ring(w_in, "tm")[:1] or [w_in]

    vmem = pl.BlockSpec(memory_space=pltpu.VMEM)
    piece = (len(cases), 3, own_frames, own)
    kept, sent, denom = pl.pallas_call(
        functools.partial(decode_kernel, tiles, spans, shares),
        out_shape=[
            jax.ShapeDtypeStruct(piece, jnp.float32),
            jax.ShapeDtypeStruct((max(spans - 1, 1),) + piece, jnp.float32),
            jax.ShapeDtypeStruct((8, own), jnp.float32),
        ],
        in_specs=[pl.BlockSpec(memory_space=pl.ANY)] + [vmem] * (2 + tiles + shares),
        out_specs=[vmem] * 3,
        scratch_shapes=[
            pltpu.VMEM(((frames + 1) * latent, len(cases) * LANES), jnp.bfloat16),
            pltpu.VMEM((frames + 2, 9, latent, pixels), jnp.bfloat16),
            pltpu.VMEM((frames, pixels, CH), jnp.float32),
            pltpu.VMEM((frames, pixels + 2 * TSIDE, CH), jnp.bfloat16),
            pltpu.VMEM((3 * CH, 9 * lanes), jnp.bfloat16),
            pltpu.VMEM((3, frames, pixels, lanes), jnp.float32),
            pltpu.VMEM((8 * (frames + 1), own), jnp.float32),
            pltpu.SemaphoreType.DMA((27,)),
        ],
        compiler_params=pltpu.CompilerParams(vmem_limit_bytes=VMEM_BYTES),
        cost_estimate=pl.CostEstimate(
            flops=2 * frames * pixels * 27 * CH * lanes, bytes_accessed=8_000_000, transcendentals=0
        ),
    )(w_mid, table, order, *latents_all, *w_in_own, *w_in_all)
    total = ring_sum(kept, sent, "tm")
    total = ring_sum(total, [total] * (shares - 1), "chan")
    numer = total[0]
    for number, (down, across) in enumerate(cases):
        steps = down * GRID_X + across
        if steps and steps < tiles:
            numer = numer + shifted(total[number], "tile", steps)
    return jnp.transpose(numer / denom[0][None, None, :], (1, 0, 2))


def solution(mesh):
    placed = (
        P("tm", "groups", "tile"),
        P("groups"),
        P(None, None, "chan"),
        P("chan"),
        P("chan"),
        P(None, None, "chan"),
        P("chan"),
        P("chan"),
        P(None, "chan"),
        P("groups", None),
    )
    whole_lanes = (
        CH % (mesh.shape["chan"] * mesh.shape["tm"] * LANES) == 0
        and mesh.shape["chan"] <= mesh.shape["tile"]
    )
    return jax.shard_map(
        lanes_body if whole_lanes else general_body,
        mesh=mesh,
        in_specs=placed,
        out_specs=P("tm", "groups", "tile"),
        check_vma=False,
    )
```

```python
import functools

import jax
import jax.numpy as jnp
from jax import lax
from jax.experimental import pallas as pl
from jax.experimental.pallas import tpu as pltpu
from jax.sharding import PartitionSpec as P

CH = 512
GROUPS = 32
TSIDE = 16
STRIDE = 12
GRID_X = 4

EPSILON = 1e-06
LANES = 128
VMEM_BYTES = 48 * 1024 * 1024


def shifted(value, axis, steps):
    count = lax.axis_size(axis)
    leading, last = (max(0, -steps), min(count, count - steps))
    return lax.ppermute(value, axis, [(source, source + steps) for source in range(leading, last)])


def window_index(tile_id, tiles):
    slots = jnp.arange(TSIDE * TSIDE, dtype=jnp.int32)
    row = tile_id // GRID_X * STRIDE + slots // TSIDE
    col = tile_id % GRID_X * STRIDE + slots % TSIDE
    valid = (row < tiles // GRID_X * STRIDE) & (col < GRID_X * STRIDE)
    block = row // STRIDE * GRID_X + col // STRIDE
    index = block * (STRIDE * STRIDE) + row % STRIDE * STRIDE + col % STRIDE
    return (jnp.where(valid, index, 0), valid)


def causal_conv(extended, weights, frames, side):
    pixels = side * side
    rows = jnp.arange(pixels, dtype=jnp.int32) // side
    cols = jnp.arange(pixels, dtype=jnp.int32) % side
    total = jnp.zeros((frames, weights.shape[2], pixels), jnp.float32)
    for depth in range(3):
        window = extended[depth : depth + frames]
        for down in range(3):
            for across in range(3):
                offset = (down - 1) * side + (across - 1)
                inside = (
                    (rows + down - 1 >= 0)
                    & (rows + down - 1 < side)
                    & (cols + across - 1 >= 0)
                    & (cols + across - 1 < side)
                )
                moved = jnp.roll(window, -offset, axis=2)
                moved = jnp.where(inside[None, None, :], moved, jnp.zeros_like(moved))
                total = total + jnp.einsum(
                    "fcp,co->fop",
                    moved,
                    weights[9 * depth + 3 * down + across],
                    preferred_element_type=jnp.float32,
                )
    return total


def with_history(values):
    frames = values.shape[0]
    earlier = shifted(values[frames - 2 :], "tm", 1)
    return jnp.concatenate([earlier, values], axis=0)


def normalize(values, gain, shift, total_frames):
    frames, chans, pixels = values.shape
    width = CH // GROUPS
    grouped = values.reshape(frames, chans // width, width, pixels)
    sums = jnp.sum(grouped, axis=(0, 2, 3))
    squares = jnp.sum(grouped * grouped, axis=(0, 2, 3))
    sums, squares = lax.psum((sums, squares), "tm")
    count = total_frames * width * pixels
    mean = sums / count
    variance = squares / count - mean * mean
    scale = lax.rsqrt(variance + EPSILON)
    normed = (grouped - mean[None, :, None, None]) * scale[None, :, None, None]
    normed = normed.reshape(frames, chans, pixels) * gain[None, :, None] + shift[None, :, None]
    return jax.nn.silu(normed).astype(jnp.bfloat16)


def spread(color, weight, index, total_pixels):
    numer = (
        jnp.zeros((color.shape[0], 3, total_pixels), jnp.float32)
        .at[:, :, index]
        .add(color * weight[None, None, :])
    )
    denom = jnp.zeros((total_pixels,), jnp.float32).at[index].add(weight)
    return (numer, denom)


def route_owned(numer, denom, tile_id, own):
    frames = numer.shape[0]
    margin = (GRID_X + 1) * own
    numer_wide = jnp.concatenate([numer, jnp.zeros((frames, 3, margin), jnp.float32)], axis=2)
    denom_wide = jnp.concatenate([denom, jnp.zeros((margin,), jnp.float32)], axis=0)
    first_pixel = tile_id * own

    def block_at(offset):
        start_pixel = first_pixel + offset * own
        return (
            lax.dynamic_slice_in_dim(numer_wide, start_pixel, own, 2),
            lax.dynamic_slice_in_dim(denom_wide, start_pixel, own, 0),
        )

    owned_numer, owned_denom = block_at(0)
    for offset in (1, GRID_X, GRID_X + 1):
        piece_numer, piece_denom = block_at(offset)
        got_numer, got_denom = shifted((piece_numer, piece_denom), "tile", offset)
        owned_numer = owned_numer + got_numer
        owned_denom = owned_denom + got_denom
    return (owned_numer, owned_denom)


def general_body(
    latents, tile_order, w_in, gain_in, shift_in, w_mid, gain_mid, shift_mid, w_out, blend_weight
):
    frames = latents.shape[0]
    total_frames = frames * lax.axis_size("tm")
    tiles = tile_order.shape[0]
    own = STRIDE * STRIDE
    total_pixels = tiles * own
    tile_id = lax.axis_index("tile")
    index, valid = window_index(tile_id, tiles)
    whole = lax.all_gather(latents, "tile", axis=2, tiled=True)
    blocks = whole.reshape(frames, whole.shape[1], tiles, own)
    image = (
        jnp.zeros_like(blocks)
        .at[:, :, tile_order]
        .set(blocks)
        .reshape(frames, whole.shape[1], total_pixels)
    )
    window = jnp.where(
        valid[None, None, :], jnp.take(image, index, axis=2), jnp.zeros((), jnp.bfloat16)
    )
    first = causal_conv(with_history(window), w_in, frames, TSIDE)
    hidden = normalize(first, gain_in, shift_in, total_frames)
    second = causal_conv(
        lax.all_gather(with_history(hidden), "chan", axis=1, tiled=True), w_mid, frames, TSIDE
    )
    upper = normalize(second, gain_mid, shift_mid, total_frames)
    color = jnp.einsum("oc,fcp->fop", w_out, upper, preferred_element_type=jnp.float32)
    weight = jnp.where(valid, blend_weight[tile_id], jnp.float32(0.0))
    numer, denom = spread(color, weight, index, total_pixels)
    numer, denom = route_owned(numer, denom, tile_id, own)
    numer = lax.psum(numer, "chan")
    return numer / denom[None, None, :]


def block_cases(tiles):
    downs = (0, 1) if tiles // GRID_X > 1 else (0,)
    return [(down, across) for down in downs for across in (0, 1)]


def group_affine(sums, squares, gain, shift, count):
    lanes = sums.shape[1]
    width = CH // GROUPS
    same = lax.broadcasted_iota(jnp.int32, (lanes, lanes), 0) // width == (
        lax.broadcasted_iota(jnp.int32, (lanes, lanes), 1) // width
    )
    total = jnp.dot(
        jnp.concatenate([sums, squares], axis=0),
        jnp.where(same, 1.0, 0.0).astype(jnp.float32),
        precision=lax.Precision.HIGHEST,
        preferred_element_type=jnp.float32,
    )
    mean = jnp.sum(total[:8], axis=0, keepdims=True) / count
    variance = jnp.sum(total[8:], axis=0, keepdims=True) / count - mean * mean
    scale = gain * lax.rsqrt(variance + EPSILON)
    return 0.5 * scale, 0.5 * (shift - mean * scale)


def silu_of_half(half):
    return half + half * jnp.tanh(half)


def fold(values):
    rows, lanes = values.shape
    return jnp.sum(values.reshape(rows // 8, 8, lanes), axis=0)


def decode_kernel(
    tiles,
    spans,
    shares,
    *refs,
):
    cases = block_cases(tiles)
    refs = list(refs)

    def take(number):
        taken = refs[:number]
        del refs[:number]
        return taken

    w_mid_ref, table_ref, order_ref = take(3)
    latent_refs, w_in_refs = take(tiles), take(shares)
    keep_ref, send_ref, denom_ref = take(3)
    chosen, taps, first, hidden, weights, partial, shown_ref, sems = take(8)

    own = denom_ref.shape[1]
    own_frames = keep_ref.shape[2]
    frames = own_frames * spans
    latent, wide = w_in_refs[0].shape[1:]
    rows_in = frames * latent
    rows_own = rows_in // spans
    depth_in = 27 * latent
    pixels = TSIDE * TSIDE
    lanes = partial.shape[3]
    tile_id = lax.axis_index("tile")
    mine = lax.axis_index("tm")
    chan_id = lax.axis_index("chan")

    copies = []
    for a in range(3):
        for b in range(3):
            for e in range(3):
                tap = 9 * a + 3 * b + e
                copy = pltpu.make_async_copy(
                    w_mid_ref.at[tap, :, pl.ds(pl.multiple_of(mine * lanes, LANES), lanes)],
                    weights.at[pl.ds(b * CH, CH), pl.ds((3 * a + e) * lanes, lanes)],
                    sems.at[tap],
                )
                copy.start()
                copies.append(copy)

    tile_row, tile_col = tile_id // GRID_X, tile_id % GRID_X
    gain_row = rows_own + 2
    w_out_row = gain_row + 2
    blend_row = w_out_row + 3
    order = order_ref[...]
    number_of = lax.broadcasted_iota(jnp.int32, order.shape, 0)
    lane_of = lax.broadcasted_iota(jnp.int32, order.shape, 1)
    rows_sent = rows_in + latent
    for number, (down, across) in enumerate(cases):
        inside = (tile_row + down < tiles // GRID_X) & (tile_col + across < GRID_X)
        wanted = tile_id + down * GRID_X + across
        found = (order == wanted.astype(jnp.float32)) & (lane_of == 0)
        place = jnp.sum(jnp.where(found, number_of.astype(jnp.float32), 0.0))
        turn = (tile_id - place.astype(jnp.int32) + tiles) % tiles
        part = slice(number * LANES, (number + 1) * LANES)
        for steps in range(tiles):

            @pl.when(inside & (turn == steps))
            def _():
                chosen[:, part] = latent_refs[steps][:rows_sent]

        @pl.when(jnp.logical_not(inside))
        def _():
            chosen[:, part] = jnp.zeros((rows_sent, LANES), chosen.dtype)

    slot = lax.broadcasted_iota(jnp.int32, (1, pixels), 1)
    up, along = slot // TSIDE, slot % TSIDE
    source = lax.broadcasted_iota(jnp.int32, (LANES, pixels), 0)
    tail = own - LANES

    def pick(swap):
        parts = []
        for down, across in cases:
            u, v = up - down * STRIDE, along - across * STRIDE
            good = (u >= 0) & (u < STRIDE) & (v >= 0) & (v < STRIDE)
            wanted = jnp.where(good, u * STRIDE + v, -1)
            if swap is not None:
                wanted = jnp.where(wanted >= LANES, wanted - LANES + tail * swap, -1)
            parts.append(jnp.where(source == wanted, 1.0, 0.0).astype(jnp.bfloat16))
        return jnp.concatenate(parts, axis=0)

    window = jnp.dot(chosen[:rows_in], pick(None), preferred_element_type=jnp.float32)
    tails = chosen[rows_in:].astype(jnp.float32)
    width = tails.shape[1]
    tails = jnp.concatenate(
        [
            pltpu.roll(tails, (-f * spans * tail) % width, 1) if f else tails
            for f in range(own_frames)
        ],
        axis=0,
    ).astype(jnp.bfloat16)
    ends = [
        jnp.dot(tails, pick(swap), preferred_element_type=jnp.float32) for swap in range(spans)
    ]
    window = window + jnp.concatenate(ends, axis=0)
    taps[0:2] = jnp.zeros((2,) + taps.shape[1:], taps.dtype)
    for b in range(3):
        for e in range(3):
            inside = (
                (up + b - 1 >= 0)
                & (up + b - 1 < TSIDE)
                & (along + e - 1 >= 0)
                & (along + e - 1 < TSIDE)
            )
            offset = (b - 1) * TSIDE + e - 1
            moved = pltpu.roll(window, (-offset) % pixels, 1) if offset else window
            moved = jnp.where(inside, moved, 0.0).astype(jnp.bfloat16)
            for swap in range(spans):
                value = moved[swap * rows_own : (swap + 1) * rows_own]
                span = pl.ds(2 + (mine + swap) % spans * own_frames, own_frames)
                taps[span, 3 * b + e] = value.reshape(own_frames, latent, pixels)

    joined = jnp.concatenate(
        [w_in_refs[s][:27].reshape(depth_in, wide) for s in range(shares)], axis=1
    )
    sums = jnp.zeros((8, CH), jnp.float32)
    squares = jnp.zeros((8, CH), jnp.float32)
    for f in range(frames):
        patch = taps[f : f + 3].reshape(depth_in, pixels)
        value = lax.dot_general(
            patch, joined, (((0,), (0,)), ((), ())), preferred_element_type=jnp.float32
        )
        first[f] = value
        sums = sums + fold(value)
        squares = squares + fold(value * value)
    count = frames * (CH // GROUPS) * pixels
    affine = []
    for s in range(shares):
        at = rows_sent
        table = latent_refs[s][at : at + wide // LANES * 4].astype(jnp.float32)
        pieces = [table[4 * lane : 4 * lane + 4] for lane in range(wide // LANES)]
        table = jnp.concatenate([part[0:2] + part[2:4] for part in pieces], axis=1)
        part = slice(s * wide, (s + 1) * wide)
        affine.append(
            group_affine(sums[:, part], squares[:, part], table[0:1], table[1:2], count)
        )
    channels = [
        pl.ds(pl.multiple_of((chan_id + s) % shares * wide, LANES), wide) for s in range(shares)
    ]

    def hide(f):
        edge = jnp.zeros((TSIDE, CH), jnp.bfloat16)
        hidden[f, 0:TSIDE] = edge
        hidden[f, TSIDE + pixels : 2 * TSIDE + pixels] = edge
        for s in range(shares):
            scale, bias = affine[s]
            value = first[f, :, s * wide : (s + 1) * wide] * scale + bias
            hidden[f, TSIDE : TSIDE + pixels, channels[s]] = silu_of_half(value).astype(
                jnp.bfloat16
            )

    def convolve(start, several, depth_taps):
        lhs = jnp.concatenate(
            [
                hidden[start : start + several, b * TSIDE : b * TSIDE + pixels].reshape(
                    several * pixels, CH
                )
                for b in range(3)
            ],
            axis=1,
        )
        low = depth_taps[0] * 3 * lanes
        product = jnp.dot(lhs, weights[:, low:], preferred_element_type=jnp.float32)
        for a in depth_taps:
            for e in range(3):
                at = (3 * a + e) * lanes - low
                for f in range(several):
                    target = start + f + 2 - a
                    value = product[f * pixels : (f + 1) * pixels, at : at + lanes]
                    if start + f == max(target - 2, 0):
                        partial[e, target] = value
                    else:
                        partial[e, target] += value

    column = lax.broadcasted_iota(jnp.int32, (pixels, lanes), 0) % TSIDE
    total = [jnp.zeros((8, lanes), jnp.float32)] * 2

    def gather(f):
        left = jnp.where(column == 0, 0.0, pltpu.roll(partial[0, f], 1, 0))
        right = jnp.where(column == TSIDE - 1, 0.0, pltpu.roll(partial[2, f], pixels - 1, 0))
        value = partial[1, f] + left + right
        partial[1, f] = value
        total[0] = total[0] + fold(value)
        total[1] = total[1] + fold(value * value)

    together = 3
    groups = [
        range(f, min(f + together, frames - 2)) for f in range(0, frames - 2, together)
    ]
    groups += [range(f, f + 1) for f in range(groups[-1].stop, frames)]
    for copy in copies:
        copy.wait()
    for f in groups[0]:
        hide(f)
    for number, group in enumerate(groups):
        if number + 1 < len(groups):
            for f in groups[number + 1]:
                hide(f)
        convolve(
            group.start,
            len(group),
            tuple(a for a in range(3) if group.stop - 1 + 2 - a < frames),
        )
        if number:
            for f in groups[number - 1]:
                gather(f)
    for f in groups[-1]:
        gather(f)

    part = pl.ds(pl.multiple_of(mine * lanes, LANES), lanes)
    scale, bias = group_affine(
        total[0],
        total[1],
        table_ref[gain_row : gain_row + 1, part],
        table_ref[gain_row + 1 : gain_row + 2, part],
        count,
    )
    blend = table_ref[pl.ds(blend_row + tile_id, 1), :]
    blend = jnp.where(
        (tile_row * STRIDE + up < tiles // GRID_X * STRIDE)
        & (tile_col * STRIDE + along < GRID_X * STRIDE),
        blend,
        0.0,
    )
    w_out = jnp.concatenate(
        [table_ref[w_out_row : w_out_row + 3, part], jnp.zeros((5, lanes), jnp.float32)], axis=0
    ).astype(jnp.bfloat16)
    colors = []
    for f in range(frames):
        upper = silu_of_half(partial[1, f] * scale + bias).astype(jnp.bfloat16)
        color = lax.dot_general(
            w_out, upper, (((1,), (1,)), ((), ())), preferred_element_type=jnp.float32
        )
        colors.append(color * blend)
    colors = jnp.concatenate(colors, axis=0)

    slot_in = lax.broadcasted_iota(jnp.int32, (pixels, own), 0)
    pixel = lax.broadcasted_iota(jnp.int32, (pixels, own), 1)
    denom = jnp.zeros((8, own), jnp.float32)
    for number, (down, across) in enumerate(cases):
        u, v = slot_in // TSIDE - down * STRIDE, slot_in % TSIDE - across * STRIDE
        good = (u >= 0) & (u < STRIDE) & (v >= 0) & (v < STRIDE) & (u * STRIDE + v == pixel)
        shown = jnp.where(good, 1.0, 0.0).astype(jnp.float32)
        inside = (tile_row >= down) & (tile_col >= across)
        other = jnp.maximum(tile_id - down * GRID_X - across, 0)
        weight = jnp.where(inside, table_ref[pl.ds(blend_row + other, 1), :], 0.0)
        piece = jnp.dot(
            jnp.concatenate([colors, jnp.broadcast_to(weight, (8, pixels))], axis=0),
            shown,
            precision=lax.Precision.HIGHEST,
            preferred_element_type=jnp.float32,
        )
        denom = denom + piece[8 * frames :]
        shown_ref[...] = piece
        for swap in range(spans):
            target = keep_ref if swap == 0 else send_ref.at[swap - 1]
            base = (mine + swap) % spans * own_frames * 8
            for at in range(own_frames):
                for o in range(3):
                    target[number, o, at : at + 1, :] = shown_ref[pl.ds(base + 8 * at + o, 1), :]

    denom_ref[...] = denom


def from_ring(value, axis):
    count = lax.axis_size(axis)
    return [
        lax.ppermute(value, axis, [((d + turn) % count, d) for d in range(count)])
        for turn in range(1, count)
    ]


def ring_sum(kept, sent, axis):
    count = lax.axis_size(axis)
    for turn in range(1, count):
        kept = kept + lax.ppermute(
            sent[turn - 1], axis, [(d, (d + turn) % count) for d in range(count)]
        )
    return kept


def small_table(*values):
    values = [value.reshape(-1, value.shape[-1]) for value in values]
    wide = max(value.shape[1] for value in values)
    height = sum(value.shape[0] for value in values)
    total, row = 0.0, 0
    for value in values:
        below = height - row - value.shape[0]
        value = jnp.pad(value.astype(jnp.float32), ((row, below), (0, wide - value.shape[1])))
        total = total + value
        row = height - below
    return total


def exchange_latents(latents, table):
    tiles, shares, spans = (lax.axis_size(name) for name in ("tile", "chan", "tm"))
    frames, latent, own = latents.shape
    tail = own - LANES
    height = frames * latent
    others = from_ring(latents.reshape(height, own), "tm")
    parts = [table[:height, :own].astype(jnp.bfloat16)] + others
    tails = sum(
        jnp.pad(
            part[f * latent : (f + 1) * latent, LANES:],
            ((0, 0), (tail * (f * spans + at), LANES - tail * (f * spans + at + 1))),
        )
        for at, part in enumerate(parts)
        for f in range(frames)
    )
    affine = table[height : height + 2]
    high = lax.reduce_precision(affine, 8, 7)
    low = lax.reduce_precision(affine - high, 8, 7)
    affine = jnp.concatenate([high, low], axis=0).astype(jnp.bfloat16)
    rows = [affine[:, at : at + LANES] for at in range(0, affine.shape[1], LANES)]
    rows = jnp.concatenate(rows, axis=0)
    rows = jnp.pad(rows, ((0, -rows.shape[0] % 16), (0, 0)))
    message = jnp.concatenate([part[:, :LANES] for part in parts] + [tails, rows], axis=0)
    got = [message]
    for steps in range(1, tiles):
        turn = steps if steps < shares else 0
        pairs = [
            (t * shares + (c + turn) % shares, (t + steps) % tiles * shares + c)
            for t in range(tiles)
            for c in range(shares)
        ]
        got.append(lax.ppermute(message, ("tile", "chan"), pairs))
    return got


def lanes_body(
    latents, tile_order, w_in, gain_in, shift_in, w_mid, gain_mid, shift_mid, w_out, blend_weight
):
    own_frames, latent, own = latents.shape
    spans = lax.axis_size("tm")
    shares = lax.axis_size("chan")
    frames = own_frames * spans
    tiles = tile_order.shape[0]
    wide = w_in.shape[2]
    lanes = wide // spans
    pixels = TSIDE * TSIDE
    cases = block_cases(tiles)

    w_in_all = from_ring(w_in, "chan")
    table = lax.optimization_barrier(
        small_table(
            latents.reshape(own_frames * latent, own),
            gain_in,
            shift_in,
            gain_mid,
            shift_mid,
            w_out,
            blend_weight,
        )
    )
    latents_all = exchange_latents(latents, table)
    _, w_in, tile_order = lax.optimization_barrier((latents_all[0], w_in, tile_order))
    order = jnp.broadcast_to(tile_order.astype(jnp.float32)[:, None], (tiles, LANES))
    w_in_own = from_ring(w_in, "tm")[:1] or [w_in]

    vmem = pl.BlockSpec(memory_space=pltpu.VMEM)
    piece = (len(cases), 3, own_frames, own)
    kept, sent, denom = pl.pallas_call(
        functools.partial(decode_kernel, tiles, spans, shares),
        out_shape=[
            jax.ShapeDtypeStruct(piece, jnp.float32),
            jax.ShapeDtypeStruct((max(spans - 1, 1),) + piece, jnp.float32),
            jax.ShapeDtypeStruct((8, own), jnp.float32),
        ],
        in_specs=[pl.BlockSpec(memory_space=pl.ANY)] + [vmem] * (2 + tiles + shares),
        out_specs=[vmem] * 3,
        scratch_shapes=[
            pltpu.VMEM(((frames + 1) * latent, len(cases) * LANES), jnp.bfloat16),
            pltpu.VMEM((frames + 2, 9, latent, pixels), jnp.bfloat16),
            pltpu.VMEM((frames, pixels, CH), jnp.float32),
            pltpu.VMEM((frames, pixels + 2 * TSIDE, CH), jnp.bfloat16),
            pltpu.VMEM((3 * CH, 9 * lanes), jnp.bfloat16),
            pltpu.VMEM((3, frames, pixels, lanes), jnp.float32),
            pltpu.VMEM((8 * (frames + 1), own), jnp.float32),
            pltpu.SemaphoreType.DMA((27,)),
        ],
        compiler_params=pltpu.CompilerParams(vmem_limit_bytes=VMEM_BYTES),
        cost_estimate=pl.CostEstimate(
            flops=2 * frames * pixels * 27 * CH * lanes, bytes_accessed=8_000_000, transcendentals=0
        ),
    )(w_mid, table, order, *latents_all, *w_in_own, *w_in_all)
    total = ring_sum(kept, sent, "tm")
    total = ring_sum(total, [total] * (shares - 1), "chan")
    numer = total[0]
    for number, (down, across) in enumerate(cases):
        steps = down * GRID_X + across
        if steps and steps < tiles:
            numer = numer + shifted(total[number], "tile", steps)
    return jnp.transpose(numer / denom[0][None, None, :], (1, 0, 2))


def solution(mesh):
    placed = (
        P("tm", "groups", "tile"),
        P("groups"),
        P(None, None, "chan"),
        P("chan"),
        P("chan"),
        P(None, None, "chan"),
        P("chan"),
        P("chan"),
        P(None, "chan"),
        P("groups", None),
    )
    whole_lanes = (
        CH % (mesh.shape["chan"] * mesh.shape["tm"] * LANES) == 0
        and mesh.shape["chan"] <= mesh.shape["tile"]
    )
    return jax.shard_map(
        lanes_body if whole_lanes else general_body,
        mesh=mesh,
        in_specs=placed,
        out_specs=P("tm", "groups", "tile"),
        check_vma=False,
    )
```

```python
import functools

import jax
import jax.numpy as jnp
from jax import lax
from jax.experimental import pallas as pl
from jax.experimental.pallas import tpu as pltpu
from jax.sharding import PartitionSpec as P

CH = 512
GROUPS = 32
TSIDE = 16
STRIDE = 12
GRID_X = 4

EPSILON = 1e-06
LANES = 128
VMEM_BYTES = 48 * 1024 * 1024


def shifted(value, axis, steps):
    count = lax.axis_size(axis)
    leading, last = (max(0, -steps), min(count, count - steps))
    return lax.ppermute(value, axis, [(source, source + steps) for source in range(leading, last)])


def window_index(tile_id, tiles):
    slots = jnp.arange(TSIDE * TSIDE, dtype=jnp.int32)
    row = tile_id // GRID_X * STRIDE + slots // TSIDE
    col = tile_id % GRID_X * STRIDE + slots % TSIDE
    valid = (row < tiles // GRID_X * STRIDE) & (col < GRID_X * STRIDE)
    block = row // STRIDE * GRID_X + col // STRIDE
    index = block * (STRIDE * STRIDE) + row % STRIDE * STRIDE + col % STRIDE
    return (jnp.where(valid, index, 0), valid)


def causal_conv(extended, weights, frames, side):
    pixels = side * side
    rows = jnp.arange(pixels, dtype=jnp.int32) // side
    cols = jnp.arange(pixels, dtype=jnp.int32) % side
    total = jnp.zeros((frames, weights.shape[2], pixels), jnp.float32)
    for depth in range(3):
        window = extended[depth : depth + frames]
        for down in range(3):
            for across in range(3):
                offset = (down - 1) * side + (across - 1)
                inside = (
                    (rows + down - 1 >= 0)
                    & (rows + down - 1 < side)
                    & (cols + across - 1 >= 0)
                    & (cols + across - 1 < side)
                )
                moved = jnp.roll(window, -offset, axis=2)
                moved = jnp.where(inside[None, None, :], moved, jnp.zeros_like(moved))
                total = total + jnp.einsum(
                    "fcp,co->fop",
                    moved,
                    weights[9 * depth + 3 * down + across],
                    preferred_element_type=jnp.float32,
                )
    return total


def with_history(values):
    frames = values.shape[0]
    earlier = shifted(values[frames - 2 :], "tm", 1)
    return jnp.concatenate([earlier, values], axis=0)


def normalize(values, gain, shift, total_frames):
    frames, chans, pixels = values.shape
    width = CH // GROUPS
    grouped = values.reshape(frames, chans // width, width, pixels)
    sums = jnp.sum(grouped, axis=(0, 2, 3))
    squares = jnp.sum(grouped * grouped, axis=(0, 2, 3))
    sums, squares = lax.psum((sums, squares), "tm")
    count = total_frames * width * pixels
    mean = sums / count
    variance = squares / count - mean * mean
    scale = lax.rsqrt(variance + EPSILON)
    normed = (grouped - mean[None, :, None, None]) * scale[None, :, None, None]
    normed = normed.reshape(frames, chans, pixels) * gain[None, :, None] + shift[None, :, None]
    return jax.nn.silu(normed).astype(jnp.bfloat16)


def spread(color, weight, index, total_pixels):
    numer = (
        jnp.zeros((color.shape[0], 3, total_pixels), jnp.float32)
        .at[:, :, index]
        .add(color * weight[None, None, :])
    )
    denom = jnp.zeros((total_pixels,), jnp.float32).at[index].add(weight)
    return (numer, denom)


def route_owned(numer, denom, tile_id, own):
    frames = numer.shape[0]
    margin = (GRID_X + 1) * own
    numer_wide = jnp.concatenate([numer, jnp.zeros((frames, 3, margin), jnp.float32)], axis=2)
    denom_wide = jnp.concatenate([denom, jnp.zeros((margin,), jnp.float32)], axis=0)
    first_pixel = tile_id * own

    def block_at(offset):
        start_pixel = first_pixel + offset * own
        return (
            lax.dynamic_slice_in_dim(numer_wide, start_pixel, own, 2),
            lax.dynamic_slice_in_dim(denom_wide, start_pixel, own, 0),
        )

    owned_numer, owned_denom = block_at(0)
    for offset in (1, GRID_X, GRID_X + 1):
        piece_numer, piece_denom = block_at(offset)
        got_numer, got_denom = shifted((piece_numer, piece_denom), "tile", offset)
        owned_numer = owned_numer + got_numer
        owned_denom = owned_denom + got_denom
    return (owned_numer, owned_denom)


def general_body(
    latents, tile_order, w_in, gain_in, shift_in, w_mid, gain_mid, shift_mid, w_out, blend_weight
):
    frames = latents.shape[0]
    total_frames = frames * lax.axis_size("tm")
    tiles = tile_order.shape[0]
    own = STRIDE * STRIDE
    total_pixels = tiles * own
    tile_id = lax.axis_index("tile")
    index, valid = window_index(tile_id, tiles)
    whole = lax.all_gather(latents, "tile", axis=2, tiled=True)
    blocks = whole.reshape(frames, whole.shape[1], tiles, own)
    image = (
        jnp.zeros_like(blocks)
        .at[:, :, tile_order]
        .set(blocks)
        .reshape(frames, whole.shape[1], total_pixels)
    )
    window = jnp.where(
        valid[None, None, :], jnp.take(image, index, axis=2), jnp.zeros((), jnp.bfloat16)
    )
    first = causal_conv(with_history(window), w_in, frames, TSIDE)
    hidden = normalize(first, gain_in, shift_in, total_frames)
    second = causal_conv(
        lax.all_gather(with_history(hidden), "chan", axis=1, tiled=True), w_mid, frames, TSIDE
    )
    upper = normalize(second, gain_mid, shift_mid, total_frames)
    color = jnp.einsum("oc,fcp->fop", w_out, upper, preferred_element_type=jnp.float32)
    weight = jnp.where(valid, blend_weight[tile_id], jnp.float32(0.0))
    numer, denom = spread(color, weight, index, total_pixels)
    numer, denom = route_owned(numer, denom, tile_id, own)
    numer = lax.psum(numer, "chan")
    return numer / denom[None, None, :]


def block_cases(tiles):
    downs = (0, 1) if tiles // GRID_X > 1 else (0,)
    return [(down, across) for down in downs for across in (0, 1)]


def exact_dot(values, ones):
    rows = values.shape[0]
    high = values.astype(jnp.bfloat16)
    rest = values - high.astype(jnp.float32)
    middle = rest.astype(jnp.bfloat16)
    low = (rest - middle.astype(jnp.float32)).astype(jnp.bfloat16)
    total = jnp.dot(
        jnp.concatenate([high, middle, low], axis=0), ones, preferred_element_type=jnp.float32
    )
    return total[:rows] + total[rows : 2 * rows] + total[2 * rows :]


def group_affine(sums, squares, gain, shift, count):
    lanes = sums.shape[1]
    width = CH // GROUPS
    same = lax.broadcasted_iota(jnp.int32, (lanes, lanes), 0) // width == (
        lax.broadcasted_iota(jnp.int32, (lanes, lanes), 1) // width
    )
    total = exact_dot(
        jnp.concatenate([sums, squares], axis=0), jnp.where(same, 1.0, 0.0).astype(jnp.bfloat16)
    )
    mean = jnp.sum(total[:8], axis=0, keepdims=True) / count
    variance = jnp.sum(total[8:], axis=0, keepdims=True) / count - mean * mean
    scale = gain * lax.rsqrt(variance + EPSILON)
    return 0.5 * scale, 0.5 * (shift - mean * scale)


def silu_of_half(half):
    return half + half * jnp.tanh(half)


def fold(values):
    rows, lanes = values.shape
    return jnp.sum(values.reshape(rows // 8, 8, lanes), axis=0)


def decode_kernel(
    tiles,
    spans,
    shares,
    *refs,
):
    cases = block_cases(tiles)
    refs = list(refs)

    def take(number):
        taken = refs[:number]
        del refs[:number]
        return taken

    w_mid_ref, table_ref, order_ref = take(3)
    latent_refs, w_in_refs = take(tiles), take(shares)
    keep_ref, send_ref, denom_ref = take(3)
    taps, first, hidden, weights, partial, shown_ref, sems = take(7)

    own = denom_ref.shape[1]
    own_frames = keep_ref.shape[2]
    frames = own_frames * spans
    latent, wide = w_in_refs[0].shape[1:]
    rows_in = frames * latent
    rows_own = rows_in // spans
    depth_in = 27 * latent
    pixels = TSIDE * TSIDE
    lanes = partial.shape[3]
    tile_id = lax.axis_index("tile")
    mine = lax.axis_index("tm")
    chan_id = lax.axis_index("chan")

    copies = []
    for a in range(3):
        for b in range(3):
            for e in range(3):
                tap = 9 * a + 3 * b + e
                copy = pltpu.make_async_copy(
                    w_mid_ref.at[tap, :, pl.ds(pl.multiple_of(mine * lanes, LANES), lanes)],
                    weights.at[pl.ds(b * CH, CH), pl.ds((3 * a + e) * lanes, lanes)],
                    sems.at[tap],
                )
                copy.start()
                copies.append(copy)

    tile_row, tile_col = tile_id // GRID_X, tile_id % GRID_X
    gain_row = rows_own + 2
    w_out_row = gain_row + 2
    blend_row = w_out_row + 3
    rows_sent = rows_in + latent
    messages = [ref[:rows_sent].astype(jnp.float32) for ref in latent_refs]
    joined = []
    for down, across in cases:
        inside = (tile_row + down < tiles // GRID_X) & (tile_col + across < GRID_X)
        wanted = jnp.where(inside, tile_id + down * GRID_X + across, -1).astype(jnp.float32)
        block = 0.0
        for steps in range(tiles):
            held = order_ref[pl.ds((tile_id - steps + tiles) % tiles, 1), :]
            block = block + jnp.where(held == wanted, 1.0, 0.0) * messages[steps]
        joined.append(block)
    chosen = jnp.concatenate(joined, axis=1)

    slot = lax.broadcasted_iota(jnp.int32, (1, pixels), 1)
    up, along = slot // TSIDE, slot % TSIDE
    source = lax.broadcasted_iota(jnp.int32, (LANES, pixels), 0)
    tail = own - LANES

    def pick(swap):
        parts = []
        for down, across in cases:
            u, v = up - down * STRIDE, along - across * STRIDE
            good = (u >= 0) & (u < STRIDE) & (v >= 0) & (v < STRIDE)
            wanted = jnp.where(good, u * STRIDE + v, -1)
            if swap is not None:
                wanted = jnp.where(wanted >= LANES, wanted - LANES + tail * swap, -1)
            parts.append(jnp.where(source == wanted, 1.0, 0.0).astype(jnp.bfloat16))
        return jnp.concatenate(parts, axis=0)

    window = jnp.dot(
        chosen[:rows_in].astype(jnp.bfloat16), pick(None), preferred_element_type=jnp.float32
    )
    tails = chosen[rows_in:]
    width = tails.shape[1]
    tails = jnp.concatenate(
        [
            pltpu.roll(tails, (-f * spans * tail) % width, 1) if f else tails
            for f in range(own_frames)
        ],
        axis=0,
    ).astype(jnp.bfloat16)
    ends = [
        jnp.dot(tails, pick(swap), preferred_element_type=jnp.float32) for swap in range(spans)
    ]
    window = window + jnp.concatenate(ends, axis=0)
    taps[0:2] = jnp.zeros((2,) + taps.shape[1:], taps.dtype)
    for b in range(3):
        for e in range(3):
            inside = (
                (up + b - 1 >= 0)
                & (up + b - 1 < TSIDE)
                & (along + e - 1 >= 0)
                & (along + e - 1 < TSIDE)
            )
            offset = (b - 1) * TSIDE + e - 1
            moved = pltpu.roll(window, (-offset) % pixels, 1) if offset else window
            moved = jnp.where(inside, moved, 0.0).astype(jnp.bfloat16)
            for swap in range(spans):
                value = moved[swap * rows_own : (swap + 1) * rows_own]
                span = pl.ds(2 + (mine + swap) % spans * own_frames, own_frames)
                taps[span, 3 * b + e] = value.reshape(own_frames, latent, pixels)

    joined = jnp.concatenate(
        [w_in_refs[s][:27].reshape(depth_in, wide) for s in range(shares)], axis=1
    )
    same = jnp.where(
        lax.broadcasted_iota(jnp.int32, (pixels, pixels), 0)
        == lax.broadcasted_iota(jnp.int32, (pixels, pixels), 1),
        1.0,
        0.0,
    ).astype(jnp.bfloat16)
    sums = jnp.zeros((8, CH), jnp.float32)
    squares = jnp.zeros((8, CH), jnp.float32)
    for f in range(frames):
        patch = taps[f : f + 3].reshape(depth_in, pixels)
        patch = lax.dot_general(
            same, patch, (((1,), (1,)), ((), ())), preferred_element_type=jnp.float32
        ).astype(jnp.bfloat16)
        value = jnp.dot(patch, joined, preferred_element_type=jnp.float32)
        first[f] = value
        sums = sums + fold(value)
        squares = squares + fold(value * value)
    count = frames * (CH // GROUPS) * pixels
    affine = []
    for s in range(shares):
        at = rows_sent
        table = latent_refs[s][at : at + wide // LANES * 4].astype(jnp.float32)
        pieces = [table[4 * lane : 4 * lane + 4] for lane in range(wide // LANES)]
        table = jnp.concatenate([part[0:2] + part[2:4] for part in pieces], axis=1)
        part = slice(s * wide, (s + 1) * wide)
        affine.append(
            group_affine(sums[:, part], squares[:, part], table[0:1], table[1:2], count)
        )
    channels = [
        pl.ds(pl.multiple_of((chan_id + s) % shares * wide, LANES), wide) for s in range(shares)
    ]

    def hide(f):
        edge = jnp.zeros((TSIDE, CH), jnp.bfloat16)
        hidden[f, 0:TSIDE] = edge
        hidden[f, TSIDE + pixels : 2 * TSIDE + pixels] = edge
        for s in range(shares):
            scale, bias = affine[s]
            value = first[f, :, s * wide : (s + 1) * wide] * scale + bias
            hidden[f, TSIDE : TSIDE + pixels, channels[s]] = silu_of_half(value).astype(
                jnp.bfloat16
            )

    def convolve(start, several, depth_taps):
        lhs = jnp.concatenate(
            [
                hidden[start : start + several, b * TSIDE : b * TSIDE + pixels].reshape(
                    several * pixels, CH
                )
                for b in range(3)
            ],
            axis=1,
        )
        low = depth_taps[0] * 3 * lanes
        product = jnp.dot(lhs, weights[:, low:], preferred_element_type=jnp.float32)
        for a in depth_taps:
            for e in range(3):
                at = (3 * a + e) * lanes - low
                for f in range(several):
                    target = start + f + 2 - a
                    value = product[f * pixels : (f + 1) * pixels, at : at + lanes]
                    if start + f == max(target - 2, 0):
                        partial[e, target] = value
                    else:
                        partial[e, target] += value

    column = lax.broadcasted_iota(jnp.int32, (pixels, lanes), 0) % TSIDE
    total = [jnp.zeros((8, lanes), jnp.float32)] * 2

    def gather(f):
        left = jnp.where(column == 0, 0.0, pltpu.roll(partial[0, f], 1, 0))
        right = jnp.where(column == TSIDE - 1, 0.0, pltpu.roll(partial[2, f], pixels - 1, 0))
        value = partial[1, f] + left + right
        partial[1, f] = value
        total[0] = total[0] + fold(value)
        total[1] = total[1] + fold(value * value)

    together = 3
    groups = [
        range(f, min(f + together, frames - 2)) for f in range(0, frames - 2, together)
    ]
    groups += [range(f, f + 1) for f in range(groups[-1].stop, frames)]
    for copy in copies:
        copy.wait()
    for f in groups[0]:
        hide(f)
    for number, group in enumerate(groups):
        if number + 1 < len(groups):
            for f in groups[number + 1]:
                hide(f)
        convolve(
            group.start,
            len(group),
            tuple(a for a in range(3) if group.stop - 1 + 2 - a < frames),
        )
        if number:
            for f in groups[number - 1]:
                gather(f)
    for f in groups[-1]:
        gather(f)

    part = pl.ds(pl.multiple_of(mine * lanes, LANES), lanes)
    scale, bias = group_affine(
        total[0],
        total[1],
        table_ref[gain_row : gain_row + 1, part],
        table_ref[gain_row + 1 : gain_row + 2, part],
        count,
    )
    blend = table_ref[pl.ds(blend_row + tile_id, 1), :]
    blend = jnp.where(
        (tile_row * STRIDE + up < tiles // GRID_X * STRIDE)
        & (tile_col * STRIDE + along < GRID_X * STRIDE),
        blend,
        0.0,
    )
    w_out = jnp.concatenate(
        [table_ref[w_out_row : w_out_row + 3, part], jnp.zeros((5, lanes), jnp.float32)], axis=0
    ).astype(jnp.bfloat16)
    colors = []
    for f in range(frames):
        upper = silu_of_half(partial[1, f] * scale + bias).astype(jnp.bfloat16)
        color = lax.dot_general(
            w_out, upper, (((1,), (1,)), ((), ())), preferred_element_type=jnp.float32
        )
        colors.append(color * blend)
    colors = jnp.concatenate(colors, axis=0)

    slot_in = lax.broadcasted_iota(jnp.int32, (pixels, own), 0)
    pixel = lax.broadcasted_iota(jnp.int32, (pixels, own), 1)
    denom = jnp.zeros((8, own), jnp.float32)
    for number, (down, across) in enumerate(cases):
        u, v = slot_in // TSIDE - down * STRIDE, slot_in % TSIDE - across * STRIDE
        good = (u >= 0) & (u < STRIDE) & (v >= 0) & (v < STRIDE) & (u * STRIDE + v == pixel)
        shown = jnp.where(good, 1.0, 0.0).astype(jnp.bfloat16)
        inside = (tile_row >= down) & (tile_col >= across)
        other = jnp.maximum(tile_id - down * GRID_X - across, 0)
        weight = jnp.where(inside, table_ref[pl.ds(blend_row + other, 1), :], 0.0)
        piece = exact_dot(
            jnp.concatenate([colors, jnp.broadcast_to(weight, (8, pixels))], axis=0), shown
        )
        denom = denom + piece[8 * frames :]
        shown_ref[...] = piece
        for swap in range(spans):
            target = keep_ref if swap == 0 else send_ref.at[swap - 1]
            base = (mine + swap) % spans * own_frames * 8
            for at in range(own_frames):
                for o in range(3):
                    target[number, o, at : at + 1, :] = shown_ref[pl.ds(base + 8 * at + o, 1), :]

    denom_ref[...] = denom


def from_ring(value, axis):
    count = lax.axis_size(axis)
    return [
        lax.ppermute(value, axis, [((d + turn) % count, d) for d in range(count)])
        for turn in range(1, count)
    ]


def ring_sum(kept, sent, axis):
    count = lax.axis_size(axis)
    for turn in range(1, count):
        kept = kept + lax.ppermute(
            sent[turn - 1], axis, [(d, (d + turn) % count) for d in range(count)]
        )
    return kept


def small_table(*values):
    values = [value.reshape(-1, value.shape[-1]) for value in values]
    wide = max(value.shape[1] for value in values)
    height = sum(value.shape[0] for value in values)
    total, row = 0.0, 0
    for value in values:
        below = height - row - value.shape[0]
        value = jnp.pad(value.astype(jnp.float32), ((row, below), (0, wide - value.shape[1])))
        total = total + value
        row = height - below
    return total


def exchange_latents(latents, table):
    tiles, shares, spans = (lax.axis_size(name) for name in ("tile", "chan", "tm"))
    frames, latent, own = latents.shape
    tail = own - LANES
    height = frames * latent
    others = from_ring(latents.reshape(height, own), "tm")
    parts = [table[:height, :own].astype(jnp.bfloat16)] + others
    tails = sum(
        jnp.pad(
            part[f * latent : (f + 1) * latent, LANES:],
            ((0, 0), (tail * (f * spans + at), LANES - tail * (f * spans + at + 1))),
        )
        for at, part in enumerate(parts)
        for f in range(frames)
    )
    affine = table[height : height + 2]
    high = lax.reduce_precision(affine, 8, 7)
    low = lax.reduce_precision(affine - high, 8, 7)
    affine = jnp.concatenate([high, low], axis=0).astype(jnp.bfloat16)
    rows = [affine[:, at : at + LANES] for at in range(0, affine.shape[1], LANES)]
    rows = jnp.concatenate(rows, axis=0)
    rows = jnp.pad(rows, ((0, -rows.shape[0] % 16), (0, 0)))
    message = jnp.concatenate([part[:, :LANES] for part in parts] + [tails, rows], axis=0)
    got = [message]
    for steps in range(1, tiles):
        turn = steps if steps < shares else 0
        pairs = [
            (t * shares + (c + turn) % shares, (t + steps) % tiles * shares + c)
            for t in range(tiles)
            for c in range(shares)
        ]
        got.append(lax.ppermute(message, ("tile", "chan"), pairs))
    return got


def lanes_body(
    latents, tile_order, w_in, gain_in, shift_in, w_mid, gain_mid, shift_mid, w_out, blend_weight
):
    own_frames, latent, own = latents.shape
    spans = lax.axis_size("tm")
    shares = lax.axis_size("chan")
    frames = own_frames * spans
    tiles = tile_order.shape[0]
    wide = w_in.shape[2]
    lanes = wide // spans
    pixels = TSIDE * TSIDE
    cases = block_cases(tiles)

    w_in_all = from_ring(w_in, "chan")
    table = lax.optimization_barrier(
        small_table(
            latents.reshape(own_frames * latent, own),
            gain_in,
            shift_in,
            gain_mid,
            shift_mid,
            w_out,
            blend_weight,
        )
    )
    latents_all = exchange_latents(latents, table)
    _, w_in, tile_order = lax.optimization_barrier((latents_all[0], w_in, tile_order))
    order = jnp.broadcast_to(tile_order.astype(jnp.float32)[:, None], (tiles, LANES))
    w_in_own = from_ring(w_in, "tm")[:1] or [w_in]

    vmem = pl.BlockSpec(memory_space=pltpu.VMEM)
    piece = (len(cases), 3, own_frames, own)
    kept, sent, denom = pl.pallas_call(
        functools.partial(decode_kernel, tiles, spans, shares),
        out_shape=[
            jax.ShapeDtypeStruct(piece, jnp.float32),
            jax.ShapeDtypeStruct((max(spans - 1, 1),) + piece, jnp.float32),
            jax.ShapeDtypeStruct((8, own), jnp.float32),
        ],
        in_specs=[pl.BlockSpec(memory_space=pl.ANY)] + [vmem] * (2 + tiles + shares),
        out_specs=[vmem] * 3,
        scratch_shapes=[
            pltpu.VMEM((frames + 2, 9, latent, pixels), jnp.bfloat16),
            pltpu.VMEM((frames, pixels, CH), jnp.float32),
            pltpu.VMEM((frames, pixels + 2 * TSIDE, CH), jnp.bfloat16),
            pltpu.VMEM((3 * CH, 9 * lanes), jnp.bfloat16),
            pltpu.VMEM((3, frames, pixels, lanes), jnp.float32),
            pltpu.VMEM((8 * (frames + 1), own), jnp.float32),
            pltpu.SemaphoreType.DMA((27,)),
        ],
        compiler_params=pltpu.CompilerParams(vmem_limit_bytes=VMEM_BYTES),
        cost_estimate=pl.CostEstimate(
            flops=2 * frames * pixels * 27 * CH * lanes, bytes_accessed=8_000_000, transcendentals=0
        ),
    )(w_mid, table, order, *latents_all, *w_in_own, *w_in_all)
    total = ring_sum(kept, sent, "tm")
    total = ring_sum(total, [total] * (shares - 1), "chan")
    numer = total[0]
    for number, (down, across) in enumerate(cases):
        steps = down * GRID_X + across
        if steps and steps < tiles:
            numer = numer + shifted(total[number], "tile", steps)
    return jnp.transpose(numer / denom[0][None, None, :], (1, 0, 2))


def solution(mesh):
    placed = (
        P("tm", "groups", "tile"),
        P("groups"),
        P(None, None, "chan"),
        P("chan"),
        P("chan"),
        P(None, None, "chan"),
        P("chan"),
        P("chan"),
        P(None, "chan"),
        P("groups", None),
    )
    whole_lanes = (
        CH % (mesh.shape["chan"] * mesh.shape["tm"] * LANES) == 0
        and mesh.shape["chan"] <= mesh.shape["tile"]
    )
    return jax.shard_map(
        lanes_body if whole_lanes else general_body,
        mesh=mesh,
        in_specs=placed,
        out_specs=P("tm", "groups", "tile"),
        check_vma=False,
    )
```

```python
import functools

import jax
import jax.numpy as jnp
from jax import lax
from jax.experimental import pallas as pl
from jax.experimental.pallas import tpu as pltpu
from jax.sharding import PartitionSpec as P

CH = 512
GROUPS = 32
TSIDE = 16
STRIDE = 12
GRID_X = 4

EPSILON = 1e-06
LANES = 128
VMEM_BYTES = 48 * 1024 * 1024


def shifted(value, axis, steps):
    count = lax.axis_size(axis)
    leading, last = (max(0, -steps), min(count, count - steps))
    return lax.ppermute(value, axis, [(source, source + steps) for source in range(leading, last)])


def window_index(tile_id, tiles):
    slots = jnp.arange(TSIDE * TSIDE, dtype=jnp.int32)
    row = tile_id // GRID_X * STRIDE + slots // TSIDE
    col = tile_id % GRID_X * STRIDE + slots % TSIDE
    valid = (row < tiles // GRID_X * STRIDE) & (col < GRID_X * STRIDE)
    block = row // STRIDE * GRID_X + col // STRIDE
    index = block * (STRIDE * STRIDE) + row % STRIDE * STRIDE + col % STRIDE
    return (jnp.where(valid, index, 0), valid)


def causal_conv(extended, weights, frames, side):
    pixels = side * side
    rows = jnp.arange(pixels, dtype=jnp.int32) // side
    cols = jnp.arange(pixels, dtype=jnp.int32) % side
    total = jnp.zeros((frames, weights.shape[2], pixels), jnp.float32)
    for depth in range(3):
        window = extended[depth : depth + frames]
        for down in range(3):
            for across in range(3):
                offset = (down - 1) * side + (across - 1)
                inside = (
                    (rows + down - 1 >= 0)
                    & (rows + down - 1 < side)
                    & (cols + across - 1 >= 0)
                    & (cols + across - 1 < side)
                )
                moved = jnp.roll(window, -offset, axis=2)
                moved = jnp.where(inside[None, None, :], moved, jnp.zeros_like(moved))
                total = total + jnp.einsum(
                    "fcp,co->fop",
                    moved,
                    weights[9 * depth + 3 * down + across],
                    preferred_element_type=jnp.float32,
                )
    return total


def with_history(values):
    frames = values.shape[0]
    earlier = shifted(values[frames - 2 :], "tm", 1)
    return jnp.concatenate([earlier, values], axis=0)


def normalize(values, gain, shift, total_frames):
    frames, chans, pixels = values.shape
    width = CH // GROUPS
    grouped = values.reshape(frames, chans // width, width, pixels)
    sums = jnp.sum(grouped, axis=(0, 2, 3))
    squares = jnp.sum(grouped * grouped, axis=(0, 2, 3))
    sums, squares = lax.psum((sums, squares), "tm")
    count = total_frames * width * pixels
    mean = sums / count
    variance = squares / count - mean * mean
    scale = lax.rsqrt(variance + EPSILON)
    normed = (grouped - mean[None, :, None, None]) * scale[None, :, None, None]
    normed = normed.reshape(frames, chans, pixels) * gain[None, :, None] + shift[None, :, None]
    return jax.nn.silu(normed).astype(jnp.bfloat16)


def spread(color, weight, index, total_pixels):
    numer = (
        jnp.zeros((color.shape[0], 3, total_pixels), jnp.float32)
        .at[:, :, index]
        .add(color * weight[None, None, :])
    )
    denom = jnp.zeros((total_pixels,), jnp.float32).at[index].add(weight)
    return (numer, denom)


def route_owned(numer, denom, tile_id, own):
    frames = numer.shape[0]
    margin = (GRID_X + 1) * own
    numer_wide = jnp.concatenate([numer, jnp.zeros((frames, 3, margin), jnp.float32)], axis=2)
    denom_wide = jnp.concatenate([denom, jnp.zeros((margin,), jnp.float32)], axis=0)
    first_pixel = tile_id * own

    def block_at(offset):
        start_pixel = first_pixel + offset * own
        return (
            lax.dynamic_slice_in_dim(numer_wide, start_pixel, own, 2),
            lax.dynamic_slice_in_dim(denom_wide, start_pixel, own, 0),
        )

    owned_numer, owned_denom = block_at(0)
    for offset in (1, GRID_X, GRID_X + 1):
        piece_numer, piece_denom = block_at(offset)
        got_numer, got_denom = shifted((piece_numer, piece_denom), "tile", offset)
        owned_numer = owned_numer + got_numer
        owned_denom = owned_denom + got_denom
    return (owned_numer, owned_denom)


def general_body(
    latents, tile_order, w_in, gain_in, shift_in, w_mid, gain_mid, shift_mid, w_out, blend_weight
):
    frames = latents.shape[0]
    total_frames = frames * lax.axis_size("tm")
    tiles = tile_order.shape[0]
    own = STRIDE * STRIDE
    total_pixels = tiles * own
    tile_id = lax.axis_index("tile")
    index, valid = window_index(tile_id, tiles)
    whole = lax.all_gather(latents, "tile", axis=2, tiled=True)
    blocks = whole.reshape(frames, whole.shape[1], tiles, own)
    image = (
        jnp.zeros_like(blocks)
        .at[:, :, tile_order]
        .set(blocks)
        .reshape(frames, whole.shape[1], total_pixels)
    )
    window = jnp.where(
        valid[None, None, :], jnp.take(image, index, axis=2), jnp.zeros((), jnp.bfloat16)
    )
    first = causal_conv(with_history(window), w_in, frames, TSIDE)
    hidden = normalize(first, gain_in, shift_in, total_frames)
    second = causal_conv(
        lax.all_gather(with_history(hidden), "chan", axis=1, tiled=True), w_mid, frames, TSIDE
    )
    upper = normalize(second, gain_mid, shift_mid, total_frames)
    color = jnp.einsum("oc,fcp->fop", w_out, upper, preferred_element_type=jnp.float32)
    weight = jnp.where(valid, blend_weight[tile_id], jnp.float32(0.0))
    numer, denom = spread(color, weight, index, total_pixels)
    numer, denom = route_owned(numer, denom, tile_id, own)
    numer = lax.psum(numer, "chan")
    return numer / denom[None, None, :]


def block_cases(tiles):
    downs = (0, 1) if tiles // GRID_X > 1 else (0,)
    return [(down, across) for down in downs for across in (0, 1)]


def exact_dot(values, ones):
    rows = values.shape[0]
    high = values.astype(jnp.bfloat16)
    rest = values - high.astype(jnp.float32)
    middle = rest.astype(jnp.bfloat16)
    low = (rest - middle.astype(jnp.float32)).astype(jnp.bfloat16)
    total = jnp.dot(
        jnp.concatenate([high, middle, low], axis=0), ones, preferred_element_type=jnp.float32
    )
    return total[:rows] + total[rows : 2 * rows] + total[2 * rows :]


def group_affine(sums, squares, gain, shift, count):
    lanes = sums.shape[1]
    width = CH // GROUPS
    same = lax.broadcasted_iota(jnp.int32, (lanes, lanes), 0) // width == (
        lax.broadcasted_iota(jnp.int32, (lanes, lanes), 1) // width
    )
    total = exact_dot(
        jnp.concatenate([sums, squares], axis=0), jnp.where(same, 1.0, 0.0).astype(jnp.bfloat16)
    )
    mean = jnp.sum(total[:8], axis=0, keepdims=True) / count
    variance = jnp.sum(total[8:], axis=0, keepdims=True) / count - mean * mean
    scale = gain * lax.rsqrt(variance + EPSILON)
    return 0.5 * scale, 0.5 * (shift - mean * scale)


def silu_of_half(half):
    return half + half * jnp.tanh(half)


def fold(values):
    rows, lanes = values.shape
    return jnp.sum(values.reshape(rows // 8, 8, lanes), axis=0)


def decode_kernel(
    tiles,
    spans,
    shares,
    *refs,
):
    cases = block_cases(tiles)
    refs = list(refs)

    def take(number):
        taken = refs[:number]
        del refs[:number]
        return taken

    w_mid_ref, table_ref, order_ref = take(3)
    latent_refs, w_in_refs = take(tiles), take(shares)
    keep_ref, send_ref, denom_ref = take(3)
    taps, first, hidden, weights, partial, shown_ref, sems = take(7)

    own = denom_ref.shape[1]
    own_frames = keep_ref.shape[2]
    frames = own_frames * spans
    latent, wide = w_in_refs[0].shape[1:]
    rows_in = frames * latent
    rows_own = rows_in // spans
    depth_in = 27 * latent
    pixels = TSIDE * TSIDE
    lanes = partial.shape[3]
    tile_id = lax.axis_index("tile")
    mine = lax.axis_index("tm")
    chan_id = lax.axis_index("chan")

    copies = []
    for a in range(3):
        for b in range(3):
            for e in range(3):
                tap = 9 * a + 3 * b + e
                copy = pltpu.make_async_copy(
                    w_mid_ref.at[tap, :, pl.ds(pl.multiple_of(mine * lanes, LANES), lanes)],
                    weights.at[pl.ds(b * CH, CH), pl.ds((3 * a + e) * lanes, lanes)],
                    sems.at[tap],
                )
                copy.start()
                copies.append(copy)

    tile_row, tile_col = tile_id // GRID_X, tile_id % GRID_X
    gain_row = rows_own + 2
    w_out_row = gain_row + 2
    blend_row = w_out_row + 3
    rows_sent = rows_in + latent
    messages = [ref[:rows_sent].astype(jnp.float32) for ref in latent_refs]
    joined = []
    for down, across in cases:
        inside = (tile_row + down < tiles // GRID_X) & (tile_col + across < GRID_X)
        wanted = jnp.where(inside, tile_id + down * GRID_X + across, -1).astype(jnp.float32)
        block = 0.0
        for steps in range(tiles):
            held = order_ref[pl.ds((tile_id - steps + tiles) % tiles, 1), :]
            block = block + jnp.where(held == wanted, 1.0, 0.0) * messages[steps]
        joined.append(block)
    chosen = jnp.concatenate(joined, axis=1)

    slot = lax.broadcasted_iota(jnp.int32, (1, pixels), 1)
    up, along = slot // TSIDE, slot % TSIDE
    source = lax.broadcasted_iota(jnp.int32, (LANES, pixels), 0)
    tail = own - LANES

    def pick(swap):
        parts = []
        for down, across in cases:
            u, v = up - down * STRIDE, along - across * STRIDE
            good = (u >= 0) & (u < STRIDE) & (v >= 0) & (v < STRIDE)
            wanted = jnp.where(good, u * STRIDE + v, -1)
            if swap is not None:
                wanted = jnp.where(wanted >= LANES, wanted - LANES + tail * swap, -1)
            parts.append(jnp.where(source == wanted, 1.0, 0.0).astype(jnp.bfloat16))
        return jnp.concatenate(parts, axis=0)

    window = jnp.dot(
        chosen[:rows_in].astype(jnp.bfloat16), pick(None), preferred_element_type=jnp.float32
    )
    tails = chosen[rows_in:]
    width = tails.shape[1]
    tails = jnp.concatenate(
        [
            pltpu.roll(tails, (-f * spans * tail) % width, 1) if f else tails
            for f in range(own_frames)
        ],
        axis=0,
    ).astype(jnp.bfloat16)
    ends = [
        jnp.dot(tails, pick(swap), preferred_element_type=jnp.float32) for swap in range(spans)
    ]
    window = window + jnp.concatenate(ends, axis=0)
    taps[0:2] = jnp.zeros((2,) + taps.shape[1:], taps.dtype)
    for b in range(3):
        for e in range(3):
            inside = (
                (up + b - 1 >= 0)
                & (up + b - 1 < TSIDE)
                & (along + e - 1 >= 0)
                & (along + e - 1 < TSIDE)
            )
            offset = (b - 1) * TSIDE + e - 1
            moved = pltpu.roll(window, (-offset) % pixels, 1) if offset else window
            moved = jnp.where(inside, moved, 0.0).astype(jnp.bfloat16)
            for swap in range(spans):
                value = moved[swap * rows_own : (swap + 1) * rows_own]
                span = pl.ds(2 + (mine + swap) % spans * own_frames, own_frames)
                taps[span, 3 * b + e] = value.reshape(own_frames, latent, pixels)

    joined = jnp.concatenate(
        [w_in_refs[s][:27].reshape(depth_in, wide) for s in range(shares)], axis=1
    )
    sums = jnp.zeros((8, CH), jnp.float32)
    squares = jnp.zeros((8, CH), jnp.float32)
    for f in range(frames):
        patch = taps[f : f + 3].reshape(depth_in, pixels)
        value = lax.dot_general(
            patch, joined, (((0,), (0,)), ((), ())), preferred_element_type=jnp.float32
        )
        first[f] = value
        sums = sums + fold(value)
        squares = squares + fold(value * value)
    count = frames * (CH // GROUPS) * pixels
    affine = []
    for s in range(shares):
        at = rows_sent
        table = latent_refs[s][at : at + wide // LANES * 4].astype(jnp.float32)
        pieces = [table[4 * lane : 4 * lane + 4] for lane in range(wide // LANES)]
        table = jnp.concatenate([part[0:2] + part[2:4] for part in pieces], axis=1)
        part = slice(s * wide, (s + 1) * wide)
        affine.append(
            group_affine(sums[:, part], squares[:, part], table[0:1], table[1:2], count)
        )
    channels = [
        pl.ds(pl.multiple_of((chan_id + s) % shares * wide, LANES), wide) for s in range(shares)
    ]

    def hide(f):
        edge = jnp.zeros((TSIDE, CH), jnp.bfloat16)
        hidden[f, 0:TSIDE] = edge
        hidden[f, TSIDE + pixels : 2 * TSIDE + pixels] = edge
        for s in range(shares):
            scale, bias = affine[s]
            value = first[f, :, s * wide : (s + 1) * wide] * scale + bias
            hidden[f, TSIDE : TSIDE + pixels, channels[s]] = silu_of_half(value).astype(
                jnp.bfloat16
            )

    def convolve(start, several, depth_taps):
        lhs = jnp.concatenate(
            [
                hidden[start : start + several, b * TSIDE : b * TSIDE + pixels].reshape(
                    several * pixels, CH
                )
                for b in range(3)
            ],
            axis=1,
        )
        low = depth_taps[0] * 3 * lanes
        product = jnp.dot(lhs, weights[:, low:], preferred_element_type=jnp.float32)
        for a in depth_taps:
            for e in range(3):
                at = (3 * a + e) * lanes - low
                for f in range(several):
                    target = start + f + 2 - a
                    value = product[f * pixels : (f + 1) * pixels, at : at + lanes]
                    if start + f == max(target - 2, 0):
                        partial[e, target] = value
                    else:
                        partial[e, target] += value

    column = lax.broadcasted_iota(jnp.int32, (pixels, lanes), 0) % TSIDE
    total = [jnp.zeros((8, lanes), jnp.float32)] * 2

    def gather(f):
        left = jnp.where(column == 0, 0.0, pltpu.roll(partial[0, f], 1, 0))
        right = jnp.where(column == TSIDE - 1, 0.0, pltpu.roll(partial[2, f], pixels - 1, 0))
        value = partial[1, f] + left + right
        partial[1, f] = value
        total[0] = total[0] + fold(value)
        total[1] = total[1] + fold(value * value)

    together = 3
    groups = [
        range(f, min(f + together, frames - 2)) for f in range(0, frames - 2, together)
    ]
    groups += [range(f, f + 1) for f in range(groups[-1].stop, frames)]
    for copy in copies:
        copy.wait()
    for f in groups[0]:
        hide(f)
    for number, group in enumerate(groups):
        if number + 1 < len(groups):
            for f in groups[number + 1]:
                hide(f)
        convolve(
            group.start,
            len(group),
            tuple(a for a in range(3) if group.stop - 1 + 2 - a < frames),
        )
        if number:
            for f in groups[number - 1]:
                gather(f)
    for f in groups[-1]:
        gather(f)

    part = pl.ds(pl.multiple_of(mine * lanes, LANES), lanes)
    scale, bias = group_affine(
        total[0],
        total[1],
        table_ref[gain_row : gain_row + 1, part],
        table_ref[gain_row + 1 : gain_row + 2, part],
        count,
    )
    blend = table_ref[pl.ds(blend_row + tile_id, 1), :]
    blend = jnp.where(
        (tile_row * STRIDE + up < tiles // GRID_X * STRIDE)
        & (tile_col * STRIDE + along < GRID_X * STRIDE),
        blend,
        0.0,
    )
    w_out = jnp.concatenate(
        [table_ref[w_out_row : w_out_row + 3, part], jnp.zeros((5, lanes), jnp.float32)], axis=0
    ).astype(jnp.bfloat16)
    colors = []
    for f in range(frames):
        upper = silu_of_half(partial[1, f] * scale + bias).astype(jnp.bfloat16)
        color = lax.dot_general(
            w_out, upper, (((1,), (1,)), ((), ())), preferred_element_type=jnp.float32
        )
        colors.append(color * blend)
    colors = jnp.concatenate(colors, axis=0)

    slot_in = lax.broadcasted_iota(jnp.int32, (pixels, own), 0)
    pixel = lax.broadcasted_iota(jnp.int32, (pixels, own), 1)
    denom = jnp.zeros((8, own), jnp.float32)
    for number, (down, across) in enumerate(cases):
        u, v = slot_in // TSIDE - down * STRIDE, slot_in % TSIDE - across * STRIDE
        good = (u >= 0) & (u < STRIDE) & (v >= 0) & (v < STRIDE) & (u * STRIDE + v == pixel)
        shown = jnp.where(good, 1.0, 0.0).astype(jnp.bfloat16)
        inside = (tile_row >= down) & (tile_col >= across)
        other = jnp.maximum(tile_id - down * GRID_X - across, 0)
        weight = jnp.where(inside, table_ref[pl.ds(blend_row + other, 1), :], 0.0)
        piece = exact_dot(
            jnp.concatenate([colors, jnp.broadcast_to(weight, (8, pixels))], axis=0), shown
        )
        denom = denom + piece[8 * frames :]
        shown_ref[...] = piece
        for swap in range(spans):
            target = keep_ref if swap == 0 else send_ref.at[swap - 1]
            base = (mine + swap) % spans * own_frames * 8
            for at in range(own_frames):
                for o in range(3):
                    target[number, o, at : at + 1, :] = shown_ref[pl.ds(base + 8 * at + o, 1), :]

    denom_ref[...] = denom


def from_ring(value, axis):
    count = lax.axis_size(axis)
    return [
        lax.ppermute(value, axis, [((d + turn) % count, d) for d in range(count)])
        for turn in range(1, count)
    ]


def ring_sum(kept, sent, axis):
    count = lax.axis_size(axis)
    for turn in range(1, count):
        kept = kept + lax.ppermute(
            sent[turn - 1], axis, [(d, (d + turn) % count) for d in range(count)]
        )
    return kept


def small_table(*values):
    values = [value.reshape(-1, value.shape[-1]) for value in values]
    wide = max(value.shape[1] for value in values)
    height = sum(value.shape[0] for value in values)
    total, row = 0.0, 0
    for value in values:
        below = height - row - value.shape[0]
        value = jnp.pad(value.astype(jnp.float32), ((row, below), (0, wide - value.shape[1])))
        total = total + value
        row = height - below
    return total


def exchange_latents(latents, table):
    tiles, shares, spans = (lax.axis_size(name) for name in ("tile", "chan", "tm"))
    frames, latent, own = latents.shape
    tail = own - LANES
    height = frames * latent
    others = from_ring(latents.reshape(height, own), "tm")
    parts = [table[:height, :own].astype(jnp.bfloat16)] + others
    tails = sum(
        jnp.pad(
            part[f * latent : (f + 1) * latent, LANES:],
            ((0, 0), (tail * (f * spans + at), LANES - tail * (f * spans + at + 1))),
        )
        for at, part in enumerate(parts)
        for f in range(frames)
    )
    affine = table[height : height + 2]
    high = lax.reduce_precision(affine, 8, 7)
    low = lax.reduce_precision(affine - high, 8, 7)
    affine = jnp.concatenate([high, low], axis=0).astype(jnp.bfloat16)
    rows = [affine[:, at : at + LANES] for at in range(0, affine.shape[1], LANES)]
    rows = jnp.concatenate(rows, axis=0)
    rows = jnp.pad(rows, ((0, -rows.shape[0] % 16), (0, 0)))
    message = jnp.concatenate([part[:, :LANES] for part in parts] + [tails, rows], axis=0)
    got = [message]
    for steps in range(1, tiles):
        turn = steps if steps < shares else 0
        pairs = [
            (t * shares + (c + turn) % shares, (t + steps) % tiles * shares + c)
            for t in range(tiles)
            for c in range(shares)
        ]
        got.append(lax.ppermute(message, ("tile", "chan"), pairs))
    return got


def lanes_body(
    latents, tile_order, w_in, gain_in, shift_in, w_mid, gain_mid, shift_mid, w_out, blend_weight
):
    own_frames, latent, own = latents.shape
    spans = lax.axis_size("tm")
    shares = lax.axis_size("chan")
    frames = own_frames * spans
    tiles = tile_order.shape[0]
    wide = w_in.shape[2]
    lanes = wide // spans
    pixels = TSIDE * TSIDE
    cases = block_cases(tiles)

    w_in_all = from_ring(w_in, "chan")
    table = lax.optimization_barrier(
        small_table(
            latents.reshape(own_frames * latent, own),
            gain_in,
            shift_in,
            gain_mid,
            shift_mid,
            w_out,
            blend_weight,
        )
    )
    latents_all = exchange_latents(latents, table)
    _, w_in, tile_order = lax.optimization_barrier((latents_all[0], w_in, tile_order))
    order = jnp.broadcast_to(tile_order.astype(jnp.float32)[:, None], (tiles, LANES))
    w_in_own = from_ring(w_in, "tm")[:1] or [w_in]

    vmem = pl.BlockSpec(memory_space=pltpu.VMEM)
    piece = (len(cases), 3, own_frames, own)
    kept, sent, denom = pl.pallas_call(
        functools.partial(decode_kernel, tiles, spans, shares),
        out_shape=[
            jax.ShapeDtypeStruct(piece, jnp.float32),
            jax.ShapeDtypeStruct((max(spans - 1, 1),) + piece, jnp.float32),
            jax.ShapeDtypeStruct((8, own), jnp.float32),
        ],
        in_specs=[pl.BlockSpec(memory_space=pl.ANY)] + [vmem] * (2 + tiles + shares),
        out_specs=[vmem] * 3,
        scratch_shapes=[
            pltpu.VMEM((frames + 2, 9, latent, pixels), jnp.bfloat16),
            pltpu.VMEM((frames, pixels, CH), jnp.float32),
            pltpu.VMEM((frames, pixels + 2 * TSIDE, CH), jnp.bfloat16),
            pltpu.VMEM((3 * CH, 9 * lanes), jnp.bfloat16),
            pltpu.VMEM((3, frames, pixels, lanes), jnp.float32),
            pltpu.VMEM((8 * (frames + 1), own), jnp.float32),
            pltpu.SemaphoreType.DMA((27,)),
        ],
        compiler_params=pltpu.CompilerParams(vmem_limit_bytes=VMEM_BYTES),
        cost_estimate=pl.CostEstimate(
            flops=2 * frames * pixels * 27 * CH * lanes, bytes_accessed=8_000_000, transcendentals=0
        ),
    )(w_mid, table, order, *latents_all, *w_in_own, *w_in_all)
    total = ring_sum(kept, sent, "tm")
    total = ring_sum(total, [total] * (shares - 1), "chan")
    numer = total[0]
    for number, (down, across) in enumerate(cases):
        steps = down * GRID_X + across
        if steps and steps < tiles:
            numer = numer + shifted(total[number], "tile", steps)
    return jnp.transpose(numer / denom[0][None, None, :], (1, 0, 2))


def solution(mesh):
    placed = (
        P("tm", "groups", "tile"),
        P("groups"),
        P(None, None, "chan"),
        P("chan"),
        P("chan"),
        P(None, None, "chan"),
        P("chan"),
        P("chan"),
        P(None, "chan"),
        P("groups", None),
    )
    whole_lanes = (
        CH % (mesh.shape["chan"] * mesh.shape["tm"] * LANES) == 0
        and mesh.shape["chan"] <= mesh.shape["tile"]
    )
    return jax.shard_map(
        lanes_body if whole_lanes else general_body,
        mesh=mesh,
        in_specs=placed,
        out_specs=P("tm", "groups", "tile"),
        check_vma=False,
    )
```

```python
import functools

import jax
import jax.numpy as jnp
from jax import lax
from jax.experimental import pallas as pl
from jax.experimental.pallas import tpu as pltpu
from jax.sharding import PartitionSpec as P

CH = 512
GROUPS = 32
TSIDE = 16
STRIDE = 12
GRID_X = 4

EPSILON = 1e-06
LANES = 128
VMEM_BYTES = 48 * 1024 * 1024


def shifted(value, axis, steps):
    count = lax.axis_size(axis)
    leading, last = (max(0, -steps), min(count, count - steps))
    return lax.ppermute(value, axis, [(source, source + steps) for source in range(leading, last)])


def window_index(tile_id, tiles):
    slots = jnp.arange(TSIDE * TSIDE, dtype=jnp.int32)
    row = tile_id // GRID_X * STRIDE + slots // TSIDE
    col = tile_id % GRID_X * STRIDE + slots % TSIDE
    valid = (row < tiles // GRID_X * STRIDE) & (col < GRID_X * STRIDE)
    block = row // STRIDE * GRID_X + col // STRIDE
    index = block * (STRIDE * STRIDE) + row % STRIDE * STRIDE + col % STRIDE
    return (jnp.where(valid, index, 0), valid)


def causal_conv(extended, weights, frames, side):
    pixels = side * side
    rows = jnp.arange(pixels, dtype=jnp.int32) // side
    cols = jnp.arange(pixels, dtype=jnp.int32) % side
    total = jnp.zeros((frames, weights.shape[2], pixels), jnp.float32)
    for depth in range(3):
        window = extended[depth : depth + frames]
        for down in range(3):
            for across in range(3):
                offset = (down - 1) * side + (across - 1)
                inside = (
                    (rows + down - 1 >= 0)
                    & (rows + down - 1 < side)
                    & (cols + across - 1 >= 0)
                    & (cols + across - 1 < side)
                )
                moved = jnp.roll(window, -offset, axis=2)
                moved = jnp.where(inside[None, None, :], moved, jnp.zeros_like(moved))
                total = total + jnp.einsum(
                    "fcp,co->fop",
                    moved,
                    weights[9 * depth + 3 * down + across],
                    preferred_element_type=jnp.float32,
                )
    return total


def with_history(values):
    frames = values.shape[0]
    earlier = shifted(values[frames - 2 :], "tm", 1)
    return jnp.concatenate([earlier, values], axis=0)


def normalize(values, gain, shift, total_frames):
    frames, chans, pixels = values.shape
    width = CH // GROUPS
    grouped = values.reshape(frames, chans // width, width, pixels)
    sums = jnp.sum(grouped, axis=(0, 2, 3))
    squares = jnp.sum(grouped * grouped, axis=(0, 2, 3))
    sums, squares = lax.psum((sums, squares), "tm")
    count = total_frames * width * pixels
    mean = sums / count
    variance = squares / count - mean * mean
    scale = lax.rsqrt(variance + EPSILON)
    normed = (grouped - mean[None, :, None, None]) * scale[None, :, None, None]
    normed = normed.reshape(frames, chans, pixels) * gain[None, :, None] + shift[None, :, None]
    return jax.nn.silu(normed).astype(jnp.bfloat16)


def spread(color, weight, index, total_pixels):
    numer = (
        jnp.zeros((color.shape[0], 3, total_pixels), jnp.float32)
        .at[:, :, index]
        .add(color * weight[None, None, :])
    )
    denom = jnp.zeros((total_pixels,), jnp.float32).at[index].add(weight)
    return (numer, denom)


def route_owned(numer, denom, tile_id, own):
    frames = numer.shape[0]
    margin = (GRID_X + 1) * own
    numer_wide = jnp.concatenate([numer, jnp.zeros((frames, 3, margin), jnp.float32)], axis=2)
    denom_wide = jnp.concatenate([denom, jnp.zeros((margin,), jnp.float32)], axis=0)
    first_pixel = tile_id * own

    def block_at(offset):
        start_pixel = first_pixel + offset * own
        return (
            lax.dynamic_slice_in_dim(numer_wide, start_pixel, own, 2),
            lax.dynamic_slice_in_dim(denom_wide, start_pixel, own, 0),
        )

    owned_numer, owned_denom = block_at(0)
    for offset in (1, GRID_X, GRID_X + 1):
        piece_numer, piece_denom = block_at(offset)
        got_numer, got_denom = shifted((piece_numer, piece_denom), "tile", offset)
        owned_numer = owned_numer + got_numer
        owned_denom = owned_denom + got_denom
    return (owned_numer, owned_denom)


def general_body(
    latents, tile_order, w_in, gain_in, shift_in, w_mid, gain_mid, shift_mid, w_out, blend_weight
):
    frames = latents.shape[0]
    total_frames = frames * lax.axis_size("tm")
    tiles = tile_order.shape[0]
    own = STRIDE * STRIDE
    total_pixels = tiles * own
    tile_id = lax.axis_index("tile")
    index, valid = window_index(tile_id, tiles)
    whole = lax.all_gather(latents, "tile", axis=2, tiled=True)
    blocks = whole.reshape(frames, whole.shape[1], tiles, own)
    image = (
        jnp.zeros_like(blocks)
        .at[:, :, tile_order]
        .set(blocks)
        .reshape(frames, whole.shape[1], total_pixels)
    )
    window = jnp.where(
        valid[None, None, :], jnp.take(image, index, axis=2), jnp.zeros((), jnp.bfloat16)
    )
    first = causal_conv(with_history(window), w_in, frames, TSIDE)
    hidden = normalize(first, gain_in, shift_in, total_frames)
    second = causal_conv(
        lax.all_gather(with_history(hidden), "chan", axis=1, tiled=True), w_mid, frames, TSIDE
    )
    upper = normalize(second, gain_mid, shift_mid, total_frames)
    color = jnp.einsum("oc,fcp->fop", w_out, upper, preferred_element_type=jnp.float32)
    weight = jnp.where(valid, blend_weight[tile_id], jnp.float32(0.0))
    numer, denom = spread(color, weight, index, total_pixels)
    numer, denom = route_owned(numer, denom, tile_id, own)
    numer = lax.psum(numer, "chan")
    return numer / denom[None, None, :]


def block_cases(tiles):
    downs = (0, 1) if tiles // GRID_X > 1 else (0,)
    return [(down, across) for down in downs for across in (0, 1)]


def exact_dot(values, ones):
    rows = values.shape[0]
    high = values.astype(jnp.bfloat16)
    rest = values - high.astype(jnp.float32)
    middle = rest.astype(jnp.bfloat16)
    low = (rest - middle.astype(jnp.float32)).astype(jnp.bfloat16)
    total = jnp.dot(
        jnp.concatenate([high, middle, low], axis=0), ones, preferred_element_type=jnp.float32
    )
    return total[:rows] + total[rows : 2 * rows] + total[2 * rows :]


def group_affine(sums, squares, gain, shift, count):
    lanes = sums.shape[1]
    width = CH // GROUPS
    same = lax.broadcasted_iota(jnp.int32, (lanes, lanes), 0) // width == (
        lax.broadcasted_iota(jnp.int32, (lanes, lanes), 1) // width
    )
    total = exact_dot(
        jnp.concatenate([sums, squares], axis=0), jnp.where(same, 1.0, 0.0).astype(jnp.bfloat16)
    )
    mean = jnp.sum(total[:8], axis=0, keepdims=True) / count
    variance = jnp.sum(total[8:], axis=0, keepdims=True) / count - mean * mean
    scale = gain * lax.rsqrt(variance + EPSILON)
    return 0.5 * scale, 0.5 * (shift - mean * scale)


def silu_of_half(half):
    return half + half * jnp.tanh(half)


def fold(values):
    rows, lanes = values.shape
    return jnp.sum(values.reshape(rows // 8, 8, lanes), axis=0)


def decode_kernel(
    tiles,
    spans,
    shares,
    *refs,
):
    cases = block_cases(tiles)
    refs = list(refs)

    def take(number):
        taken = refs[:number]
        del refs[:number]
        return taken

    w_mid_ref, table_ref, order_ref = take(3)
    latent_refs, w_in_refs = take(tiles), take(shares)
    keep_ref, send_ref, denom_ref = take(3)
    chosen, taps, first, hidden, weights, partial, shown_ref, sems = take(8)

    own = denom_ref.shape[1]
    own_frames = keep_ref.shape[2]
    frames = own_frames * spans
    latent, wide = w_in_refs[0].shape[1:]
    rows_in = frames * latent
    rows_own = rows_in // spans
    depth_in = 27 * latent
    pixels = TSIDE * TSIDE
    lanes = partial.shape[3]
    tile_id = lax.axis_index("tile")
    mine = lax.axis_index("tm")
    chan_id = lax.axis_index("chan")

    copies = []
    for a in range(3):
        for b in range(3):
            for e in range(3):
                tap = 9 * a + 3 * b + e
                copy = pltpu.make_async_copy(
                    w_mid_ref.at[tap, :, pl.ds(pl.multiple_of(mine * lanes, LANES), lanes)],
                    weights.at[pl.ds(b * CH, CH), pl.ds((3 * a + e) * lanes, lanes)],
                    sems.at[tap],
                )
                copy.start()
                copies.append(copy)

    tile_row, tile_col = tile_id // GRID_X, tile_id % GRID_X
    gain_row = rows_own + 2
    w_out_row = gain_row + 2
    blend_row = w_out_row + 3
    order = order_ref[...]
    number_of = lax.broadcasted_iota(jnp.int32, order.shape, 0)
    lane_of = lax.broadcasted_iota(jnp.int32, order.shape, 1)
    rows_sent = rows_in + latent
    for number, (down, across) in enumerate(cases):
        inside = (tile_row + down < tiles // GRID_X) & (tile_col + across < GRID_X)
        wanted = tile_id + down * GRID_X + across
        found = (order == wanted.astype(jnp.float32)) & (lane_of == 0)
        place = jnp.sum(jnp.where(found, number_of.astype(jnp.float32), 0.0))
        turn = (tile_id - place.astype(jnp.int32) + tiles) % tiles
        part = slice(number * LANES, (number + 1) * LANES)
        for steps in range(tiles):

            @pl.when(inside & (turn == steps))
            def _():
                chosen[:, part] = latent_refs[steps][:rows_sent]

        @pl.when(jnp.logical_not(inside))
        def _():
            chosen[:, part] = jnp.zeros((rows_sent, LANES), chosen.dtype)

    slot = lax.broadcasted_iota(jnp.int32, (1, pixels), 1)
    up, along = slot // TSIDE, slot % TSIDE
    source = lax.broadcasted_iota(jnp.int32, (LANES, pixels), 0)
    tail = own - LANES

    def pick(swap):
        parts = []
        for down, across in cases:
            u, v = up - down * STRIDE, along - across * STRIDE
            good = (u >= 0) & (u < STRIDE) & (v >= 0) & (v < STRIDE)
            wanted = jnp.where(good, u * STRIDE + v, -1)
            if swap is not None:
                wanted = jnp.where(wanted >= LANES, wanted - LANES + tail * swap, -1)
            parts.append(jnp.where(source == wanted, 1.0, 0.0).astype(jnp.bfloat16))
        return jnp.concatenate(parts, axis=0)

    window = jnp.dot(
        chosen[:rows_in], pick(None), preferred_element_type=jnp.float32
    )
    tails = chosen[rows_in:].astype(jnp.float32)
    width = tails.shape[1]
    tails = jnp.concatenate(
        [
            pltpu.roll(tails, (-f * spans * tail) % width, 1) if f else tails
            for f in range(own_frames)
        ],
        axis=0,
    ).astype(jnp.bfloat16)
    ends = [
        jnp.dot(tails, pick(swap), preferred_element_type=jnp.float32) for swap in range(spans)
    ]
    window = window + jnp.concatenate(ends, axis=0)
    taps[0:2] = jnp.zeros((2,) + taps.shape[1:], taps.dtype)
    for b in range(3):
        for e in range(3):
            inside = (
                (up + b - 1 >= 0)
                & (up + b - 1 < TSIDE)
                & (along + e - 1 >= 0)
                & (along + e - 1 < TSIDE)
            )
            offset = (b - 1) * TSIDE + e - 1
            moved = pltpu.roll(window, (-offset) % pixels, 1) if offset else window
            moved = jnp.where(inside, moved, 0.0).astype(jnp.bfloat16)
            for swap in range(spans):
                value = moved[swap * rows_own : (swap + 1) * rows_own]
                span = pl.ds(2 + (mine + swap) % spans * own_frames, own_frames)
                taps[span, 3 * b + e] = value.reshape(own_frames, latent, pixels)

    joined = jnp.concatenate(
        [w_in_refs[s][:27].reshape(depth_in, wide) for s in range(shares)], axis=1
    )
    sums = jnp.zeros((8, CH), jnp.float32)
    squares = jnp.zeros((8, CH), jnp.float32)
    for f in range(frames):
        patch = taps[f : f + 3].reshape(depth_in, pixels)
        value = lax.dot_general(
            patch, joined, (((0,), (0,)), ((), ())), preferred_element_type=jnp.float32
        )
        first[f] = value
        sums = sums + fold(value)
        squares = squares + fold(value * value)
    count = frames * (CH // GROUPS) * pixels
    affine = []
    for s in range(shares):
        at = rows_sent
        table = latent_refs[s][at : at + wide // LANES * 4].astype(jnp.float32)
        pieces = [table[4 * lane : 4 * lane + 4] for lane in range(wide // LANES)]
        table = jnp.concatenate([part[0:2] + part[2:4] for part in pieces], axis=1)
        part = slice(s * wide, (s + 1) * wide)
        affine.append(
            group_affine(sums[:, part], squares[:, part], table[0:1], table[1:2], count)
        )
    channels = [
        pl.ds(pl.multiple_of((chan_id + s) % shares * wide, LANES), wide) for s in range(shares)
    ]

    def hide(f):
        edge = jnp.zeros((TSIDE, CH), jnp.bfloat16)
        hidden[f, 0:TSIDE] = edge
        hidden[f, TSIDE + pixels : 2 * TSIDE + pixels] = edge
        for s in range(shares):
            scale, bias = affine[s]
            value = first[f, :, s * wide : (s + 1) * wide] * scale + bias
            hidden[f, TSIDE : TSIDE + pixels, channels[s]] = silu_of_half(value).astype(
                jnp.bfloat16
            )

    def convolve(start, several, depth_taps):
        lhs = jnp.concatenate(
            [
                hidden[start : start + several, b * TSIDE : b * TSIDE + pixels].reshape(
                    several * pixels, CH
                )
                for b in range(3)
            ],
            axis=1,
        )
        low = depth_taps[0] * 3 * lanes
        product = jnp.dot(lhs, weights[:, low:], preferred_element_type=jnp.float32)
        for a in depth_taps:
            for e in range(3):
                at = (3 * a + e) * lanes - low
                for f in range(several):
                    target = start + f + 2 - a
                    value = product[f * pixels : (f + 1) * pixels, at : at + lanes]
                    if start + f == max(target - 2, 0):
                        partial[e, target] = value
                    else:
                        partial[e, target] += value

    column = lax.broadcasted_iota(jnp.int32, (pixels, lanes), 0) % TSIDE
    total = [jnp.zeros((8, lanes), jnp.float32)] * 2

    def gather(f):
        left = jnp.where(column == 0, 0.0, pltpu.roll(partial[0, f], 1, 0))
        right = jnp.where(column == TSIDE - 1, 0.0, pltpu.roll(partial[2, f], pixels - 1, 0))
        value = partial[1, f] + left + right
        partial[1, f] = value
        total[0] = total[0] + fold(value)
        total[1] = total[1] + fold(value * value)

    together = 3
    groups = [
        range(f, min(f + together, frames - 2)) for f in range(0, frames - 2, together)
    ]
    groups += [range(f, f + 1) for f in range(groups[-1].stop, frames)]
    for copy in copies:
        copy.wait()
    for f in groups[0]:
        hide(f)
    for number, group in enumerate(groups):
        if number + 1 < len(groups):
            for f in groups[number + 1]:
                hide(f)
        convolve(
            group.start,
            len(group),
            tuple(a for a in range(3) if group.stop - 1 + 2 - a < frames),
        )
        if number:
            for f in groups[number - 1]:
                gather(f)
    for f in groups[-1]:
        gather(f)

    part = pl.ds(pl.multiple_of(mine * lanes, LANES), lanes)
    scale, bias = group_affine(
        total[0],
        total[1],
        table_ref[gain_row : gain_row + 1, part],
        table_ref[gain_row + 1 : gain_row + 2, part],
        count,
    )
    blend = table_ref[pl.ds(blend_row + tile_id, 1), :]
    blend = jnp.where(
        (tile_row * STRIDE + up < tiles // GRID_X * STRIDE)
        & (tile_col * STRIDE + along < GRID_X * STRIDE),
        blend,
        0.0,
    )
    w_out = jnp.concatenate(
        [table_ref[w_out_row : w_out_row + 3, part], jnp.zeros((5, lanes), jnp.float32)], axis=0
    ).astype(jnp.bfloat16)
    colors = []
    for f in range(frames):
        upper = silu_of_half(partial[1, f] * scale + bias).astype(jnp.bfloat16)
        color = lax.dot_general(
            w_out, upper, (((1,), (1,)), ((), ())), preferred_element_type=jnp.float32
        )
        colors.append(color * blend)
    colors = jnp.concatenate(colors, axis=0)

    slot_in = lax.broadcasted_iota(jnp.int32, (pixels, own), 0)
    pixel = lax.broadcasted_iota(jnp.int32, (pixels, own), 1)
    denom = jnp.zeros((8, own), jnp.float32)
    for number, (down, across) in enumerate(cases):
        u, v = slot_in // TSIDE - down * STRIDE, slot_in % TSIDE - across * STRIDE
        good = (u >= 0) & (u < STRIDE) & (v >= 0) & (v < STRIDE) & (u * STRIDE + v == pixel)
        shown = jnp.where(good, 1.0, 0.0).astype(jnp.bfloat16)
        inside = (tile_row >= down) & (tile_col >= across)
        other = jnp.maximum(tile_id - down * GRID_X - across, 0)
        weight = jnp.where(inside, table_ref[pl.ds(blend_row + other, 1), :], 0.0)
        piece = exact_dot(
            jnp.concatenate([colors, jnp.broadcast_to(weight, (8, pixels))], axis=0), shown
        )
        denom = denom + piece[8 * frames :]
        shown_ref[...] = piece
        for swap in range(spans):
            target = keep_ref if swap == 0 else send_ref.at[swap - 1]
            base = (mine + swap) % spans * own_frames * 8
            for at in range(own_frames):
                for o in range(3):
                    target[number, o, at : at + 1, :] = shown_ref[pl.ds(base + 8 * at + o, 1), :]

    denom_ref[...] = denom


def from_ring(value, axis):
    count = lax.axis_size(axis)
    return [
        lax.ppermute(value, axis, [((d + turn) % count, d) for d in range(count)])
        for turn in range(1, count)
    ]


def small_table(*values):
    values = [value.reshape(-1, value.shape[-1]) for value in values]
    wide = max(value.shape[1] for value in values)
    height = sum(value.shape[0] for value in values)
    total, row = 0.0, 0
    for value in values:
        below = height - row - value.shape[0]
        value = jnp.pad(value.astype(jnp.float32), ((row, below), (0, wide - value.shape[1])))
        total = total + value
        row = height - below
    return total


def exchange_latents(latents, table):
    tiles, shares, spans = (lax.axis_size(name) for name in ("tile", "chan", "tm"))
    frames, latent, own = latents.shape
    tail = own - LANES
    height = frames * latent
    others = from_ring(latents.reshape(height, own), "tm")
    parts = [table[:height, :own].astype(jnp.bfloat16)] + others
    tails = sum(
        jnp.pad(
            part[f * latent : (f + 1) * latent, LANES:],
            ((0, 0), (tail * (f * spans + at), LANES - tail * (f * spans + at + 1))),
        )
        for at, part in enumerate(parts)
        for f in range(frames)
    )
    affine = table[height : height + 2]
    high = lax.reduce_precision(affine, 8, 7)
    low = lax.reduce_precision(affine - high, 8, 7)
    affine = jnp.concatenate([high, low], axis=0).astype(jnp.bfloat16)
    rows = [affine[:, at : at + LANES] for at in range(0, affine.shape[1], LANES)]
    rows = jnp.concatenate(rows, axis=0)
    rows = jnp.pad(rows, ((0, -rows.shape[0] % 16), (0, 0)))
    message = jnp.concatenate([part[:, :LANES] for part in parts] + [tails, rows], axis=0)
    got = [message]
    for steps in range(1, tiles):
        turn = steps if steps < shares else 0
        pairs = [
            (t * shares + (c + turn) % shares, (t + steps) % tiles * shares + c)
            for t in range(tiles)
            for c in range(shares)
        ]
        got.append(lax.ppermute(message, ("tile", "chan"), pairs))
    return got


def lanes_body(
    latents, tile_order, w_in, gain_in, shift_in, w_mid, gain_mid, shift_mid, w_out, blend_weight
):
    own_frames, latent, own = latents.shape
    spans = lax.axis_size("tm")
    shares = lax.axis_size("chan")
    frames = own_frames * spans
    tiles = tile_order.shape[0]
    wide = w_in.shape[2]
    lanes = wide // spans
    pixels = TSIDE * TSIDE
    cases = block_cases(tiles)

    w_in_all = from_ring(w_in, "chan")
    table = lax.optimization_barrier(
        small_table(
            latents.reshape(own_frames * latent, own),
            gain_in,
            shift_in,
            gain_mid,
            shift_mid,
            w_out,
            blend_weight,
        )
    )
    latents_all = exchange_latents(latents, table)
    _, w_in, tile_order = lax.optimization_barrier((latents_all[0], w_in, tile_order))
    order = jnp.broadcast_to(tile_order.astype(jnp.float32)[:, None], (tiles, LANES))
    w_in_own = from_ring(w_in, "tm")[:1] or [w_in]

    vmem = pl.BlockSpec(memory_space=pltpu.VMEM)
    piece = (len(cases), 3, own_frames, own)
    kept, sent, denom = pl.pallas_call(
        functools.partial(decode_kernel, tiles, spans, shares),
        out_shape=[
            jax.ShapeDtypeStruct(piece, jnp.float32),
            jax.ShapeDtypeStruct((max(spans - 1, 1),) + piece, jnp.float32),
            jax.ShapeDtypeStruct((8, own), jnp.float32),
        ],
        in_specs=[pl.BlockSpec(memory_space=pl.ANY)] + [vmem] * (2 + tiles + shares),
        out_specs=[vmem] * 3,
        scratch_shapes=[
            pltpu.VMEM(((frames + 1) * latent, len(cases) * LANES), jnp.bfloat16),
            pltpu.VMEM((frames + 2, 9, latent, pixels), jnp.bfloat16),
            pltpu.VMEM((frames, pixels, CH), jnp.float32),
            pltpu.VMEM((frames, pixels + 2 * TSIDE, CH), jnp.bfloat16),
            pltpu.VMEM((3 * CH, 9 * lanes), jnp.bfloat16),
            pltpu.VMEM((3, frames, pixels, lanes), jnp.float32),
            pltpu.VMEM((8 * (frames + 1), own), jnp.float32),
            pltpu.SemaphoreType.DMA((27,)),
        ],
        compiler_params=pltpu.CompilerParams(vmem_limit_bytes=VMEM_BYTES),
        cost_estimate=pl.CostEstimate(
            flops=2 * frames * pixels * 27 * CH * lanes, bytes_accessed=8_000_000, transcendentals=0
        ),
    )(w_mid, table, order, *latents_all, *w_in_own, *w_in_all)
    total = kept
    for turn in range(shares):
        for swap in range(spans):
            if turn or swap:
                pairs = [
                    (c * spans + m, (c + turn) % shares * spans + (m + swap) % spans)
                    for c in range(shares)
                    for m in range(spans)
                ]
                piece = sent[swap - 1] if swap else kept
                total = total + lax.ppermute(piece, ("chan", "tm"), pairs)
    numer = total[0]
    for number, (down, across) in enumerate(cases):
        steps = down * GRID_X + across
        if steps and steps < tiles:
            numer = numer + shifted(total[number], "tile", steps)
    return jnp.transpose(numer / denom[0][None, None, :], (1, 0, 2))


def solution(mesh):
    placed = (
        P("tm", "groups", "tile"),
        P("groups"),
        P(None, None, "chan"),
        P("chan"),
        P("chan"),
        P(None, None, "chan"),
        P("chan"),
        P("chan"),
        P(None, "chan"),
        P("groups", None),
    )
    whole_lanes = (
        CH % (mesh.shape["chan"] * mesh.shape["tm"] * LANES) == 0
        and mesh.shape["chan"] <= mesh.shape["tile"]
    )
    return jax.shard_map(
        lanes_body if whole_lanes else general_body,
        mesh=mesh,
        in_specs=placed,
        out_specs=P("tm", "groups", "tile"),
        check_vma=False,
    )
```

```python
import functools

import jax
import jax.numpy as jnp
from jax import lax
from jax.experimental import pallas as pl
from jax.experimental.pallas import tpu as pltpu
from jax.sharding import PartitionSpec as P

CH = 512
GROUPS = 32
TSIDE = 16
STRIDE = 12
GRID_X = 4

EPSILON = 1e-06
LANES = 128
VMEM_BYTES = 48 * 1024 * 1024


def shifted(value, axis, steps):
    count = lax.axis_size(axis)
    leading, last = (max(0, -steps), min(count, count - steps))
    return lax.ppermute(value, axis, [(source, source + steps) for source in range(leading, last)])


def window_index(tile_id, tiles):
    slots = jnp.arange(TSIDE * TSIDE, dtype=jnp.int32)
    row = tile_id // GRID_X * STRIDE + slots // TSIDE
    col = tile_id % GRID_X * STRIDE + slots % TSIDE
    valid = (row < tiles // GRID_X * STRIDE) & (col < GRID_X * STRIDE)
    block = row // STRIDE * GRID_X + col // STRIDE
    index = block * (STRIDE * STRIDE) + row % STRIDE * STRIDE + col % STRIDE
    return (jnp.where(valid, index, 0), valid)


def causal_conv(extended, weights, frames, side):
    pixels = side * side
    rows = jnp.arange(pixels, dtype=jnp.int32) // side
    cols = jnp.arange(pixels, dtype=jnp.int32) % side
    total = jnp.zeros((frames, weights.shape[2], pixels), jnp.float32)
    for depth in range(3):
        window = extended[depth : depth + frames]
        for down in range(3):
            for across in range(3):
                offset = (down - 1) * side + (across - 1)
                inside = (
                    (rows + down - 1 >= 0)
                    & (rows + down - 1 < side)
                    & (cols + across - 1 >= 0)
                    & (cols + across - 1 < side)
                )
                moved = jnp.roll(window, -offset, axis=2)
                moved = jnp.where(inside[None, None, :], moved, jnp.zeros_like(moved))
                total = total + jnp.einsum(
                    "fcp,co->fop",
                    moved,
                    weights[9 * depth + 3 * down + across],
                    preferred_element_type=jnp.float32,
                )
    return total


def with_history(values):
    frames = values.shape[0]
    earlier = shifted(values[frames - 2 :], "tm", 1)
    return jnp.concatenate([earlier, values], axis=0)


def normalize(values, gain, shift, total_frames):
    frames, chans, pixels = values.shape
    width = CH // GROUPS
    grouped = values.reshape(frames, chans // width, width, pixels)
    sums = jnp.sum(grouped, axis=(0, 2, 3))
    squares = jnp.sum(grouped * grouped, axis=(0, 2, 3))
    sums, squares = lax.psum((sums, squares), "tm")
    count = total_frames * width * pixels
    mean = sums / count
    variance = squares / count - mean * mean
    scale = lax.rsqrt(variance + EPSILON)
    normed = (grouped - mean[None, :, None, None]) * scale[None, :, None, None]
    normed = normed.reshape(frames, chans, pixels) * gain[None, :, None] + shift[None, :, None]
    return jax.nn.silu(normed).astype(jnp.bfloat16)


def spread(color, weight, index, total_pixels):
    numer = (
        jnp.zeros((color.shape[0], 3, total_pixels), jnp.float32)
        .at[:, :, index]
        .add(color * weight[None, None, :])
    )
    denom = jnp.zeros((total_pixels,), jnp.float32).at[index].add(weight)
    return (numer, denom)


def route_owned(numer, denom, tile_id, own):
    frames = numer.shape[0]
    margin = (GRID_X + 1) * own
    numer_wide = jnp.concatenate([numer, jnp.zeros((frames, 3, margin), jnp.float32)], axis=2)
    denom_wide = jnp.concatenate([denom, jnp.zeros((margin,), jnp.float32)], axis=0)
    first_pixel = tile_id * own

    def block_at(offset):
        start_pixel = first_pixel + offset * own
        return (
            lax.dynamic_slice_in_dim(numer_wide, start_pixel, own, 2),
            lax.dynamic_slice_in_dim(denom_wide, start_pixel, own, 0),
        )

    owned_numer, owned_denom = block_at(0)
    for offset in (1, GRID_X, GRID_X + 1):
        piece_numer, piece_denom = block_at(offset)
        got_numer, got_denom = shifted((piece_numer, piece_denom), "tile", offset)
        owned_numer = owned_numer + got_numer
        owned_denom = owned_denom + got_denom
    return (owned_numer, owned_denom)


def general_body(
    latents, tile_order, w_in, gain_in, shift_in, w_mid, gain_mid, shift_mid, w_out, blend_weight
):
    frames = latents.shape[0]
    total_frames = frames * lax.axis_size("tm")
    tiles = tile_order.shape[0]
    own = STRIDE * STRIDE
    total_pixels = tiles * own
    tile_id = lax.axis_index("tile")
    index, valid = window_index(tile_id, tiles)
    whole = lax.all_gather(latents, "tile", axis=2, tiled=True)
    blocks = whole.reshape(frames, whole.shape[1], tiles, own)
    image = (
        jnp.zeros_like(blocks)
        .at[:, :, tile_order]
        .set(blocks)
        .reshape(frames, whole.shape[1], total_pixels)
    )
    window = jnp.where(
        valid[None, None, :], jnp.take(image, index, axis=2), jnp.zeros((), jnp.bfloat16)
    )
    first = causal_conv(with_history(window), w_in, frames, TSIDE)
    hidden = normalize(first, gain_in, shift_in, total_frames)
    second = causal_conv(
        lax.all_gather(with_history(hidden), "chan", axis=1, tiled=True), w_mid, frames, TSIDE
    )
    upper = normalize(second, gain_mid, shift_mid, total_frames)
    color = jnp.einsum("oc,fcp->fop", w_out, upper, preferred_element_type=jnp.float32)
    weight = jnp.where(valid, blend_weight[tile_id], jnp.float32(0.0))
    numer, denom = spread(color, weight, index, total_pixels)
    numer, denom = route_owned(numer, denom, tile_id, own)
    numer = lax.psum(numer, "chan")
    return numer / denom[None, None, :]


def block_cases(tiles):
    downs = (0, 1) if tiles // GRID_X > 1 else (0,)
    return [(down, across) for down in downs for across in (0, 1)]


def exact_dot(values, ones):
    rows = values.shape[0]
    high = values.astype(jnp.bfloat16)
    rest = values - high.astype(jnp.float32)
    middle = rest.astype(jnp.bfloat16)
    low = (rest - middle.astype(jnp.float32)).astype(jnp.bfloat16)
    total = jnp.dot(
        jnp.concatenate([high, middle, low], axis=0), ones, preferred_element_type=jnp.float32
    )
    return total[:rows] + total[rows : 2 * rows] + total[2 * rows :]


def group_affine(sums, squares, gain, shift, count):
    lanes = sums.shape[1]
    width = CH // GROUPS
    same = lax.broadcasted_iota(jnp.int32, (lanes, lanes), 0) // width == (
        lax.broadcasted_iota(jnp.int32, (lanes, lanes), 1) // width
    )
    total = exact_dot(
        jnp.concatenate([sums, squares], axis=0), jnp.where(same, 1.0, 0.0).astype(jnp.bfloat16)
    )
    mean = jnp.sum(total[:8], axis=0, keepdims=True) / count
    variance = jnp.sum(total[8:], axis=0, keepdims=True) / count - mean * mean
    scale = gain * lax.rsqrt(variance + EPSILON)
    return 0.5 * scale, 0.5 * (shift - mean * scale)


def silu_of_half(half):
    return half + half * jnp.tanh(half)


def fold(values):
    rows, lanes = values.shape
    return jnp.sum(values.reshape(rows // 8, 8, lanes), axis=0)


def decode_kernel(
    tiles,
    spans,
    shares,
    *refs,
):
    cases = block_cases(tiles)
    refs = list(refs)

    def take(number):
        taken = refs[:number]
        del refs[:number]
        return taken

    w_mid_ref, table_ref, order_ref = take(3)
    latent_refs, w_in_refs = take(spans), take(shares)
    keep_ref, send_ref, denom_ref = take(3)
    chosen, taps, first, hidden, weights, partial, shown_ref, sems = take(8)

    own = denom_ref.shape[1]
    own_frames = keep_ref.shape[2]
    frames = own_frames * spans
    latent, wide = w_in_refs[0].shape[1:]
    rows_in = frames * latent
    rows_own = rows_in // spans
    depth_in = 27 * latent
    pixels = TSIDE * TSIDE
    lanes = partial.shape[3]
    tile_id = lax.axis_index("tile")
    mine = lax.axis_index("tm")
    chan_id = lax.axis_index("chan")

    copies = []
    for a in range(3):
        for b in range(3):
            for e in range(3):
                tap = 9 * a + 3 * b + e
                copy = pltpu.make_async_copy(
                    w_mid_ref.at[tap, :, pl.ds(pl.multiple_of(mine * lanes, LANES), lanes)],
                    weights.at[pl.ds(b * CH, CH), pl.ds((3 * a + e) * lanes, lanes)],
                    sems.at[tap],
                )
                copy.start()
                copies.append(copy)

    tile_row, tile_col = tile_id // GRID_X, tile_id % GRID_X
    gain_row = rows_own + 2
    w_out_row = gain_row + 2
    blend_row = w_out_row + 3
    order = order_ref[...]
    number_of = lax.broadcasted_iota(jnp.int32, order.shape, 0)
    lane_of = lax.broadcasted_iota(jnp.int32, order.shape, 1)
    rows_all = latent_refs[0].shape[0] // tiles
    for number, (down, across) in enumerate(cases):
        inside = (tile_row + down < tiles // GRID_X) & (tile_col + across < GRID_X)
        wanted = tile_id + down * GRID_X + across
        found = (order == wanted.astype(jnp.float32)) & (lane_of == 0)
        place = jnp.sum(jnp.where(found, number_of.astype(jnp.float32), 0.0))
        turn = (tile_id - place.astype(jnp.int32) + tiles) % tiles
        part = slice(number * LANES, (number + 1) * LANES)
        for steps in range(tiles):

            @pl.when(inside & (turn == steps))
            def _():
                for swap in range(spans):
                    at, tail_at = swap * rows_own, rows_in + swap * latent
                    block = latent_refs[swap][steps * rows_all : (steps + 1) * rows_all]
                    chosen[at : at + rows_own, part] = block[:rows_own]
                    chosen[tail_at : tail_at + latent, part] = block[rows_own : rows_own + latent]

        @pl.when(jnp.logical_not(inside))
        def _():
            chosen[:, part] = jnp.zeros((chosen.shape[0], LANES), chosen.dtype)

    slot = lax.broadcasted_iota(jnp.int32, (1, pixels), 1)
    up, along = slot // TSIDE, slot % TSIDE
    source = lax.broadcasted_iota(jnp.int32, (LANES, pixels), 0)
    tail = own - LANES

    def pick(first_pixel):
        parts = []
        for down, across in cases:
            u, v = up - down * STRIDE, along - across * STRIDE
            good = (u >= 0) & (u < STRIDE) & (v >= 0) & (v < STRIDE)
            wanted = jnp.where(good, u * STRIDE + v - first_pixel, -1)
            parts.append(jnp.where(source == wanted, 1.0, 0.0).astype(jnp.bfloat16))
        return jnp.concatenate(parts, axis=0)

    tails = chosen[rows_in:].astype(jnp.float32)
    width = tails.shape[1]
    turned = [pltpu.roll(tails, (-f * tail) % width, 1) if f else tails for f in range(own_frames)]
    tails = jnp.concatenate(
        [
            turned[f][swap * latent : (swap + 1) * latent]
            for swap in range(spans)
            for f in range(own_frames)
        ],
        axis=0,
    ).astype(jnp.bfloat16)
    in_tail = lax.broadcasted_iota(jnp.int32, tails.shape, 1) % LANES < tail
    tails = jnp.where(in_tail, tails.astype(jnp.float32), 0.0).astype(jnp.bfloat16)
    window = jnp.dot(
        chosen[:rows_in], pick(0), preferred_element_type=jnp.float32
    ) + jnp.dot(tails, pick(LANES), preferred_element_type=jnp.float32)
    taps[0:2] = jnp.zeros((2,) + taps.shape[1:], taps.dtype)
    for b in range(3):
        for e in range(3):
            inside = (
                (up + b - 1 >= 0)
                & (up + b - 1 < TSIDE)
                & (along + e - 1 >= 0)
                & (along + e - 1 < TSIDE)
            )
            offset = (b - 1) * TSIDE + e - 1
            moved = pltpu.roll(window, (-offset) % pixels, 1) if offset else window
            moved = jnp.where(inside, moved, 0.0).astype(jnp.bfloat16)
            for swap in range(spans):
                value = moved[swap * rows_own : (swap + 1) * rows_own]
                span = pl.ds(2 + (mine + swap) % spans * own_frames, own_frames)
                taps[span, 3 * b + e] = value.reshape(own_frames, latent, pixels)

    joined = jnp.concatenate(
        [w_in_refs[s][:27].reshape(depth_in, wide) for s in range(shares)], axis=1
    )
    sums = jnp.zeros((8, CH), jnp.float32)
    squares = jnp.zeros((8, CH), jnp.float32)
    for f in range(frames):
        patch = taps[f : f + 3].reshape(depth_in, pixels)
        value = lax.dot_general(
            patch, joined, (((0,), (0,)), ((), ())), preferred_element_type=jnp.float32
        )
        first[f] = value
        sums = sums + fold(value)
        squares = squares + fold(value * value)
    count = frames * (CH // GROUPS) * pixels
    affine = []
    for s in range(shares):
        at = s * rows_all + rows_own + latent
        table = latent_refs[0][at : at + wide // LANES * 4].astype(jnp.float32)
        pieces = [table[4 * lane : 4 * lane + 4] for lane in range(wide // LANES)]
        table = jnp.concatenate([part[0:2] + part[2:4] for part in pieces], axis=1)
        part = slice(s * wide, (s + 1) * wide)
        affine.append(
            group_affine(sums[:, part], squares[:, part], table[0:1], table[1:2], count)
        )
    channels = [
        pl.ds(pl.multiple_of((chan_id + s) % shares * wide, LANES), wide) for s in range(shares)
    ]

    def hide(f):
        edge = jnp.zeros((TSIDE, CH), jnp.bfloat16)
        hidden[f, 0:TSIDE] = edge
        hidden[f, TSIDE + pixels : 2 * TSIDE + pixels] = edge
        for s in range(shares):
            scale, bias = affine[s]
            value = first[f, :, s * wide : (s + 1) * wide] * scale + bias
            hidden[f, TSIDE : TSIDE + pixels, channels[s]] = silu_of_half(value).astype(
                jnp.bfloat16
            )

    def convolve(start, several, depth_taps):
        lhs = jnp.concatenate(
            [
                hidden[start : start + several, b * TSIDE : b * TSIDE + pixels].reshape(
                    several * pixels, CH
                )
                for b in range(3)
            ],
            axis=1,
        )
        low = depth_taps[0] * 3 * lanes
        product = jnp.dot(lhs, weights[:, low:], preferred_element_type=jnp.float32)
        for a in depth_taps:
            for e in range(3):
                at = (3 * a + e) * lanes - low
                for f in range(several):
                    target = start + f + 2 - a
                    value = product[f * pixels : (f + 1) * pixels, at : at + lanes]
                    if start + f == max(target - 2, 0):
                        partial[e, target] = value
                    else:
                        partial[e, target] += value

    column = lax.broadcasted_iota(jnp.int32, (pixels, lanes), 0) % TSIDE
    total = [jnp.zeros((8, lanes), jnp.float32)] * 2

    def gather(f):
        left = jnp.where(column == 0, 0.0, pltpu.roll(partial[0, f], 1, 0))
        right = jnp.where(column == TSIDE - 1, 0.0, pltpu.roll(partial[2, f], pixels - 1, 0))
        value = partial[1, f] + left + right
        partial[1, f] = value
        total[0] = total[0] + fold(value)
        total[1] = total[1] + fold(value * value)

    together = 3
    groups = [
        range(f, min(f + together, frames - 2)) for f in range(0, frames - 2, together)
    ]
    groups += [range(f, f + 1) for f in range(groups[-1].stop, frames)]
    for copy in copies:
        copy.wait()
    for f in groups[0]:
        hide(f)
    for number, group in enumerate(groups):
        if number + 1 < len(groups):
            for f in groups[number + 1]:
                hide(f)
        convolve(
            group.start,
            len(group),
            tuple(a for a in range(3) if group.stop - 1 + 2 - a < frames),
        )
        if number:
            for f in groups[number - 1]:
                gather(f)
    for f in groups[-1]:
        gather(f)

    part = pl.ds(pl.multiple_of(mine * lanes, LANES), lanes)
    scale, bias = group_affine(
        total[0],
        total[1],
        table_ref[gain_row : gain_row + 1, part],
        table_ref[gain_row + 1 : gain_row + 2, part],
        count,
    )
    blend = table_ref[pl.ds(blend_row + tile_id, 1), :]
    blend = jnp.where(
        (tile_row * STRIDE + up < tiles // GRID_X * STRIDE)
        & (tile_col * STRIDE + along < GRID_X * STRIDE),
        blend,
        0.0,
    )
    w_out = jnp.concatenate(
        [table_ref[w_out_row : w_out_row + 3, part], jnp.zeros((5, lanes), jnp.float32)], axis=0
    ).astype(jnp.bfloat16)
    colors = []
    for f in range(frames):
        upper = silu_of_half(partial[1, f] * scale + bias).astype(jnp.bfloat16)
        color = lax.dot_general(
            w_out, upper, (((1,), (1,)), ((), ())), preferred_element_type=jnp.float32
        )
        colors.append(color * blend)
    colors = jnp.concatenate(colors, axis=0)

    slot_in = lax.broadcasted_iota(jnp.int32, (pixels, own), 0)
    pixel = lax.broadcasted_iota(jnp.int32, (pixels, own), 1)
    denom = jnp.zeros((8, own), jnp.float32)
    for number, (down, across) in enumerate(cases):
        u, v = slot_in // TSIDE - down * STRIDE, slot_in % TSIDE - across * STRIDE
        good = (u >= 0) & (u < STRIDE) & (v >= 0) & (v < STRIDE) & (u * STRIDE + v == pixel)
        shown = jnp.where(good, 1.0, 0.0).astype(jnp.bfloat16)
        inside = (tile_row >= down) & (tile_col >= across)
        other = jnp.maximum(tile_id - down * GRID_X - across, 0)
        weight = jnp.where(inside, table_ref[pl.ds(blend_row + other, 1), :], 0.0)
        piece = exact_dot(
            jnp.concatenate([colors, jnp.broadcast_to(weight, (8, pixels))], axis=0), shown
        )
        denom = denom + piece[8 * frames :]
        shown_ref[...] = piece
        for swap in range(spans):
            target = keep_ref if swap == 0 else send_ref.at[swap - 1]
            base = (mine + swap) % spans * own_frames * 8
            for at in range(own_frames):
                for o in range(3):
                    target[number, o, at : at + 1, :] = shown_ref[pl.ds(base + 8 * at + o, 1), :]

    denom_ref[...] = denom


def from_ring(value, axis):
    count = lax.axis_size(axis)
    return [
        lax.ppermute(value, axis, [((d + turn) % count, d) for d in range(count)])
        for turn in range(1, count)
    ]


def small_table(*values):
    values = [value.reshape(-1, value.shape[-1]) for value in values]
    wide = max(value.shape[1] for value in values)
    height = sum(value.shape[0] for value in values)
    total, row = 0.0, 0
    for value in values:
        below = height - row - value.shape[0]
        value = jnp.pad(value.astype(jnp.float32), ((row, below), (0, wide - value.shape[1])))
        total = total + value
        row = height - below
    return total


def exchange_latents(frames, latent, own, table):
    tiles, shares = lax.axis_size("tile"), lax.axis_size("chan")
    tail = own - LANES
    height = frames * latent
    mine = table[:height, :own].astype(jnp.bfloat16)
    tails = sum(
        jnp.pad(
            mine[f * latent : (f + 1) * latent, LANES:],
            ((0, 0), (tail * f, LANES - tail * (f + 1))),
        )
        for f in range(frames)
    )
    affine = table[height : height + 2]
    high = lax.reduce_precision(affine, 8, 7)
    low = lax.reduce_precision(affine - high, 8, 7)
    affine = jnp.concatenate([high, low], axis=0).astype(jnp.bfloat16)
    rows = [affine[:, at : at + LANES] for at in range(0, affine.shape[1], LANES)]
    rows = jnp.concatenate(rows, axis=0)
    rows = jnp.pad(rows, ((0, -rows.shape[0] % 16), (0, 0)))
    message = jnp.concatenate([mine[:, :LANES], tails, rows], axis=0)
    got = [message]
    for steps in range(1, tiles):
        turn = steps if steps < shares else 0
        pairs = [
            (t * shares + (c + turn) % shares, (t + steps) % tiles * shares + c)
            for t in range(tiles)
            for c in range(shares)
        ]
        got.append(lax.ppermute(message, ("tile", "chan"), pairs))
    stack = jnp.concatenate(got, axis=0)
    return [stack] + from_ring(stack, "tm")


def lanes_body(
    latents, tile_order, w_in, gain_in, shift_in, w_mid, gain_mid, shift_mid, w_out, blend_weight
):
    own_frames, latent, own = latents.shape
    spans = lax.axis_size("tm")
    shares = lax.axis_size("chan")
    frames = own_frames * spans
    tiles = tile_order.shape[0]
    wide = w_in.shape[2]
    lanes = wide // spans
    pixels = TSIDE * TSIDE
    cases = block_cases(tiles)

    w_in_all = from_ring(w_in, "chan")
    table = lax.optimization_barrier(
        small_table(
            latents.reshape(own_frames * latent, own),
            gain_in,
            shift_in,
            gain_mid,
            shift_mid,
            w_out,
            blend_weight,
        )
    )
    latents_all = exchange_latents(own_frames, latent, own, table)
    _, w_in, tile_order = lax.optimization_barrier((table, w_in, tile_order))
    order = jnp.broadcast_to(tile_order.astype(jnp.float32)[:, None], (tiles, LANES))
    w_in_own = from_ring(w_in, "tm")[:1] or [w_in]

    vmem = pl.BlockSpec(memory_space=pltpu.VMEM)
    piece = (len(cases), 3, own_frames, own)
    kept, sent, denom = pl.pallas_call(
        functools.partial(decode_kernel, tiles, spans, shares),
        out_shape=[
            jax.ShapeDtypeStruct(piece, jnp.float32),
            jax.ShapeDtypeStruct((max(spans - 1, 1),) + piece, jnp.float32),
            jax.ShapeDtypeStruct((8, own), jnp.float32),
        ],
        in_specs=[pl.BlockSpec(memory_space=pl.ANY)] + [vmem] * (2 + spans + shares),
        out_specs=[vmem] * 3,
        scratch_shapes=[
            pltpu.VMEM(((frames + spans) * latent, len(cases) * LANES), jnp.bfloat16),
            pltpu.VMEM((frames + 2, 9, latent, pixels), jnp.bfloat16),
            pltpu.VMEM((frames, pixels, CH), jnp.float32),
            pltpu.VMEM((frames, pixels + 2 * TSIDE, CH), jnp.bfloat16),
            pltpu.VMEM((3 * CH, 9 * lanes), jnp.bfloat16),
            pltpu.VMEM((3, frames, pixels, lanes), jnp.float32),
            pltpu.VMEM((8 * (frames + 1), own), jnp.float32),
            pltpu.SemaphoreType.DMA((27,)),
        ],
        compiler_params=pltpu.CompilerParams(vmem_limit_bytes=VMEM_BYTES),
        cost_estimate=pl.CostEstimate(
            flops=2 * frames * pixels * 27 * CH * lanes, bytes_accessed=8_000_000, transcendentals=0
        ),
    )(w_mid, table, order, *latents_all, *w_in_own, *w_in_all)
    total = kept
    for turn in range(shares):
        for swap in range(spans):
            if turn or swap:
                pairs = [
                    (c * spans + m, (c + turn) % shares * spans + (m + swap) % spans)
                    for c in range(shares)
                    for m in range(spans)
                ]
                piece = sent[swap - 1] if swap else kept
                total = total + lax.ppermute(piece, ("chan", "tm"), pairs)
    numer = total[0]
    for number, (down, across) in enumerate(cases):
        steps = down * GRID_X + across
        if steps and steps < tiles:
            numer = numer + shifted(total[number], "tile", steps)
    return jnp.transpose(numer / denom[0][None, None, :], (1, 0, 2))


def solution(mesh):
    placed = (
        P("tm", "groups", "tile"),
        P("groups"),
        P(None, None, "chan"),
        P("chan"),
        P("chan"),
        P(None, None, "chan"),
        P("chan"),
        P("chan"),
        P(None, "chan"),
        P("groups", None),
    )
    whole_lanes = (
        CH % (mesh.shape["chan"] * mesh.shape["tm"] * LANES) == 0
        and mesh.shape["chan"] <= mesh.shape["tile"]
    )
    return jax.shard_map(
        lanes_body if whole_lanes else general_body,
        mesh=mesh,
        in_specs=placed,
        out_specs=P("tm", "groups", "tile"),
        check_vma=False,
    )
```

```python
import functools

import jax
import jax.numpy as jnp
from jax import lax
from jax.experimental import pallas as pl
from jax.experimental.pallas import tpu as pltpu
from jax.sharding import PartitionSpec as P

CH = 512
GROUPS = 32
TSIDE = 16
STRIDE = 12
GRID_X = 4

EPSILON = 1e-06
LANES = 128
VMEM_BYTES = 48 * 1024 * 1024


def shifted(value, axis, steps):
    count = lax.axis_size(axis)
    leading, last = (max(0, -steps), min(count, count - steps))
    return lax.ppermute(value, axis, [(source, source + steps) for source in range(leading, last)])


def window_index(tile_id, tiles):
    slots = jnp.arange(TSIDE * TSIDE, dtype=jnp.int32)
    row = tile_id // GRID_X * STRIDE + slots // TSIDE
    col = tile_id % GRID_X * STRIDE + slots % TSIDE
    valid = (row < tiles // GRID_X * STRIDE) & (col < GRID_X * STRIDE)
    block = row // STRIDE * GRID_X + col // STRIDE
    index = block * (STRIDE * STRIDE) + row % STRIDE * STRIDE + col % STRIDE
    return (jnp.where(valid, index, 0), valid)


def causal_conv(extended, weights, frames, side):
    pixels = side * side
    rows = jnp.arange(pixels, dtype=jnp.int32) // side
    cols = jnp.arange(pixels, dtype=jnp.int32) % side
    total = jnp.zeros((frames, weights.shape[2], pixels), jnp.float32)
    for depth in range(3):
        window = extended[depth : depth + frames]
        for down in range(3):
            for across in range(3):
                offset = (down - 1) * side + (across - 1)
                inside = (
                    (rows + down - 1 >= 0)
                    & (rows + down - 1 < side)
                    & (cols + across - 1 >= 0)
                    & (cols + across - 1 < side)
                )
                moved = jnp.roll(window, -offset, axis=2)
                moved = jnp.where(inside[None, None, :], moved, jnp.zeros_like(moved))
                total = total + jnp.einsum(
                    "fcp,co->fop",
                    moved,
                    weights[9 * depth + 3 * down + across],
                    preferred_element_type=jnp.float32,
                )
    return total


def with_history(values):
    frames = values.shape[0]
    earlier = shifted(values[frames - 2 :], "tm", 1)
    return jnp.concatenate([earlier, values], axis=0)


def normalize(values, gain, shift, total_frames):
    frames, chans, pixels = values.shape
    width = CH // GROUPS
    grouped = values.reshape(frames, chans // width, width, pixels)
    sums = jnp.sum(grouped, axis=(0, 2, 3))
    squares = jnp.sum(grouped * grouped, axis=(0, 2, 3))
    sums, squares = lax.psum((sums, squares), "tm")
    count = total_frames * width * pixels
    mean = sums / count
    variance = squares / count - mean * mean
    scale = lax.rsqrt(variance + EPSILON)
    normed = (grouped - mean[None, :, None, None]) * scale[None, :, None, None]
    normed = normed.reshape(frames, chans, pixels) * gain[None, :, None] + shift[None, :, None]
    return jax.nn.silu(normed).astype(jnp.bfloat16)


def spread(color, weight, index, total_pixels):
    numer = (
        jnp.zeros((color.shape[0], 3, total_pixels), jnp.float32)
        .at[:, :, index]
        .add(color * weight[None, None, :])
    )
    denom = jnp.zeros((total_pixels,), jnp.float32).at[index].add(weight)
    return (numer, denom)


def route_owned(numer, denom, tile_id, own):
    frames = numer.shape[0]
    margin = (GRID_X + 1) * own
    numer_wide = jnp.concatenate([numer, jnp.zeros((frames, 3, margin), jnp.float32)], axis=2)
    denom_wide = jnp.concatenate([denom, jnp.zeros((margin,), jnp.float32)], axis=0)
    first_pixel = tile_id * own

    def block_at(offset):
        start_pixel = first_pixel + offset * own
        return (
            lax.dynamic_slice_in_dim(numer_wide, start_pixel, own, 2),
            lax.dynamic_slice_in_dim(denom_wide, start_pixel, own, 0),
        )

    owned_numer, owned_denom = block_at(0)
    for offset in (1, GRID_X, GRID_X + 1):
        piece_numer, piece_denom = block_at(offset)
        got_numer, got_denom = shifted((piece_numer, piece_denom), "tile", offset)
        owned_numer = owned_numer + got_numer
        owned_denom = owned_denom + got_denom
    return (owned_numer, owned_denom)


def general_body(
    latents, tile_order, w_in, gain_in, shift_in, w_mid, gain_mid, shift_mid, w_out, blend_weight
):
    frames = latents.shape[0]
    total_frames = frames * lax.axis_size("tm")
    tiles = tile_order.shape[0]
    own = STRIDE * STRIDE
    total_pixels = tiles * own
    tile_id = lax.axis_index("tile")
    index, valid = window_index(tile_id, tiles)
    whole = lax.all_gather(latents, "tile", axis=2, tiled=True)
    blocks = whole.reshape(frames, whole.shape[1], tiles, own)
    image = (
        jnp.zeros_like(blocks)
        .at[:, :, tile_order]
        .set(blocks)
        .reshape(frames, whole.shape[1], total_pixels)
    )
    window = jnp.where(
        valid[None, None, :], jnp.take(image, index, axis=2), jnp.zeros((), jnp.bfloat16)
    )
    first = causal_conv(with_history(window), w_in, frames, TSIDE)
    hidden = normalize(first, gain_in, shift_in, total_frames)
    second = causal_conv(
        lax.all_gather(with_history(hidden), "chan", axis=1, tiled=True), w_mid, frames, TSIDE
    )
    upper = normalize(second, gain_mid, shift_mid, total_frames)
    color = jnp.einsum("oc,fcp->fop", w_out, upper, preferred_element_type=jnp.float32)
    weight = jnp.where(valid, blend_weight[tile_id], jnp.float32(0.0))
    numer, denom = spread(color, weight, index, total_pixels)
    numer, denom = route_owned(numer, denom, tile_id, own)
    numer = lax.psum(numer, "chan")
    return numer / denom[None, None, :]


def block_cases(tiles):
    downs = (0, 1) if tiles // GRID_X > 1 else (0,)
    return [(down, across) for down in downs for across in (0, 1)]


def exact_dot(values, ones):
    rows = values.shape[0]
    high = values.astype(jnp.bfloat16)
    rest = values - high.astype(jnp.float32)
    middle = rest.astype(jnp.bfloat16)
    low = (rest - middle.astype(jnp.float32)).astype(jnp.bfloat16)
    total = jnp.dot(
        jnp.concatenate([high, middle, low], axis=0), ones, preferred_element_type=jnp.float32
    )
    return total[:rows] + total[rows : 2 * rows] + total[2 * rows :]


def group_affine(sums, squares, gain, shift, count):
    lanes = sums.shape[1]
    width = CH // GROUPS
    same = lax.broadcasted_iota(jnp.int32, (lanes, lanes), 0) // width == (
        lax.broadcasted_iota(jnp.int32, (lanes, lanes), 1) // width
    )
    total = exact_dot(
        jnp.concatenate([sums, squares], axis=0), jnp.where(same, 1.0, 0.0).astype(jnp.bfloat16)
    )
    mean = jnp.sum(total[:8], axis=0, keepdims=True) / count
    variance = jnp.sum(total[8:], axis=0, keepdims=True) / count - mean * mean
    scale = gain * lax.rsqrt(variance + EPSILON)
    return 0.5 * scale, 0.5 * (shift - mean * scale)


def silu_of_half(half):
    return half + half * jnp.tanh(half)


def fold(values):
    rows, lanes = values.shape
    return jnp.sum(values.reshape(rows // 8, 8, lanes), axis=0)


def decode_kernel(
    tiles,
    spans,
    shares,
    *refs,
):
    cases = block_cases(tiles)
    refs = list(refs)

    def take(number):
        taken = refs[:number]
        del refs[:number]
        return taken

    w_mid_ref, table_ref, order_ref = take(3)
    latent_refs, w_in_refs = take(spans), take(shares)
    keep_ref, send_ref, denom_ref = take(3)
    chosen, taps, first, hidden, weights, partial, shown_ref, sems = take(8)

    own = denom_ref.shape[1]
    own_frames = keep_ref.shape[2]
    frames = own_frames * spans
    latent, wide = w_in_refs[0].shape[1:]
    rows_in = frames * latent
    rows_own = rows_in // spans
    depth_in = 27 * latent
    pixels = TSIDE * TSIDE
    lanes = partial.shape[3]
    tile_id = lax.axis_index("tile")
    mine = lax.axis_index("tm")
    chan_id = lax.axis_index("chan")

    copies = []
    for a in range(3):
        for b in range(3):
            for e in range(3):
                tap = 9 * a + 3 * b + e
                copy = pltpu.make_async_copy(
                    w_mid_ref.at[tap, :, pl.ds(pl.multiple_of(mine * lanes, LANES), lanes)],
                    weights.at[pl.ds(b * CH, CH), pl.ds((3 * a + e) * lanes, lanes)],
                    sems.at[tap],
                )
                copy.start()
                copies.append(copy)

    tile_row, tile_col = tile_id // GRID_X, tile_id % GRID_X
    gain_row = rows_own + 2
    w_out_row = gain_row + 2
    blend_row = w_out_row + 3
    order = order_ref[...]
    number_of = lax.broadcasted_iota(jnp.int32, order.shape, 0)
    lane_of = lax.broadcasted_iota(jnp.int32, order.shape, 1)
    rows_all = latent_refs[0].shape[0] // tiles
    for number, (down, across) in enumerate(cases):
        inside = (tile_row + down < tiles // GRID_X) & (tile_col + across < GRID_X)
        wanted = tile_id + down * GRID_X + across
        found = (order == wanted.astype(jnp.float32)) & (lane_of == 0)
        place = jnp.sum(jnp.where(found, number_of.astype(jnp.float32), 0.0))
        turn = (tile_id - place.astype(jnp.int32) + tiles) % tiles
        part = slice(number * LANES, (number + 1) * LANES)
        for steps in range(tiles):

            @pl.when(inside & (turn == steps))
            def _():
                for swap in range(spans):
                    at, tail_at = swap * rows_own, rows_in + swap * latent
                    block = latent_refs[swap][steps * rows_all : (steps + 1) * rows_all]
                    chosen[at : at + rows_own, part] = block[:rows_own]
                    chosen[tail_at : tail_at + latent, part] = block[rows_own : rows_own + latent]

        @pl.when(jnp.logical_not(inside))
        def _():
            chosen[:, part] = jnp.zeros((chosen.shape[0], LANES), chosen.dtype)

    slot = lax.broadcasted_iota(jnp.int32, (1, pixels), 1)
    up, along = slot // TSIDE, slot % TSIDE
    source = lax.broadcasted_iota(jnp.int32, (LANES, pixels), 0)
    tail = own - LANES

    def pick(first_pixel):
        parts = []
        for down, across in cases:
            u, v = up - down * STRIDE, along - across * STRIDE
            good = (u >= 0) & (u < STRIDE) & (v >= 0) & (v < STRIDE)
            wanted = jnp.where(good, u * STRIDE + v - first_pixel, -1)
            parts.append(jnp.where(source == wanted, 1.0, 0.0).astype(jnp.bfloat16))
        return jnp.concatenate(parts, axis=0)

    tails = chosen[rows_in:].astype(jnp.float32)
    width = tails.shape[1]
    turned = [pltpu.roll(tails, (-f * tail) % width, 1) if f else tails for f in range(own_frames)]
    tails = jnp.concatenate(
        [
            turned[f][swap * latent : (swap + 1) * latent]
            for swap in range(spans)
            for f in range(own_frames)
        ],
        axis=0,
    ).astype(jnp.bfloat16)
    in_tail = lax.broadcasted_iota(jnp.int32, tails.shape, 1) % LANES < tail
    tails = jnp.where(in_tail, tails.astype(jnp.float32), 0.0).astype(jnp.bfloat16)
    window = jnp.dot(
        chosen[:rows_in], pick(0), preferred_element_type=jnp.float32
    ) + jnp.dot(tails, pick(LANES), preferred_element_type=jnp.float32)
    taps[0:2] = jnp.zeros((2,) + taps.shape[1:], taps.dtype)
    for b in range(3):
        for e in range(3):
            inside = (
                (up + b - 1 >= 0)
                & (up + b - 1 < TSIDE)
                & (along + e - 1 >= 0)
                & (along + e - 1 < TSIDE)
            )
            offset = (b - 1) * TSIDE + e - 1
            moved = pltpu.roll(window, (-offset) % pixels, 1) if offset else window
            moved = jnp.where(inside, moved, 0.0).astype(jnp.bfloat16)
            for swap in range(spans):
                value = moved[swap * rows_own : (swap + 1) * rows_own]
                span = pl.ds(2 + (mine + swap) % spans * own_frames, own_frames)
                taps[span, 3 * b + e] = value.reshape(own_frames, latent, pixels)

    joined = jnp.concatenate(
        [w_in_refs[s][:27].reshape(depth_in, wide) for s in range(shares)], axis=1
    )
    sums = jnp.zeros((8, CH), jnp.float32)
    squares = jnp.zeros((8, CH), jnp.float32)
    for f in range(frames):
        patch = taps[f : f + 3].reshape(depth_in, pixels)
        value = lax.dot_general(
            patch, joined, (((0,), (0,)), ((), ())), preferred_element_type=jnp.float32
        )
        first[f] = value
        sums = sums + fold(value)
        squares = squares + fold(value * value)
    count = frames * (CH // GROUPS) * pixels
    affine = []
    for s in range(shares):
        at = s * rows_all + rows_own + latent
        table = latent_refs[0][at : at + wide // LANES * 4].astype(jnp.float32)
        pieces = [table[4 * lane : 4 * lane + 4] for lane in range(wide // LANES)]
        table = jnp.concatenate([part[0:2] + part[2:4] for part in pieces], axis=1)
        part = slice(s * wide, (s + 1) * wide)
        affine.append(
            group_affine(sums[:, part], squares[:, part], table[0:1], table[1:2], count)
        )
    channels = [
        pl.ds(pl.multiple_of((chan_id + s) % shares * wide, LANES), wide) for s in range(shares)
    ]

    def hide(f):
        edge = jnp.zeros((TSIDE, CH), jnp.bfloat16)
        hidden[f, 0:TSIDE] = edge
        hidden[f, TSIDE + pixels : 2 * TSIDE + pixels] = edge
        for s in range(shares):
            scale, bias = affine[s]
            value = first[f, :, s * wide : (s + 1) * wide] * scale + bias
            hidden[f, TSIDE : TSIDE + pixels, channels[s]] = silu_of_half(value).astype(
                jnp.bfloat16
            )

    def convolve(start, several, depth_taps):
        lhs = jnp.concatenate(
            [
                hidden[start : start + several, b * TSIDE : b * TSIDE + pixels].reshape(
                    several * pixels, CH
                )
                for b in range(3)
            ],
            axis=1,
        )
        low = depth_taps[0] * 3 * lanes
        product = jnp.dot(lhs, weights[:, low:], preferred_element_type=jnp.float32)
        for a in depth_taps:
            for e in range(3):
                at = (3 * a + e) * lanes - low
                for f in range(several):
                    target = start + f + 2 - a
                    value = product[f * pixels : (f + 1) * pixels, at : at + lanes]
                    if start + f == max(target - 2, 0):
                        partial[e, target] = value
                    else:
                        partial[e, target] += value

    column = lax.broadcasted_iota(jnp.int32, (pixels, lanes), 0) % TSIDE
    total = [jnp.zeros((8, lanes), jnp.float32)] * 2

    def gather(f):
        left = jnp.where(column == 0, 0.0, pltpu.roll(partial[0, f], 1, 0))
        right = jnp.where(column == TSIDE - 1, 0.0, pltpu.roll(partial[2, f], pixels - 1, 0))
        value = partial[1, f] + left + right
        partial[1, f] = value
        total[0] = total[0] + fold(value)
        total[1] = total[1] + fold(value * value)

    together = 3
    groups = [
        range(f, min(f + together, frames - 2)) for f in range(0, frames - 2, together)
    ]
    groups += [range(f, f + 1) for f in range(groups[-1].stop, frames)]
    for copy in copies:
        copy.wait()
    for f in groups[0]:
        hide(f)
    for number, group in enumerate(groups):
        if number + 1 < len(groups):
            for f in groups[number + 1]:
                hide(f)
        convolve(
            group.start,
            len(group),
            tuple(a for a in range(3) if group.stop - 1 + 2 - a < frames),
        )
        if number:
            for f in groups[number - 1]:
                gather(f)
    for f in groups[-1]:
        gather(f)

    part = pl.ds(pl.multiple_of(mine * lanes, LANES), lanes)
    scale, bias = group_affine(
        total[0],
        total[1],
        table_ref[gain_row : gain_row + 1, part],
        table_ref[gain_row + 1 : gain_row + 2, part],
        count,
    )
    blend = table_ref[pl.ds(blend_row + tile_id, 1), :]
    blend = jnp.where(
        (tile_row * STRIDE + up < tiles // GRID_X * STRIDE)
        & (tile_col * STRIDE + along < GRID_X * STRIDE),
        blend,
        0.0,
    )
    w_out = jnp.concatenate(
        [table_ref[w_out_row : w_out_row + 3, part], jnp.zeros((5, lanes), jnp.float32)], axis=0
    ).astype(jnp.bfloat16)
    colors = []
    for f in range(frames):
        upper = silu_of_half(partial[1, f] * scale + bias).astype(jnp.bfloat16)
        color = lax.dot_general(
            w_out, upper, (((1,), (1,)), ((), ())), preferred_element_type=jnp.float32
        )
        colors.append(color * blend)
    colors = jnp.concatenate(colors, axis=0)

    slot_in = lax.broadcasted_iota(jnp.int32, (pixels, own), 0)
    pixel = lax.broadcasted_iota(jnp.int32, (pixels, own), 1)
    denom = jnp.zeros((8, own), jnp.float32)
    for number, (down, across) in enumerate(cases):
        u, v = slot_in // TSIDE - down * STRIDE, slot_in % TSIDE - across * STRIDE
        good = (u >= 0) & (u < STRIDE) & (v >= 0) & (v < STRIDE) & (u * STRIDE + v == pixel)
        shown = jnp.where(good, 1.0, 0.0).astype(jnp.bfloat16)
        inside = (tile_row >= down) & (tile_col >= across)
        other = jnp.maximum(tile_id - down * GRID_X - across, 0)
        weight = jnp.where(inside, table_ref[pl.ds(blend_row + other, 1), :], 0.0)
        piece = exact_dot(
            jnp.concatenate([colors, jnp.broadcast_to(weight, (8, pixels))], axis=0), shown
        )
        denom = denom + piece[8 * frames :]
        shown_ref[...] = piece
        for swap in range(spans):
            target = keep_ref if swap == 0 else send_ref.at[swap - 1]
            base = (mine + swap) % spans * own_frames * 8
            for at in range(own_frames):
                for o in range(3):
                    target[number, o, at : at + 1, :] = shown_ref[pl.ds(base + 8 * at + o, 1), :]

    denom_ref[...] = denom


def from_ring(value, axis):
    count = lax.axis_size(axis)
    return [
        lax.ppermute(value, axis, [((d + turn) % count, d) for d in range(count)])
        for turn in range(1, count)
    ]


def small_table(*values):
    values = [value.reshape(-1, value.shape[-1]) for value in values]
    wide = max(value.shape[1] for value in values)
    height = sum(value.shape[0] for value in values)
    total, row = 0.0, 0
    for value in values:
        below = height - row - value.shape[0]
        value = jnp.pad(value.astype(jnp.float32), ((row, below), (0, wide - value.shape[1])))
        total = total + value
        row = height - below
    return total


def exchange_latents(frames, latent, own, table):
    tiles, shares = lax.axis_size("tile"), lax.axis_size("chan")
    tail = own - LANES
    height = frames * latent
    mine = table[:height, :own].astype(jnp.bfloat16)
    tails = sum(
        jnp.pad(
            mine[f * latent : (f + 1) * latent, LANES:],
            ((0, 0), (tail * f, LANES - tail * (f + 1))),
        )
        for f in range(frames)
    )
    affine = table[height : height + 2]
    high = lax.reduce_precision(affine, 8, 7)
    low = lax.reduce_precision(affine - high, 8, 7)
    affine = jnp.concatenate([high, low], axis=0).astype(jnp.bfloat16)
    rows = [affine[:, at : at + LANES] for at in range(0, affine.shape[1], LANES)]
    rows = jnp.concatenate(rows, axis=0)
    rows = jnp.pad(rows, ((0, -rows.shape[0] % 16), (0, 0)))
    message = jnp.concatenate([mine[:, :LANES], tails, rows], axis=0)
    got = [message]
    for steps in range(1, tiles):
        turn = steps if steps < shares else 0
        pairs = [
            (t * shares + (c + turn) % shares, (t + steps) % tiles * shares + c)
            for t in range(tiles)
            for c in range(shares)
        ]
        got.append(lax.ppermute(message, ("tile", "chan"), pairs))
    stack = jnp.concatenate(got, axis=0)
    return [stack] + from_ring(stack, "tm")


def lanes_body(
    latents, tile_order, w_in, gain_in, shift_in, w_mid, gain_mid, shift_mid, w_out, blend_weight
):
    own_frames, latent, own = latents.shape
    spans = lax.axis_size("tm")
    shares = lax.axis_size("chan")
    frames = own_frames * spans
    tiles = tile_order.shape[0]
    wide = w_in.shape[2]
    lanes = wide // spans
    pixels = TSIDE * TSIDE
    cases = block_cases(tiles)

    w_in_all = [(from_ring(other, "tm") or [other])[0] for other in from_ring(w_in, "chan")]
    table = lax.optimization_barrier(
        small_table(
            latents.reshape(own_frames * latent, own),
            gain_in,
            shift_in,
            gain_mid,
            shift_mid,
            w_out,
            blend_weight,
        )
    )
    latents_all = exchange_latents(own_frames, latent, own, table)
    _, w_in, tile_order = lax.optimization_barrier((table, w_in, tile_order))
    order = jnp.broadcast_to(tile_order.astype(jnp.float32)[:, None], (tiles, LANES))
    w_in_own = from_ring(w_in, "tm")[:1] or [w_in]

    vmem = pl.BlockSpec(memory_space=pltpu.VMEM)
    piece = (len(cases), 3, own_frames, own)
    kept, sent, denom = pl.pallas_call(
        functools.partial(decode_kernel, tiles, spans, shares),
        out_shape=[
            jax.ShapeDtypeStruct(piece, jnp.float32),
            jax.ShapeDtypeStruct((max(spans - 1, 1),) + piece, jnp.float32),
            jax.ShapeDtypeStruct((8, own), jnp.float32),
        ],
        in_specs=[pl.BlockSpec(memory_space=pl.ANY)] + [vmem] * (2 + spans + shares),
        out_specs=[vmem] * 3,
        scratch_shapes=[
            pltpu.VMEM(((frames + spans) * latent, len(cases) * LANES), jnp.bfloat16),
            pltpu.VMEM((frames + 2, 9, latent, pixels), jnp.bfloat16),
            pltpu.VMEM((frames, pixels, CH), jnp.float32),
            pltpu.VMEM((frames, pixels + 2 * TSIDE, CH), jnp.bfloat16),
            pltpu.VMEM((3 * CH, 9 * lanes), jnp.bfloat16),
            pltpu.VMEM((3, frames, pixels, lanes), jnp.float32),
            pltpu.VMEM((8 * (frames + 1), own), jnp.float32),
            pltpu.SemaphoreType.DMA((27,)),
        ],
        compiler_params=pltpu.CompilerParams(vmem_limit_bytes=VMEM_BYTES),
        cost_estimate=pl.CostEstimate(
            flops=2 * frames * pixels * 27 * CH * lanes, bytes_accessed=8_000_000, transcendentals=0
        ),
    )(w_mid, table, order, *latents_all, *w_in_own, *w_in_all)
    total = kept
    for turn in range(shares):
        for swap in range(spans):
            if turn or swap:
                pairs = [
                    (c * spans + m, (c + turn) % shares * spans + (m + swap) % spans)
                    for c in range(shares)
                    for m in range(spans)
                ]
                piece = sent[swap - 1] if swap else kept
                total = total + lax.ppermute(piece, ("chan", "tm"), pairs)
    numer = total[0]
    for number, (down, across) in enumerate(cases):
        steps = down * GRID_X + across
        if steps and steps < tiles:
            numer = numer + shifted(total[number], "tile", steps)
    return jnp.transpose(numer / denom[0][None, None, :], (1, 0, 2))


def solution(mesh):
    placed = (
        P("tm", "groups", "tile"),
        P("groups"),
        P(None, None, "chan"),
        P("chan"),
        P("chan"),
        P(None, None, "chan"),
        P("chan"),
        P("chan"),
        P(None, "chan"),
        P("groups", None),
    )
    whole_lanes = (
        CH % (mesh.shape["chan"] * mesh.shape["tm"] * LANES) == 0
        and mesh.shape["chan"] <= mesh.shape["tile"]
    )
    return jax.shard_map(
        lanes_body if whole_lanes else general_body,
        mesh=mesh,
        in_specs=placed,
        out_specs=P("tm", "groups", "tile"),
        check_vma=False,
    )
```

```python
import functools

import jax
import jax.numpy as jnp
from jax import lax
from jax.experimental import pallas as pl
from jax.experimental.pallas import tpu as pltpu
from jax.sharding import PartitionSpec as P

CH = 512
GROUPS = 32
TSIDE = 16
STRIDE = 12
GRID_X = 4

EPSILON = 1e-06
LANES = 128
VMEM_BYTES = 48 * 1024 * 1024


def shifted(value, axis, steps):
    count = lax.axis_size(axis)
    leading, last = (max(0, -steps), min(count, count - steps))
    return lax.ppermute(value, axis, [(source, source + steps) for source in range(leading, last)])


def window_index(tile_id, tiles):
    slots = jnp.arange(TSIDE * TSIDE, dtype=jnp.int32)
    row = tile_id // GRID_X * STRIDE + slots // TSIDE
    col = tile_id % GRID_X * STRIDE + slots % TSIDE
    valid = (row < tiles // GRID_X * STRIDE) & (col < GRID_X * STRIDE)
    block = row // STRIDE * GRID_X + col // STRIDE
    index = block * (STRIDE * STRIDE) + row % STRIDE * STRIDE + col % STRIDE
    return (jnp.where(valid, index, 0), valid)


def causal_conv(extended, weights, frames, side):
    pixels = side * side
    rows = jnp.arange(pixels, dtype=jnp.int32) // side
    cols = jnp.arange(pixels, dtype=jnp.int32) % side
    total = jnp.zeros((frames, weights.shape[2], pixels), jnp.float32)
    for depth in range(3):
        window = extended[depth : depth + frames]
        for down in range(3):
            for across in range(3):
                offset = (down - 1) * side + (across - 1)
                inside = (
                    (rows + down - 1 >= 0)
                    & (rows + down - 1 < side)
                    & (cols + across - 1 >= 0)
                    & (cols + across - 1 < side)
                )
                moved = jnp.roll(window, -offset, axis=2)
                moved = jnp.where(inside[None, None, :], moved, jnp.zeros_like(moved))
                total = total + jnp.einsum(
                    "fcp,co->fop",
                    moved,
                    weights[9 * depth + 3 * down + across],
                    preferred_element_type=jnp.float32,
                )
    return total


def with_history(values):
    frames = values.shape[0]
    earlier = shifted(values[frames - 2 :], "tm", 1)
    return jnp.concatenate([earlier, values], axis=0)


def normalize(values, gain, shift, total_frames):
    frames, chans, pixels = values.shape
    width = CH // GROUPS
    grouped = values.reshape(frames, chans // width, width, pixels)
    sums = jnp.sum(grouped, axis=(0, 2, 3))
    squares = jnp.sum(grouped * grouped, axis=(0, 2, 3))
    sums, squares = lax.psum((sums, squares), "tm")
    count = total_frames * width * pixels
    mean = sums / count
    variance = squares / count - mean * mean
    scale = lax.rsqrt(variance + EPSILON)
    normed = (grouped - mean[None, :, None, None]) * scale[None, :, None, None]
    normed = normed.reshape(frames, chans, pixels) * gain[None, :, None] + shift[None, :, None]
    return jax.nn.silu(normed).astype(jnp.bfloat16)


def spread(color, weight, index, total_pixels):
    numer = (
        jnp.zeros((color.shape[0], 3, total_pixels), jnp.float32)
        .at[:, :, index]
        .add(color * weight[None, None, :])
    )
    denom = jnp.zeros((total_pixels,), jnp.float32).at[index].add(weight)
    return (numer, denom)


def route_owned(numer, denom, tile_id, own):
    frames = numer.shape[0]
    margin = (GRID_X + 1) * own
    numer_wide = jnp.concatenate([numer, jnp.zeros((frames, 3, margin), jnp.float32)], axis=2)
    denom_wide = jnp.concatenate([denom, jnp.zeros((margin,), jnp.float32)], axis=0)
    first_pixel = tile_id * own

    def block_at(offset):
        start_pixel = first_pixel + offset * own
        return (
            lax.dynamic_slice_in_dim(numer_wide, start_pixel, own, 2),
            lax.dynamic_slice_in_dim(denom_wide, start_pixel, own, 0),
        )

    owned_numer, owned_denom = block_at(0)
    for offset in (1, GRID_X, GRID_X + 1):
        piece_numer, piece_denom = block_at(offset)
        got_numer, got_denom = shifted((piece_numer, piece_denom), "tile", offset)
        owned_numer = owned_numer + got_numer
        owned_denom = owned_denom + got_denom
    return (owned_numer, owned_denom)


def general_body(
    latents, tile_order, w_in, gain_in, shift_in, w_mid, gain_mid, shift_mid, w_out, blend_weight
):
    frames = latents.shape[0]
    total_frames = frames * lax.axis_size("tm")
    tiles = tile_order.shape[0]
    own = STRIDE * STRIDE
    total_pixels = tiles * own
    tile_id = lax.axis_index("tile")
    index, valid = window_index(tile_id, tiles)
    whole = lax.all_gather(latents, "tile", axis=2, tiled=True)
    blocks = whole.reshape(frames, whole.shape[1], tiles, own)
    image = (
        jnp.zeros_like(blocks)
        .at[:, :, tile_order]
        .set(blocks)
        .reshape(frames, whole.shape[1], total_pixels)
    )
    window = jnp.where(
        valid[None, None, :], jnp.take(image, index, axis=2), jnp.zeros((), jnp.bfloat16)
    )
    first = causal_conv(with_history(window), w_in, frames, TSIDE)
    hidden = normalize(first, gain_in, shift_in, total_frames)
    second = causal_conv(
        lax.all_gather(with_history(hidden), "chan", axis=1, tiled=True), w_mid, frames, TSIDE
    )
    upper = normalize(second, gain_mid, shift_mid, total_frames)
    color = jnp.einsum("oc,fcp->fop", w_out, upper, preferred_element_type=jnp.float32)
    weight = jnp.where(valid, blend_weight[tile_id], jnp.float32(0.0))
    numer, denom = spread(color, weight, index, total_pixels)
    numer, denom = route_owned(numer, denom, tile_id, own)
    numer = lax.psum(numer, "chan")
    return numer / denom[None, None, :]


def block_cases(tiles):
    downs = (0, 1) if tiles // GRID_X > 1 else (0,)
    return [(down, across) for down in downs for across in (0, 1)]


def exact_dot(values, ones):
    rows = values.shape[0]
    high = values.astype(jnp.bfloat16)
    rest = values - high.astype(jnp.float32)
    middle = rest.astype(jnp.bfloat16)
    low = (rest - middle.astype(jnp.float32)).astype(jnp.bfloat16)
    total = jnp.dot(
        jnp.concatenate([high, middle, low], axis=0), ones, preferred_element_type=jnp.float32
    )
    return total[:rows] + total[rows : 2 * rows] + total[2 * rows :]


def group_affine(sums, squares, gain, shift, count):
    lanes = sums.shape[1]
    width = CH // GROUPS
    same = lax.broadcasted_iota(jnp.int32, (lanes, lanes), 0) // width == (
        lax.broadcasted_iota(jnp.int32, (lanes, lanes), 1) // width
    )
    total = exact_dot(
        jnp.concatenate([sums, squares], axis=0), jnp.where(same, 1.0, 0.0).astype(jnp.bfloat16)
    )
    mean = jnp.sum(total[:8], axis=0, keepdims=True) / count
    variance = jnp.sum(total[8:], axis=0, keepdims=True) / count - mean * mean
    scale = gain * lax.rsqrt(variance + EPSILON)
    return 0.5 * scale, 0.5 * (shift - mean * scale)


def silu_of_half(half):
    return half + half * jnp.tanh(half)


def fold(values):
    rows, lanes = values.shape
    return jnp.sum(values.reshape(rows // 8, 8, lanes), axis=0)


def decode_kernel(
    tiles,
    spans,
    shares,
    *refs,
):
    cases = block_cases(tiles)
    refs = list(refs)

    def take(number):
        taken = refs[:number]
        del refs[:number]
        return taken

    w_mid_ref, table_ref, order_ref = take(3)
    latent_refs, w_in_refs = take(spans), take(shares)
    keep_ref, send_ref, denom_ref = take(3)
    chosen, taps, first, hidden, weights, partial, shown_ref, sems = take(8)

    own = denom_ref.shape[1]
    own_frames = keep_ref.shape[2]
    frames = own_frames * spans
    latent, wide = w_in_refs[0].shape[1:]
    rows_in = frames * latent
    rows_own = rows_in // spans
    depth_in = 27 * latent
    pixels = TSIDE * TSIDE
    lanes = partial.shape[3]
    tile_id = lax.axis_index("tile")
    mine = lax.axis_index("tm")
    chan_id = lax.axis_index("chan")

    copies = []
    for a in range(3):
        for b in range(3):
            for e in range(3):
                tap = 9 * a + 3 * b + e
                copy = pltpu.make_async_copy(
                    w_mid_ref.at[tap, :, pl.ds(pl.multiple_of(mine * lanes, LANES), lanes)],
                    weights.at[pl.ds(b * CH, CH), pl.ds((3 * a + e) * lanes, lanes)],
                    sems.at[tap],
                )
                copy.start()
                copies.append(copy)

    tile_row, tile_col = tile_id // GRID_X, tile_id % GRID_X
    gain_row = rows_own + 2
    w_out_row = gain_row + 2
    blend_row = w_out_row + 3
    order = order_ref[...]
    number_of = lax.broadcasted_iota(jnp.int32, order.shape, 0)
    lane_of = lax.broadcasted_iota(jnp.int32, order.shape, 1)
    rows_all = latent_refs[0].shape[0] // tiles
    for number, (down, across) in enumerate(cases):
        inside = (tile_row + down < tiles // GRID_X) & (tile_col + across < GRID_X)
        wanted = tile_id + down * GRID_X + across
        found = (order == wanted.astype(jnp.float32)) & (lane_of == 0)
        place = jnp.sum(jnp.where(found, number_of.astype(jnp.float32), 0.0))
        turn = (tile_id - place.astype(jnp.int32) + tiles) % tiles
        part = slice(number * LANES, (number + 1) * LANES)
        for steps in range(tiles):

            @pl.when(inside & (turn == steps))
            def _():
                for swap in range(spans):
                    at, tail_at = swap * rows_own, rows_in + swap * latent
                    block = latent_refs[swap][steps * rows_all : (steps + 1) * rows_all]
                    chosen[at : at + rows_own, part] = block[:rows_own]
                    chosen[tail_at : tail_at + latent, part] = block[rows_own : rows_own + latent]

        @pl.when(jnp.logical_not(inside))
        def _():
            chosen[:, part] = jnp.zeros((chosen.shape[0], LANES), chosen.dtype)

    slot = lax.broadcasted_iota(jnp.int32, (1, pixels), 1)
    up, along = slot // TSIDE, slot % TSIDE
    source = lax.broadcasted_iota(jnp.int32, (LANES, pixels), 0)
    tail = own - LANES

    def pick(first_pixel):
        parts = []
        for down, across in cases:
            u, v = up - down * STRIDE, along - across * STRIDE
            good = (u >= 0) & (u < STRIDE) & (v >= 0) & (v < STRIDE)
            wanted = jnp.where(good, u * STRIDE + v - first_pixel, -1)
            parts.append(jnp.where(source == wanted, 1.0, 0.0).astype(jnp.bfloat16))
        return jnp.concatenate(parts, axis=0)

    tails = chosen[rows_in:].astype(jnp.float32)
    width = tails.shape[1]
    turned = [pltpu.roll(tails, (-f * tail) % width, 1) if f else tails for f in range(own_frames)]
    tails = jnp.concatenate(
        [
            turned[f][swap * latent : (swap + 1) * latent]
            for swap in range(spans)
            for f in range(own_frames)
        ],
        axis=0,
    ).astype(jnp.bfloat16)
    in_tail = lax.broadcasted_iota(jnp.int32, tails.shape, 1) % LANES < tail
    tails = jnp.where(in_tail, tails.astype(jnp.float32), 0.0).astype(jnp.bfloat16)
    window = jnp.dot(
        chosen[:rows_in], pick(0), preferred_element_type=jnp.float32
    ) + jnp.dot(tails, pick(LANES), preferred_element_type=jnp.float32)
    taps[0:2] = jnp.zeros((2,) + taps.shape[1:], taps.dtype)
    for b in range(3):
        for e in range(3):
            inside = (
                (up + b - 1 >= 0)
                & (up + b - 1 < TSIDE)
                & (along + e - 1 >= 0)
                & (along + e - 1 < TSIDE)
            )
            offset = (b - 1) * TSIDE + e - 1
            moved = pltpu.roll(window, (-offset) % pixels, 1) if offset else window
            moved = jnp.where(inside, moved, 0.0).astype(jnp.bfloat16)
            for swap in range(spans):
                value = moved[swap * rows_own : (swap + 1) * rows_own]
                span = pl.ds(2 + (mine + swap) % spans * own_frames, own_frames)
                taps[span, 3 * b + e] = value.reshape(own_frames, latent, pixels)

    joined = jnp.concatenate(
        [w_in_refs[s][:27].reshape(depth_in, wide) for s in range(shares)], axis=1
    )
    sums = jnp.zeros((8, CH), jnp.float32)
    squares = jnp.zeros((8, CH), jnp.float32)
    for f in range(frames):
        patch = taps[f : f + 3].reshape(depth_in, pixels)
        value = lax.dot_general(
            patch, joined, (((0,), (0,)), ((), ())), preferred_element_type=jnp.float32
        )
        first[f] = value
        sums = sums + fold(value)
        squares = squares + fold(value * value)
    count = frames * (CH // GROUPS) * pixels
    affine = []
    for s in range(shares):
        at = s * rows_all + rows_own + latent
        table = latent_refs[0][at : at + wide // LANES * 4].astype(jnp.float32)
        pieces = [table[4 * lane : 4 * lane + 4] for lane in range(wide // LANES)]
        table = jnp.concatenate([part[0:2] + part[2:4] for part in pieces], axis=1)
        part = slice(s * wide, (s + 1) * wide)
        affine.append(
            group_affine(sums[:, part], squares[:, part], table[0:1], table[1:2], count)
        )
    channels = [
        pl.ds(pl.multiple_of((chan_id + s) % shares * wide, LANES), wide) for s in range(shares)
    ]

    def hide(f):
        edge = jnp.zeros((TSIDE, CH), jnp.bfloat16)
        hidden[f, 0:TSIDE] = edge
        hidden[f, TSIDE + pixels : 2 * TSIDE + pixels] = edge
        for s in range(shares):
            scale, bias = affine[s]
            value = first[f, :, s * wide : (s + 1) * wide] * scale + bias
            hidden[f, TSIDE : TSIDE + pixels, channels[s]] = silu_of_half(value).astype(
                jnp.bfloat16
            )

    def convolve(start, several, depth_taps):
        lhs = jnp.concatenate(
            [
                hidden[start : start + several, b * TSIDE : b * TSIDE + pixels].reshape(
                    several * pixels, CH
                )
                for b in range(3)
            ],
            axis=1,
        )
        low = depth_taps[0] * 3 * lanes
        product = jnp.dot(lhs, weights[:, low:], preferred_element_type=jnp.float32)
        for a in depth_taps:
            for e in range(3):
                at = (3 * a + e) * lanes - low
                for f in range(several):
                    target = start + f + 2 - a
                    value = product[f * pixels : (f + 1) * pixels, at : at + lanes]
                    if start + f == max(target - 2, 0):
                        partial[e, target] = value
                    else:
                        partial[e, target] += value

    column = lax.broadcasted_iota(jnp.int32, (pixels, lanes), 0) % TSIDE
    total = [jnp.zeros((8, lanes), jnp.float32)] * 2

    def gather(f):
        left = jnp.where(column == 0, 0.0, pltpu.roll(partial[0, f], 1, 0))
        right = jnp.where(column == TSIDE - 1, 0.0, pltpu.roll(partial[2, f], pixels - 1, 0))
        value = partial[1, f] + left + right
        partial[1, f] = value
        total[0] = total[0] + fold(value)
        total[1] = total[1] + fold(value * value)

    together = 3
    groups = [
        range(f, min(f + together, frames - 2)) for f in range(0, frames - 2, together)
    ]
    groups += [range(f, f + 1) for f in range(groups[-1].stop, frames)]
    for copy in copies:
        copy.wait()
    for f in groups[0]:
        hide(f)
    for number, group in enumerate(groups):
        if number + 1 < len(groups):
            for f in groups[number + 1]:
                hide(f)
        convolve(
            group.start,
            len(group),
            tuple(a for a in range(3) if group.stop - 1 + 2 - a < frames),
        )
        if number:
            for f in groups[number - 1]:
                gather(f)
    for f in groups[-1]:
        gather(f)

    part = pl.ds(pl.multiple_of(mine * lanes, LANES), lanes)
    scale, bias = group_affine(
        total[0],
        total[1],
        table_ref[gain_row : gain_row + 1, part],
        table_ref[gain_row + 1 : gain_row + 2, part],
        count,
    )
    blend = table_ref[pl.ds(blend_row + tile_id, 1), :]
    blend = jnp.where(
        (tile_row * STRIDE + up < tiles // GRID_X * STRIDE)
        & (tile_col * STRIDE + along < GRID_X * STRIDE),
        blend,
        0.0,
    )
    w_out = jnp.concatenate(
        [table_ref[w_out_row : w_out_row + 3, part], jnp.zeros((5, lanes), jnp.float32)], axis=0
    ).astype(jnp.bfloat16)
    colors = []
    for f in range(frames):
        upper = silu_of_half(partial[1, f] * scale + bias).astype(jnp.bfloat16)
        color = lax.dot_general(
            w_out, upper, (((1,), (1,)), ((), ())), preferred_element_type=jnp.float32
        )
        colors.append(color * blend)
    colors = jnp.concatenate(colors, axis=0)

    slot_in = lax.broadcasted_iota(jnp.int32, (pixels, own), 0)
    pixel = lax.broadcasted_iota(jnp.int32, (pixels, own), 1)
    denom = jnp.zeros((8, own), jnp.float32)
    for number, (down, across) in enumerate(cases):
        u, v = slot_in // TSIDE - down * STRIDE, slot_in % TSIDE - across * STRIDE
        good = (u >= 0) & (u < STRIDE) & (v >= 0) & (v < STRIDE) & (u * STRIDE + v == pixel)
        shown = jnp.where(good, 1.0, 0.0).astype(jnp.bfloat16)
        inside = (tile_row >= down) & (tile_col >= across)
        other = jnp.maximum(tile_id - down * GRID_X - across, 0)
        weight = jnp.where(inside, table_ref[pl.ds(blend_row + other, 1), :], 0.0)
        piece = exact_dot(
            jnp.concatenate([colors, jnp.broadcast_to(weight, (8, pixels))], axis=0), shown
        )
        denom = denom + piece[8 * frames :]
        shown_ref[...] = piece
        for swap in range(spans):
            target = keep_ref if swap == 0 else send_ref.at[swap - 1]
            base = (mine + swap) % spans * own_frames * 8
            for at in range(own_frames):
                for o in range(3):
                    target[number, o, at : at + 1, :] = shown_ref[pl.ds(base + 8 * at + o, 1), :]

    denom_ref[...] = denom


def from_ring(value, axis):
    count = lax.axis_size(axis)
    return [
        lax.ppermute(value, axis, [((d + turn) % count, d) for d in range(count)])
        for turn in range(1, count)
    ]


def small_table(*values):
    values = [value.reshape(-1, value.shape[-1]) for value in values]
    wide = max(value.shape[1] for value in values)
    height = sum(value.shape[0] for value in values)
    total, row = 0.0, 0
    for value in values:
        below = height - row - value.shape[0]
        value = jnp.pad(value.astype(jnp.float32), ((row, below), (0, wide - value.shape[1])))
        total = total + value
        row = height - below
    return total


def exchange_latents(frames, latent, own, table):
    tiles, shares = lax.axis_size("tile"), lax.axis_size("chan")
    tail = own - LANES
    height = frames * latent
    mine = table[:height, :own].astype(jnp.bfloat16)
    tails = sum(
        jnp.pad(
            mine[f * latent : (f + 1) * latent, LANES:],
            ((0, 0), (tail * f, LANES - tail * (f + 1))),
        )
        for f in range(frames)
    )
    affine = table[height : height + 2]
    high = lax.reduce_precision(affine, 8, 7)
    low = lax.reduce_precision(affine - high, 8, 7)
    affine = jnp.concatenate([high, low], axis=0).astype(jnp.bfloat16)
    rows = [affine[:, at : at + LANES] for at in range(0, affine.shape[1], LANES)]
    rows = jnp.concatenate(rows, axis=0)
    rows = jnp.pad(rows, ((0, -rows.shape[0] % 16), (0, 0)))
    message = jnp.concatenate([mine[:, :LANES], tails, rows], axis=0)
    got = [message]
    for steps in range(1, tiles):
        turn = steps if steps < shares else 0
        pairs = [
            (t * shares + (c + turn) % shares, (t + steps) % tiles * shares + c)
            for t in range(tiles)
            for c in range(shares)
        ]
        got.append(lax.ppermute(message, ("tile", "chan"), pairs))
    stack = jnp.concatenate(got, axis=0)
    return [stack] + from_ring(stack, "tm")


def lanes_body(
    latents, tile_order, w_in, gain_in, shift_in, w_mid, gain_mid, shift_mid, w_out, blend_weight
):
    own_frames, latent, own = latents.shape
    spans = lax.axis_size("tm")
    shares = lax.axis_size("chan")
    frames = own_frames * spans
    tiles = tile_order.shape[0]
    wide = w_in.shape[2]
    lanes = wide // spans
    pixels = TSIDE * TSIDE
    cases = block_cases(tiles)

    w_in_all = [(from_ring(other, "tm") or [other])[0] for other in from_ring(w_in, "chan")]
    table = lax.optimization_barrier(
        small_table(
            latents.reshape(own_frames * latent, own),
            gain_in,
            shift_in,
            gain_mid,
            shift_mid,
            w_out,
            blend_weight,
        )
    )
    latents_all = exchange_latents(own_frames, latent, own, table)
    _, w_in, tile_order = lax.optimization_barrier((table, w_in, tile_order))
    order = jnp.broadcast_to(tile_order.astype(jnp.float32)[:, None], (tiles, LANES))
    w_in_own = from_ring(w_in, "tm")[:1] or [w_in]

    vmem = pl.BlockSpec(memory_space=pltpu.VMEM)
    piece = (len(cases), 3, own_frames, own)
    kept, sent, denom = pl.pallas_call(
        functools.partial(decode_kernel, tiles, spans, shares),
        out_shape=[
            jax.ShapeDtypeStruct(piece, jnp.float32),
            jax.ShapeDtypeStruct((max(spans - 1, 1),) + piece, jnp.float32),
            jax.ShapeDtypeStruct((8, own), jnp.float32),
        ],
        in_specs=[pl.BlockSpec(memory_space=pl.ANY)] + [vmem] * (2 + spans + shares),
        out_specs=[vmem] * 3,
        scratch_shapes=[
            pltpu.VMEM(((frames + spans) * latent, len(cases) * LANES), jnp.bfloat16),
            pltpu.VMEM((frames + 2, 9, latent, pixels), jnp.bfloat16),
            pltpu.VMEM((frames, pixels, CH), jnp.float32),
            pltpu.VMEM((frames, pixels + 2 * TSIDE, CH), jnp.bfloat16),
            pltpu.VMEM((3 * CH, 9 * lanes), jnp.bfloat16),
            pltpu.VMEM((3, frames, pixels, lanes), jnp.float32),
            pltpu.VMEM((8 * (frames + 1), own), jnp.float32),
            pltpu.SemaphoreType.DMA((27,)),
        ],
        compiler_params=pltpu.CompilerParams(vmem_limit_bytes=VMEM_BYTES),
        cost_estimate=pl.CostEstimate(
            flops=2 * frames * pixels * 27 * CH * lanes, bytes_accessed=8_000_000, transcendentals=0
        ),
    )(w_mid, table, order, *latents_all, *w_in_own, *w_in_all)
    total = kept
    for turn in range(shares):
        for swap in range(spans):
            if turn or swap:
                pairs = [
                    (c * spans + m, (c + turn) % shares * spans + (m + swap) % spans)
                    for c in range(shares)
                    for m in range(spans)
                ]
                piece = sent[swap - 1] if swap else kept
                total = total + lax.ppermute(piece, ("chan", "tm"), pairs)
    numer = total[0]
    for number, (down, across) in enumerate(cases):
        steps = down * GRID_X + across
        for parity in range(2):
            pairs = [(t, t + steps) for t in range(tiles - steps) if t // max(steps, 1) % 2 == parity]
            if steps and pairs:
                numer = numer + lax.ppermute(total[number], "tile", pairs)
    return jnp.transpose(numer / denom[0][None, None, :], (1, 0, 2))


def solution(mesh):
    placed = (
        P("tm", "groups", "tile"),
        P("groups"),
        P(None, None, "chan"),
        P("chan"),
        P("chan"),
        P(None, None, "chan"),
        P("chan"),
        P("chan"),
        P(None, "chan"),
        P("groups", None),
    )
    whole_lanes = (
        CH % (mesh.shape["chan"] * mesh.shape["tm"] * LANES) == 0
        and mesh.shape["chan"] <= mesh.shape["tile"]
    )
    return jax.shard_map(
        lanes_body if whole_lanes else general_body,
        mesh=mesh,
        in_specs=placed,
        out_specs=P("tm", "groups", "tile"),
        check_vma=False,
    )
```

```python
import functools

import jax
import jax.numpy as jnp
from jax import lax
from jax.experimental import pallas as pl
from jax.experimental.pallas import tpu as pltpu
from jax.sharding import PartitionSpec as P

CH = 512
GROUPS = 32
TSIDE = 16
STRIDE = 12
GRID_X = 4

EPSILON = 1e-06
LANES = 128
VMEM_BYTES = 48 * 1024 * 1024


def shifted(value, axis, steps):
    count = lax.axis_size(axis)
    leading, last = (max(0, -steps), min(count, count - steps))
    return lax.ppermute(value, axis, [(source, source + steps) for source in range(leading, last)])


def window_index(tile_id, tiles):
    slots = jnp.arange(TSIDE * TSIDE, dtype=jnp.int32)
    row = tile_id // GRID_X * STRIDE + slots // TSIDE
    col = tile_id % GRID_X * STRIDE + slots % TSIDE
    valid = (row < tiles // GRID_X * STRIDE) & (col < GRID_X * STRIDE)
    block = row // STRIDE * GRID_X + col // STRIDE
    index = block * (STRIDE * STRIDE) + row % STRIDE * STRIDE + col % STRIDE
    return (jnp.where(valid, index, 0), valid)


def causal_conv(extended, weights, frames, side):
    pixels = side * side
    rows = jnp.arange(pixels, dtype=jnp.int32) // side
    cols = jnp.arange(pixels, dtype=jnp.int32) % side
    total = jnp.zeros((frames, weights.shape[2], pixels), jnp.float32)
    for depth in range(3):
        window = extended[depth : depth + frames]
        for down in range(3):
            for across in range(3):
                offset = (down - 1) * side + (across - 1)
                inside = (
                    (rows + down - 1 >= 0)
                    & (rows + down - 1 < side)
                    & (cols + across - 1 >= 0)
                    & (cols + across - 1 < side)
                )
                moved = jnp.roll(window, -offset, axis=2)
                moved = jnp.where(inside[None, None, :], moved, jnp.zeros_like(moved))
                total = total + jnp.einsum(
                    "fcp,co->fop",
                    moved,
                    weights[9 * depth + 3 * down + across],
                    preferred_element_type=jnp.float32,
                )
    return total


def with_history(values):
    frames = values.shape[0]
    earlier = shifted(values[frames - 2 :], "tm", 1)
    return jnp.concatenate([earlier, values], axis=0)


def normalize(values, gain, shift, total_frames):
    frames, chans, pixels = values.shape
    width = CH // GROUPS
    grouped = values.reshape(frames, chans // width, width, pixels)
    sums = jnp.sum(grouped, axis=(0, 2, 3))
    squares = jnp.sum(grouped * grouped, axis=(0, 2, 3))
    sums, squares = lax.psum((sums, squares), "tm")
    count = total_frames * width * pixels
    mean = sums / count
    variance = squares / count - mean * mean
    scale = lax.rsqrt(variance + EPSILON)
    normed = (grouped - mean[None, :, None, None]) * scale[None, :, None, None]
    normed = normed.reshape(frames, chans, pixels) * gain[None, :, None] + shift[None, :, None]
    return jax.nn.silu(normed).astype(jnp.bfloat16)


def spread(color, weight, index, total_pixels):
    numer = (
        jnp.zeros((color.shape[0], 3, total_pixels), jnp.float32)
        .at[:, :, index]
        .add(color * weight[None, None, :])
    )
    denom = jnp.zeros((total_pixels,), jnp.float32).at[index].add(weight)
    return (numer, denom)


def route_owned(numer, denom, tile_id, own):
    frames = numer.shape[0]
    margin = (GRID_X + 1) * own
    numer_wide = jnp.concatenate([numer, jnp.zeros((frames, 3, margin), jnp.float32)], axis=2)
    denom_wide = jnp.concatenate([denom, jnp.zeros((margin,), jnp.float32)], axis=0)
    first_pixel = tile_id * own

    def block_at(offset):
        start_pixel = first_pixel + offset * own
        return (
            lax.dynamic_slice_in_dim(numer_wide, start_pixel, own, 2),
            lax.dynamic_slice_in_dim(denom_wide, start_pixel, own, 0),
        )

    owned_numer, owned_denom = block_at(0)
    for offset in (1, GRID_X, GRID_X + 1):
        piece_numer, piece_denom = block_at(offset)
        got_numer, got_denom = shifted((piece_numer, piece_denom), "tile", offset)
        owned_numer = owned_numer + got_numer
        owned_denom = owned_denom + got_denom
    return (owned_numer, owned_denom)


def general_body(
    latents, tile_order, w_in, gain_in, shift_in, w_mid, gain_mid, shift_mid, w_out, blend_weight
):
    frames = latents.shape[0]
    total_frames = frames * lax.axis_size("tm")
    tiles = tile_order.shape[0]
    own = STRIDE * STRIDE
    total_pixels = tiles * own
    tile_id = lax.axis_index("tile")
    index, valid = window_index(tile_id, tiles)
    whole = lax.all_gather(latents, "tile", axis=2, tiled=True)
    blocks = whole.reshape(frames, whole.shape[1], tiles, own)
    image = (
        jnp.zeros_like(blocks)
        .at[:, :, tile_order]
        .set(blocks)
        .reshape(frames, whole.shape[1], total_pixels)
    )
    window = jnp.where(
        valid[None, None, :], jnp.take(image, index, axis=2), jnp.zeros((), jnp.bfloat16)
    )
    first = causal_conv(with_history(window), w_in, frames, TSIDE)
    hidden = normalize(first, gain_in, shift_in, total_frames)
    second = causal_conv(
        lax.all_gather(with_history(hidden), "chan", axis=1, tiled=True), w_mid, frames, TSIDE
    )
    upper = normalize(second, gain_mid, shift_mid, total_frames)
    color = jnp.einsum("oc,fcp->fop", w_out, upper, preferred_element_type=jnp.float32)
    weight = jnp.where(valid, blend_weight[tile_id], jnp.float32(0.0))
    numer, denom = spread(color, weight, index, total_pixels)
    numer, denom = route_owned(numer, denom, tile_id, own)
    numer = lax.psum(numer, "chan")
    return numer / denom[None, None, :]


def block_cases(tiles):
    downs = (0, 1) if tiles // GRID_X > 1 else (0,)
    return [(down, across) for down in downs for across in (0, 1)]


def exact_dot(values, ones):
    rows = values.shape[0]
    high = values.astype(jnp.bfloat16)
    rest = values - high.astype(jnp.float32)
    middle = rest.astype(jnp.bfloat16)
    low = (rest - middle.astype(jnp.float32)).astype(jnp.bfloat16)
    total = jnp.dot(
        jnp.concatenate([high, middle, low], axis=0), ones, preferred_element_type=jnp.float32
    )
    return total[:rows] + total[rows : 2 * rows] + total[2 * rows :]


def group_affine(sums, squares, gain, shift, count):
    lanes = sums.shape[1]
    width = CH // GROUPS
    same = lax.broadcasted_iota(jnp.int32, (lanes, lanes), 0) // width == (
        lax.broadcasted_iota(jnp.int32, (lanes, lanes), 1) // width
    )
    total = exact_dot(
        jnp.concatenate([sums, squares], axis=0), jnp.where(same, 1.0, 0.0).astype(jnp.bfloat16)
    )
    mean = jnp.sum(total[:8], axis=0, keepdims=True) / count
    variance = jnp.sum(total[8:], axis=0, keepdims=True) / count - mean * mean
    scale = gain * lax.rsqrt(variance + EPSILON)
    return 0.5 * scale, 0.5 * (shift - mean * scale)


def silu_of_half(half):
    return half + half * jnp.tanh(half)


def fold(values):
    rows, lanes = values.shape
    return jnp.sum(values.reshape(rows // 8, 8, lanes), axis=0)


def decode_kernel(
    tiles,
    spans,
    shares,
    *refs,
):
    cases = block_cases(tiles)
    refs = list(refs)

    def take(number):
        taken = refs[:number]
        del refs[:number]
        return taken

    w_mid_ref, table_ref, order_ref = take(3)
    latent_refs, w_in_refs = take(spans), take(shares)
    keep_ref, send_ref, denom_ref = take(3)
    taps, first, hidden, weights, partial, shown_ref, sems = take(7)

    own = denom_ref.shape[1]
    own_frames = keep_ref.shape[2]
    frames = own_frames * spans
    latent, wide = w_in_refs[0].shape[1:]
    rows_in = frames * latent
    rows_own = rows_in // spans
    depth_in = 27 * latent
    pixels = TSIDE * TSIDE
    lanes = partial.shape[3]
    tile_id = lax.axis_index("tile")
    mine = lax.axis_index("tm")
    chan_id = lax.axis_index("chan")

    copies = [
        pltpu.make_async_copy(
            w_mid_ref.at[
                9 * a + 3 * b + e, :, pl.ds(pl.multiple_of(mine * lanes, LANES), lanes)
            ],
            weights.at[pl.ds(b * CH, CH), pl.ds((3 * a + e) * lanes, lanes)],
            sems.at[9 * a + 3 * b + e],
        )
        for a in range(3)
        for b in range(3)
        for e in range(3)
    ]

    @pl.when(tile_id >= 0)
    def _():
        for copy in copies:
            copy.start()

    tile_row, tile_col = tile_id // GRID_X, tile_id % GRID_X
    gain_row = rows_own + 2
    w_out_row = gain_row + 2
    blend_row = w_out_row + 3
    rows_all = latent_refs[0].shape[0] // tiles
    messages = [
        [
            latent_refs[swap][steps * rows_all : steps * rows_all + rows_own + latent].astype(
                jnp.float32
            )
            for swap in range(spans)
        ]
        for steps in range(tiles)
    ]
    mains, tails = [], []
    for down, across in cases:
        inside = (tile_row + down < tiles // GRID_X) & (tile_col + across < GRID_X)
        wanted = jnp.where(inside, tile_id + down * GRID_X + across, -1).astype(jnp.float32)
        blocks = [0.0] * spans
        for steps in range(tiles):
            held = order_ref[pl.ds((tile_id - steps + tiles) % tiles, 1), :]
            chosen = jnp.where(held == wanted, 1.0, 0.0)
            for swap in range(spans):
                blocks[swap] = blocks[swap] + chosen * messages[steps][swap]
        mains.append(jnp.concatenate([block[:rows_own] for block in blocks], axis=0))
        tails.append(jnp.concatenate([block[rows_own:] for block in blocks], axis=0))
    mains = jnp.concatenate(mains, axis=1).astype(jnp.bfloat16)
    tails = jnp.concatenate(tails, axis=1)

    slot = lax.broadcasted_iota(jnp.int32, (1, pixels), 1)
    up, along = slot // TSIDE, slot % TSIDE
    source = lax.broadcasted_iota(jnp.int32, (LANES, pixels), 0)
    tail = own - LANES

    def pick(first_pixel):
        parts = []
        for down, across in cases:
            u, v = up - down * STRIDE, along - across * STRIDE
            good = (u >= 0) & (u < STRIDE) & (v >= 0) & (v < STRIDE)
            wanted = jnp.where(good, u * STRIDE + v - first_pixel, -1)
            parts.append(jnp.where(source == wanted, 1.0, 0.0).astype(jnp.bfloat16))
        return jnp.concatenate(parts, axis=0)

    width = tails.shape[1]
    turned = [pltpu.roll(tails, (-f * tail) % width, 1) if f else tails for f in range(own_frames)]
    tails = jnp.concatenate(
        [
            turned[f][swap * latent : (swap + 1) * latent]
            for swap in range(spans)
            for f in range(own_frames)
        ],
        axis=0,
    ).astype(jnp.bfloat16)
    window = jnp.dot(mains, pick(0), preferred_element_type=jnp.float32) + jnp.dot(
        tails, pick(LANES), preferred_element_type=jnp.float32
    )
    taps[0:2] = jnp.zeros((2,) + taps.shape[1:], taps.dtype)
    for b in range(3):
        for e in range(3):
            inside = (
                (up + b - 1 >= 0)
                & (up + b - 1 < TSIDE)
                & (along + e - 1 >= 0)
                & (along + e - 1 < TSIDE)
            )
            offset = (b - 1) * TSIDE + e - 1
            moved = pltpu.roll(window, (-offset) % pixels, 1) if offset else window
            moved = jnp.where(inside, moved, 0.0).astype(jnp.bfloat16)
            for swap in range(spans):
                value = moved[swap * rows_own : (swap + 1) * rows_own]
                span = pl.ds(2 + (mine + swap) % spans * own_frames, own_frames)
                taps[span, 3 * b + e] = value.reshape(own_frames, latent, pixels)

    joined = jnp.concatenate(
        [w_in_refs[s][:27].reshape(depth_in, wide) for s in range(shares)], axis=1
    )
    sums = jnp.zeros((8, CH), jnp.float32)
    squares = jnp.zeros((8, CH), jnp.float32)
    for f in range(frames):
        patch = taps[f : f + 3].reshape(depth_in, pixels)
        value = lax.dot_general(
            patch, joined, (((0,), (0,)), ((), ())), preferred_element_type=jnp.float32
        )
        first[f] = value
        sums = sums + fold(value)
        squares = squares + fold(value * value)
    count = frames * (CH // GROUPS) * pixels
    affine = []
    for s in range(shares):
        at = s * rows_all + rows_own + latent
        table = latent_refs[0][at : at + wide // LANES * 4].astype(jnp.float32)
        pieces = [table[4 * lane : 4 * lane + 4] for lane in range(wide // LANES)]
        table = jnp.concatenate([part[0:2] + part[2:4] for part in pieces], axis=1)
        part = slice(s * wide, (s + 1) * wide)
        affine.append(
            group_affine(sums[:, part], squares[:, part], table[0:1], table[1:2], count)
        )
    channels = [
        pl.ds(pl.multiple_of((chan_id + s) % shares * wide, LANES), wide) for s in range(shares)
    ]

    def hide(f):
        edge = jnp.zeros((TSIDE, CH), jnp.bfloat16)
        hidden[f, 0:TSIDE] = edge
        hidden[f, TSIDE + pixels : 2 * TSIDE + pixels] = edge
        for s in range(shares):
            scale, bias = affine[s]
            value = first[f, :, s * wide : (s + 1) * wide] * scale + bias
            hidden[f, TSIDE : TSIDE + pixels, channels[s]] = silu_of_half(value).astype(
                jnp.bfloat16
            )

    def convolve(start, several, depth_taps):
        lhs = jnp.concatenate(
            [
                hidden[start : start + several, b * TSIDE : b * TSIDE + pixels].reshape(
                    several * pixels, CH
                )
                for b in range(3)
            ],
            axis=1,
        )
        low = depth_taps[0] * 3 * lanes
        product = jnp.dot(lhs, weights[:, low:], preferred_element_type=jnp.float32)
        for a in depth_taps:
            for e in range(3):
                at = (3 * a + e) * lanes - low
                for f in range(several):
                    target = start + f + 2 - a
                    value = product[f * pixels : (f + 1) * pixels, at : at + lanes]
                    if start + f == max(target - 2, 0):
                        partial[e, target] = value
                    else:
                        partial[e, target] += value

    column = lax.broadcasted_iota(jnp.int32, (pixels, lanes), 0) % TSIDE
    total = [jnp.zeros((8, lanes), jnp.float32)] * 2

    def gather(f):
        left = jnp.where(column == 0, 0.0, pltpu.roll(partial[0, f], 1, 0))
        right = jnp.where(column == TSIDE - 1, 0.0, pltpu.roll(partial[2, f], pixels - 1, 0))
        value = partial[1, f] + left + right
        partial[1, f] = value
        total[0] = total[0] + fold(value)
        total[1] = total[1] + fold(value * value)

    bounds = [0, 2, frames - 2, frames - 1, frames]
    groups = [range(low, high) for low, high in zip(bounds, bounds[1:]) if high > low]
    for copy in copies:
        copy.wait()
    for f in groups[0]:
        hide(f)
    for number, group in enumerate(groups):
        if number + 1 < len(groups):
            for f in groups[number + 1]:
                hide(f)
        convolve(
            group.start,
            len(group),
            tuple(a for a in range(3) if group.stop - 1 + 2 - a < frames),
        )
        if number:
            for f in groups[number - 1]:
                gather(f)
    for f in groups[-1]:
        gather(f)

    part = pl.ds(pl.multiple_of(mine * lanes, LANES), lanes)
    scale, bias = group_affine(
        total[0],
        total[1],
        table_ref[gain_row : gain_row + 1, part],
        table_ref[gain_row + 1 : gain_row + 2, part],
        count,
    )
    blend = table_ref[pl.ds(blend_row + tile_id, 1), :]
    blend = jnp.where(
        (tile_row * STRIDE + up < tiles // GRID_X * STRIDE)
        & (tile_col * STRIDE + along < GRID_X * STRIDE),
        blend,
        0.0,
    )
    w_out = jnp.concatenate(
        [table_ref[w_out_row : w_out_row + 3, part], jnp.zeros((5, lanes), jnp.float32)], axis=0
    ).astype(jnp.bfloat16)
    colors = []
    for f in range(frames):
        upper = silu_of_half(partial[1, f] * scale + bias).astype(jnp.bfloat16)
        color = lax.dot_general(
            w_out, upper, (((1,), (1,)), ((), ())), preferred_element_type=jnp.float32
        )
        colors.append(color * blend)
    colors = jnp.concatenate(colors, axis=0)

    slot_in = lax.broadcasted_iota(jnp.int32, (pixels, own), 0)
    pixel = lax.broadcasted_iota(jnp.int32, (pixels, own), 1)
    denom = jnp.zeros((8, own), jnp.float32)
    for number, (down, across) in enumerate(cases):
        u, v = slot_in // TSIDE - down * STRIDE, slot_in % TSIDE - across * STRIDE
        good = (u >= 0) & (u < STRIDE) & (v >= 0) & (v < STRIDE) & (u * STRIDE + v == pixel)
        shown = jnp.where(good, 1.0, 0.0).astype(jnp.bfloat16)
        inside = (tile_row >= down) & (tile_col >= across)
        other = jnp.maximum(tile_id - down * GRID_X - across, 0)
        weight = jnp.where(inside, table_ref[pl.ds(blend_row + other, 1), :], 0.0)
        piece = exact_dot(
            jnp.concatenate([colors, jnp.broadcast_to(weight, (8, pixels))], axis=0), shown
        )
        denom = denom + piece[8 * frames :]
        shown_ref[...] = piece
        for swap in range(spans):
            target = keep_ref if swap == 0 else send_ref.at[swap - 1]
            base = (mine + swap) % spans * own_frames * 8
            for at in range(own_frames):
                for o in range(3):
                    target[number, o, at : at + 1, :] = shown_ref[pl.ds(base + 8 * at + o, 1), :]

    denom_ref[...] = denom


def from_ring(value, axis):
    count = lax.axis_size(axis)
    return [
        lax.ppermute(value, axis, [((d + turn) % count, d) for d in range(count)])
        for turn in range(1, count)
    ]


def small_table(*values):
    values = [value.reshape(-1, value.shape[-1]) for value in values]
    wide = max(value.shape[1] for value in values)
    height = sum(value.shape[0] for value in values)
    total, row = 0.0, 0
    for value in values:
        below = height - row - value.shape[0]
        value = jnp.pad(value.astype(jnp.float32), ((row, below), (0, wide - value.shape[1])))
        total = total + value
        row = height - below
    return total


def exchange_latents(frames, latent, own, table):
    tiles, shares = lax.axis_size("tile"), lax.axis_size("chan")
    tail = own - LANES
    height = frames * latent
    mine = table[:height, :own].astype(jnp.bfloat16)
    tails = sum(
        jnp.pad(
            mine[f * latent : (f + 1) * latent, LANES:],
            ((0, 0), (tail * f, LANES - tail * (f + 1))),
        )
        for f in range(frames)
    )
    affine = table[height : height + 2]
    high = lax.reduce_precision(affine, 8, 7)
    low = lax.reduce_precision(affine - high, 8, 7)
    affine = jnp.concatenate([high, low], axis=0).astype(jnp.bfloat16)
    rows = [affine[:, at : at + LANES] for at in range(0, affine.shape[1], LANES)]
    rows = jnp.concatenate(rows, axis=0)
    rows = jnp.pad(rows, ((0, -rows.shape[0] % 16), (0, 0)))
    message = jnp.concatenate([mine[:, :LANES], tails, rows], axis=0)
    got = [message]
    for steps in range(1, tiles):
        turn = steps if steps < shares else 0
        pairs = [
            (t * shares + (c + turn) % shares, (t + steps) % tiles * shares + c)
            for t in range(tiles)
            for c in range(shares)
        ]
        got.append(lax.ppermute(message, ("tile", "chan"), pairs))
    stack = jnp.concatenate(got, axis=0)
    return [stack] + from_ring(stack, "tm")


def lanes_body(
    latents, tile_order, w_in, gain_in, shift_in, w_mid, gain_mid, shift_mid, w_out, blend_weight
):
    own_frames, latent, own = latents.shape
    spans = lax.axis_size("tm")
    shares = lax.axis_size("chan")
    frames = own_frames * spans
    tiles = tile_order.shape[0]
    wide = w_in.shape[2]
    lanes = wide // spans
    pixels = TSIDE * TSIDE
    cases = block_cases(tiles)

    w_in_all = [(from_ring(other, "tm") or [other])[0] for other in from_ring(w_in, "chan")]
    table = lax.optimization_barrier(
        small_table(
            latents.reshape(own_frames * latent, own),
            gain_in,
            shift_in,
            gain_mid,
            shift_mid,
            w_out,
            blend_weight,
        )
    )
    latents_all = exchange_latents(own_frames, latent, own, table)
    _, w_in, tile_order = lax.optimization_barrier((table, w_in, tile_order))
    order = jnp.broadcast_to(tile_order.astype(jnp.float32)[:, None], (tiles, LANES))
    w_in_own = from_ring(w_in, "tm")[:1] or [w_in]

    vmem = pl.BlockSpec(memory_space=pltpu.VMEM)
    piece = (len(cases), 3, own_frames, own)
    kept, sent, denom = pl.pallas_call(
        functools.partial(decode_kernel, tiles, spans, shares),
        out_shape=[
            jax.ShapeDtypeStruct(piece, jnp.float32),
            jax.ShapeDtypeStruct((max(spans - 1, 1),) + piece, jnp.float32),
            jax.ShapeDtypeStruct((8, own), jnp.float32),
        ],
        in_specs=[pl.BlockSpec(memory_space=pl.ANY)] + [vmem] * (2 + spans + shares),
        out_specs=[vmem] * 3,
        scratch_shapes=[
            pltpu.VMEM((frames + 2, 9, latent, pixels), jnp.bfloat16),
            pltpu.VMEM((frames, pixels, CH), jnp.float32),
            pltpu.VMEM((frames, pixels + 2 * TSIDE, CH), jnp.bfloat16),
            pltpu.VMEM((3 * CH, 9 * lanes), jnp.bfloat16),
            pltpu.VMEM((3, frames, pixels, lanes), jnp.float32),
            pltpu.VMEM((8 * (frames + 1), own), jnp.float32),
            pltpu.SemaphoreType.DMA((27,)),
        ],
        compiler_params=pltpu.CompilerParams(vmem_limit_bytes=VMEM_BYTES),
        cost_estimate=pl.CostEstimate(
            flops=2 * frames * pixels * 27 * CH * lanes, bytes_accessed=8_000_000, transcendentals=0
        ),
    )(w_mid, table, order, *latents_all, *w_in_own, *w_in_all)
    total = kept
    for turn in range(shares):
        for swap in range(spans):
            if turn or swap:
                pairs = [
                    (c * spans + m, (c + turn) % shares * spans + (m + swap) % spans)
                    for c in range(shares)
                    for m in range(spans)
                ]
                piece = sent[swap - 1] if swap else kept
                total = total + lax.ppermute(piece, ("chan", "tm"), pairs)
    numer = total[0]
    for number, (down, across) in enumerate(cases):
        steps = down * GRID_X + across
        if steps and steps < tiles:
            numer = numer + shifted(total[number], "tile", steps)
    return jnp.transpose(numer / denom[0][None, None, :], (1, 0, 2))


def solution(mesh):
    placed = (
        P("tm", "groups", "tile"),
        P("groups"),
        P(None, None, "chan"),
        P("chan"),
        P("chan"),
        P(None, None, "chan"),
        P("chan"),
        P("chan"),
        P(None, "chan"),
        P("groups", None),
    )
    whole_lanes = (
        CH % (mesh.shape["chan"] * mesh.shape["tm"] * LANES) == 0
        and mesh.shape["chan"] <= mesh.shape["tile"]
    )
    return jax.shard_map(
        lanes_body if whole_lanes else general_body,
        mesh=mesh,
        in_specs=placed,
        out_specs=P("tm", "groups", "tile"),
        check_vma=False,
    )
```

```python
import functools

import jax
import jax.numpy as jnp
from jax import lax
from jax.experimental import pallas as pl
from jax.experimental.pallas import tpu as pltpu
from jax.sharding import PartitionSpec as P

CH = 512
GROUPS = 32
TSIDE = 16
STRIDE = 12
GRID_X = 4

EPSILON = 1e-06
LANES = 128
VMEM_BYTES = 48 * 1024 * 1024


def shifted(value, axis, steps):
    count = lax.axis_size(axis)
    leading, last = (max(0, -steps), min(count, count - steps))
    return lax.ppermute(value, axis, [(source, source + steps) for source in range(leading, last)])


def window_index(tile_id, tiles):
    slots = jnp.arange(TSIDE * TSIDE, dtype=jnp.int32)
    row = tile_id // GRID_X * STRIDE + slots // TSIDE
    col = tile_id % GRID_X * STRIDE + slots % TSIDE
    valid = (row < tiles // GRID_X * STRIDE) & (col < GRID_X * STRIDE)
    block = row // STRIDE * GRID_X + col // STRIDE
    index = block * (STRIDE * STRIDE) + row % STRIDE * STRIDE + col % STRIDE
    return (jnp.where(valid, index, 0), valid)


def causal_conv(extended, weights, frames, side):
    pixels = side * side
    rows = jnp.arange(pixels, dtype=jnp.int32) // side
    cols = jnp.arange(pixels, dtype=jnp.int32) % side
    total = jnp.zeros((frames, weights.shape[2], pixels), jnp.float32)
    for depth in range(3):
        window = extended[depth : depth + frames]
        for down in range(3):
            for across in range(3):
                offset = (down - 1) * side + (across - 1)
                inside = (
                    (rows + down - 1 >= 0)
                    & (rows + down - 1 < side)
                    & (cols + across - 1 >= 0)
                    & (cols + across - 1 < side)
                )
                moved = jnp.roll(window, -offset, axis=2)
                moved = jnp.where(inside[None, None, :], moved, jnp.zeros_like(moved))
                total = total + jnp.einsum(
                    "fcp,co->fop",
                    moved,
                    weights[9 * depth + 3 * down + across],
                    preferred_element_type=jnp.float32,
                )
    return total


def with_history(values):
    frames = values.shape[0]
    earlier = shifted(values[frames - 2 :], "tm", 1)
    return jnp.concatenate([earlier, values], axis=0)


def normalize(values, gain, shift, total_frames):
    frames, chans, pixels = values.shape
    width = CH // GROUPS
    grouped = values.reshape(frames, chans // width, width, pixels)
    sums = jnp.sum(grouped, axis=(0, 2, 3))
    squares = jnp.sum(grouped * grouped, axis=(0, 2, 3))
    sums, squares = lax.psum((sums, squares), "tm")
    count = total_frames * width * pixels
    mean = sums / count
    variance = squares / count - mean * mean
    scale = lax.rsqrt(variance + EPSILON)
    normed = (grouped - mean[None, :, None, None]) * scale[None, :, None, None]
    normed = normed.reshape(frames, chans, pixels) * gain[None, :, None] + shift[None, :, None]
    return jax.nn.silu(normed).astype(jnp.bfloat16)


def spread(color, weight, index, total_pixels):
    numer = (
        jnp.zeros((color.shape[0], 3, total_pixels), jnp.float32)
        .at[:, :, index]
        .add(color * weight[None, None, :])
    )
    denom = jnp.zeros((total_pixels,), jnp.float32).at[index].add(weight)
    return (numer, denom)


def route_owned(numer, denom, tile_id, own):
    frames = numer.shape[0]
    margin = (GRID_X + 1) * own
    numer_wide = jnp.concatenate([numer, jnp.zeros((frames, 3, margin), jnp.float32)], axis=2)
    denom_wide = jnp.concatenate([denom, jnp.zeros((margin,), jnp.float32)], axis=0)
    first_pixel = tile_id * own

    def block_at(offset):
        start_pixel = first_pixel + offset * own
        return (
            lax.dynamic_slice_in_dim(numer_wide, start_pixel, own, 2),
            lax.dynamic_slice_in_dim(denom_wide, start_pixel, own, 0),
        )

    owned_numer, owned_denom = block_at(0)
    for offset in (1, GRID_X, GRID_X + 1):
        piece_numer, piece_denom = block_at(offset)
        got_numer, got_denom = shifted((piece_numer, piece_denom), "tile", offset)
        owned_numer = owned_numer + got_numer
        owned_denom = owned_denom + got_denom
    return (owned_numer, owned_denom)


def general_body(
    latents, tile_order, w_in, gain_in, shift_in, w_mid, gain_mid, shift_mid, w_out, blend_weight
):
    frames = latents.shape[0]
    total_frames = frames * lax.axis_size("tm")
    tiles = tile_order.shape[0]
    own = STRIDE * STRIDE
    total_pixels = tiles * own
    tile_id = lax.axis_index("tile")
    index, valid = window_index(tile_id, tiles)
    whole = lax.all_gather(latents, "tile", axis=2, tiled=True)
    blocks = whole.reshape(frames, whole.shape[1], tiles, own)
    image = (
        jnp.zeros_like(blocks)
        .at[:, :, tile_order]
        .set(blocks)
        .reshape(frames, whole.shape[1], total_pixels)
    )
    window = jnp.where(
        valid[None, None, :], jnp.take(image, index, axis=2), jnp.zeros((), jnp.bfloat16)
    )
    first = causal_conv(with_history(window), w_in, frames, TSIDE)
    hidden = normalize(first, gain_in, shift_in, total_frames)
    second = causal_conv(
        lax.all_gather(with_history(hidden), "chan", axis=1, tiled=True), w_mid, frames, TSIDE
    )
    upper = normalize(second, gain_mid, shift_mid, total_frames)
    color = jnp.einsum("oc,fcp->fop", w_out, upper, preferred_element_type=jnp.float32)
    weight = jnp.where(valid, blend_weight[tile_id], jnp.float32(0.0))
    numer, denom = spread(color, weight, index, total_pixels)
    numer, denom = route_owned(numer, denom, tile_id, own)
    numer = lax.psum(numer, "chan")
    return numer / denom[None, None, :]


def block_cases(tiles):
    downs = (0, 1) if tiles // GRID_X > 1 else (0,)
    return [(down, across) for down in downs for across in (0, 1)]


def exact_dot(values, ones):
    rows = values.shape[0]
    high = values.astype(jnp.bfloat16)
    rest = values - high.astype(jnp.float32)
    middle = rest.astype(jnp.bfloat16)
    low = (rest - middle.astype(jnp.float32)).astype(jnp.bfloat16)
    total = jnp.dot(
        jnp.concatenate([high, middle, low], axis=0), ones, preferred_element_type=jnp.float32
    )
    return total[:rows] + total[rows : 2 * rows] + total[2 * rows :]


def group_affine(sums, squares, gain, shift, count):
    lanes = sums.shape[1]
    width = CH // GROUPS
    same = lax.broadcasted_iota(jnp.int32, (lanes, lanes), 0) // width == (
        lax.broadcasted_iota(jnp.int32, (lanes, lanes), 1) // width
    )
    total = exact_dot(
        jnp.concatenate([sums, squares], axis=0), jnp.where(same, 1.0, 0.0).astype(jnp.bfloat16)
    )
    mean = jnp.sum(total[:8], axis=0, keepdims=True) / count
    variance = jnp.sum(total[8:], axis=0, keepdims=True) / count - mean * mean
    scale = gain * lax.rsqrt(variance + EPSILON)
    return 0.5 * scale, 0.5 * (shift - mean * scale)


def silu_of_half(half):
    return half + half * jnp.tanh(half)


def fold(values):
    rows, lanes = values.shape
    return jnp.sum(values.reshape(rows // 8, 8, lanes), axis=0)


def decode_kernel(
    tiles,
    spans,
    shares,
    *refs,
):
    cases = block_cases(tiles)
    refs = list(refs)

    def take(number):
        taken = refs[:number]
        del refs[:number]
        return taken

    w_mid_ref, table_ref, order_ref = take(3)
    latent_refs, w_in_refs = take(spans), take(shares)
    keep_ref, send_ref, denom_ref = take(3)
    chosen, taps, first, hidden, weights, partial, shown_ref = take(7)
    sums_ref, totals_ref, sems = take(3)

    own = denom_ref.shape[1]
    own_frames = keep_ref.shape[2]
    frames = own_frames * spans
    latent, wide = w_in_refs[0].shape[1:]
    rows_in = frames * latent
    rows_own = rows_in // spans
    depth_in = 27 * latent
    pixels = TSIDE * TSIDE
    lanes = partial.shape[3]
    tile_id = lax.axis_index("tile")
    mine = lax.axis_index("tm")
    chan_id = lax.axis_index("chan")

    copies = []
    for a in range(3):
        for b in range(3):
            for e in range(3):
                tap = 9 * a + 3 * b + e
                copy = pltpu.make_async_copy(
                    w_mid_ref.at[tap, :, pl.ds(pl.multiple_of(mine * lanes, LANES), lanes)],
                    weights.at[pl.ds(b * CH, CH), pl.ds((3 * a + e) * lanes, lanes)],
                    sems.at[tap],
                )
                copy.start()
                copies.append(copy)

    tile_row, tile_col = tile_id // GRID_X, tile_id % GRID_X
    gain_row = rows_own + 2
    w_out_row = gain_row + 2
    blend_row = w_out_row + 3
    order = order_ref[...]
    number_of = lax.broadcasted_iota(jnp.int32, order.shape, 0)
    lane_of = lax.broadcasted_iota(jnp.int32, order.shape, 1)
    rows_all = latent_refs[0].shape[0] // tiles
    for number, (down, across) in enumerate(cases):
        inside = (tile_row + down < tiles // GRID_X) & (tile_col + across < GRID_X)
        wanted = tile_id + down * GRID_X + across
        found = (order == wanted.astype(jnp.float32)) & (lane_of == 0)
        place = jnp.sum(jnp.where(found, number_of.astype(jnp.float32), 0.0))
        turn = (tile_id - place.astype(jnp.int32) + tiles) % tiles
        part = slice(number * LANES, (number + 1) * LANES)
        for steps in range(tiles):

            @pl.when(inside & (turn == steps))
            def _():
                for swap in range(spans):
                    at, tail_at = swap * rows_own, rows_in + swap * latent
                    block = latent_refs[swap][steps * rows_all : (steps + 1) * rows_all]
                    chosen[at : at + rows_own, part] = block[:rows_own]
                    chosen[tail_at : tail_at + latent, part] = block[rows_own : rows_own + latent]

        @pl.when(jnp.logical_not(inside))
        def _():
            chosen[:, part] = jnp.zeros((chosen.shape[0], LANES), chosen.dtype)

    slot = lax.broadcasted_iota(jnp.int32, (1, pixels), 1)
    up, along = slot // TSIDE, slot % TSIDE
    source = lax.broadcasted_iota(jnp.int32, (LANES, pixels), 0)
    tail = own - LANES

    def pick(first_pixel):
        parts = []
        for down, across in cases:
            u, v = up - down * STRIDE, along - across * STRIDE
            good = (u >= 0) & (u < STRIDE) & (v >= 0) & (v < STRIDE)
            wanted = jnp.where(good, u * STRIDE + v - first_pixel, -1)
            parts.append(jnp.where(source == wanted, 1.0, 0.0).astype(jnp.bfloat16))
        return jnp.concatenate(parts, axis=0)

    always = tile_id >= 0

    @pl.when(always)
    def _():
        tails = chosen[rows_in:].astype(jnp.float32)
        width = tails.shape[1]
        turned = [pltpu.roll(tails, (-f * tail) % width, 1) if f else tails for f in range(own_frames)]
        tails = jnp.concatenate(
            [
                turned[f][swap * latent : (swap + 1) * latent]
                for swap in range(spans)
                for f in range(own_frames)
            ],
            axis=0,
        ).astype(jnp.bfloat16)
        in_tail = lax.broadcasted_iota(jnp.int32, tails.shape, 1) % LANES < tail
        tails = jnp.where(in_tail, tails.astype(jnp.float32), 0.0).astype(jnp.bfloat16)
        window = jnp.dot(
            chosen[:rows_in], pick(0), preferred_element_type=jnp.float32
        ) + jnp.dot(tails, pick(LANES), preferred_element_type=jnp.float32)
        taps[0:2] = jnp.zeros((2,) + taps.shape[1:], taps.dtype)
        for b in range(3):
            for e in range(3):
                inside = (
                    (up + b - 1 >= 0)
                    & (up + b - 1 < TSIDE)
                    & (along + e - 1 >= 0)
                    & (along + e - 1 < TSIDE)
                )
                offset = (b - 1) * TSIDE + e - 1
                moved = pltpu.roll(window, (-offset) % pixels, 1) if offset else window
                moved = jnp.where(inside, moved, 0.0).astype(jnp.bfloat16)
                for swap in range(spans):
                    value = moved[swap * rows_own : (swap + 1) * rows_own]
                    span = pl.ds(2 + (mine + swap) % spans * own_frames, own_frames)
                    taps[span, 3 * b + e] = value.reshape(own_frames, latent, pixels)

    @pl.when(always)
    def _():
        joined = jnp.concatenate(
            [w_in_refs[s][:27].reshape(depth_in, wide) for s in range(shares)], axis=1
        )
        sums = jnp.zeros((8, CH), jnp.float32)
        squares = jnp.zeros((8, CH), jnp.float32)
        for f in range(frames):
            patch = taps[f : f + 3].reshape(depth_in, pixels)
            value = lax.dot_general(
                patch, joined, (((0,), (0,)), ((), ())), preferred_element_type=jnp.float32
            )
            first[f] = value
            sums = sums + fold(value)
            squares = squares + fold(value * value)
        sums_ref[0] = sums
        sums_ref[1] = squares

    count = frames * (CH // GROUPS) * pixels
    affine = []
    for s in range(shares):
        at = s * rows_all + rows_own + latent
        table = latent_refs[0][at : at + wide // LANES * 4].astype(jnp.float32)
        pieces = [table[4 * lane : 4 * lane + 4] for lane in range(wide // LANES)]
        table = jnp.concatenate([part[0:2] + part[2:4] for part in pieces], axis=1)
        part = slice(s * wide, (s + 1) * wide)
        affine.append(
            group_affine(sums_ref[0, :, part], sums_ref[1, :, part], table[0:1], table[1:2], count)
        )
    channels = [
        pl.ds(pl.multiple_of((chan_id + s) % shares * wide, LANES), wide) for s in range(shares)
    ]

    def hide(f):
        edge = jnp.zeros((TSIDE, CH), jnp.bfloat16)
        hidden[f, 0:TSIDE] = edge
        hidden[f, TSIDE + pixels : 2 * TSIDE + pixels] = edge
        for s in range(shares):
            scale, bias = affine[s]
            value = first[f, :, s * wide : (s + 1) * wide] * scale + bias
            hidden[f, TSIDE : TSIDE + pixels, channels[s]] = silu_of_half(value).astype(
                jnp.bfloat16
            )

    def convolve(start, several, depth_taps):
        lhs = jnp.concatenate(
            [
                hidden[start : start + several, b * TSIDE : b * TSIDE + pixels].reshape(
                    several * pixels, CH
                )
                for b in range(3)
            ],
            axis=1,
        )
        low = depth_taps[0] * 3 * lanes
        product = jnp.dot(lhs, weights[:, low:], preferred_element_type=jnp.float32)
        for a in depth_taps:
            for e in range(3):
                at = (3 * a + e) * lanes - low
                for f in range(several):
                    target = start + f + 2 - a
                    value = product[f * pixels : (f + 1) * pixels, at : at + lanes]
                    if start + f == max(target - 2, 0):
                        partial[e, target] = value
                    else:
                        partial[e, target] += value

    column = lax.broadcasted_iota(jnp.int32, (pixels, lanes), 0) % TSIDE
    total = [jnp.zeros((8, lanes), jnp.float32)] * 2

    def gather(f):
        left = jnp.where(column == 0, 0.0, pltpu.roll(partial[0, f], 1, 0))
        right = jnp.where(column == TSIDE - 1, 0.0, pltpu.roll(partial[2, f], pixels - 1, 0))
        value = partial[1, f] + left + right
        partial[1, f] = value
        total[0] = total[0] + fold(value)
        total[1] = total[1] + fold(value * value)

    together = 3
    groups = [
        range(f, min(f + together, frames - 2)) for f in range(0, frames - 2, together)
    ]
    groups += [range(f, f + 1) for f in range(groups[-1].stop, frames)]
    for copy in copies:
        copy.wait()
    for f in groups[0]:
        hide(f)
    for number, group in enumerate(groups):
        if number + 1 < len(groups):
            for f in groups[number + 1]:
                hide(f)
        convolve(
            group.start,
            len(group),
            tuple(a for a in range(3) if group.stop - 1 + 2 - a < frames),
        )
        if number:
            for f in groups[number - 1]:
                gather(f)
    for f in groups[-1]:
        gather(f)
    totals_ref[0] = total[0]
    totals_ref[1] = total[1]

    @pl.when(always)
    def _():
        part = pl.ds(pl.multiple_of(mine * lanes, LANES), lanes)
        scale, bias = group_affine(
            totals_ref[0],
            totals_ref[1],
            table_ref[gain_row : gain_row + 1, part],
            table_ref[gain_row + 1 : gain_row + 2, part],
            count,
        )
        blend = table_ref[pl.ds(blend_row + tile_id, 1), :]
        blend = jnp.where(
            (tile_row * STRIDE + up < tiles // GRID_X * STRIDE)
            & (tile_col * STRIDE + along < GRID_X * STRIDE),
            blend,
            0.0,
        )
        w_out = jnp.concatenate(
            [table_ref[w_out_row : w_out_row + 3, part], jnp.zeros((5, lanes), jnp.float32)], axis=0
        ).astype(jnp.bfloat16)
        colors = []
        for f in range(frames):
            upper = silu_of_half(partial[1, f] * scale + bias).astype(jnp.bfloat16)
            color = lax.dot_general(
                w_out, upper, (((1,), (1,)), ((), ())), preferred_element_type=jnp.float32
            )
            colors.append(color * blend)
        colors = jnp.concatenate(colors, axis=0)

        slot_in = lax.broadcasted_iota(jnp.int32, (pixels, own), 0)
        pixel = lax.broadcasted_iota(jnp.int32, (pixels, own), 1)
        denom = jnp.zeros((8, own), jnp.float32)
        for number, (down, across) in enumerate(cases):
            u, v = slot_in // TSIDE - down * STRIDE, slot_in % TSIDE - across * STRIDE
            good = (u >= 0) & (u < STRIDE) & (v >= 0) & (v < STRIDE) & (u * STRIDE + v == pixel)
            shown = jnp.where(good, 1.0, 0.0).astype(jnp.bfloat16)
            inside = (tile_row >= down) & (tile_col >= across)
            other = jnp.maximum(tile_id - down * GRID_X - across, 0)
            weight = jnp.where(inside, table_ref[pl.ds(blend_row + other, 1), :], 0.0)
            piece = exact_dot(
                jnp.concatenate([colors, jnp.broadcast_to(weight, (8, pixels))], axis=0), shown
            )
            denom = denom + piece[8 * frames :]
            shown_ref[...] = piece
            for swap in range(spans):
                target = keep_ref if swap == 0 else send_ref.at[swap - 1]
                base = (mine + swap) % spans * own_frames * 8
                for at in range(own_frames):
                    for o in range(3):
                        target[number, o, at : at + 1, :] = shown_ref[pl.ds(base + 8 * at + o, 1), :]

        denom_ref[...] = denom


def from_ring(value, axis):
    count = lax.axis_size(axis)
    return [
        lax.ppermute(value, axis, [((d + turn) % count, d) for d in range(count)])
        for turn in range(1, count)
    ]


def small_table(*values):
    values = [value.reshape(-1, value.shape[-1]) for value in values]
    wide = max(value.shape[1] for value in values)
    height = sum(value.shape[0] for value in values)
    total, row = 0.0, 0
    for value in values:
        below = height - row - value.shape[0]
        value = jnp.pad(value.astype(jnp.float32), ((row, below), (0, wide - value.shape[1])))
        total = total + value
        row = height - below
    return total


def exchange_latents(frames, latent, own, table):
    tiles, shares = lax.axis_size("tile"), lax.axis_size("chan")
    tail = own - LANES
    height = frames * latent
    mine = table[:height, :own].astype(jnp.bfloat16)
    tails = sum(
        jnp.pad(
            mine[f * latent : (f + 1) * latent, LANES:],
            ((0, 0), (tail * f, LANES - tail * (f + 1))),
        )
        for f in range(frames)
    )
    affine = table[height : height + 2]
    high = lax.reduce_precision(affine, 8, 7)
    low = lax.reduce_precision(affine - high, 8, 7)
    affine = jnp.concatenate([high, low], axis=0).astype(jnp.bfloat16)
    rows = [affine[:, at : at + LANES] for at in range(0, affine.shape[1], LANES)]
    rows = jnp.concatenate(rows, axis=0)
    rows = jnp.pad(rows, ((0, -rows.shape[0] % 16), (0, 0)))
    message = jnp.concatenate([mine[:, :LANES], tails, rows], axis=0)
    got = [message]
    for steps in range(1, tiles):
        turn = steps if steps < shares else 0
        pairs = [
            (t * shares + (c + turn) % shares, (t + steps) % tiles * shares + c)
            for t in range(tiles)
            for c in range(shares)
        ]
        got.append(lax.ppermute(message, ("tile", "chan"), pairs))
    stack = jnp.concatenate(got, axis=0)
    return [stack] + from_ring(stack, "tm")


def lanes_body(
    latents, tile_order, w_in, gain_in, shift_in, w_mid, gain_mid, shift_mid, w_out, blend_weight
):
    own_frames, latent, own = latents.shape
    spans = lax.axis_size("tm")
    shares = lax.axis_size("chan")
    frames = own_frames * spans
    tiles = tile_order.shape[0]
    wide = w_in.shape[2]
    lanes = wide // spans
    pixels = TSIDE * TSIDE
    cases = block_cases(tiles)

    w_in_all = [(from_ring(other, "tm") or [other])[0] for other in from_ring(w_in, "chan")]
    table = lax.optimization_barrier(
        small_table(
            latents.reshape(own_frames * latent, own),
            gain_in,
            shift_in,
            gain_mid,
            shift_mid,
            w_out,
            blend_weight,
        )
    )
    latents_all = exchange_latents(own_frames, latent, own, table)
    _, w_in, tile_order = lax.optimization_barrier((table, w_in, tile_order))
    order = jnp.broadcast_to(tile_order.astype(jnp.float32)[:, None], (tiles, LANES))
    w_in_own = from_ring(w_in, "tm")[:1] or [w_in]

    vmem = pl.BlockSpec(memory_space=pltpu.VMEM)
    piece = (len(cases), 3, own_frames, own)
    kept, sent, denom = pl.pallas_call(
        functools.partial(decode_kernel, tiles, spans, shares),
        out_shape=[
            jax.ShapeDtypeStruct(piece, jnp.float32),
            jax.ShapeDtypeStruct((max(spans - 1, 1),) + piece, jnp.float32),
            jax.ShapeDtypeStruct((8, own), jnp.float32),
        ],
        in_specs=[pl.BlockSpec(memory_space=pl.ANY)] + [vmem] * (2 + spans + shares),
        out_specs=[vmem] * 3,
        scratch_shapes=[
            pltpu.VMEM(((frames + spans) * latent, len(cases) * LANES), jnp.bfloat16),
            pltpu.VMEM((frames + 2, 9, latent, pixels), jnp.bfloat16),
            pltpu.VMEM((frames, pixels, CH), jnp.float32),
            pltpu.VMEM((frames, pixels + 2 * TSIDE, CH), jnp.bfloat16),
            pltpu.VMEM((3 * CH, 9 * lanes), jnp.bfloat16),
            pltpu.VMEM((3, frames, pixels, lanes), jnp.float32),
            pltpu.VMEM((8 * (frames + 1), own), jnp.float32),
            pltpu.VMEM((2, 8, CH), jnp.float32),
            pltpu.VMEM((2, 8, lanes), jnp.float32),
            pltpu.SemaphoreType.DMA((27,)),
        ],
        compiler_params=pltpu.CompilerParams(vmem_limit_bytes=VMEM_BYTES),
        cost_estimate=pl.CostEstimate(
            flops=2 * frames * pixels * 27 * CH * lanes, bytes_accessed=8_000_000, transcendentals=0
        ),
    )(w_mid, table, order, *latents_all, *w_in_own, *w_in_all)
    total = kept
    for turn in range(shares):
        for swap in range(spans):
            if turn or swap:
                pairs = [
                    (c * spans + m, (c + turn) % shares * spans + (m + swap) % spans)
                    for c in range(shares)
                    for m in range(spans)
                ]
                piece = sent[swap - 1] if swap else kept
                total = total + lax.ppermute(piece, ("chan", "tm"), pairs)
    numer = total[0]
    for number, (down, across) in enumerate(cases):
        steps = down * GRID_X + across
        if steps and steps < tiles:
            numer = numer + shifted(total[number], "tile", steps)
    return jnp.transpose(numer / denom[0][None, None, :], (1, 0, 2))


def solution(mesh):
    placed = (
        P("tm", "groups", "tile"),
        P("groups"),
        P(None, None, "chan"),
        P("chan"),
        P("chan"),
        P(None, None, "chan"),
        P("chan"),
        P("chan"),
        P(None, "chan"),
        P("groups", None),
    )
    whole_lanes = (
        CH % (mesh.shape["chan"] * mesh.shape["tm"] * LANES) == 0
        and mesh.shape["chan"] <= mesh.shape["tile"]
    )
    return jax.shard_map(
        lanes_body if whole_lanes else general_body,
        mesh=mesh,
        in_specs=placed,
        out_specs=P("tm", "groups", "tile"),
        check_vma=False,
    )
```

```python
import functools

import jax
import jax.numpy as jnp
from jax import lax
from jax.experimental import pallas as pl
from jax.experimental.pallas import tpu as pltpu
from jax.sharding import PartitionSpec as P

CH = 512
GROUPS = 32
TSIDE = 16
STRIDE = 12
GRID_X = 4

EPSILON = 1e-06
LANES = 128
VMEM_BYTES = 48 * 1024 * 1024


def shifted(value, axis, steps):
    count = lax.axis_size(axis)
    leading, last = (max(0, -steps), min(count, count - steps))
    return lax.ppermute(value, axis, [(source, source + steps) for source in range(leading, last)])


def window_index(tile_id, tiles):
    slots = jnp.arange(TSIDE * TSIDE, dtype=jnp.int32)
    row = tile_id // GRID_X * STRIDE + slots // TSIDE
    col = tile_id % GRID_X * STRIDE + slots % TSIDE
    valid = (row < tiles // GRID_X * STRIDE) & (col < GRID_X * STRIDE)
    block = row // STRIDE * GRID_X + col // STRIDE
    index = block * (STRIDE * STRIDE) + row % STRIDE * STRIDE + col % STRIDE
    return (jnp.where(valid, index, 0), valid)


def causal_conv(extended, weights, frames, side):
    pixels = side * side
    rows = jnp.arange(pixels, dtype=jnp.int32) // side
    cols = jnp.arange(pixels, dtype=jnp.int32) % side
    total = jnp.zeros((frames, weights.shape[2], pixels), jnp.float32)
    for depth in range(3):
        window = extended[depth : depth + frames]
        for down in range(3):
            for across in range(3):
                offset = (down - 1) * side + (across - 1)
                inside = (
                    (rows + down - 1 >= 0)
                    & (rows + down - 1 < side)
                    & (cols + across - 1 >= 0)
                    & (cols + across - 1 < side)
                )
                moved = jnp.roll(window, -offset, axis=2)
                moved = jnp.where(inside[None, None, :], moved, jnp.zeros_like(moved))
                total = total + jnp.einsum(
                    "fcp,co->fop",
                    moved,
                    weights[9 * depth + 3 * down + across],
                    preferred_element_type=jnp.float32,
                )
    return total


def with_history(values):
    frames = values.shape[0]
    earlier = shifted(values[frames - 2 :], "tm", 1)
    return jnp.concatenate([earlier, values], axis=0)


def normalize(values, gain, shift, total_frames):
    frames, chans, pixels = values.shape
    width = CH // GROUPS
    grouped = values.reshape(frames, chans // width, width, pixels)
    sums = jnp.sum(grouped, axis=(0, 2, 3))
    squares = jnp.sum(grouped * grouped, axis=(0, 2, 3))
    sums, squares = lax.psum((sums, squares), "tm")
    count = total_frames * width * pixels
    mean = sums / count
    variance = squares / count - mean * mean
    scale = lax.rsqrt(variance + EPSILON)
    normed = (grouped - mean[None, :, None, None]) * scale[None, :, None, None]
    normed = normed.reshape(frames, chans, pixels) * gain[None, :, None] + shift[None, :, None]
    return jax.nn.silu(normed).astype(jnp.bfloat16)


def spread(color, weight, index, total_pixels):
    numer = (
        jnp.zeros((color.shape[0], 3, total_pixels), jnp.float32)
        .at[:, :, index]
        .add(color * weight[None, None, :])
    )
    denom = jnp.zeros((total_pixels,), jnp.float32).at[index].add(weight)
    return (numer, denom)


def route_owned(numer, denom, tile_id, own):
    frames = numer.shape[0]
    margin = (GRID_X + 1) * own
    numer_wide = jnp.concatenate([numer, jnp.zeros((frames, 3, margin), jnp.float32)], axis=2)
    denom_wide = jnp.concatenate([denom, jnp.zeros((margin,), jnp.float32)], axis=0)
    first_pixel = tile_id * own

    def block_at(offset):
        start_pixel = first_pixel + offset * own
        return (
            lax.dynamic_slice_in_dim(numer_wide, start_pixel, own, 2),
            lax.dynamic_slice_in_dim(denom_wide, start_pixel, own, 0),
        )

    owned_numer, owned_denom = block_at(0)
    for offset in (1, GRID_X, GRID_X + 1):
        piece_numer, piece_denom = block_at(offset)
        got_numer, got_denom = shifted((piece_numer, piece_denom), "tile", offset)
        owned_numer = owned_numer + got_numer
        owned_denom = owned_denom + got_denom
    return (owned_numer, owned_denom)


def general_body(
    latents, tile_order, w_in, gain_in, shift_in, w_mid, gain_mid, shift_mid, w_out, blend_weight
):
    frames = latents.shape[0]
    total_frames = frames * lax.axis_size("tm")
    tiles = tile_order.shape[0]
    own = STRIDE * STRIDE
    total_pixels = tiles * own
    tile_id = lax.axis_index("tile")
    index, valid = window_index(tile_id, tiles)
    whole = lax.all_gather(latents, "tile", axis=2, tiled=True)
    blocks = whole.reshape(frames, whole.shape[1], tiles, own)
    image = (
        jnp.zeros_like(blocks)
        .at[:, :, tile_order]
        .set(blocks)
        .reshape(frames, whole.shape[1], total_pixels)
    )
    window = jnp.where(
        valid[None, None, :], jnp.take(image, index, axis=2), jnp.zeros((), jnp.bfloat16)
    )
    first = causal_conv(with_history(window), w_in, frames, TSIDE)
    hidden = normalize(first, gain_in, shift_in, total_frames)
    second = causal_conv(
        lax.all_gather(with_history(hidden), "chan", axis=1, tiled=True), w_mid, frames, TSIDE
    )
    upper = normalize(second, gain_mid, shift_mid, total_frames)
    color = jnp.einsum("oc,fcp->fop", w_out, upper, preferred_element_type=jnp.float32)
    weight = jnp.where(valid, blend_weight[tile_id], jnp.float32(0.0))
    numer, denom = spread(color, weight, index, total_pixels)
    numer, denom = route_owned(numer, denom, tile_id, own)
    numer = lax.psum(numer, "chan")
    return numer / denom[None, None, :]


def block_cases(tiles):
    downs = (0, 1) if tiles // GRID_X > 1 else (0,)
    return [(down, across) for down in downs for across in (0, 1)]


def exact_dot(values, ones):
    rows = values.shape[0]
    high = values.astype(jnp.bfloat16)
    rest = values - high.astype(jnp.float32)
    middle = rest.astype(jnp.bfloat16)
    low = (rest - middle.astype(jnp.float32)).astype(jnp.bfloat16)
    total = jnp.dot(
        jnp.concatenate([high, middle, low], axis=0), ones, preferred_element_type=jnp.float32
    )
    return total[:rows] + total[rows : 2 * rows] + total[2 * rows :]


def group_affine(sums, squares, gain, shift, count):
    lanes = sums.shape[1]
    width = CH // GROUPS
    same = lax.broadcasted_iota(jnp.int32, (lanes, lanes), 0) // width == (
        lax.broadcasted_iota(jnp.int32, (lanes, lanes), 1) // width
    )
    total = exact_dot(
        jnp.concatenate([sums, squares], axis=0), jnp.where(same, 1.0, 0.0).astype(jnp.bfloat16)
    )
    mean = jnp.sum(total[:8], axis=0, keepdims=True) / count
    variance = jnp.sum(total[8:], axis=0, keepdims=True) / count - mean * mean
    scale = gain * lax.rsqrt(variance + EPSILON)
    return 0.5 * scale, 0.5 * (shift - mean * scale)


def silu_of_half(half):
    return half + half * jnp.tanh(half)


def fold(values):
    rows, lanes = values.shape
    return jnp.sum(values.reshape(rows // 8, 8, lanes), axis=0)


def decode_kernel(
    tiles,
    spans,
    shares,
    *refs,
):
    cases = block_cases(tiles)
    refs = list(refs)

    def take(number):
        taken = refs[:number]
        del refs[:number]
        return taken

    w_mid_ref, table_ref, order_ref = take(3)
    latent_refs, w_in_refs = take(spans), take(shares)
    keep_ref, send_ref, denom_ref = take(3)
    chosen, taps, first, hidden, weights, partial, shown_ref, sems = take(8)

    own = denom_ref.shape[1]
    own_frames = keep_ref.shape[2]
    frames = own_frames * spans
    latent, wide = w_in_refs[0].shape[1:]
    rows_in = frames * latent
    rows_own = rows_in // spans
    depth_in = 27 * latent
    pixels = TSIDE * TSIDE
    lanes = partial.shape[3]
    tile_id = lax.axis_index("tile")
    mine = lax.axis_index("tm")
    chan_id = lax.axis_index("chan")

    copies = []
    for tap in range(27):
        copy = pltpu.make_async_copy(w_mid_ref.at[tap], weights.at[tap], sems.at[tap])
        copy.start()
        copies.append(copy)
    part_mine = pl.ds(pl.multiple_of(mine * lanes, LANES), lanes)

    tile_row, tile_col = tile_id // GRID_X, tile_id % GRID_X
    gain_row = rows_own + 2
    w_out_row = gain_row + 2
    blend_row = w_out_row + 3
    order = order_ref[...]
    number_of = lax.broadcasted_iota(jnp.int32, order.shape, 0)
    lane_of = lax.broadcasted_iota(jnp.int32, order.shape, 1)
    rows_all = latent_refs[0].shape[0] // tiles
    for number, (down, across) in enumerate(cases):
        inside = (tile_row + down < tiles // GRID_X) & (tile_col + across < GRID_X)
        wanted = tile_id + down * GRID_X + across
        found = (order == wanted.astype(jnp.float32)) & (lane_of == 0)
        place = jnp.sum(jnp.where(found, number_of.astype(jnp.float32), 0.0))
        turn = (tile_id - place.astype(jnp.int32) + tiles) % tiles
        part = slice(number * LANES, (number + 1) * LANES)
        for steps in range(tiles):

            @pl.when(inside & (turn == steps))
            def _():
                for swap in range(spans):
                    at, tail_at = swap * rows_own, rows_in + swap * latent
                    block = latent_refs[swap][steps * rows_all : (steps + 1) * rows_all]
                    chosen[at : at + rows_own, part] = block[:rows_own]
                    chosen[tail_at : tail_at + latent, part] = block[rows_own : rows_own + latent]

        @pl.when(jnp.logical_not(inside))
        def _():
            chosen[:, part] = jnp.zeros((chosen.shape[0], LANES), chosen.dtype)

    slot = lax.broadcasted_iota(jnp.int32, (1, pixels), 1)
    up, along = slot // TSIDE, slot % TSIDE
    source = lax.broadcasted_iota(jnp.int32, (LANES, pixels), 0)
    tail = own - LANES

    def pick(first_pixel):
        parts = []
        for down, across in cases:
            u, v = up - down * STRIDE, along - across * STRIDE
            good = (u >= 0) & (u < STRIDE) & (v >= 0) & (v < STRIDE)
            wanted = jnp.where(good, u * STRIDE + v - first_pixel, -1)
            parts.append(jnp.where(source == wanted, 1.0, 0.0).astype(jnp.bfloat16))
        return jnp.concatenate(parts, axis=0)

    tails = chosen[rows_in:].astype(jnp.float32)
    width = tails.shape[1]
    turned = [pltpu.roll(tails, (-f * tail) % width, 1) if f else tails for f in range(own_frames)]
    tails = jnp.concatenate(
        [
            turned[f][swap * latent : (swap + 1) * latent]
            for swap in range(spans)
            for f in range(own_frames)
        ],
        axis=0,
    ).astype(jnp.bfloat16)
    in_tail = lax.broadcasted_iota(jnp.int32, tails.shape, 1) % LANES < tail
    tails = jnp.where(in_tail, tails.astype(jnp.float32), 0.0).astype(jnp.bfloat16)
    window = jnp.dot(
        chosen[:rows_in], pick(0), preferred_element_type=jnp.float32
    ) + jnp.dot(tails, pick(LANES), preferred_element_type=jnp.float32)
    taps[0:2] = jnp.zeros((2,) + taps.shape[1:], taps.dtype)
    for b in range(3):
        for e in range(3):
            inside = (
                (up + b - 1 >= 0)
                & (up + b - 1 < TSIDE)
                & (along + e - 1 >= 0)
                & (along + e - 1 < TSIDE)
            )
            offset = (b - 1) * TSIDE + e - 1
            moved = pltpu.roll(window, (-offset) % pixels, 1) if offset else window
            moved = jnp.where(inside, moved, 0.0).astype(jnp.bfloat16)
            for swap in range(spans):
                value = moved[swap * rows_own : (swap + 1) * rows_own]
                span = pl.ds(2 + (mine + swap) % spans * own_frames, own_frames)
                taps[span, 3 * b + e] = value.reshape(own_frames, latent, pixels)

    joined = jnp.concatenate(
        [w_in_refs[s][:27].reshape(depth_in, wide) for s in range(shares)], axis=1
    )
    sums = jnp.zeros((8, CH), jnp.float32)
    squares = jnp.zeros((8, CH), jnp.float32)
    for f in range(frames):
        patch = taps[f : f + 3].reshape(depth_in, pixels)
        value = lax.dot_general(
            patch, joined, (((0,), (0,)), ((), ())), preferred_element_type=jnp.float32
        )
        first[f] = value
        sums = sums + fold(value)
        squares = squares + fold(value * value)
    count = frames * (CH // GROUPS) * pixels
    affine = []
    for s in range(shares):
        at = s * rows_all + rows_own + latent
        table = latent_refs[0][at : at + wide // LANES * 4].astype(jnp.float32)
        pieces = [table[4 * lane : 4 * lane + 4] for lane in range(wide // LANES)]
        table = jnp.concatenate([part[0:2] + part[2:4] for part in pieces], axis=1)
        part = slice(s * wide, (s + 1) * wide)
        affine.append(
            group_affine(sums[:, part], squares[:, part], table[0:1], table[1:2], count)
        )
    channels = [
        pl.ds(pl.multiple_of((chan_id + s) % shares * wide, LANES), wide) for s in range(shares)
    ]

    def hide(f):
        edge = jnp.zeros((TSIDE, CH), jnp.bfloat16)
        hidden[f, 0:TSIDE] = edge
        hidden[f, TSIDE + pixels : 2 * TSIDE + pixels] = edge
        for s in range(shares):
            scale, bias = affine[s]
            value = first[f, :, s * wide : (s + 1) * wide] * scale + bias
            hidden[f, TSIDE : TSIDE + pixels, channels[s]] = silu_of_half(value).astype(
                jnp.bfloat16
            )

    def convolve(start, several, depth_taps):
        lhs = jnp.concatenate(
            [
                hidden[start : start + several, b * TSIDE : b * TSIDE + pixels].reshape(
                    several * pixels, CH
                )
                for b in range(3)
            ],
            axis=1,
        )
        low = depth_taps[0] * 3 * lanes
        rhs = jnp.concatenate(
            [
                jnp.concatenate(
                    [
                        weights[9 * a + 3 * b + e, :, part_mine]
                        for a in depth_taps
                        for e in range(3)
                    ],
                    axis=1,
                )
                for b in range(3)
            ],
            axis=0,
        )
        product = jnp.dot(lhs, rhs, preferred_element_type=jnp.float32)
        for a in depth_taps:
            for e in range(3):
                at = (3 * a + e) * lanes - low
                for f in range(several):
                    target = start + f + 2 - a
                    value = product[f * pixels : (f + 1) * pixels, at : at + lanes]
                    if start + f == max(target - 2, 0):
                        partial[e, target] = value
                    else:
                        partial[e, target] += value

    column = lax.broadcasted_iota(jnp.int32, (pixels, lanes), 0) % TSIDE
    total = [jnp.zeros((8, lanes), jnp.float32)] * 2

    def gather(f):
        left = jnp.where(column == 0, 0.0, pltpu.roll(partial[0, f], 1, 0))
        right = jnp.where(column == TSIDE - 1, 0.0, pltpu.roll(partial[2, f], pixels - 1, 0))
        value = partial[1, f] + left + right
        partial[1, f] = value
        total[0] = total[0] + fold(value)
        total[1] = total[1] + fold(value * value)

    together = 3
    groups = [
        range(f, min(f + together, frames - 2)) for f in range(0, frames - 2, together)
    ]
    groups += [range(f, f + 1) for f in range(groups[-1].stop, frames)]
    for copy in copies:
        copy.wait()
    for f in groups[0]:
        hide(f)
    for number, group in enumerate(groups):
        if number + 1 < len(groups):
            for f in groups[number + 1]:
                hide(f)
        convolve(
            group.start,
            len(group),
            tuple(a for a in range(3) if group.stop - 1 + 2 - a < frames),
        )
        if number:
            for f in groups[number - 1]:
                gather(f)
    for f in groups[-1]:
        gather(f)

    part = pl.ds(pl.multiple_of(mine * lanes, LANES), lanes)
    scale, bias = group_affine(
        total[0],
        total[1],
        table_ref[gain_row : gain_row + 1, part],
        table_ref[gain_row + 1 : gain_row + 2, part],
        count,
    )
    blend = table_ref[pl.ds(blend_row + tile_id, 1), :]
    blend = jnp.where(
        (tile_row * STRIDE + up < tiles // GRID_X * STRIDE)
        & (tile_col * STRIDE + along < GRID_X * STRIDE),
        blend,
        0.0,
    )
    w_out = jnp.concatenate(
        [table_ref[w_out_row : w_out_row + 3, part], jnp.zeros((5, lanes), jnp.float32)], axis=0
    ).astype(jnp.bfloat16)
    colors = []
    for f in range(frames):
        upper = silu_of_half(partial[1, f] * scale + bias).astype(jnp.bfloat16)
        color = lax.dot_general(
            w_out, upper, (((1,), (1,)), ((), ())), preferred_element_type=jnp.float32
        )
        colors.append(color * blend)
    colors = jnp.concatenate(colors, axis=0)

    slot_in = lax.broadcasted_iota(jnp.int32, (pixels, own), 0)
    pixel = lax.broadcasted_iota(jnp.int32, (pixels, own), 1)
    denom = jnp.zeros((8, own), jnp.float32)
    for number, (down, across) in enumerate(cases):
        u, v = slot_in // TSIDE - down * STRIDE, slot_in % TSIDE - across * STRIDE
        good = (u >= 0) & (u < STRIDE) & (v >= 0) & (v < STRIDE) & (u * STRIDE + v == pixel)
        shown = jnp.where(good, 1.0, 0.0).astype(jnp.bfloat16)
        inside = (tile_row >= down) & (tile_col >= across)
        other = jnp.maximum(tile_id - down * GRID_X - across, 0)
        weight = jnp.where(inside, table_ref[pl.ds(blend_row + other, 1), :], 0.0)
        piece = exact_dot(
            jnp.concatenate([colors, jnp.broadcast_to(weight, (8, pixels))], axis=0), shown
        )
        denom = denom + piece[8 * frames :]
        shown_ref[...] = piece
        for swap in range(spans):
            target = keep_ref if swap == 0 else send_ref.at[swap - 1]
            base = (mine + swap) % spans * own_frames * 8
            for at in range(own_frames):
                for o in range(3):
                    target[number, o, at : at + 1, :] = shown_ref[pl.ds(base + 8 * at + o, 1), :]

    denom_ref[...] = denom


def from_ring(value, axis):
    count = lax.axis_size(axis)
    return [
        lax.ppermute(value, axis, [((d + turn) % count, d) for d in range(count)])
        for turn in range(1, count)
    ]


def small_table(*values):
    values = [value.reshape(-1, value.shape[-1]) for value in values]
    wide = max(value.shape[1] for value in values)
    height = sum(value.shape[0] for value in values)
    total, row = 0.0, 0
    for value in values:
        below = height - row - value.shape[0]
        value = jnp.pad(value.astype(jnp.float32), ((row, below), (0, wide - value.shape[1])))
        total = total + value
        row = height - below
    return total


def exchange_latents(frames, latent, own, table):
    tiles, shares = lax.axis_size("tile"), lax.axis_size("chan")
    tail = own - LANES
    height = frames * latent
    mine = table[:height, :own].astype(jnp.bfloat16)
    tails = sum(
        jnp.pad(
            mine[f * latent : (f + 1) * latent, LANES:],
            ((0, 0), (tail * f, LANES - tail * (f + 1))),
        )
        for f in range(frames)
    )
    affine = table[height : height + 2]
    high = lax.reduce_precision(affine, 8, 7)
    low = lax.reduce_precision(affine - high, 8, 7)
    affine = jnp.concatenate([high, low], axis=0).astype(jnp.bfloat16)
    rows = [affine[:, at : at + LANES] for at in range(0, affine.shape[1], LANES)]
    rows = jnp.concatenate(rows, axis=0)
    rows = jnp.pad(rows, ((0, -rows.shape[0] % 16), (0, 0)))
    message = jnp.concatenate([mine[:, :LANES], tails, rows], axis=0)
    got = [message]
    for steps in range(1, tiles):
        turn = steps if steps < shares else 0
        pairs = [
            (t * shares + (c + turn) % shares, (t + steps) % tiles * shares + c)
            for t in range(tiles)
            for c in range(shares)
        ]
        got.append(lax.ppermute(message, ("tile", "chan"), pairs))
    stack = jnp.concatenate(got, axis=0)
    return [stack] + from_ring(stack, "tm")


def lanes_body(
    latents, tile_order, w_in, gain_in, shift_in, w_mid, gain_mid, shift_mid, w_out, blend_weight
):
    own_frames, latent, own = latents.shape
    spans = lax.axis_size("tm")
    shares = lax.axis_size("chan")
    frames = own_frames * spans
    tiles = tile_order.shape[0]
    wide = w_in.shape[2]
    lanes = wide // spans
    pixels = TSIDE * TSIDE
    cases = block_cases(tiles)

    w_in_all = [(from_ring(other, "tm") or [other])[0] for other in from_ring(w_in, "chan")]
    table = lax.optimization_barrier(
        small_table(
            latents.reshape(own_frames * latent, own),
            gain_in,
            shift_in,
            gain_mid,
            shift_mid,
            w_out,
            blend_weight,
        )
    )
    latents_all = exchange_latents(own_frames, latent, own, table)
    _, w_in, tile_order = lax.optimization_barrier((table, w_in, tile_order))
    order = jnp.broadcast_to(tile_order.astype(jnp.float32)[:, None], (tiles, LANES))
    w_in_own = from_ring(w_in, "tm")[:1] or [w_in]

    vmem = pl.BlockSpec(memory_space=pltpu.VMEM)
    piece = (len(cases), 3, own_frames, own)
    kept, sent, denom = pl.pallas_call(
        functools.partial(decode_kernel, tiles, spans, shares),
        out_shape=[
            jax.ShapeDtypeStruct(piece, jnp.float32),
            jax.ShapeDtypeStruct((max(spans - 1, 1),) + piece, jnp.float32),
            jax.ShapeDtypeStruct((8, own), jnp.float32),
        ],
        in_specs=[pl.BlockSpec(memory_space=pl.ANY)] + [vmem] * (2 + spans + shares),
        out_specs=[vmem] * 3,
        scratch_shapes=[
            pltpu.VMEM(((frames + spans) * latent, len(cases) * LANES), jnp.bfloat16),
            pltpu.VMEM((frames + 2, 9, latent, pixels), jnp.bfloat16),
            pltpu.VMEM((frames, pixels, CH), jnp.float32),
            pltpu.VMEM((frames, pixels + 2 * TSIDE, CH), jnp.bfloat16),
            pltpu.VMEM((27, CH, wide), jnp.bfloat16),
            pltpu.VMEM((3, frames, pixels, lanes), jnp.float32),
            pltpu.VMEM((8 * (frames + 1), own), jnp.float32),
            pltpu.SemaphoreType.DMA((27,)),
        ],
        compiler_params=pltpu.CompilerParams(vmem_limit_bytes=VMEM_BYTES),
        cost_estimate=pl.CostEstimate(
            flops=2 * frames * pixels * 27 * CH * lanes, bytes_accessed=8_000_000, transcendentals=0
        ),
    )(w_mid, table, order, *latents_all, *w_in_own, *w_in_all)
    total = kept
    for turn in range(shares):
        for swap in range(spans):
            if turn or swap:
                pairs = [
                    (c * spans + m, (c + turn) % shares * spans + (m + swap) % spans)
                    for c in range(shares)
                    for m in range(spans)
                ]
                piece = sent[swap - 1] if swap else kept
                total = total + lax.ppermute(piece, ("chan", "tm"), pairs)
    numer = total[0]
    for number, (down, across) in enumerate(cases):
        steps = down * GRID_X + across
        if steps and steps < tiles:
            numer = numer + shifted(total[number], "tile", steps)
    return jnp.transpose(numer / denom[0][None, None, :], (1, 0, 2))


def solution(mesh):
    placed = (
        P("tm", "groups", "tile"),
        P("groups"),
        P(None, None, "chan"),
        P("chan"),
        P("chan"),
        P(None, None, "chan"),
        P("chan"),
        P("chan"),
        P(None, "chan"),
        P("groups", None),
    )
    whole_lanes = (
        CH % (mesh.shape["chan"] * mesh.shape["tm"] * LANES) == 0
        and mesh.shape["chan"] <= mesh.shape["tile"]
    )
    return jax.shard_map(
        lanes_body if whole_lanes else general_body,
        mesh=mesh,
        in_specs=placed,
        out_specs=P("tm", "groups", "tile"),
        check_vma=False,
    )
```

```python
import functools

import jax
import jax.numpy as jnp
from jax import lax
from jax.experimental import pallas as pl
from jax.experimental.pallas import tpu as pltpu
from jax.sharding import PartitionSpec as P

CH = 512
GROUPS = 32
TSIDE = 16
STRIDE = 12
GRID_X = 4

EPSILON = 1e-06
LANES = 128
VMEM_BYTES = 48 * 1024 * 1024


def shifted(value, axis, steps):
    count = lax.axis_size(axis)
    leading, last = (max(0, -steps), min(count, count - steps))
    return lax.ppermute(value, axis, [(source, source + steps) for source in range(leading, last)])


def window_index(tile_id, tiles):
    slots = jnp.arange(TSIDE * TSIDE, dtype=jnp.int32)
    row = tile_id // GRID_X * STRIDE + slots // TSIDE
    col = tile_id % GRID_X * STRIDE + slots % TSIDE
    valid = (row < tiles // GRID_X * STRIDE) & (col < GRID_X * STRIDE)
    block = row // STRIDE * GRID_X + col // STRIDE
    index = block * (STRIDE * STRIDE) + row % STRIDE * STRIDE + col % STRIDE
    return (jnp.where(valid, index, 0), valid)


def causal_conv(extended, weights, frames, side):
    pixels = side * side
    rows = jnp.arange(pixels, dtype=jnp.int32) // side
    cols = jnp.arange(pixels, dtype=jnp.int32) % side
    total = jnp.zeros((frames, weights.shape[2], pixels), jnp.float32)
    for depth in range(3):
        window = extended[depth : depth + frames]
        for down in range(3):
            for across in range(3):
                offset = (down - 1) * side + (across - 1)
                inside = (
                    (rows + down - 1 >= 0)
                    & (rows + down - 1 < side)
                    & (cols + across - 1 >= 0)
                    & (cols + across - 1 < side)
                )
                moved = jnp.roll(window, -offset, axis=2)
                moved = jnp.where(inside[None, None, :], moved, jnp.zeros_like(moved))
                total = total + jnp.einsum(
                    "fcp,co->fop",
                    moved,
                    weights[9 * depth + 3 * down + across],
                    preferred_element_type=jnp.float32,
                )
    return total


def with_history(values):
    frames = values.shape[0]
    earlier = shifted(values[frames - 2 :], "tm", 1)
    return jnp.concatenate([earlier, values], axis=0)


def normalize(values, gain, shift, total_frames):
    frames, chans, pixels = values.shape
    width = CH // GROUPS
    grouped = values.reshape(frames, chans // width, width, pixels)
    sums = jnp.sum(grouped, axis=(0, 2, 3))
    squares = jnp.sum(grouped * grouped, axis=(0, 2, 3))
    sums, squares = lax.psum((sums, squares), "tm")
    count = total_frames * width * pixels
    mean = sums / count
    variance = squares / count - mean * mean
    scale = lax.rsqrt(variance + EPSILON)
    normed = (grouped - mean[None, :, None, None]) * scale[None, :, None, None]
    normed = normed.reshape(frames, chans, pixels) * gain[None, :, None] + shift[None, :, None]
    return jax.nn.silu(normed).astype(jnp.bfloat16)


def spread(color, weight, index, total_pixels):
    numer = (
        jnp.zeros((color.shape[0], 3, total_pixels), jnp.float32)
        .at[:, :, index]
        .add(color * weight[None, None, :])
    )
    denom = jnp.zeros((total_pixels,), jnp.float32).at[index].add(weight)
    return (numer, denom)


def route_owned(numer, denom, tile_id, own):
    frames = numer.shape[0]
    margin = (GRID_X + 1) * own
    numer_wide = jnp.concatenate([numer, jnp.zeros((frames, 3, margin), jnp.float32)], axis=2)
    denom_wide = jnp.concatenate([denom, jnp.zeros((margin,), jnp.float32)], axis=0)
    first_pixel = tile_id * own

    def block_at(offset):
        start_pixel = first_pixel + offset * own
        return (
            lax.dynamic_slice_in_dim(numer_wide, start_pixel, own, 2),
            lax.dynamic_slice_in_dim(denom_wide, start_pixel, own, 0),
        )

    owned_numer, owned_denom = block_at(0)
    for offset in (1, GRID_X, GRID_X + 1):
        piece_numer, piece_denom = block_at(offset)
        got_numer, got_denom = shifted((piece_numer, piece_denom), "tile", offset)
        owned_numer = owned_numer + got_numer
        owned_denom = owned_denom + got_denom
    return (owned_numer, owned_denom)


def general_body(
    latents, tile_order, w_in, gain_in, shift_in, w_mid, gain_mid, shift_mid, w_out, blend_weight
):
    frames = latents.shape[0]
    total_frames = frames * lax.axis_size("tm")
    tiles = tile_order.shape[0]
    own = STRIDE * STRIDE
    total_pixels = tiles * own
    tile_id = lax.axis_index("tile")
    index, valid = window_index(tile_id, tiles)
    whole = lax.all_gather(latents, "tile", axis=2, tiled=True)
    blocks = whole.reshape(frames, whole.shape[1], tiles, own)
    image = (
        jnp.zeros_like(blocks)
        .at[:, :, tile_order]
        .set(blocks)
        .reshape(frames, whole.shape[1], total_pixels)
    )
    window = jnp.where(
        valid[None, None, :], jnp.take(image, index, axis=2), jnp.zeros((), jnp.bfloat16)
    )
    first = causal_conv(with_history(window), w_in, frames, TSIDE)
    hidden = normalize(first, gain_in, shift_in, total_frames)
    second = causal_conv(
        lax.all_gather(with_history(hidden), "chan", axis=1, tiled=True), w_mid, frames, TSIDE
    )
    upper = normalize(second, gain_mid, shift_mid, total_frames)
    color = jnp.einsum("oc,fcp->fop", w_out, upper, preferred_element_type=jnp.float32)
    weight = jnp.where(valid, blend_weight[tile_id], jnp.float32(0.0))
    numer, denom = spread(color, weight, index, total_pixels)
    numer, denom = route_owned(numer, denom, tile_id, own)
    numer = lax.psum(numer, "chan")
    return numer / denom[None, None, :]


def block_cases(tiles):
    downs = (0, 1) if tiles // GRID_X > 1 else (0,)
    return [(down, across) for down in downs for across in (0, 1)]


def exact_dot(values, ones):
    rows = values.shape[0]
    high = values.astype(jnp.bfloat16)
    rest = values - high.astype(jnp.float32)
    middle = rest.astype(jnp.bfloat16)
    low = (rest - middle.astype(jnp.float32)).astype(jnp.bfloat16)
    total = jnp.dot(
        jnp.concatenate([high, middle, low], axis=0), ones, preferred_element_type=jnp.float32
    )
    return total[:rows] + total[rows : 2 * rows] + total[2 * rows :]


def group_affine(sums, squares, gain, shift, count):
    lanes = sums.shape[1]
    width = CH // GROUPS
    same = lax.broadcasted_iota(jnp.int32, (lanes, lanes), 0) // width == (
        lax.broadcasted_iota(jnp.int32, (lanes, lanes), 1) // width
    )
    total = exact_dot(
        jnp.concatenate([sums, squares], axis=0), jnp.where(same, 1.0, 0.0).astype(jnp.bfloat16)
    )
    mean = jnp.sum(total[:8], axis=0, keepdims=True) / count
    variance = jnp.sum(total[8:], axis=0, keepdims=True) / count - mean * mean
    scale = gain * lax.rsqrt(variance + EPSILON)
    return 0.5 * scale, 0.5 * (shift - mean * scale)


def silu_of_half(half):
    return half + half * jnp.tanh(half)


def fold(values):
    rows, lanes = values.shape
    return jnp.sum(values.reshape(rows // 8, 8, lanes), axis=0)


def decode_kernel(
    tiles,
    spans,
    shares,
    *refs,
):
    cases = block_cases(tiles)
    refs = list(refs)

    def take(number):
        taken = refs[:number]
        del refs[:number]
        return taken

    w_mid_ref, table_ref, order_ref = take(3)
    latent_refs, w_in_refs = take(spans), take(shares)
    keep_ref, send_ref, denom_ref = take(3)
    chosen, taps, first, hidden, weights, partial, shown_ref, sems = take(8)

    own = denom_ref.shape[1]
    own_frames = keep_ref.shape[2]
    frames = own_frames * spans
    latent, wide = w_in_refs[0].shape[1:]
    rows_in = frames * latent
    rows_own = rows_in // spans
    depth_in = 27 * latent
    pixels = TSIDE * TSIDE
    lanes = partial.shape[3]
    tile_id = lax.axis_index("tile")
    mine = lax.axis_index("tm")
    chan_id = lax.axis_index("chan")

    copies = [[], [], []]
    for a in (2, 1, 0):
        for b in range(3):
            for e in range(3):
                tap = 9 * a + 3 * b + e
                copy = pltpu.make_async_copy(
                    w_mid_ref.at[tap, :, pl.ds(pl.multiple_of(mine * lanes, LANES), lanes)],
                    weights.at[pl.ds(b * CH, CH), pl.ds((3 * a + e) * lanes, lanes)],
                    sems.at[tap],
                )
                copy.start()
                copies[a].append(copy)

    tile_row, tile_col = tile_id // GRID_X, tile_id % GRID_X
    gain_row = rows_own + 2
    w_out_row = gain_row + 2
    blend_row = w_out_row + 3
    order = order_ref[...]
    number_of = lax.broadcasted_iota(jnp.int32, order.shape, 0)
    lane_of = lax.broadcasted_iota(jnp.int32, order.shape, 1)
    rows_all = latent_refs[0].shape[0] // tiles
    for number, (down, across) in enumerate(cases):
        inside = (tile_row + down < tiles // GRID_X) & (tile_col + across < GRID_X)
        wanted = tile_id + down * GRID_X + across
        found = (order == wanted.astype(jnp.float32)) & (lane_of == 0)
        place = jnp.sum(jnp.where(found, number_of.astype(jnp.float32), 0.0))
        turn = (tile_id - place.astype(jnp.int32) + tiles) % tiles
        part = slice(number * LANES, (number + 1) * LANES)
        for steps in range(tiles):

            @pl.when(inside & (turn == steps))
            def _():
                for swap in range(spans):
                    at, tail_at = swap * rows_own, rows_in + swap * latent
                    block = latent_refs[swap][steps * rows_all : (steps + 1) * rows_all]
                    chosen[at : at + rows_own, part] = block[:rows_own]
                    chosen[tail_at : tail_at + latent, part] = block[rows_own : rows_own + latent]

        @pl.when(jnp.logical_not(inside))
        def _():
            chosen[:, part] = jnp.zeros((chosen.shape[0], LANES), chosen.dtype)

    slot = lax.broadcasted_iota(jnp.int32, (1, pixels), 1)
    up, along = slot // TSIDE, slot % TSIDE
    source = lax.broadcasted_iota(jnp.int32, (LANES, pixels), 0)
    tail = own - LANES

    def pick(first_pixel):
        parts = []
        for down, across in cases:
            u, v = up - down * STRIDE, along - across * STRIDE
            good = (u >= 0) & (u < STRIDE) & (v >= 0) & (v < STRIDE)
            wanted = jnp.where(good, u * STRIDE + v - first_pixel, -1)
            parts.append(jnp.where(source == wanted, 1.0, 0.0).astype(jnp.bfloat16))
        return jnp.concatenate(parts, axis=0)

    tails = chosen[rows_in:].astype(jnp.float32)
    width = tails.shape[1]
    turned = [pltpu.roll(tails, (-f * tail) % width, 1) if f else tails for f in range(own_frames)]
    tails = jnp.concatenate(
        [
            turned[f][swap * latent : (swap + 1) * latent]
            for swap in range(spans)
            for f in range(own_frames)
        ],
        axis=0,
    ).astype(jnp.bfloat16)
    in_tail = lax.broadcasted_iota(jnp.int32, tails.shape, 1) % LANES < tail
    tails = jnp.where(in_tail, tails.astype(jnp.float32), 0.0).astype(jnp.bfloat16)
    window = jnp.dot(
        chosen[:rows_in], pick(0), preferred_element_type=jnp.float32
    ) + jnp.dot(tails, pick(LANES), preferred_element_type=jnp.float32)
    taps[0:2] = jnp.zeros((2,) + taps.shape[1:], taps.dtype)
    for b in range(3):
        for e in range(3):
            inside = (
                (up + b - 1 >= 0)
                & (up + b - 1 < TSIDE)
                & (along + e - 1 >= 0)
                & (along + e - 1 < TSIDE)
            )
            offset = (b - 1) * TSIDE + e - 1
            moved = pltpu.roll(window, (-offset) % pixels, 1) if offset else window
            moved = jnp.where(inside, moved, 0.0).astype(jnp.bfloat16)
            for swap in range(spans):
                value = moved[swap * rows_own : (swap + 1) * rows_own]
                span = pl.ds(2 + (mine + swap) % spans * own_frames, own_frames)
                taps[span, 3 * b + e] = value.reshape(own_frames, latent, pixels)

    joined = jnp.concatenate(
        [w_in_refs[s][:27].reshape(depth_in, wide) for s in range(shares)], axis=1
    )
    sums = jnp.zeros((8, CH), jnp.float32)
    squares = jnp.zeros((8, CH), jnp.float32)
    for f in range(frames):
        patch = taps[f : f + 3].reshape(depth_in, pixels)
        value = lax.dot_general(
            patch, joined, (((0,), (0,)), ((), ())), preferred_element_type=jnp.float32
        )
        first[f] = value
        sums = sums + fold(value)
        squares = squares + fold(value * value)
    count = frames * (CH // GROUPS) * pixels
    affine = []
    for s in range(shares):
        at = s * rows_all + rows_own + latent
        table = latent_refs[0][at : at + wide // LANES * 4].astype(jnp.float32)
        pieces = [table[4 * lane : 4 * lane + 4] for lane in range(wide // LANES)]
        table = jnp.concatenate([part[0:2] + part[2:4] for part in pieces], axis=1)
        part = slice(s * wide, (s + 1) * wide)
        affine.append(
            group_affine(sums[:, part], squares[:, part], table[0:1], table[1:2], count)
        )
    channels = [
        pl.ds(pl.multiple_of((chan_id + s) % shares * wide, LANES), wide) for s in range(shares)
    ]

    def hide(f):
        edge = jnp.zeros((TSIDE, CH), jnp.bfloat16)
        hidden[f, 0:TSIDE] = edge
        hidden[f, TSIDE + pixels : 2 * TSIDE + pixels] = edge
        for s in range(shares):
            scale, bias = affine[s]
            value = first[f, :, s * wide : (s + 1) * wide] * scale + bias
            hidden[f, TSIDE : TSIDE + pixels, channels[s]] = silu_of_half(value).astype(
                jnp.bfloat16
            )

    begun = set()

    def convolve(start, several, depth_taps):
        lhs = jnp.concatenate(
            [
                hidden[start : start + several, b * TSIDE : b * TSIDE + pixels].reshape(
                    several * pixels, CH
                )
                for b in range(3)
            ],
            axis=1,
        )
        low, high = depth_taps[0] * 3 * lanes, (depth_taps[-1] + 1) * 3 * lanes
        product = jnp.dot(lhs, weights[:, low:high], preferred_element_type=jnp.float32)
        for a in depth_taps:
            for e in range(3):
                at = (3 * a + e) * lanes - low
                for f in range(several):
                    target = start + f + 2 - a
                    value = product[f * pixels : (f + 1) * pixels, at : at + lanes]
                    if (e, target) in begun:
                        partial[e, target] += value
                    else:
                        partial[e, target] = value
                        begun.add((e, target))

    column = lax.broadcasted_iota(jnp.int32, (pixels, lanes), 0) % TSIDE
    total = [jnp.zeros((8, lanes), jnp.float32)] * 2

    def gather(f):
        left = jnp.where(column == 0, 0.0, pltpu.roll(partial[0, f], 1, 0))
        right = jnp.where(column == TSIDE - 1, 0.0, pltpu.roll(partial[2, f], pixels - 1, 0))
        value = partial[1, f] + left + right
        partial[1, f] = value
        total[0] = total[0] + fold(value)
        total[1] = total[1] + fold(value * value)

    together = 3
    groups = [
        range(f, min(f + together, frames - 2)) for f in range(0, frames - 2, together)
    ]
    groups += [range(f, f + 1) for f in range(groups[-1].stop, frames)]
    for f in groups[0]:
        hide(f)
    for number, group in enumerate(groups):
        if number + 1 < len(groups):
            for f in groups[number + 1]:
                hide(f)
        depth_taps = tuple(a for a in range(3) if group.stop - 1 + 2 - a < frames)
        parts = [depth_taps] if number else [depth_taps[2:], depth_taps[:2]]
        for part in parts:
            if number == 0:
                for copy in sum((copies[a] for a in part), []):
                    copy.wait()
            convolve(group.start, len(group), part)
        if number:
            for f in groups[number - 1]:
                gather(f)
    for f in groups[-1]:
        gather(f)

    part = pl.ds(pl.multiple_of(mine * lanes, LANES), lanes)
    scale, bias = group_affine(
        total[0],
        total[1],
        table_ref[gain_row : gain_row + 1, part],
        table_ref[gain_row + 1 : gain_row + 2, part],
        count,
    )
    blend = table_ref[pl.ds(blend_row + tile_id, 1), :]
    blend = jnp.where(
        (tile_row * STRIDE + up < tiles // GRID_X * STRIDE)
        & (tile_col * STRIDE + along < GRID_X * STRIDE),
        blend,
        0.0,
    )
    w_out = jnp.concatenate(
        [table_ref[w_out_row : w_out_row + 3, part], jnp.zeros((5, lanes), jnp.float32)], axis=0
    ).astype(jnp.bfloat16)
    colors = []
    for f in range(frames):
        upper = silu_of_half(partial[1, f] * scale + bias).astype(jnp.bfloat16)
        color = lax.dot_general(
            w_out, upper, (((1,), (1,)), ((), ())), preferred_element_type=jnp.float32
        )
        colors.append(color * blend)
    colors = jnp.concatenate(colors, axis=0)

    slot_in = lax.broadcasted_iota(jnp.int32, (pixels, own), 0)
    pixel = lax.broadcasted_iota(jnp.int32, (pixels, own), 1)
    denom = jnp.zeros((8, own), jnp.float32)
    for number, (down, across) in enumerate(cases):
        u, v = slot_in // TSIDE - down * STRIDE, slot_in % TSIDE - across * STRIDE
        good = (u >= 0) & (u < STRIDE) & (v >= 0) & (v < STRIDE) & (u * STRIDE + v == pixel)
        shown = jnp.where(good, 1.0, 0.0).astype(jnp.bfloat16)
        inside = (tile_row >= down) & (tile_col >= across)
        other = jnp.maximum(tile_id - down * GRID_X - across, 0)
        weight = jnp.where(inside, table_ref[pl.ds(blend_row + other, 1), :], 0.0)
        piece = exact_dot(
            jnp.concatenate([colors, jnp.broadcast_to(weight, (8, pixels))], axis=0), shown
        )
        denom = denom + piece[8 * frames :]
        shown_ref[...] = piece
        for swap in range(spans):
            target = keep_ref if swap == 0 else send_ref.at[swap - 1]
            base = (mine + swap) % spans * own_frames * 8
            for at in range(own_frames):
                for o in range(3):
                    target[number, o, at : at + 1, :] = shown_ref[pl.ds(base + 8 * at + o, 1), :]

    denom_ref[...] = denom


def from_ring(value, axis):
    count = lax.axis_size(axis)
    return [
        lax.ppermute(value, axis, [((d + turn) % count, d) for d in range(count)])
        for turn in range(1, count)
    ]


def small_table(*values):
    values = [value.reshape(-1, value.shape[-1]) for value in values]
    wide = max(value.shape[1] for value in values)
    height = sum(value.shape[0] for value in values)
    total, row = 0.0, 0
    for value in values:
        below = height - row - value.shape[0]
        value = jnp.pad(value.astype(jnp.float32), ((row, below), (0, wide - value.shape[1])))
        total = total + value
        row = height - below
    return total


def exchange_latents(frames, latent, own, table):
    tiles, shares = lax.axis_size("tile"), lax.axis_size("chan")
    tail = own - LANES
    height = frames * latent
    mine = table[:height, :own].astype(jnp.bfloat16)
    tails = sum(
        jnp.pad(
            mine[f * latent : (f + 1) * latent, LANES:],
            ((0, 0), (tail * f, LANES - tail * (f + 1))),
        )
        for f in range(frames)
    )
    affine = table[height : height + 2]
    high = lax.reduce_precision(affine, 8, 7)
    low = lax.reduce_precision(affine - high, 8, 7)
    affine = jnp.concatenate([high, low], axis=0).astype(jnp.bfloat16)
    rows = [affine[:, at : at + LANES] for at in range(0, affine.shape[1], LANES)]
    rows = jnp.concatenate(rows, axis=0)
    rows = jnp.pad(rows, ((0, -rows.shape[0] % 16), (0, 0)))
    message = jnp.concatenate([mine[:, :LANES], tails, rows], axis=0)
    got = [message]
    for steps in range(1, tiles):
        turn = steps if steps < shares else 0
        pairs = [
            (t * shares + (c + turn) % shares, (t + steps) % tiles * shares + c)
            for t in range(tiles)
            for c in range(shares)
        ]
        got.append(lax.ppermute(message, ("tile", "chan"), pairs))
    stack = jnp.concatenate(got, axis=0)
    return [stack] + from_ring(stack, "tm")


def lanes_body(
    latents, tile_order, w_in, gain_in, shift_in, w_mid, gain_mid, shift_mid, w_out, blend_weight
):
    own_frames, latent, own = latents.shape
    spans = lax.axis_size("tm")
    shares = lax.axis_size("chan")
    frames = own_frames * spans
    tiles = tile_order.shape[0]
    wide = w_in.shape[2]
    lanes = wide // spans
    pixels = TSIDE * TSIDE
    cases = block_cases(tiles)

    w_in_all = [(from_ring(other, "tm") or [other])[0] for other in from_ring(w_in, "chan")]
    table = lax.optimization_barrier(
        small_table(
            latents.reshape(own_frames * latent, own),
            gain_in,
            shift_in,
            gain_mid,
            shift_mid,
            w_out,
            blend_weight,
        )
    )
    latents_all = exchange_latents(own_frames, latent, own, table)
    _, w_in, tile_order = lax.optimization_barrier((table, w_in, tile_order))
    order = jnp.broadcast_to(tile_order.astype(jnp.float32)[:, None], (tiles, LANES))
    w_in_own = from_ring(w_in, "tm")[:1] or [w_in]

    vmem = pl.BlockSpec(memory_space=pltpu.VMEM)
    piece = (len(cases), 3, own_frames, own)
    kept, sent, denom = pl.pallas_call(
        functools.partial(decode_kernel, tiles, spans, shares),
        out_shape=[
            jax.ShapeDtypeStruct(piece, jnp.float32),
            jax.ShapeDtypeStruct((max(spans - 1, 1),) + piece, jnp.float32),
            jax.ShapeDtypeStruct((8, own), jnp.float32),
        ],
        in_specs=[pl.BlockSpec(memory_space=pl.ANY)] + [vmem] * (2 + spans + shares),
        out_specs=[vmem] * 3,
        scratch_shapes=[
            pltpu.VMEM(((frames + spans) * latent, len(cases) * LANES), jnp.bfloat16),
            pltpu.VMEM((frames + 2, 9, latent, pixels), jnp.bfloat16),
            pltpu.VMEM((frames, pixels, CH), jnp.float32),
            pltpu.VMEM((frames, pixels + 2 * TSIDE, CH), jnp.bfloat16),
            pltpu.VMEM((3 * CH, 9 * lanes), jnp.bfloat16),
            pltpu.VMEM((3, frames, pixels, lanes), jnp.float32),
            pltpu.VMEM((8 * (frames + 1), own), jnp.float32),
            pltpu.SemaphoreType.DMA((27,)),
        ],
        compiler_params=pltpu.CompilerParams(vmem_limit_bytes=VMEM_BYTES),
        cost_estimate=pl.CostEstimate(
            flops=2 * frames * pixels * 27 * CH * lanes, bytes_accessed=8_000_000, transcendentals=0
        ),
    )(w_mid, table, order, *latents_all, *w_in_own, *w_in_all)
    total = kept
    for turn in range(shares):
        for swap in range(spans):
            if turn or swap:
                pairs = [
                    (c * spans + m, (c + turn) % shares * spans + (m + swap) % spans)
                    for c in range(shares)
                    for m in range(spans)
                ]
                piece = sent[swap - 1] if swap else kept
                total = total + lax.ppermute(piece, ("chan", "tm"), pairs)
    numer = total[0]
    for number, (down, across) in enumerate(cases):
        steps = down * GRID_X + across
        if steps and steps < tiles:
            numer = numer + shifted(total[number], "tile", steps)
    return jnp.transpose(numer / denom[0][None, None, :], (1, 0, 2))


def solution(mesh):
    placed = (
        P("tm", "groups", "tile"),
        P("groups"),
        P(None, None, "chan"),
        P("chan"),
        P("chan"),
        P(None, None, "chan"),
        P("chan"),
        P("chan"),
        P(None, "chan"),
        P("groups", None),
    )
    whole_lanes = (
        CH % (mesh.shape["chan"] * mesh.shape["tm"] * LANES) == 0
        and mesh.shape["chan"] <= mesh.shape["tile"]
    )
    return jax.shard_map(
        lanes_body if whole_lanes else general_body,
        mesh=mesh,
        in_specs=placed,
        out_specs=P("tm", "groups", "tile"),
        check_vma=False,
    )
```

```python
import functools

import jax
import jax.numpy as jnp
from jax import lax
from jax.experimental import pallas as pl
from jax.experimental.pallas import tpu as pltpu
from jax.sharding import PartitionSpec as P

CH = 512
GROUPS = 32
TSIDE = 16
STRIDE = 12
GRID_X = 4

EPSILON = 1e-06
LANES = 128
VMEM_BYTES = 48 * 1024 * 1024


def shifted(value, axis, steps):
    count = lax.axis_size(axis)
    leading, last = (max(0, -steps), min(count, count - steps))
    return lax.ppermute(value, axis, [(source, source + steps) for source in range(leading, last)])


def window_index(tile_id, tiles):
    slots = jnp.arange(TSIDE * TSIDE, dtype=jnp.int32)
    row = tile_id // GRID_X * STRIDE + slots // TSIDE
    col = tile_id % GRID_X * STRIDE + slots % TSIDE
    valid = (row < tiles // GRID_X * STRIDE) & (col < GRID_X * STRIDE)
    block = row // STRIDE * GRID_X + col // STRIDE
    index = block * (STRIDE * STRIDE) + row % STRIDE * STRIDE + col % STRIDE
    return (jnp.where(valid, index, 0), valid)


def causal_conv(extended, weights, frames, side):
    pixels = side * side
    rows = jnp.arange(pixels, dtype=jnp.int32) // side
    cols = jnp.arange(pixels, dtype=jnp.int32) % side
    total = jnp.zeros((frames, weights.shape[2], pixels), jnp.float32)
    for depth in range(3):
        window = extended[depth : depth + frames]
        for down in range(3):
            for across in range(3):
                offset = (down - 1) * side + (across - 1)
                inside = (
                    (rows + down - 1 >= 0)
                    & (rows + down - 1 < side)
                    & (cols + across - 1 >= 0)
                    & (cols + across - 1 < side)
                )
                moved = jnp.roll(window, -offset, axis=2)
                moved = jnp.where(inside[None, None, :], moved, jnp.zeros_like(moved))
                total = total + jnp.einsum(
                    "fcp,co->fop",
                    moved,
                    weights[9 * depth + 3 * down + across],
                    preferred_element_type=jnp.float32,
                )
    return total


def with_history(values):
    frames = values.shape[0]
    earlier = shifted(values[frames - 2 :], "tm", 1)
    return jnp.concatenate([earlier, values], axis=0)


def normalize(values, gain, shift, total_frames):
    frames, chans, pixels = values.shape
    width = CH // GROUPS
    grouped = values.reshape(frames, chans // width, width, pixels)
    sums = jnp.sum(grouped, axis=(0, 2, 3))
    squares = jnp.sum(grouped * grouped, axis=(0, 2, 3))
    sums, squares = lax.psum((sums, squares), "tm")
    count = total_frames * width * pixels
    mean = sums / count
    variance = squares / count - mean * mean
    scale = lax.rsqrt(variance + EPSILON)
    normed = (grouped - mean[None, :, None, None]) * scale[None, :, None, None]
    normed = normed.reshape(frames, chans, pixels) * gain[None, :, None] + shift[None, :, None]
    return jax.nn.silu(normed).astype(jnp.bfloat16)


def spread(color, weight, index, total_pixels):
    numer = (
        jnp.zeros((color.shape[0], 3, total_pixels), jnp.float32)
        .at[:, :, index]
        .add(color * weight[None, None, :])
    )
    denom = jnp.zeros((total_pixels,), jnp.float32).at[index].add(weight)
    return (numer, denom)


def route_owned(numer, denom, tile_id, own):
    frames = numer.shape[0]
    margin = (GRID_X + 1) * own
    numer_wide = jnp.concatenate([numer, jnp.zeros((frames, 3, margin), jnp.float32)], axis=2)
    denom_wide = jnp.concatenate([denom, jnp.zeros((margin,), jnp.float32)], axis=0)
    first_pixel = tile_id * own

    def block_at(offset):
        start_pixel = first_pixel + offset * own
        return (
            lax.dynamic_slice_in_dim(numer_wide, start_pixel, own, 2),
            lax.dynamic_slice_in_dim(denom_wide, start_pixel, own, 0),
        )

    owned_numer, owned_denom = block_at(0)
    for offset in (1, GRID_X, GRID_X + 1):
        piece_numer, piece_denom = block_at(offset)
        got_numer, got_denom = shifted((piece_numer, piece_denom), "tile", offset)
        owned_numer = owned_numer + got_numer
        owned_denom = owned_denom + got_denom
    return (owned_numer, owned_denom)


def general_body(
    latents, tile_order, w_in, gain_in, shift_in, w_mid, gain_mid, shift_mid, w_out, blend_weight
):
    frames = latents.shape[0]
    total_frames = frames * lax.axis_size("tm")
    tiles = tile_order.shape[0]
    own = STRIDE * STRIDE
    total_pixels = tiles * own
    tile_id = lax.axis_index("tile")
    index, valid = window_index(tile_id, tiles)
    whole = lax.all_gather(latents, "tile", axis=2, tiled=True)
    blocks = whole.reshape(frames, whole.shape[1], tiles, own)
    image = (
        jnp.zeros_like(blocks)
        .at[:, :, tile_order]
        .set(blocks)
        .reshape(frames, whole.shape[1], total_pixels)
    )
    window = jnp.where(
        valid[None, None, :], jnp.take(image, index, axis=2), jnp.zeros((), jnp.bfloat16)
    )
    first = causal_conv(with_history(window), w_in, frames, TSIDE)
    hidden = normalize(first, gain_in, shift_in, total_frames)
    second = causal_conv(
        lax.all_gather(with_history(hidden), "chan", axis=1, tiled=True), w_mid, frames, TSIDE
    )
    upper = normalize(second, gain_mid, shift_mid, total_frames)
    color = jnp.einsum("oc,fcp->fop", w_out, upper, preferred_element_type=jnp.float32)
    weight = jnp.where(valid, blend_weight[tile_id], jnp.float32(0.0))
    numer, denom = spread(color, weight, index, total_pixels)
    numer, denom = route_owned(numer, denom, tile_id, own)
    numer = lax.psum(numer, "chan")
    return numer / denom[None, None, :]


def block_cases(tiles):
    downs = (0, 1) if tiles // GRID_X > 1 else (0,)
    return [(down, across) for down in downs for across in (0, 1)]


def exact_dot(values, ones):
    rows = values.shape[0]
    high = values.astype(jnp.bfloat16)
    rest = values - high.astype(jnp.float32)
    middle = rest.astype(jnp.bfloat16)
    low = (rest - middle.astype(jnp.float32)).astype(jnp.bfloat16)
    total = jnp.dot(
        jnp.concatenate([high, middle, low], axis=0), ones, preferred_element_type=jnp.float32
    )
    return total[:rows] + total[rows : 2 * rows] + total[2 * rows :]


def group_affine(sums, squares, gain, shift, count):
    lanes = sums.shape[1]
    width = CH // GROUPS
    same = lax.broadcasted_iota(jnp.int32, (lanes, lanes), 0) // width == (
        lax.broadcasted_iota(jnp.int32, (lanes, lanes), 1) // width
    )
    total = exact_dot(
        jnp.concatenate([sums, squares], axis=0), jnp.where(same, 1.0, 0.0).astype(jnp.bfloat16)
    )
    mean = jnp.sum(total[:8], axis=0, keepdims=True) / count
    variance = jnp.sum(total[8:], axis=0, keepdims=True) / count - mean * mean
    scale = gain * lax.rsqrt(variance + EPSILON)
    return 0.5 * scale, 0.5 * (shift - mean * scale)


def silu_of_half(half):
    return half + half * jnp.tanh(half)


def fold(values):
    rows, lanes = values.shape
    return jnp.sum(values.reshape(rows // 8, 8, lanes), axis=0)


def decode_kernel(
    tiles,
    spans,
    shares,
    *refs,
):
    cases = block_cases(tiles)
    refs = list(refs)

    def take(number):
        taken = refs[:number]
        del refs[:number]
        return taken

    w_mid_ref, table_ref, order_ref = take(3)
    latent_refs, w_in_refs = take(spans), take(shares)
    keep_ref, send_ref, denom_ref = take(3)
    chosen, taps, first, hidden, weights, partial, shown_ref, sems = take(8)

    own = denom_ref.shape[1]
    own_frames = keep_ref.shape[2]
    frames = own_frames * spans
    latent, wide = w_in_refs[0].shape[1:]
    rows_in = frames * latent
    rows_own = rows_in // spans
    depth_in = 27 * latent
    pixels = TSIDE * TSIDE
    lanes = partial.shape[3]
    tile_id = lax.axis_index("tile")
    mine = lax.axis_index("tm")
    chan_id = lax.axis_index("chan")

    copies = []
    for a in range(3):
        for b in range(3):
            for e in range(3):
                tap = 9 * a + 3 * b + e
                copy = pltpu.make_async_copy(
                    w_mid_ref.at[tap, :, pl.ds(pl.multiple_of(mine * lanes, LANES), lanes)],
                    weights.at[pl.ds(b * CH, CH), pl.ds((3 * a + e) * lanes, lanes)],
                    sems.at[tap],
                )
                copy.start()
                copies.append(copy)

    tile_row, tile_col = tile_id // GRID_X, tile_id % GRID_X
    gain_row = rows_own + 2
    w_out_row = gain_row + 2
    blend_row = w_out_row + 3
    order = order_ref[...]
    number_of = lax.broadcasted_iota(jnp.int32, order.shape, 0)
    lane_of = lax.broadcasted_iota(jnp.int32, order.shape, 1)
    rows_all = latent_refs[0].shape[0] // tiles
    for number, (down, across) in enumerate(cases):
        inside = (tile_row + down < tiles // GRID_X) & (tile_col + across < GRID_X)
        wanted = tile_id + down * GRID_X + across
        found = (order == wanted.astype(jnp.float32)) & (lane_of == 0)
        place = jnp.sum(jnp.where(found, number_of.astype(jnp.float32), 0.0))
        turn = (tile_id - place.astype(jnp.int32) + tiles) % tiles
        part = slice(number * LANES, (number + 1) * LANES)
        for steps in range(tiles):

            @pl.when(inside & (turn == steps))
            def _():
                for swap in range(spans):
                    at, tail_at = swap * rows_own, rows_in + swap * latent
                    block = latent_refs[swap][steps * rows_all : (steps + 1) * rows_all]
                    chosen[at : at + rows_own, part] = block[:rows_own]
                    chosen[tail_at : tail_at + latent, part] = block[rows_own : rows_own + latent]

        @pl.when(jnp.logical_not(inside))
        def _():
            chosen[:, part] = jnp.zeros((chosen.shape[0], LANES), chosen.dtype)

    slot = lax.broadcasted_iota(jnp.int32, (1, pixels), 1)
    up, along = slot // TSIDE, slot % TSIDE
    source = lax.broadcasted_iota(jnp.int32, (LANES, pixels), 0)
    tail = own - LANES

    def pick(first_pixel):
        parts = []
        for down, across in cases:
            u, v = up - down * STRIDE, along - across * STRIDE
            good = (u >= 0) & (u < STRIDE) & (v >= 0) & (v < STRIDE)
            wanted = jnp.where(good, u * STRIDE + v - first_pixel, -1)
            parts.append(jnp.where(source == wanted, 1.0, 0.0).astype(jnp.bfloat16))
        return jnp.concatenate(parts, axis=0)

    tails = chosen[rows_in:].astype(jnp.float32)
    width = tails.shape[1]
    turned = [pltpu.roll(tails, (-f * tail) % width, 1) if f else tails for f in range(own_frames)]
    tails = jnp.concatenate(
        [
            turned[f][swap * latent : (swap + 1) * latent]
            for swap in range(spans)
            for f in range(own_frames)
        ],
        axis=0,
    ).astype(jnp.bfloat16)
    in_tail = lax.broadcasted_iota(jnp.int32, tails.shape, 1) % LANES < tail
    tails = jnp.where(in_tail, tails.astype(jnp.float32), 0.0).astype(jnp.bfloat16)
    window = jnp.dot(
        chosen[:rows_in], pick(0), preferred_element_type=jnp.float32
    ) + jnp.dot(tails, pick(LANES), preferred_element_type=jnp.float32)
    taps[0:2] = jnp.zeros((2,) + taps.shape[1:], taps.dtype)
    for b in range(3):
        for e in range(3):
            inside = (
                (up + b - 1 >= 0)
                & (up + b - 1 < TSIDE)
                & (along + e - 1 >= 0)
                & (along + e - 1 < TSIDE)
            )
            offset = (b - 1) * TSIDE + e - 1
            moved = pltpu.roll(window, (-offset) % pixels, 1) if offset else window
            moved = jnp.where(inside, moved, 0.0).astype(jnp.bfloat16)
            for swap in range(spans):
                value = moved[swap * rows_own : (swap + 1) * rows_own]
                span = pl.ds(2 + (mine + swap) % spans * own_frames, own_frames)
                taps[span, 3 * b + e] = value.reshape(own_frames, latent, pixels)

    joined = jnp.concatenate(
        [w_in_refs[s][:27].reshape(depth_in, wide) for s in range(shares)], axis=1
    )
    sums = jnp.zeros((8, CH), jnp.float32)
    squares = jnp.zeros((8, CH), jnp.float32)
    for f in range(frames):
        patch = taps[f : f + 3].reshape(depth_in, pixels)
        value = lax.dot_general(
            patch, joined, (((0,), (0,)), ((), ())), preferred_element_type=jnp.float32
        )
        first[f] = value
        sums = sums + fold(value)
        squares = squares + fold(value * value)
    count = frames * (CH // GROUPS) * pixels
    affine = []
    for s in range(shares):
        at = s * rows_all + rows_own + latent
        table = latent_refs[0][at : at + wide // LANES * 4].astype(jnp.float32)
        pieces = [table[4 * lane : 4 * lane + 4] for lane in range(wide // LANES)]
        table = jnp.concatenate([part[0:2] + part[2:4] for part in pieces], axis=1)
        part = slice(s * wide, (s + 1) * wide)
        affine.append(
            group_affine(sums[:, part], squares[:, part], table[0:1], table[1:2], count)
        )
    channels = [
        pl.ds(pl.multiple_of((chan_id + s) % shares * wide, LANES), wide) for s in range(shares)
    ]

    def hide(f):
        edge = jnp.zeros((TSIDE, CH), jnp.bfloat16)
        hidden[f, 0:TSIDE] = edge
        hidden[f, TSIDE + pixels : 2 * TSIDE + pixels] = edge
        for s in range(shares):
            scale, bias = affine[s]
            value = first[f, :, s * wide : (s + 1) * wide] * scale + bias
            hidden[f, TSIDE : TSIDE + pixels, channels[s]] = silu_of_half(value).astype(
                jnp.bfloat16
            )

    def convolve(start, several, depth_taps):
        lhs = jnp.concatenate(
            [
                hidden[start : start + several, b * TSIDE : b * TSIDE + pixels].reshape(
                    several * pixels, CH
                )
                for b in range(3)
            ],
            axis=1,
        )
        low = depth_taps[0] * 3 * lanes
        product = jnp.dot(lhs, weights[:, low:], preferred_element_type=jnp.float32)
        for a in depth_taps:
            for e in range(3):
                at = (3 * a + e) * lanes - low
                for f in range(several):
                    target = start + f + 2 - a
                    value = product[f * pixels : (f + 1) * pixels, at : at + lanes]
                    if start + f == max(target - 2, 0):
                        partial[e, target] = value
                    else:
                        partial[e, target] += value

    column = lax.broadcasted_iota(jnp.int32, (pixels, lanes), 0) % TSIDE
    total = [jnp.zeros((8, lanes), jnp.float32)] * 2

    def gather(f):
        left = jnp.where(column == 0, 0.0, pltpu.roll(partial[0, f], 1, 0))
        right = jnp.where(column == TSIDE - 1, 0.0, pltpu.roll(partial[2, f], pixels - 1, 0))
        value = partial[1, f] + left + right
        partial[1, f] = value
        total[0] = total[0] + fold(value)
        total[1] = total[1] + fold(value * value)

    together = 3
    groups = [
        range(f, min(f + together, frames - 2)) for f in range(0, frames - 2, together)
    ]
    groups += [range(f, f + 1) for f in range(groups[-1].stop, frames)]
    for copy in copies:
        copy.wait()
    for f in groups[0]:
        hide(f)
    for number, group in enumerate(groups):
        if number + 1 < len(groups):
            for f in groups[number + 1]:
                hide(f)
        convolve(
            group.start,
            len(group),
            tuple(a for a in range(3) if group.stop - 1 + 2 - a < frames),
        )
        if number:
            for f in groups[number - 1]:
                gather(f)
    for f in groups[-1]:
        gather(f)

    part = pl.ds(pl.multiple_of(mine * lanes, LANES), lanes)
    scale, bias = group_affine(
        total[0],
        total[1],
        table_ref[gain_row : gain_row + 1, part],
        table_ref[gain_row + 1 : gain_row + 2, part],
        count,
    )
    blend = table_ref[pl.ds(blend_row + tile_id, 1), :]
    blend = jnp.where(
        (tile_row * STRIDE + up < tiles // GRID_X * STRIDE)
        & (tile_col * STRIDE + along < GRID_X * STRIDE),
        blend,
        0.0,
    )
    w_out = jnp.concatenate(
        [table_ref[w_out_row : w_out_row + 3, part], jnp.zeros((5, lanes), jnp.float32)], axis=0
    ).astype(jnp.bfloat16)
    colors = []
    for f in range(frames):
        upper = silu_of_half(partial[1, f] * scale + bias).astype(jnp.bfloat16)
        color = lax.dot_general(
            w_out, upper, (((1,), (1,)), ((), ())), preferred_element_type=jnp.float32
        )
        colors.append(color * blend)
    colors = jnp.concatenate(colors, axis=0)

    slot_in = lax.broadcasted_iota(jnp.int32, (pixels, own), 0)
    pixel = lax.broadcasted_iota(jnp.int32, (pixels, own), 1)
    denom = jnp.zeros((8, own), jnp.float32)
    for number, (down, across) in enumerate(cases):
        u, v = slot_in // TSIDE - down * STRIDE, slot_in % TSIDE - across * STRIDE
        good = (u >= 0) & (u < STRIDE) & (v >= 0) & (v < STRIDE) & (u * STRIDE + v == pixel)
        shown = jnp.where(good, 1.0, 0.0).astype(jnp.bfloat16)
        inside = (tile_row >= down) & (tile_col >= across)
        other = jnp.maximum(tile_id - down * GRID_X - across, 0)
        weight = jnp.where(inside, table_ref[pl.ds(blend_row + other, 1), :], 0.0)
        piece = exact_dot(
            jnp.concatenate([colors, jnp.broadcast_to(weight, (8, pixels))], axis=0), shown
        )
        denom = denom + piece[8 * frames :]
        shown_ref[...] = piece
        for swap in range(spans):
            target = keep_ref if swap == 0 else send_ref.at[swap - 1]
            base = (mine + swap) % spans * own_frames * 8
            for at in range(own_frames):
                for o in range(3):
                    target[number, o, at : at + 1, :] = shown_ref[pl.ds(base + 8 * at + o, 1), :]

    denom_ref[...] = denom


def from_ring(value, axis):
    count = lax.axis_size(axis)
    return [
        lax.ppermute(value, axis, [((d + turn) % count, d) for d in range(count)])
        for turn in range(1, count)
    ]


def ring_sum(kept, sent, axis):
    count = lax.axis_size(axis)
    for turn in range(1, count):
        kept = kept + lax.ppermute(
            sent[turn - 1], axis, [(d, (d + turn) % count) for d in range(count)]
        )
    return kept


def small_table(*values):
    values = [value.reshape(-1, value.shape[-1]) for value in values]
    wide = max(value.shape[1] for value in values)
    height = sum(value.shape[0] for value in values)
    total, row = 0.0, 0
    for value in values:
        below = height - row - value.shape[0]
        value = jnp.pad(value.astype(jnp.float32), ((row, below), (0, wide - value.shape[1])))
        total = total + value
        row = height - below
    return total


def exchange_latents(frames, latent, own, table):
    tiles, shares = lax.axis_size("tile"), lax.axis_size("chan")
    tail = own - LANES
    height = frames * latent
    mine = table[:height, :own].astype(jnp.bfloat16)
    tails = sum(
        jnp.pad(
            mine[f * latent : (f + 1) * latent, LANES:],
            ((0, 0), (tail * f, LANES - tail * (f + 1))),
        )
        for f in range(frames)
    )
    affine = table[height : height + 2]
    high = lax.reduce_precision(affine, 8, 7)
    low = lax.reduce_precision(affine - high, 8, 7)
    affine = jnp.concatenate([high, low], axis=0).astype(jnp.bfloat16)
    rows = [affine[:, at : at + LANES] for at in range(0, affine.shape[1], LANES)]
    rows = jnp.concatenate(rows, axis=0)
    rows = jnp.pad(rows, ((0, -rows.shape[0] % 16), (0, 0)))
    message = jnp.concatenate([mine[:, :LANES], tails, rows], axis=0)
    got = [message]
    for steps in range(1, tiles):
        turn = steps if steps < shares else 0
        pairs = [
            (t * shares + (c + turn) % shares, (t + steps) % tiles * shares + c)
            for t in range(tiles)
            for c in range(shares)
        ]
        got.append(lax.ppermute(message, ("tile", "chan"), pairs))
    stack = jnp.concatenate(got, axis=0)
    return [stack] + from_ring(stack, "tm")


def lanes_body(
    latents, tile_order, w_in, gain_in, shift_in, w_mid, gain_mid, shift_mid, w_out, blend_weight
):
    own_frames, latent, own = latents.shape
    spans = lax.axis_size("tm")
    shares = lax.axis_size("chan")
    frames = own_frames * spans
    tiles = tile_order.shape[0]
    wide = w_in.shape[2]
    lanes = wide // spans
    pixels = TSIDE * TSIDE
    cases = block_cases(tiles)

    w_in_all = [(from_ring(other, "tm") or [other])[0] for other in from_ring(w_in, "chan")]
    table = lax.optimization_barrier(
        small_table(
            latents.reshape(own_frames * latent, own),
            gain_in,
            shift_in,
            gain_mid,
            shift_mid,
            w_out,
            blend_weight,
        )
    )
    latents_all = exchange_latents(own_frames, latent, own, table)
    _, w_in, tile_order = lax.optimization_barrier((table, w_in, tile_order))
    order = jnp.broadcast_to(tile_order.astype(jnp.float32)[:, None], (tiles, LANES))
    w_in_own = from_ring(w_in, "tm")[:1] or [w_in]

    vmem = pl.BlockSpec(memory_space=pltpu.VMEM)
    piece = (len(cases), 3, own_frames, own)
    kept, sent, denom = pl.pallas_call(
        functools.partial(decode_kernel, tiles, spans, shares),
        out_shape=[
            jax.ShapeDtypeStruct(piece, jnp.float32),
            jax.ShapeDtypeStruct((max(spans - 1, 1),) + piece, jnp.float32),
            jax.ShapeDtypeStruct((8, own), jnp.float32),
        ],
        in_specs=[pl.BlockSpec(memory_space=pl.ANY)] + [vmem] * (2 + spans + shares),
        out_specs=[vmem] * 3,
        scratch_shapes=[
            pltpu.VMEM(((frames + spans) * latent, len(cases) * LANES), jnp.bfloat16),
            pltpu.VMEM((frames + 2, 9, latent, pixels), jnp.bfloat16),
            pltpu.VMEM((frames, pixels, CH), jnp.float32),
            pltpu.VMEM((frames, pixels + 2 * TSIDE, CH), jnp.bfloat16),
            pltpu.VMEM((3 * CH, 9 * lanes), jnp.bfloat16),
            pltpu.VMEM((3, frames, pixels, lanes), jnp.float32),
            pltpu.VMEM((8 * (frames + 1), own), jnp.float32),
            pltpu.SemaphoreType.DMA((27,)),
        ],
        compiler_params=pltpu.CompilerParams(vmem_limit_bytes=VMEM_BYTES),
        cost_estimate=pl.CostEstimate(
            flops=2 * frames * pixels * 27 * CH * lanes, bytes_accessed=8_000_000, transcendentals=0
        ),
    )(w_mid, table, order, *latents_all, *w_in_own, *w_in_all)
    total = ring_sum(kept, sent, "tm")
    total = ring_sum(total, [total] * (shares - 1), "chan")
    numer = total[0]
    for number, (down, across) in enumerate(cases):
        steps = down * GRID_X + across
        if steps and steps < tiles:
            numer = numer + shifted(total[number], "tile", steps)
    return jnp.transpose(numer / denom[0][None, None, :], (1, 0, 2))


def solution(mesh):
    placed = (
        P("tm", "groups", "tile"),
        P("groups"),
        P(None, None, "chan"),
        P("chan"),
        P("chan"),
        P(None, None, "chan"),
        P("chan"),
        P("chan"),
        P(None, "chan"),
        P("groups", None),
    )
    whole_lanes = (
        CH % (mesh.shape["chan"] * mesh.shape["tm"] * LANES) == 0
        and mesh.shape["chan"] <= mesh.shape["tile"]
    )
    return jax.shard_map(
        lanes_body if whole_lanes else general_body,
        mesh=mesh,
        in_specs=placed,
        out_specs=P("tm", "groups", "tile"),
        check_vma=False,
    )
```

```python
import functools

import jax
import jax.numpy as jnp
from jax import lax
from jax.experimental import pallas as pl
from jax.experimental.pallas import tpu as pltpu
from jax.sharding import PartitionSpec as P

CH = 512
GROUPS = 32
TSIDE = 16
STRIDE = 12
GRID_X = 4

EPSILON = 1e-06
LANES = 128
VMEM_BYTES = 48 * 1024 * 1024


def shifted(value, axis, steps):
    count = lax.axis_size(axis)
    leading, last = (max(0, -steps), min(count, count - steps))
    return lax.ppermute(value, axis, [(source, source + steps) for source in range(leading, last)])


def window_index(tile_id, tiles):
    slots = jnp.arange(TSIDE * TSIDE, dtype=jnp.int32)
    row = tile_id // GRID_X * STRIDE + slots // TSIDE
    col = tile_id % GRID_X * STRIDE + slots % TSIDE
    valid = (row < tiles // GRID_X * STRIDE) & (col < GRID_X * STRIDE)
    block = row // STRIDE * GRID_X + col // STRIDE
    index = block * (STRIDE * STRIDE) + row % STRIDE * STRIDE + col % STRIDE
    return (jnp.where(valid, index, 0), valid)


def causal_conv(extended, weights, frames, side):
    pixels = side * side
    rows = jnp.arange(pixels, dtype=jnp.int32) // side
    cols = jnp.arange(pixels, dtype=jnp.int32) % side
    total = jnp.zeros((frames, weights.shape[2], pixels), jnp.float32)
    for depth in range(3):
        window = extended[depth : depth + frames]
        for down in range(3):
            for across in range(3):
                offset = (down - 1) * side + (across - 1)
                inside = (
                    (rows + down - 1 >= 0)
                    & (rows + down - 1 < side)
                    & (cols + across - 1 >= 0)
                    & (cols + across - 1 < side)
                )
                moved = jnp.roll(window, -offset, axis=2)
                moved = jnp.where(inside[None, None, :], moved, jnp.zeros_like(moved))
                total = total + jnp.einsum(
                    "fcp,co->fop",
                    moved,
                    weights[9 * depth + 3 * down + across],
                    preferred_element_type=jnp.float32,
                )
    return total


def with_history(values):
    frames = values.shape[0]
    earlier = shifted(values[frames - 2 :], "tm", 1)
    return jnp.concatenate([earlier, values], axis=0)


def normalize(values, gain, shift, total_frames):
    frames, chans, pixels = values.shape
    width = CH // GROUPS
    grouped = values.reshape(frames, chans // width, width, pixels)
    sums = jnp.sum(grouped, axis=(0, 2, 3))
    squares = jnp.sum(grouped * grouped, axis=(0, 2, 3))
    sums, squares = lax.psum((sums, squares), "tm")
    count = total_frames * width * pixels
    mean = sums / count
    variance = squares / count - mean * mean
    scale = lax.rsqrt(variance + EPSILON)
    normed = (grouped - mean[None, :, None, None]) * scale[None, :, None, None]
    normed = normed.reshape(frames, chans, pixels) * gain[None, :, None] + shift[None, :, None]
    return jax.nn.silu(normed).astype(jnp.bfloat16)


def spread(color, weight, index, total_pixels):
    numer = (
        jnp.zeros((color.shape[0], 3, total_pixels), jnp.float32)
        .at[:, :, index]
        .add(color * weight[None, None, :])
    )
    denom = jnp.zeros((total_pixels,), jnp.float32).at[index].add(weight)
    return (numer, denom)


def route_owned(numer, denom, tile_id, own):
    frames = numer.shape[0]
    margin = (GRID_X + 1) * own
    numer_wide = jnp.concatenate([numer, jnp.zeros((frames, 3, margin), jnp.float32)], axis=2)
    denom_wide = jnp.concatenate([denom, jnp.zeros((margin,), jnp.float32)], axis=0)
    first_pixel = tile_id * own

    def block_at(offset):
        start_pixel = first_pixel + offset * own
        return (
            lax.dynamic_slice_in_dim(numer_wide, start_pixel, own, 2),
            lax.dynamic_slice_in_dim(denom_wide, start_pixel, own, 0),
        )

    owned_numer, owned_denom = block_at(0)
    for offset in (1, GRID_X, GRID_X + 1):
        piece_numer, piece_denom = block_at(offset)
        got_numer, got_denom = shifted((piece_numer, piece_denom), "tile", offset)
        owned_numer = owned_numer + got_numer
        owned_denom = owned_denom + got_denom
    return (owned_numer, owned_denom)


def general_body(
    latents, tile_order, w_in, gain_in, shift_in, w_mid, gain_mid, shift_mid, w_out, blend_weight
):
    frames = latents.shape[0]
    total_frames = frames * lax.axis_size("tm")
    tiles = tile_order.shape[0]
    own = STRIDE * STRIDE
    total_pixels = tiles * own
    tile_id = lax.axis_index("tile")
    index, valid = window_index(tile_id, tiles)
    whole = lax.all_gather(latents, "tile", axis=2, tiled=True)
    blocks = whole.reshape(frames, whole.shape[1], tiles, own)
    image = (
        jnp.zeros_like(blocks)
        .at[:, :, tile_order]
        .set(blocks)
        .reshape(frames, whole.shape[1], total_pixels)
    )
    window = jnp.where(
        valid[None, None, :], jnp.take(image, index, axis=2), jnp.zeros((), jnp.bfloat16)
    )
    first = causal_conv(with_history(window), w_in, frames, TSIDE)
    hidden = normalize(first, gain_in, shift_in, total_frames)
    second = causal_conv(
        lax.all_gather(with_history(hidden), "chan", axis=1, tiled=True), w_mid, frames, TSIDE
    )
    upper = normalize(second, gain_mid, shift_mid, total_frames)
    color = jnp.einsum("oc,fcp->fop", w_out, upper, preferred_element_type=jnp.float32)
    weight = jnp.where(valid, blend_weight[tile_id], jnp.float32(0.0))
    numer, denom = spread(color, weight, index, total_pixels)
    numer, denom = route_owned(numer, denom, tile_id, own)
    numer = lax.psum(numer, "chan")
    return numer / denom[None, None, :]


def block_cases(tiles):
    downs = (0, 1) if tiles // GRID_X > 1 else (0,)
    return [(down, across) for down in downs for across in (0, 1)]


def exact_dot(values, ones):
    rows = values.shape[0]
    high = values.astype(jnp.bfloat16)
    rest = values - high.astype(jnp.float32)
    middle = rest.astype(jnp.bfloat16)
    low = (rest - middle.astype(jnp.float32)).astype(jnp.bfloat16)
    total = jnp.dot(
        jnp.concatenate([high, middle, low], axis=0), ones, preferred_element_type=jnp.float32
    )
    return total[:rows] + total[rows : 2 * rows] + total[2 * rows :]


def group_affine(sums, squares, gain, shift, count):
    lanes = sums.shape[1]
    width = CH // GROUPS
    same = lax.broadcasted_iota(jnp.int32, (lanes, lanes), 0) // width == (
        lax.broadcasted_iota(jnp.int32, (lanes, lanes), 1) // width
    )
    total = exact_dot(
        jnp.concatenate([sums, squares], axis=0), jnp.where(same, 1.0, 0.0).astype(jnp.bfloat16)
    )
    mean = jnp.sum(total[:8], axis=0, keepdims=True) / count
    variance = jnp.sum(total[8:], axis=0, keepdims=True) / count - mean * mean
    scale = gain * lax.rsqrt(variance + EPSILON)
    return 0.5 * scale, 0.5 * (shift - mean * scale)


def silu_of_half(half):
    return half + half * jnp.tanh(half)


def fold(values):
    rows, lanes = values.shape
    return jnp.sum(values.reshape(rows // 8, 8, lanes), axis=0)


def decode_kernel(
    tiles,
    spans,
    shares,
    *refs,
):
    cases = block_cases(tiles)
    refs = list(refs)

    def take(number):
        taken = refs[:number]
        del refs[:number]
        return taken

    w_mid_ref, table_ref, order_ref = take(3)
    latent_refs, w_in_refs = take(spans), take(shares)
    keep_ref, send_ref, denom_ref = take(3)
    chosen, taps, first, hidden, weights, partial, shown_ref, sems = take(8)

    own = denom_ref.shape[1]
    own_frames = keep_ref.shape[2]
    frames = own_frames * spans
    latent, wide = w_in_refs[0].shape[1:]
    rows_in = frames * latent
    rows_own = rows_in // spans
    depth_in = 27 * latent
    pixels = TSIDE * TSIDE
    lanes = partial.shape[3]
    tile_id = lax.axis_index("tile")
    mine = lax.axis_index("tm")
    chan_id = lax.axis_index("chan")

    copies = []
    for a in range(3):
        for b in range(3):
            for e in range(3):
                tap = 9 * a + 3 * b + e
                copy = pltpu.make_async_copy(
                    w_mid_ref.at[tap, :, pl.ds(pl.multiple_of(mine * lanes, LANES), lanes)],
                    weights.at[pl.ds(b * CH, CH), pl.ds((3 * a + e) * lanes, lanes)],
                    sems.at[tap],
                )
                copy.start()
                copies.append(copy)

    tile_row, tile_col = tile_id // GRID_X, tile_id % GRID_X
    gain_row = rows_own + 2
    w_out_row = gain_row + 2
    blend_row = w_out_row + 3
    order = order_ref[...]
    number_of = lax.broadcasted_iota(jnp.int32, order.shape, 0)
    lane_of = lax.broadcasted_iota(jnp.int32, order.shape, 1)
    rows_all = latent_refs[0].shape[0] // tiles
    turns = []
    for down, across in cases:
        wanted = tile_id + down * GRID_X + across
        found = (order == wanted.astype(jnp.float32)) & (lane_of == 0)
        place = jnp.sum(jnp.where(found, number_of.astype(jnp.float32), 0.0))
        turns.append((tile_id - place.astype(jnp.int32) + tiles) % tiles)
    for number, (down, across) in enumerate(cases):
        inside = (tile_row + down < tiles // GRID_X) & (tile_col + across < GRID_X)
        turn = turns[number]
        part = slice(number * LANES, (number + 1) * LANES)
        for steps in range(tiles):

            @pl.when(inside & (turn == steps))
            def _():
                for swap in range(spans):
                    at, tail_at = swap * rows_own, rows_in + swap * latent
                    block = latent_refs[swap][steps * rows_all : (steps + 1) * rows_all]
                    chosen[at : at + rows_own, part] = block[:rows_own]
                    chosen[tail_at : tail_at + latent, part] = block[rows_own : rows_own + latent]

        @pl.when(jnp.logical_not(inside))
        def _():
            chosen[:, part] = jnp.zeros((chosen.shape[0], LANES), chosen.dtype)

    slot = lax.broadcasted_iota(jnp.int32, (1, pixels), 1)
    up, along = slot // TSIDE, slot % TSIDE
    source = lax.broadcasted_iota(jnp.int32, (LANES, pixels), 0)
    tail = own - LANES

    def pick(first_pixel):
        parts = []
        for down, across in cases:
            u, v = up - down * STRIDE, along - across * STRIDE
            good = (u >= 0) & (u < STRIDE) & (v >= 0) & (v < STRIDE)
            wanted = jnp.where(good, u * STRIDE + v - first_pixel, -1)
            parts.append(jnp.where(source == wanted, 1.0, 0.0).astype(jnp.bfloat16))
        return jnp.concatenate(parts, axis=0)

    tails = chosen[rows_in:].astype(jnp.float32)
    width = tails.shape[1]
    turned = [pltpu.roll(tails, (-f * tail) % width, 1) if f else tails for f in range(own_frames)]
    tails = jnp.concatenate(
        [
            turned[f][swap * latent : (swap + 1) * latent]
            for swap in range(spans)
            for f in range(own_frames)
        ],
        axis=0,
    ).astype(jnp.bfloat16)
    in_tail = lax.broadcasted_iota(jnp.int32, tails.shape, 1) % LANES < tail
    tails = jnp.where(in_tail, tails.astype(jnp.float32), 0.0).astype(jnp.bfloat16)
    window = jnp.dot(
        chosen[:rows_in], pick(0), preferred_element_type=jnp.float32
    ) + jnp.dot(tails, pick(LANES), preferred_element_type=jnp.float32)
    taps[0:2] = jnp.zeros((2,) + taps.shape[1:], taps.dtype)
    for b in range(3):
        for e in range(3):
            inside = (
                (up + b - 1 >= 0)
                & (up + b - 1 < TSIDE)
                & (along + e - 1 >= 0)
                & (along + e - 1 < TSIDE)
            )
            offset = (b - 1) * TSIDE + e - 1
            moved = pltpu.roll(window, (-offset) % pixels, 1) if offset else window
            moved = jnp.where(inside, moved, 0.0).astype(jnp.bfloat16)
            for swap in range(spans):
                value = moved[swap * rows_own : (swap + 1) * rows_own]
                span = pl.ds(2 + (mine + swap) % spans * own_frames, own_frames)
                taps[span, 3 * b + e] = value.reshape(own_frames, latent, pixels)

    joined = jnp.concatenate(
        [w_in_refs[s][:27].reshape(depth_in, wide) for s in range(shares)], axis=1
    )
    sums = jnp.zeros((8, CH), jnp.float32)
    squares = jnp.zeros((8, CH), jnp.float32)
    for low in range(0, frames, 2):
        several = range(low, min(low + 2, frames))
        patches = [taps[f : f + 3].reshape(depth_in, pixels) for f in several]
        values = lax.dot_general(
            jnp.concatenate(patches, axis=1),
            joined,
            (((0,), (0,)), ((), ())),
            preferred_element_type=jnp.float32,
        )
        for f in several:
            value = values[(f - low) * pixels : (f - low + 1) * pixels]
            first[f] = value
            sums = sums + fold(value)
            squares = squares + fold(value * value)
    count = frames * (CH // GROUPS) * pixels
    affine = []
    for s in range(shares):
        at = s * rows_all + rows_own + latent
        table = latent_refs[0][at : at + wide // LANES * 4].astype(jnp.float32)
        pieces = [table[4 * lane : 4 * lane + 4] for lane in range(wide // LANES)]
        table = jnp.concatenate([part[0:2] + part[2:4] for part in pieces], axis=1)
        part = slice(s * wide, (s + 1) * wide)
        affine.append(
            group_affine(sums[:, part], squares[:, part], table[0:1], table[1:2], count)
        )
    channels = [
        pl.ds(pl.multiple_of((chan_id + s) % shares * wide, LANES), wide) for s in range(shares)
    ]

    def hide(f):
        edge = jnp.zeros((TSIDE, CH), jnp.bfloat16)
        hidden[f, 0:TSIDE] = edge
        hidden[f, TSIDE + pixels : 2 * TSIDE + pixels] = edge
        for s in range(shares):
            scale, bias = affine[s]
            value = first[f, :, s * wide : (s + 1) * wide] * scale + bias
            hidden[f, TSIDE : TSIDE + pixels, channels[s]] = silu_of_half(value).astype(
                jnp.bfloat16
            )

    def convolve(start, several, depth_taps):
        lhs = jnp.concatenate(
            [
                hidden[start : start + several, b * TSIDE : b * TSIDE + pixels].reshape(
                    several * pixels, CH
                )
                for b in range(3)
            ],
            axis=1,
        )
        low = depth_taps[0] * 3 * lanes
        product = jnp.dot(lhs, weights[:, low:], preferred_element_type=jnp.float32)
        for a in depth_taps:
            for e in range(3):
                at = (3 * a + e) * lanes - low
                for f in range(several):
                    target = start + f + 2 - a
                    value = product[f * pixels : (f + 1) * pixels, at : at + lanes]
                    if start + f == max(target - 2, 0):
                        partial[e, target] = value
                    else:
                        partial[e, target] += value

    column = lax.broadcasted_iota(jnp.int32, (pixels, lanes), 0) % TSIDE
    total = [jnp.zeros((8, lanes), jnp.float32)] * 2

    def gather(f):
        left = jnp.where(column == 0, 0.0, pltpu.roll(partial[0, f], 1, 0))
        right = jnp.where(column == TSIDE - 1, 0.0, pltpu.roll(partial[2, f], pixels - 1, 0))
        value = partial[1, f] + left + right
        partial[1, f] = value
        total[0] = total[0] + fold(value)
        total[1] = total[1] + fold(value * value)

    bounds = [0, 2, frames - 2, frames - 1, frames]
    groups = [range(low, high) for low, high in zip(bounds, bounds[1:]) if high > low]
    for copy in copies:
        copy.wait()
    for f in groups[0]:
        hide(f)
    for number, group in enumerate(groups):
        if number + 1 < len(groups):
            for f in groups[number + 1]:
                hide(f)
        convolve(
            group.start,
            len(group),
            tuple(a for a in range(3) if group.stop - 1 + 2 - a < frames),
        )
        if number:
            for f in groups[number - 1]:
                gather(f)
    for f in groups[-1]:
        gather(f)

    part = pl.ds(pl.multiple_of(mine * lanes, LANES), lanes)
    scale, bias = group_affine(
        total[0],
        total[1],
        table_ref[gain_row : gain_row + 1, part],
        table_ref[gain_row + 1 : gain_row + 2, part],
        count,
    )
    blend = table_ref[pl.ds(blend_row + tile_id, 1), :]
    blend = jnp.where(
        (tile_row * STRIDE + up < tiles // GRID_X * STRIDE)
        & (tile_col * STRIDE + along < GRID_X * STRIDE),
        blend,
        0.0,
    )
    w_out = jnp.concatenate(
        [table_ref[w_out_row : w_out_row + 3, part], jnp.zeros((5, lanes), jnp.float32)], axis=0
    ).astype(jnp.bfloat16)
    colors = []
    for f in range(frames):
        upper = silu_of_half(partial[1, f] * scale + bias).astype(jnp.bfloat16)
        color = lax.dot_general(
            w_out, upper, (((1,), (1,)), ((), ())), preferred_element_type=jnp.float32
        )
        colors.append(color * blend)
    colors = jnp.concatenate(colors, axis=0)

    slot_in = lax.broadcasted_iota(jnp.int32, (pixels, pixels), 0)
    pixel = lax.broadcasted_iota(jnp.int32, (pixels, pixels), 1)
    shown, weight_rows = [], []
    for down, across in cases:
        u, v = slot_in // TSIDE - down * STRIDE, slot_in % TSIDE - across * STRIDE
        good = (u >= 0) & (u < STRIDE) & (v >= 0) & (v < STRIDE) & (u * STRIDE + v == pixel)
        shown.append(jnp.where(good, 1.0, 0.0).astype(jnp.bfloat16))
        inside = (tile_row >= down) & (tile_col >= across)
        other = jnp.maximum(tile_id - down * GRID_X - across, 0)
        weight = jnp.where(inside, table_ref[pl.ds(blend_row + other, 1), :], 0.0)
        weight_rows.append(jnp.broadcast_to(weight, (8, pixels)))
    shown_ref[...] = exact_dot(
        jnp.concatenate([colors] + weight_rows, axis=0), jnp.concatenate(shown, axis=1)
    )
    denom = jnp.zeros((8, own), jnp.float32)
    for number in range(len(cases)):
        lane = slice(number * pixels, number * pixels + own)
        row = 8 * (frames + number)
        denom = denom + shown_ref[row : row + 8, lane]
        for swap in range(spans):
            target = keep_ref if swap == 0 else send_ref.at[swap - 1]
            base = (mine + swap) % spans * own_frames * 8
            for at in range(own_frames):
                for o in range(3):
                    target[number, o, at : at + 1, :] = shown_ref[
                        pl.ds(base + 8 * at + o, 1), lane
                    ]
    denom_ref[...] = denom


def from_ring(value, axis):
    count = lax.axis_size(axis)
    return [
        lax.ppermute(value, axis, [((d + turn) % count, d) for d in range(count)])
        for turn in range(1, count)
    ]


def ring_sum(kept, sent, axis):
    count = lax.axis_size(axis)
    for turn in range(1, count):
        kept = kept + lax.ppermute(
            sent[turn - 1], axis, [(d, (d + turn) % count) for d in range(count)]
        )
    return kept


def small_table(*values):
    values = [value.reshape(-1, value.shape[-1]) for value in values]
    wide = max(value.shape[1] for value in values)
    height = sum(value.shape[0] for value in values)
    total, row = 0.0, 0
    for value in values:
        below = height - row - value.shape[0]
        value = jnp.pad(value.astype(jnp.float32), ((row, below), (0, wide - value.shape[1])))
        total = total + value
        row = height - below
    return total


def exchange_latents(frames, latent, own, table):
    tiles, shares = lax.axis_size("tile"), lax.axis_size("chan")
    tail = own - LANES
    height = frames * latent
    mine = table[:height, :own].astype(jnp.bfloat16)
    tails = sum(
        jnp.pad(
            mine[f * latent : (f + 1) * latent, LANES:],
            ((0, 0), (tail * f, LANES - tail * (f + 1))),
        )
        for f in range(frames)
    )
    affine = table[height : height + 2]
    high = lax.reduce_precision(affine, 8, 7)
    low = lax.reduce_precision(affine - high, 8, 7)
    affine = jnp.concatenate([high, low], axis=0).astype(jnp.bfloat16)
    rows = [affine[:, at : at + LANES] for at in range(0, affine.shape[1], LANES)]
    rows = jnp.concatenate(rows, axis=0)
    rows = jnp.pad(rows, ((0, -rows.shape[0] % 16), (0, 0)))
    message = jnp.concatenate([mine[:, :LANES], tails, rows], axis=0)
    got = [message]
    for steps in range(1, tiles):
        turn = steps if steps < shares else 0
        pairs = [
            (t * shares + (c + turn) % shares, (t + steps) % tiles * shares + c)
            for t in range(tiles)
            for c in range(shares)
        ]
        got.append(lax.ppermute(message, ("tile", "chan"), pairs))
    stack = jnp.concatenate(got, axis=0)
    return [stack] + from_ring(stack, "tm")


def lanes_body(
    latents, tile_order, w_in, gain_in, shift_in, w_mid, gain_mid, shift_mid, w_out, blend_weight
):
    own_frames, latent, own = latents.shape
    spans = lax.axis_size("tm")
    shares = lax.axis_size("chan")
    frames = own_frames * spans
    tiles = tile_order.shape[0]
    wide = w_in.shape[2]
    lanes = wide // spans
    pixels = TSIDE * TSIDE
    cases = block_cases(tiles)

    w_in_all = [(from_ring(other, "tm") or [other])[0] for other in from_ring(w_in, "chan")]
    table = lax.optimization_barrier(
        small_table(
            latents.reshape(own_frames * latent, own),
            gain_in,
            shift_in,
            gain_mid,
            shift_mid,
            w_out,
            blend_weight,
        )
    )
    latents_all = exchange_latents(own_frames, latent, own, table)
    _, w_in, tile_order = lax.optimization_barrier((table, w_in, tile_order))
    order = jnp.broadcast_to(tile_order.astype(jnp.float32)[:, None], (tiles, LANES))
    w_in_own = from_ring(w_in, "tm")[:1] or [w_in]

    vmem = pl.BlockSpec(memory_space=pltpu.VMEM)
    piece = (len(cases), 3, own_frames, own)
    kept, sent, denom = pl.pallas_call(
        functools.partial(decode_kernel, tiles, spans, shares),
        out_shape=[
            jax.ShapeDtypeStruct(piece, jnp.float32),
            jax.ShapeDtypeStruct((max(spans - 1, 1),) + piece, jnp.float32),
            jax.ShapeDtypeStruct((8, own), jnp.float32),
        ],
        in_specs=[pl.BlockSpec(memory_space=pl.ANY)] + [vmem] * (2 + spans + shares),
        out_specs=[vmem] * 3,
        scratch_shapes=[
            pltpu.VMEM(((frames + spans) * latent, len(cases) * LANES), jnp.bfloat16),
            pltpu.VMEM((frames + 2, 9, latent, pixels), jnp.bfloat16),
            pltpu.VMEM((frames, pixels, CH), jnp.float32),
            pltpu.VMEM((frames, pixels + 2 * TSIDE, CH), jnp.bfloat16),
            pltpu.VMEM((3 * CH, 9 * lanes), jnp.bfloat16),
            pltpu.VMEM((3, frames, pixels, lanes), jnp.float32),
            pltpu.VMEM((8 * (frames + len(cases)), len(cases) * pixels), jnp.float32),
            pltpu.SemaphoreType.DMA((27,)),
        ],
        compiler_params=pltpu.CompilerParams(vmem_limit_bytes=VMEM_BYTES),
        cost_estimate=pl.CostEstimate(
            flops=2 * frames * pixels * 27 * CH * lanes, bytes_accessed=8_000_000, transcendentals=0
        ),
    )(w_mid, table, order, *latents_all, *w_in_own, *w_in_all)
    total = ring_sum(kept, sent, "tm")
    total = ring_sum(total, [total] * (shares - 1), "chan")
    numer = total[0]
    for number, (down, across) in enumerate(cases):
        steps = down * GRID_X + across
        if steps and steps < tiles:
            numer = numer + shifted(total[number], "tile", steps)
    return jnp.transpose(numer / denom[0][None, None, :], (1, 0, 2))


def solution(mesh):
    placed = (
        P("tm", "groups", "tile"),
        P("groups"),
        P(None, None, "chan"),
        P("chan"),
        P("chan"),
        P(None, None, "chan"),
        P("chan"),
        P("chan"),
        P(None, "chan"),
        P("groups", None),
    )
    whole_lanes = (
        CH % (mesh.shape["chan"] * mesh.shape["tm"] * LANES) == 0
        and mesh.shape["chan"] <= mesh.shape["tile"]
    )
    return jax.shard_map(
        lanes_body if whole_lanes else general_body,
        mesh=mesh,
        in_specs=placed,
        out_specs=P("tm", "groups", "tile"),
        check_vma=False,
    )
```

```python
import functools

import jax
import jax.numpy as jnp
from jax import lax
from jax.experimental import pallas as pl
from jax.experimental.pallas import tpu as pltpu
from jax.sharding import PartitionSpec as P

CH = 512
GROUPS = 32
TSIDE = 16
STRIDE = 12
GRID_X = 4

EPSILON = 1e-06
LANES = 128
VMEM_BYTES = 48 * 1024 * 1024


def shifted(value, axis, steps):
    count = lax.axis_size(axis)
    leading, last = (max(0, -steps), min(count, count - steps))
    return lax.ppermute(value, axis, [(source, source + steps) for source in range(leading, last)])


def window_index(tile_id, tiles):
    slots = jnp.arange(TSIDE * TSIDE, dtype=jnp.int32)
    row = tile_id // GRID_X * STRIDE + slots // TSIDE
    col = tile_id % GRID_X * STRIDE + slots % TSIDE
    valid = (row < tiles // GRID_X * STRIDE) & (col < GRID_X * STRIDE)
    block = row // STRIDE * GRID_X + col // STRIDE
    index = block * (STRIDE * STRIDE) + row % STRIDE * STRIDE + col % STRIDE
    return (jnp.where(valid, index, 0), valid)


def causal_conv(extended, weights, frames, side):
    pixels = side * side
    rows = jnp.arange(pixels, dtype=jnp.int32) // side
    cols = jnp.arange(pixels, dtype=jnp.int32) % side
    total = jnp.zeros((frames, weights.shape[2], pixels), jnp.float32)
    for depth in range(3):
        window = extended[depth : depth + frames]
        for down in range(3):
            for across in range(3):
                offset = (down - 1) * side + (across - 1)
                inside = (
                    (rows + down - 1 >= 0)
                    & (rows + down - 1 < side)
                    & (cols + across - 1 >= 0)
                    & (cols + across - 1 < side)
                )
                moved = jnp.roll(window, -offset, axis=2)
                moved = jnp.where(inside[None, None, :], moved, jnp.zeros_like(moved))
                total = total + jnp.einsum(
                    "fcp,co->fop",
                    moved,
                    weights[9 * depth + 3 * down + across],
                    preferred_element_type=jnp.float32,
                )
    return total


def with_history(values):
    frames = values.shape[0]
    earlier = shifted(values[frames - 2 :], "tm", 1)
    return jnp.concatenate([earlier, values], axis=0)


def normalize(values, gain, shift, total_frames):
    frames, chans, pixels = values.shape
    width = CH // GROUPS
    grouped = values.reshape(frames, chans // width, width, pixels)
    sums = jnp.sum(grouped, axis=(0, 2, 3))
    squares = jnp.sum(grouped * grouped, axis=(0, 2, 3))
    sums, squares = lax.psum((sums, squares), "tm")
    count = total_frames * width * pixels
    mean = sums / count
    variance = squares / count - mean * mean
    scale = lax.rsqrt(variance + EPSILON)
    normed = (grouped - mean[None, :, None, None]) * scale[None, :, None, None]
    normed = normed.reshape(frames, chans, pixels) * gain[None, :, None] + shift[None, :, None]
    return jax.nn.silu(normed).astype(jnp.bfloat16)


def spread(color, weight, index, total_pixels):
    numer = (
        jnp.zeros((color.shape[0], 3, total_pixels), jnp.float32)
        .at[:, :, index]
        .add(color * weight[None, None, :])
    )
    denom = jnp.zeros((total_pixels,), jnp.float32).at[index].add(weight)
    return (numer, denom)


def route_owned(numer, denom, tile_id, own):
    frames = numer.shape[0]
    margin = (GRID_X + 1) * own
    numer_wide = jnp.concatenate([numer, jnp.zeros((frames, 3, margin), jnp.float32)], axis=2)
    denom_wide = jnp.concatenate([denom, jnp.zeros((margin,), jnp.float32)], axis=0)
    first_pixel = tile_id * own

    def block_at(offset):
        start_pixel = first_pixel + offset * own
        return (
            lax.dynamic_slice_in_dim(numer_wide, start_pixel, own, 2),
            lax.dynamic_slice_in_dim(denom_wide, start_pixel, own, 0),
        )

    owned_numer, owned_denom = block_at(0)
    for offset in (1, GRID_X, GRID_X + 1):
        piece_numer, piece_denom = block_at(offset)
        got_numer, got_denom = shifted((piece_numer, piece_denom), "tile", offset)
        owned_numer = owned_numer + got_numer
        owned_denom = owned_denom + got_denom
    return (owned_numer, owned_denom)


def general_body(
    latents, tile_order, w_in, gain_in, shift_in, w_mid, gain_mid, shift_mid, w_out, blend_weight
):
    frames = latents.shape[0]
    total_frames = frames * lax.axis_size("tm")
    tiles = tile_order.shape[0]
    own = STRIDE * STRIDE
    total_pixels = tiles * own
    tile_id = lax.axis_index("tile")
    index, valid = window_index(tile_id, tiles)
    whole = lax.all_gather(latents, "tile", axis=2, tiled=True)
    blocks = whole.reshape(frames, whole.shape[1], tiles, own)
    image = (
        jnp.zeros_like(blocks)
        .at[:, :, tile_order]
        .set(blocks)
        .reshape(frames, whole.shape[1], total_pixels)
    )
    window = jnp.where(
        valid[None, None, :], jnp.take(image, index, axis=2), jnp.zeros((), jnp.bfloat16)
    )
    first = causal_conv(with_history(window), w_in, frames, TSIDE)
    hidden = normalize(first, gain_in, shift_in, total_frames)
    second = causal_conv(
        lax.all_gather(with_history(hidden), "chan", axis=1, tiled=True), w_mid, frames, TSIDE
    )
    upper = normalize(second, gain_mid, shift_mid, total_frames)
    color = jnp.einsum("oc,fcp->fop", w_out, upper, preferred_element_type=jnp.float32)
    weight = jnp.where(valid, blend_weight[tile_id], jnp.float32(0.0))
    numer, denom = spread(color, weight, index, total_pixels)
    numer, denom = route_owned(numer, denom, tile_id, own)
    numer = lax.psum(numer, "chan")
    return numer / denom[None, None, :]


def block_cases(tiles):
    downs = (0, 1) if tiles // GRID_X > 1 else (0,)
    return [(down, across) for down in downs for across in (0, 1)]


def exact_dot(values, ones):
    rows = values.shape[0]
    high = values.astype(jnp.bfloat16)
    rest = values - high.astype(jnp.float32)
    middle = rest.astype(jnp.bfloat16)
    low = (rest - middle.astype(jnp.float32)).astype(jnp.bfloat16)
    total = jnp.dot(
        jnp.concatenate([high, middle, low], axis=0), ones, preferred_element_type=jnp.float32
    )
    return total[:rows] + total[rows : 2 * rows] + total[2 * rows :]


def group_affine(sums, squares, gain, shift, count):
    lanes = sums.shape[1]
    width = CH // GROUPS
    same = lax.broadcasted_iota(jnp.int32, (lanes, lanes), 0) // width == (
        lax.broadcasted_iota(jnp.int32, (lanes, lanes), 1) // width
    )
    total = exact_dot(
        jnp.concatenate([sums, squares], axis=0), jnp.where(same, 1.0, 0.0).astype(jnp.bfloat16)
    )
    mean = jnp.sum(total[:8], axis=0, keepdims=True) / count
    variance = jnp.sum(total[8:], axis=0, keepdims=True) / count - mean * mean
    scale = gain * lax.rsqrt(variance + EPSILON)
    return 0.5 * scale, 0.5 * (shift - mean * scale)


def silu_of_half(half):
    return half + half * jnp.tanh(half)


def fold(values):
    rows, lanes = values.shape
    return jnp.sum(values.reshape(rows // 8, 8, lanes), axis=0)


def decode_kernel(
    tiles,
    spans,
    shares,
    *refs,
):
    cases = block_cases(tiles)
    refs = list(refs)

    def take(number):
        taken = refs[:number]
        del refs[:number]
        return taken

    w_mid_ref, table_ref, order_ref = take(3)
    latent_refs, w_in_refs = take(spans), take(shares)
    keep_ref, send_ref, denom_ref = take(3)
    chosen, taps, first, hidden, weights, partial, shown_ref, sems = take(8)

    own = denom_ref.shape[1]
    own_frames = keep_ref.shape[2]
    frames = own_frames * spans
    latent, wide = w_in_refs[0].shape[1:]
    rows_in = frames * latent
    rows_own = rows_in // spans
    depth_in = 27 * latent
    pixels = TSIDE * TSIDE
    lanes = partial.shape[3]
    tile_id = lax.axis_index("tile")
    mine = lax.axis_index("tm")
    chan_id = lax.axis_index("chan")

    copies = []
    for a in range(3):
        for b in range(3):
            for e in range(3):
                tap = 9 * a + 3 * b + e
                copy = pltpu.make_async_copy(
                    w_mid_ref.at[tap, :, pl.ds(pl.multiple_of(mine * lanes, LANES), lanes)],
                    weights.at[pl.ds(b * CH, CH), pl.ds((3 * a + e) * lanes, lanes)],
                    sems.at[tap],
                )
                copy.start()
                copies.append(copy)

    tile_row, tile_col = tile_id // GRID_X, tile_id % GRID_X
    gain_row = rows_own + 2
    w_out_row = gain_row + 2
    blend_row = w_out_row + 3
    order = order_ref[...]
    number_of = lax.broadcasted_iota(jnp.int32, order.shape, 0)
    lane_of = lax.broadcasted_iota(jnp.int32, order.shape, 1)
    rows_all = latent_refs[0].shape[0] // tiles
    turns = []
    for down, across in cases:
        wanted = tile_id + down * GRID_X + across
        found = (order == wanted.astype(jnp.float32)) & (lane_of == 0)
        place = jnp.sum(jnp.where(found, number_of.astype(jnp.float32), 0.0))
        turns.append((tile_id - place.astype(jnp.int32) + tiles) % tiles)
    for number, (down, across) in enumerate(cases):
        inside = (tile_row + down < tiles // GRID_X) & (tile_col + across < GRID_X)
        turn = turns[number]
        part = slice(number * LANES, (number + 1) * LANES)
        for steps in range(tiles):

            @pl.when(inside & (turn == steps))
            def _():
                for swap in range(spans):
                    at, tail_at = swap * rows_own, rows_in + swap * latent
                    block = latent_refs[swap][steps * rows_all : (steps + 1) * rows_all]
                    chosen[at : at + rows_own, part] = block[:rows_own]
                    chosen[tail_at : tail_at + latent, part] = block[rows_own : rows_own + latent]

        @pl.when(jnp.logical_not(inside))
        def _():
            chosen[:, part] = jnp.zeros((chosen.shape[0], LANES), chosen.dtype)

    slot = lax.broadcasted_iota(jnp.int32, (1, pixels), 1)
    up, along = slot // TSIDE, slot % TSIDE
    source = lax.broadcasted_iota(jnp.int32, (LANES, pixels), 0)
    tail = own - LANES

    def pick(first_pixel):
        parts = []
        for down, across in cases:
            u, v = up - down * STRIDE, along - across * STRIDE
            good = (u >= 0) & (u < STRIDE) & (v >= 0) & (v < STRIDE)
            wanted = jnp.where(good, u * STRIDE + v - first_pixel, -1)
            parts.append(jnp.where(source == wanted, 1.0, 0.0).astype(jnp.bfloat16))
        return jnp.concatenate(parts, axis=0)

    tails = chosen[rows_in:].astype(jnp.float32)
    width = tails.shape[1]
    turned = [pltpu.roll(tails, (-f * tail) % width, 1) if f else tails for f in range(own_frames)]
    tails = jnp.concatenate(
        [
            turned[f][swap * latent : (swap + 1) * latent]
            for swap in range(spans)
            for f in range(own_frames)
        ],
        axis=0,
    ).astype(jnp.bfloat16)
    in_tail = lax.broadcasted_iota(jnp.int32, tails.shape, 1) % LANES < tail
    tails = jnp.where(in_tail, tails.astype(jnp.float32), 0.0).astype(jnp.bfloat16)
    window = jnp.dot(
        chosen[:rows_in], pick(0), preferred_element_type=jnp.float32
    ) + jnp.dot(tails, pick(LANES), preferred_element_type=jnp.float32)
    taps[0:2] = jnp.zeros((2,) + taps.shape[1:], taps.dtype)
    for b in range(3):
        for e in range(3):
            inside = (
                (up + b - 1 >= 0)
                & (up + b - 1 < TSIDE)
                & (along + e - 1 >= 0)
                & (along + e - 1 < TSIDE)
            )
            offset = (b - 1) * TSIDE + e - 1
            moved = pltpu.roll(window, (-offset) % pixels, 1) if offset else window
            moved = jnp.where(inside, moved, 0.0).astype(jnp.bfloat16)
            for swap in range(spans):
                value = moved[swap * rows_own : (swap + 1) * rows_own]
                span = pl.ds(2 + (mine + swap) % spans * own_frames, own_frames)
                taps[span, 3 * b + e] = value.reshape(own_frames, latent, pixels)

    joined = jnp.concatenate(
        [w_in_refs[s][...].reshape(depth_in, wide) for s in range(shares)], axis=1
    )
    together = 2

    def first_step(step, carry):
        sums, squares = carry
        low = step * together
        patches = [taps[pl.ds(low + f, 3)].reshape(depth_in, pixels) for f in range(together)]
        values = lax.dot_general(
            jnp.concatenate(patches, axis=1),
            joined,
            (((0,), (0,)), ((), ())),
            preferred_element_type=jnp.float32,
        )
        for f in range(together):
            value = values[f * pixels : (f + 1) * pixels]
            first[low + f] = value
            sums = sums + fold(value)
            squares = squares + fold(value * value)
        return sums, squares

    zeros = jnp.zeros((8, CH), jnp.float32)
    sums, squares = lax.fori_loop(0, frames // together, first_step, (zeros, zeros))
    count = frames * (CH // GROUPS) * pixels
    affine = []
    for s in range(shares):
        at = s * rows_all + rows_own + latent
        table = latent_refs[0][at : at + wide // LANES * 4].astype(jnp.float32)
        pieces = [table[4 * lane : 4 * lane + 4] for lane in range(wide // LANES)]
        table = jnp.concatenate([part[0:2] + part[2:4] for part in pieces], axis=1)
        part = slice(s * wide, (s + 1) * wide)
        affine.append(
            group_affine(sums[:, part], squares[:, part], table[0:1], table[1:2], count)
        )
    channels = [
        pl.ds(pl.multiple_of((chan_id + s) % shares * wide, LANES), wide) for s in range(shares)
    ]

    def hide(f):
        edge = jnp.zeros((TSIDE, CH), jnp.bfloat16)
        hidden[f, 0:TSIDE] = edge
        hidden[f, TSIDE + pixels : 2 * TSIDE + pixels] = edge
        for s in range(shares):
            scale, bias = affine[s]
            value = first[f, :, s * wide : (s + 1) * wide] * scale + bias
            hidden[f, TSIDE : TSIDE + pixels, channels[s]] = silu_of_half(value).astype(
                jnp.bfloat16
            )

    def convolve(start, several, depth_taps):
        lhs = jnp.concatenate(
            [
                hidden[start : start + several, b * TSIDE : b * TSIDE + pixels].reshape(
                    several * pixels, CH
                )
                for b in range(3)
            ],
            axis=1,
        )
        low = depth_taps[0] * 3 * lanes
        product = jnp.dot(lhs, weights[:, low:], preferred_element_type=jnp.float32)
        for a in depth_taps:
            for e in range(3):
                at = (3 * a + e) * lanes - low
                for f in range(several):
                    target = start + f + 2 - a
                    value = product[f * pixels : (f + 1) * pixels, at : at + lanes]
                    if start + f == max(target - 2, 0):
                        partial[e, target] = value
                    else:
                        partial[e, target] += value

    column = lax.broadcasted_iota(jnp.int32, (pixels, lanes), 0) % TSIDE
    total = [jnp.zeros((8, lanes), jnp.float32)] * 2

    def gather(f):
        left = jnp.where(column == 0, 0.0, pltpu.roll(partial[0, f], 1, 0))
        right = jnp.where(column == TSIDE - 1, 0.0, pltpu.roll(partial[2, f], pixels - 1, 0))
        value = partial[1, f] + left + right
        partial[1, f] = value
        total[0] = total[0] + fold(value)
        total[1] = total[1] + fold(value * value)

    bounds = [0, 2, frames - 2, frames - 1, frames]
    groups = [range(low, high) for low, high in zip(bounds, bounds[1:]) if high > low]
    for copy in copies:
        copy.wait()
    for f in groups[0]:
        hide(f)
    for number, group in enumerate(groups):
        if number + 1 < len(groups):
            for f in groups[number + 1]:
                hide(f)
        convolve(
            group.start,
            len(group),
            tuple(a for a in range(3) if group.stop - 1 + 2 - a < frames),
        )
        if number:
            for f in groups[number - 1]:
                gather(f)
    for f in groups[-1]:
        gather(f)

    part = pl.ds(pl.multiple_of(mine * lanes, LANES), lanes)
    scale, bias = group_affine(
        total[0],
        total[1],
        table_ref[gain_row : gain_row + 1, part],
        table_ref[gain_row + 1 : gain_row + 2, part],
        count,
    )
    blend = table_ref[pl.ds(blend_row + tile_id, 1), :]
    blend = jnp.where(
        (tile_row * STRIDE + up < tiles // GRID_X * STRIDE)
        & (tile_col * STRIDE + along < GRID_X * STRIDE),
        blend,
        0.0,
    )
    w_out = jnp.concatenate(
        [table_ref[w_out_row : w_out_row + 3, part], jnp.zeros((5, lanes), jnp.float32)], axis=0
    ).astype(jnp.bfloat16)
    colors = []
    for f in range(frames):
        upper = silu_of_half(partial[1, f] * scale + bias).astype(jnp.bfloat16)
        color = lax.dot_general(
            w_out, upper, (((1,), (1,)), ((), ())), preferred_element_type=jnp.float32
        )
        colors.append(color * blend)
    colors = jnp.concatenate(colors, axis=0)

    slot_in = lax.broadcasted_iota(jnp.int32, (pixels, pixels), 0)
    pixel = lax.broadcasted_iota(jnp.int32, (pixels, pixels), 1)
    shown, weight_rows = [], []
    for down, across in cases:
        u, v = slot_in // TSIDE - down * STRIDE, slot_in % TSIDE - across * STRIDE
        good = (u >= 0) & (u < STRIDE) & (v >= 0) & (v < STRIDE) & (u * STRIDE + v == pixel)
        shown.append(jnp.where(good, 1.0, 0.0).astype(jnp.bfloat16))
        inside = (tile_row >= down) & (tile_col >= across)
        other = jnp.maximum(tile_id - down * GRID_X - across, 0)
        weight = jnp.where(inside, table_ref[pl.ds(blend_row + other, 1), :], 0.0)
        weight_rows.append(jnp.broadcast_to(weight, (8, pixels)))
    shown_ref[...] = exact_dot(
        jnp.concatenate([colors] + weight_rows, axis=0), jnp.concatenate(shown, axis=1)
    )
    denom = jnp.zeros((8, own), jnp.float32)
    for number in range(len(cases)):
        lane = slice(number * pixels, number * pixels + own)
        row = 8 * (frames + number)
        denom = denom + shown_ref[row : row + 8, lane]
        for swap in range(spans):
            target = keep_ref if swap == 0 else send_ref.at[swap - 1]
            base = (mine + swap) % spans * own_frames * 8
            for at in range(own_frames):
                for o in range(3):
                    target[number, o, at : at + 1, :] = shown_ref[
                        pl.ds(base + 8 * at + o, 1), lane
                    ]
    denom_ref[...] = denom


def from_ring(value, axis):
    count = lax.axis_size(axis)
    return [
        lax.ppermute(value, axis, [((d + turn) % count, d) for d in range(count)])
        for turn in range(1, count)
    ]


def ring_sum(kept, sent, axis):
    count = lax.axis_size(axis)
    for turn in range(1, count):
        kept = kept + lax.ppermute(
            sent[turn - 1], axis, [(d, (d + turn) % count) for d in range(count)]
        )
    return kept


def small_table(*values):
    values = [value.reshape(-1, value.shape[-1]) for value in values]
    wide = max(value.shape[1] for value in values)
    height = sum(value.shape[0] for value in values)
    total, row = 0.0, 0
    for value in values:
        below = height - row - value.shape[0]
        value = jnp.pad(value.astype(jnp.float32), ((row, below), (0, wide - value.shape[1])))
        total = total + value
        row = height - below
    return total


def exchange_latents(frames, latent, own, table):
    tiles, shares = lax.axis_size("tile"), lax.axis_size("chan")
    tail = own - LANES
    height = frames * latent
    mine = table[:height, :own].astype(jnp.bfloat16)
    tails = sum(
        jnp.pad(
            mine[f * latent : (f + 1) * latent, LANES:],
            ((0, 0), (tail * f, LANES - tail * (f + 1))),
        )
        for f in range(frames)
    )
    affine = table[height : height + 2]
    high = lax.reduce_precision(affine, 8, 7)
    low = lax.reduce_precision(affine - high, 8, 7)
    affine = jnp.concatenate([high, low], axis=0).astype(jnp.bfloat16)
    rows = [affine[:, at : at + LANES] for at in range(0, affine.shape[1], LANES)]
    rows = jnp.concatenate(rows, axis=0)
    rows = jnp.pad(rows, ((0, -rows.shape[0] % 16), (0, 0)))
    message = jnp.concatenate([mine[:, :LANES], tails, rows], axis=0)
    got = [message]
    for steps in range(1, tiles):
        turn = steps if steps < shares else 0
        pairs = [
            (t * shares + (c + turn) % shares, (t + steps) % tiles * shares + c)
            for t in range(tiles)
            for c in range(shares)
        ]
        got.append(lax.ppermute(message, ("tile", "chan"), pairs))
    stack = jnp.concatenate(got, axis=0)
    return [stack] + from_ring(stack, "tm")


def lanes_body(
    latents, tile_order, w_in, gain_in, shift_in, w_mid, gain_mid, shift_mid, w_out, blend_weight
):
    own_frames, latent, own = latents.shape
    spans = lax.axis_size("tm")
    shares = lax.axis_size("chan")
    frames = own_frames * spans
    tiles = tile_order.shape[0]
    wide = w_in.shape[2]
    lanes = wide // spans
    pixels = TSIDE * TSIDE
    cases = block_cases(tiles)

    w_in_all = [(from_ring(other, "tm") or [other])[0] for other in from_ring(w_in, "chan")]
    table = lax.optimization_barrier(
        small_table(
            latents.reshape(own_frames * latent, own),
            gain_in,
            shift_in,
            gain_mid,
            shift_mid,
            w_out,
            blend_weight,
        )
    )
    latents_all = exchange_latents(own_frames, latent, own, table)
    _, w_in, tile_order = lax.optimization_barrier((table, w_in, tile_order))
    order = jnp.broadcast_to(tile_order.astype(jnp.float32)[:, None], (tiles, LANES))
    w_in_own = from_ring(w_in, "tm")[:1] or [w_in]

    vmem = pl.BlockSpec(memory_space=pltpu.VMEM)
    piece = (len(cases), 3, own_frames, own)
    kept, sent, denom = pl.pallas_call(
        functools.partial(decode_kernel, tiles, spans, shares),
        out_shape=[
            jax.ShapeDtypeStruct(piece, jnp.float32),
            jax.ShapeDtypeStruct((max(spans - 1, 1),) + piece, jnp.float32),
            jax.ShapeDtypeStruct((8, own), jnp.float32),
        ],
        in_specs=[pl.BlockSpec(memory_space=pl.ANY)] + [vmem] * (2 + spans + shares),
        out_specs=[vmem] * 3,
        scratch_shapes=[
            pltpu.VMEM(((frames + spans) * latent, len(cases) * LANES), jnp.bfloat16),
            pltpu.VMEM((frames + 2, 9, latent, pixels), jnp.bfloat16),
            pltpu.VMEM((frames, pixels, CH), jnp.float32),
            pltpu.VMEM((frames, pixels + 2 * TSIDE, CH), jnp.bfloat16),
            pltpu.VMEM((3 * CH, 9 * lanes), jnp.bfloat16),
            pltpu.VMEM((3, frames, pixels, lanes), jnp.float32),
            pltpu.VMEM((8 * (frames + len(cases)), len(cases) * pixels), jnp.float32),
            pltpu.SemaphoreType.DMA((27,)),
        ],
        compiler_params=pltpu.CompilerParams(vmem_limit_bytes=VMEM_BYTES),
        cost_estimate=pl.CostEstimate(
            flops=2 * frames * pixels * 27 * CH * lanes, bytes_accessed=8_000_000, transcendentals=0
        ),
    )(w_mid, table, order, *latents_all, *w_in_own, *w_in_all)
    total = ring_sum(kept, sent, "tm")
    total = ring_sum(total, [total] * (shares - 1), "chan")
    numer = total[0]
    for number, (down, across) in enumerate(cases):
        steps = down * GRID_X + across
        if steps and steps < tiles:
            numer = numer + shifted(total[number], "tile", steps)
    return jnp.transpose(numer / denom[0][None, None, :], (1, 0, 2))


def solution(mesh):
    placed = (
        P("tm", "groups", "tile"),
        P("groups"),
        P(None, None, "chan"),
        P("chan"),
        P("chan"),
        P(None, None, "chan"),
        P("chan"),
        P("chan"),
        P(None, "chan"),
        P("groups", None),
    )
    whole_lanes = (
        CH % (mesh.shape["chan"] * mesh.shape["tm"] * LANES) == 0
        and mesh.shape["chan"] <= mesh.shape["tile"]
    )
    return jax.shard_map(
        lanes_body if whole_lanes else general_body,
        mesh=mesh,
        in_specs=placed,
        out_specs=P("tm", "groups", "tile"),
        check_vma=False,
    )
```

```python
import functools

import jax
import jax.numpy as jnp
from jax import lax
from jax.experimental import pallas as pl
from jax.experimental.pallas import tpu as pltpu
from jax.sharding import PartitionSpec as P

CH = 512
GROUPS = 32
TSIDE = 16
STRIDE = 12
GRID_X = 4

EPSILON = 1e-06
LANES = 128
VMEM_BYTES = 48 * 1024 * 1024


def shifted(value, axis, steps):
    count = lax.axis_size(axis)
    leading, last = (max(0, -steps), min(count, count - steps))
    return lax.ppermute(value, axis, [(source, source + steps) for source in range(leading, last)])


def window_index(tile_id, tiles):
    slots = jnp.arange(TSIDE * TSIDE, dtype=jnp.int32)
    row = tile_id // GRID_X * STRIDE + slots // TSIDE
    col = tile_id % GRID_X * STRIDE + slots % TSIDE
    valid = (row < tiles // GRID_X * STRIDE) & (col < GRID_X * STRIDE)
    block = row // STRIDE * GRID_X + col // STRIDE
    index = block * (STRIDE * STRIDE) + row % STRIDE * STRIDE + col % STRIDE
    return (jnp.where(valid, index, 0), valid)


def causal_conv(extended, weights, frames, side):
    pixels = side * side
    rows = jnp.arange(pixels, dtype=jnp.int32) // side
    cols = jnp.arange(pixels, dtype=jnp.int32) % side
    total = jnp.zeros((frames, weights.shape[2], pixels), jnp.float32)
    for depth in range(3):
        window = extended[depth : depth + frames]
        for down in range(3):
            for across in range(3):
                offset = (down - 1) * side + (across - 1)
                inside = (
                    (rows + down - 1 >= 0)
                    & (rows + down - 1 < side)
                    & (cols + across - 1 >= 0)
                    & (cols + across - 1 < side)
                )
                moved = jnp.roll(window, -offset, axis=2)
                moved = jnp.where(inside[None, None, :], moved, jnp.zeros_like(moved))
                total = total + jnp.einsum(
                    "fcp,co->fop",
                    moved,
                    weights[9 * depth + 3 * down + across],
                    preferred_element_type=jnp.float32,
                )
    return total


def with_history(values):
    frames = values.shape[0]
    earlier = shifted(values[frames - 2 :], "tm", 1)
    return jnp.concatenate([earlier, values], axis=0)


def normalize(values, gain, shift, total_frames):
    frames, chans, pixels = values.shape
    width = CH // GROUPS
    grouped = values.reshape(frames, chans // width, width, pixels)
    sums = jnp.sum(grouped, axis=(0, 2, 3))
    squares = jnp.sum(grouped * grouped, axis=(0, 2, 3))
    sums, squares = lax.psum((sums, squares), "tm")
    count = total_frames * width * pixels
    mean = sums / count
    variance = squares / count - mean * mean
    scale = lax.rsqrt(variance + EPSILON)
    normed = (grouped - mean[None, :, None, None]) * scale[None, :, None, None]
    normed = normed.reshape(frames, chans, pixels) * gain[None, :, None] + shift[None, :, None]
    return jax.nn.silu(normed).astype(jnp.bfloat16)


def spread(color, weight, index, total_pixels):
    numer = (
        jnp.zeros((color.shape[0], 3, total_pixels), jnp.float32)
        .at[:, :, index]
        .add(color * weight[None, None, :])
    )
    denom = jnp.zeros((total_pixels,), jnp.float32).at[index].add(weight)
    return (numer, denom)


def route_owned(numer, denom, tile_id, own):
    frames = numer.shape[0]
    margin = (GRID_X + 1) * own
    numer_wide = jnp.concatenate([numer, jnp.zeros((frames, 3, margin), jnp.float32)], axis=2)
    denom_wide = jnp.concatenate([denom, jnp.zeros((margin,), jnp.float32)], axis=0)
    first_pixel = tile_id * own

    def block_at(offset):
        start_pixel = first_pixel + offset * own
        return (
            lax.dynamic_slice_in_dim(numer_wide, start_pixel, own, 2),
            lax.dynamic_slice_in_dim(denom_wide, start_pixel, own, 0),
        )

    owned_numer, owned_denom = block_at(0)
    for offset in (1, GRID_X, GRID_X + 1):
        piece_numer, piece_denom = block_at(offset)
        got_numer, got_denom = shifted((piece_numer, piece_denom), "tile", offset)
        owned_numer = owned_numer + got_numer
        owned_denom = owned_denom + got_denom
    return (owned_numer, owned_denom)


def general_body(
    latents, tile_order, w_in, gain_in, shift_in, w_mid, gain_mid, shift_mid, w_out, blend_weight
):
    frames = latents.shape[0]
    total_frames = frames * lax.axis_size("tm")
    tiles = tile_order.shape[0]
    own = STRIDE * STRIDE
    total_pixels = tiles * own
    tile_id = lax.axis_index("tile")
    index, valid = window_index(tile_id, tiles)
    whole = lax.all_gather(latents, "tile", axis=2, tiled=True)
    blocks = whole.reshape(frames, whole.shape[1], tiles, own)
    image = (
        jnp.zeros_like(blocks)
        .at[:, :, tile_order]
        .set(blocks)
        .reshape(frames, whole.shape[1], total_pixels)
    )
    window = jnp.where(
        valid[None, None, :], jnp.take(image, index, axis=2), jnp.zeros((), jnp.bfloat16)
    )
    first = causal_conv(with_history(window), w_in, frames, TSIDE)
    hidden = normalize(first, gain_in, shift_in, total_frames)
    second = causal_conv(
        lax.all_gather(with_history(hidden), "chan", axis=1, tiled=True), w_mid, frames, TSIDE
    )
    upper = normalize(second, gain_mid, shift_mid, total_frames)
    color = jnp.einsum("oc,fcp->fop", w_out, upper, preferred_element_type=jnp.float32)
    weight = jnp.where(valid, blend_weight[tile_id], jnp.float32(0.0))
    numer, denom = spread(color, weight, index, total_pixels)
    numer, denom = route_owned(numer, denom, tile_id, own)
    numer = lax.psum(numer, "chan")
    return numer / denom[None, None, :]


def block_cases(tiles):
    downs = (0, 1) if tiles // GRID_X > 1 else (0,)
    return [(down, across) for down in downs for across in (0, 1)]


def exact_dot(values, ones):
    rows = values.shape[0]
    high = values.astype(jnp.bfloat16)
    rest = values - high.astype(jnp.float32)
    middle = rest.astype(jnp.bfloat16)
    low = (rest - middle.astype(jnp.float32)).astype(jnp.bfloat16)
    total = jnp.dot(
        jnp.concatenate([high, middle, low], axis=0), ones, preferred_element_type=jnp.float32
    )
    return total[:rows] + total[rows : 2 * rows] + total[2 * rows :]


def group_affine(sums, squares, gain, shift, count):
    lanes = sums.shape[1]
    width = CH // GROUPS
    same = lax.broadcasted_iota(jnp.int32, (lanes, lanes), 0) // width == (
        lax.broadcasted_iota(jnp.int32, (lanes, lanes), 1) // width
    )
    total = exact_dot(
        jnp.concatenate([sums, squares], axis=0), jnp.where(same, 1.0, 0.0).astype(jnp.bfloat16)
    )
    mean = jnp.sum(total[:8], axis=0, keepdims=True) / count
    variance = jnp.sum(total[8:], axis=0, keepdims=True) / count - mean * mean
    scale = gain * lax.rsqrt(variance + EPSILON)
    return 0.5 * scale, 0.5 * (shift - mean * scale)


def silu_of_half(half):
    return half + half * jnp.tanh(half)


def fold(values):
    rows, lanes = values.shape
    return jnp.sum(values.reshape(rows // 8, 8, lanes), axis=0)


def decode_kernel(
    tiles,
    spans,
    shares,
    *refs,
):
    cases = block_cases(tiles)
    refs = list(refs)

    def take(number):
        taken = refs[:number]
        del refs[:number]
        return taken

    w_mid_ref, table_ref, order_ref = take(3)
    latent_refs, w_in_refs = take(spans), take(shares)
    keep_ref, send_ref, denom_ref = take(3)
    chosen, taps, first, hidden, weights, partial, shown_ref, sems = take(8)

    own = denom_ref.shape[1]
    own_frames = keep_ref.shape[2]
    frames = own_frames * spans
    latent, wide = w_in_refs[0].shape[1:]
    rows_in = frames * latent
    rows_own = rows_in // spans
    depth_in = 27 * latent
    pixels = TSIDE * TSIDE
    lanes = partial.shape[3]
    tile_id = lax.axis_index("tile")
    mine = lax.axis_index("tm")
    chan_id = lax.axis_index("chan")

    copies = []
    for a in range(3):
        for b in range(3):
            for e in range(3):
                tap = 9 * a + 3 * b + e
                copy = pltpu.make_async_copy(
                    w_mid_ref.at[tap, :, pl.ds(pl.multiple_of(mine * lanes, LANES), lanes)],
                    weights.at[pl.ds(b * CH, CH), pl.ds((3 * a + e) * lanes, lanes)],
                    sems.at[tap],
                )
                copy.start()
                copies.append(copy)

    tile_row, tile_col = tile_id // GRID_X, tile_id % GRID_X
    gain_row = rows_own + 2
    w_out_row = gain_row + 2
    blend_row = w_out_row + 3
    order = order_ref[...]
    number_of = lax.broadcasted_iota(jnp.int32, order.shape, 0)
    lane_of = lax.broadcasted_iota(jnp.int32, order.shape, 1)
    rows_all = latent_refs[0].shape[0] // tiles
    turns = []
    for down, across in cases:
        wanted = tile_id + down * GRID_X + across
        found = (order == wanted.astype(jnp.float32)) & (lane_of == 0)
        place = jnp.sum(jnp.where(found, number_of.astype(jnp.float32), 0.0))
        turns.append((tile_id - place.astype(jnp.int32) + tiles) % tiles)
    for number, (down, across) in enumerate(cases):
        inside = (tile_row + down < tiles // GRID_X) & (tile_col + across < GRID_X)
        turn = turns[number]
        part = slice(number * LANES, (number + 1) * LANES)
        for steps in range(tiles):

            @pl.when(inside & (turn == steps))
            def _():
                for swap in range(spans):
                    at, tail_at = swap * rows_own, rows_in + swap * latent
                    block = latent_refs[swap][steps * rows_all : (steps + 1) * rows_all]
                    chosen[at : at + rows_own, part] = block[:rows_own]
                    chosen[tail_at : tail_at + latent, part] = block[rows_own : rows_own + latent]

        @pl.when(jnp.logical_not(inside))
        def _():
            chosen[:, part] = jnp.zeros((chosen.shape[0], LANES), chosen.dtype)

    slot = lax.broadcasted_iota(jnp.int32, (1, pixels), 1)
    up, along = slot // TSIDE, slot % TSIDE
    source = lax.broadcasted_iota(jnp.int32, (LANES, pixels), 0)
    tail = own - LANES

    def pick(first_pixel):
        parts = []
        for down, across in cases:
            u, v = up - down * STRIDE, along - across * STRIDE
            good = (u >= 0) & (u < STRIDE) & (v >= 0) & (v < STRIDE)
            wanted = jnp.where(good, u * STRIDE + v - first_pixel, -1)
            parts.append(jnp.where(source == wanted, 1.0, 0.0).astype(jnp.bfloat16))
        return jnp.concatenate(parts, axis=0)

    tails = chosen[rows_in:].astype(jnp.float32)
    width = tails.shape[1]
    turned = [pltpu.roll(tails, (-f * tail) % width, 1) if f else tails for f in range(own_frames)]
    tails = jnp.concatenate(
        [
            turned[f][swap * latent : (swap + 1) * latent]
            for swap in range(spans)
            for f in range(own_frames)
        ],
        axis=0,
    ).astype(jnp.bfloat16)
    in_tail = lax.broadcasted_iota(jnp.int32, tails.shape, 1) % LANES < tail
    tails = jnp.where(in_tail, tails.astype(jnp.float32), 0.0).astype(jnp.bfloat16)
    window = jnp.dot(
        chosen[:rows_in], pick(0), preferred_element_type=jnp.float32
    ) + jnp.dot(tails, pick(LANES), preferred_element_type=jnp.float32)
    taps[0:2] = jnp.zeros((2,) + taps.shape[1:], taps.dtype)
    for b in range(3):
        for e in range(3):
            inside = (
                (up + b - 1 >= 0)
                & (up + b - 1 < TSIDE)
                & (along + e - 1 >= 0)
                & (along + e - 1 < TSIDE)
            )
            offset = (b - 1) * TSIDE + e - 1
            moved = pltpu.roll(window, (-offset) % pixels, 1) if offset else window
            moved = jnp.where(inside, moved, 0.0).astype(jnp.bfloat16)
            for swap in range(spans):
                value = moved[swap * rows_own : (swap + 1) * rows_own]
                span = pl.ds(2 + (mine + swap) % spans * own_frames, own_frames)
                taps[span, 3 * b + e] = value.reshape(own_frames, latent, pixels)

    joined = jnp.concatenate(
        [w_in_refs[s][:27].reshape(depth_in, wide) for s in range(shares)], axis=1
    )
    sums = jnp.zeros((8, CH), jnp.float32)
    squares = jnp.zeros((8, CH), jnp.float32)
    for low in range(0, frames, 2):
        several = range(low, min(low + 2, frames))
        patches = [taps[f : f + 3].reshape(depth_in, pixels) for f in several]
        values = lax.dot_general(
            jnp.concatenate(patches, axis=1),
            joined,
            (((0,), (0,)), ((), ())),
            preferred_element_type=jnp.float32,
        )
        for f in several:
            value = values[(f - low) * pixels : (f - low + 1) * pixels]
            first[f] = value
            sums = sums + fold(value)
            squares = squares + fold(value * value)
    count = frames * (CH // GROUPS) * pixels
    affine = []
    for s in range(shares):
        at = s * rows_all + rows_own + latent
        table = latent_refs[0][at : at + wide // LANES * 4].astype(jnp.float32)
        pieces = [table[4 * lane : 4 * lane + 4] for lane in range(wide // LANES)]
        table = jnp.concatenate([part[0:2] + part[2:4] for part in pieces], axis=1)
        part = slice(s * wide, (s + 1) * wide)
        affine.append(
            group_affine(sums[:, part], squares[:, part], table[0:1], table[1:2], count)
        )
    channels = [
        pl.ds(pl.multiple_of((chan_id + s) % shares * wide, LANES), wide) for s in range(shares)
    ]

    def hide(f):
        edge = jnp.zeros((TSIDE, CH), jnp.bfloat16)
        hidden[f, 0:TSIDE] = edge
        hidden[f, TSIDE + pixels : 2 * TSIDE + pixels] = edge
        for s in range(shares):
            scale, bias = affine[s]
            value = first[f, :, s * wide : (s + 1) * wide] * scale + bias
            hidden[f, TSIDE : TSIDE + pixels, channels[s]] = silu_of_half(value).astype(
                jnp.bfloat16
            )

    def convolve(start, several, depth_taps):
        lhs = jnp.concatenate(
            [
                hidden[start : start + several, b * TSIDE : b * TSIDE + pixels].reshape(
                    several * pixels, CH
                )
                for b in range(3)
            ],
            axis=1,
        )
        low = depth_taps[0] * 3 * lanes
        odd = len(depth_taps) % 2
        product = jnp.dot(
            lhs, weights[:, low : (9 - odd) * lanes], preferred_element_type=jnp.float32
        )
        if odd:
            rows = jnp.concatenate(
                [weights[b * CH : (b + 1) * CH, 8 * lanes :] for b in range(3)], axis=1
            )
            apart = jnp.dot(lhs[:, CH : 2 * CH], rows, preferred_element_type=jnp.float32)
        edge = jnp.zeros((TSIDE, lanes), jnp.float32)
        for a in depth_taps:
            for e in range(3):
                at = (3 * a + e) * lanes - low
                for f in range(several):
                    target = start + f + 2 - a
                    if odd and (a, e) == (2, 2):
                        value = apart[f * pixels : (f + 1) * pixels]
                        above = value[: pixels - TSIDE, :lanes]
                        below = value[TSIDE:, 2 * lanes :]
                        value = (
                            value[:, lanes : 2 * lanes]
                            + jnp.concatenate([edge, above], axis=0)
                            + jnp.concatenate([below, edge], axis=0)
                        )
                    else:
                        value = product[f * pixels : (f + 1) * pixels, at : at + lanes]
                    if start + f == max(target - 2, 0):
                        partial[e, target] = value
                    else:
                        partial[e, target] += value

    column = lax.broadcasted_iota(jnp.int32, (pixels, lanes), 0) % TSIDE
    total = [jnp.zeros((8, lanes), jnp.float32)] * 2

    def gather(f):
        left = jnp.where(column == 0, 0.0, pltpu.roll(partial[0, f], 1, 0))
        right = jnp.where(column == TSIDE - 1, 0.0, pltpu.roll(partial[2, f], pixels - 1, 0))
        value = partial[1, f] + left + right
        partial[1, f] = value
        total[0] = total[0] + fold(value)
        total[1] = total[1] + fold(value * value)

    bounds = [0, 2, frames - 2, frames - 1, frames]
    groups = [range(low, high) for low, high in zip(bounds, bounds[1:]) if high > low]
    for copy in copies:
        copy.wait()
    for f in groups[0]:
        hide(f)
    for number, group in enumerate(groups):
        if number + 1 < len(groups):
            for f in groups[number + 1]:
                hide(f)
        convolve(
            group.start,
            len(group),
            tuple(a for a in range(3) if group.stop - 1 + 2 - a < frames),
        )
        if number:
            for f in groups[number - 1]:
                gather(f)
    for f in groups[-1]:
        gather(f)

    part = pl.ds(pl.multiple_of(mine * lanes, LANES), lanes)
    scale, bias = group_affine(
        total[0],
        total[1],
        table_ref[gain_row : gain_row + 1, part],
        table_ref[gain_row + 1 : gain_row + 2, part],
        count,
    )
    blend = table_ref[pl.ds(blend_row + tile_id, 1), :]
    blend = jnp.where(
        (tile_row * STRIDE + up < tiles // GRID_X * STRIDE)
        & (tile_col * STRIDE + along < GRID_X * STRIDE),
        blend,
        0.0,
    )
    w_out = jnp.concatenate(
        [table_ref[w_out_row : w_out_row + 3, part], jnp.zeros((5, lanes), jnp.float32)], axis=0
    ).astype(jnp.bfloat16)
    colors = []
    for f in range(frames):
        upper = silu_of_half(partial[1, f] * scale + bias).astype(jnp.bfloat16)
        color = lax.dot_general(
            w_out, upper, (((1,), (1,)), ((), ())), preferred_element_type=jnp.float32
        )
        colors.append(color * blend)
    colors = jnp.concatenate(colors, axis=0)

    slot_in = lax.broadcasted_iota(jnp.int32, (pixels, pixels), 0)
    pixel = lax.broadcasted_iota(jnp.int32, (pixels, pixels), 1)
    shown, weight_rows = [], []
    for down, across in cases:
        u, v = slot_in // TSIDE - down * STRIDE, slot_in % TSIDE - across * STRIDE
        good = (u >= 0) & (u < STRIDE) & (v >= 0) & (v < STRIDE) & (u * STRIDE + v == pixel)
        shown.append(jnp.where(good, 1.0, 0.0).astype(jnp.bfloat16))
        inside = (tile_row >= down) & (tile_col >= across)
        other = jnp.maximum(tile_id - down * GRID_X - across, 0)
        weight = jnp.where(inside, table_ref[pl.ds(blend_row + other, 1), :], 0.0)
        weight_rows.append(jnp.broadcast_to(weight, (8, pixels)))
    shown_ref[...] = exact_dot(
        jnp.concatenate([colors] + weight_rows, axis=0), jnp.concatenate(shown, axis=1)
    )
    denom = jnp.zeros((8, own), jnp.float32)
    for number in range(len(cases)):
        lane = slice(number * pixels, number * pixels + own)
        row = 8 * (frames + number)
        denom = denom + shown_ref[row : row + 8, lane]
        for swap in range(spans):
            target = keep_ref if swap == 0 else send_ref.at[swap - 1]
            base = (mine + swap) % spans * own_frames * 8
            for at in range(own_frames):
                for o in range(3):
                    target[number, o, at : at + 1, :] = shown_ref[
                        pl.ds(base + 8 * at + o, 1), lane
                    ]
    denom_ref[...] = denom


def from_ring(value, axis):
    count = lax.axis_size(axis)
    return [
        lax.ppermute(value, axis, [((d + turn) % count, d) for d in range(count)])
        for turn in range(1, count)
    ]


def ring_sum(kept, sent, axis):
    count = lax.axis_size(axis)
    for turn in range(1, count):
        kept = kept + lax.ppermute(
            sent[turn - 1], axis, [(d, (d + turn) % count) for d in range(count)]
        )
    return kept


def small_table(*values):
    values = [value.reshape(-1, value.shape[-1]) for value in values]
    wide = max(value.shape[1] for value in values)
    height = sum(value.shape[0] for value in values)
    total, row = 0.0, 0
    for value in values:
        below = height - row - value.shape[0]
        value = jnp.pad(value.astype(jnp.float32), ((row, below), (0, wide - value.shape[1])))
        total = total + value
        row = height - below
    return total


def exchange_latents(frames, latent, own, table):
    tiles, shares = lax.axis_size("tile"), lax.axis_size("chan")
    tail = own - LANES
    height = frames * latent
    mine = table[:height, :own].astype(jnp.bfloat16)
    tails = sum(
        jnp.pad(
            mine[f * latent : (f + 1) * latent, LANES:],
            ((0, 0), (tail * f, LANES - tail * (f + 1))),
        )
        for f in range(frames)
    )
    affine = table[height : height + 2]
    high = lax.reduce_precision(affine, 8, 7)
    low = lax.reduce_precision(affine - high, 8, 7)
    affine = jnp.concatenate([high, low], axis=0).astype(jnp.bfloat16)
    rows = [affine[:, at : at + LANES] for at in range(0, affine.shape[1], LANES)]
    rows = jnp.concatenate(rows, axis=0)
    rows = jnp.pad(rows, ((0, -rows.shape[0] % 16), (0, 0)))
    message = jnp.concatenate([mine[:, :LANES], tails, rows], axis=0)
    got = [message]
    for steps in range(1, tiles):
        turn = steps if steps < shares else 0
        pairs = [
            (t * shares + (c + turn) % shares, (t + steps) % tiles * shares + c)
            for t in range(tiles)
            for c in range(shares)
        ]
        got.append(lax.ppermute(message, ("tile", "chan"), pairs))
    stack = jnp.concatenate(got, axis=0)
    return [stack] + from_ring(stack, "tm")


def lanes_body(
    latents, tile_order, w_in, gain_in, shift_in, w_mid, gain_mid, shift_mid, w_out, blend_weight
):
    own_frames, latent, own = latents.shape
    spans = lax.axis_size("tm")
    shares = lax.axis_size("chan")
    frames = own_frames * spans
    tiles = tile_order.shape[0]
    wide = w_in.shape[2]
    lanes = wide // spans
    pixels = TSIDE * TSIDE
    cases = block_cases(tiles)

    w_in_all = [(from_ring(other, "tm") or [other])[0] for other in from_ring(w_in, "chan")]
    table = lax.optimization_barrier(
        small_table(
            latents.reshape(own_frames * latent, own),
            gain_in,
            shift_in,
            gain_mid,
            shift_mid,
            w_out,
            blend_weight,
        )
    )
    latents_all = exchange_latents(own_frames, latent, own, table)
    _, w_in, tile_order = lax.optimization_barrier((table, w_in, tile_order))
    order = jnp.broadcast_to(tile_order.astype(jnp.float32)[:, None], (tiles, LANES))
    w_in_own = from_ring(w_in, "tm")[:1] or [w_in]

    vmem = pl.BlockSpec(memory_space=pltpu.VMEM)
    piece = (len(cases), 3, own_frames, own)
    kept, sent, denom = pl.pallas_call(
        functools.partial(decode_kernel, tiles, spans, shares),
        out_shape=[
            jax.ShapeDtypeStruct(piece, jnp.float32),
            jax.ShapeDtypeStruct((max(spans - 1, 1),) + piece, jnp.float32),
            jax.ShapeDtypeStruct((8, own), jnp.float32),
        ],
        in_specs=[pl.BlockSpec(memory_space=pl.ANY)] + [vmem] * (2 + spans + shares),
        out_specs=[vmem] * 3,
        scratch_shapes=[
            pltpu.VMEM(((frames + spans) * latent, len(cases) * LANES), jnp.bfloat16),
            pltpu.VMEM((frames + 2, 9, latent, pixels), jnp.bfloat16),
            pltpu.VMEM((frames, pixels, CH), jnp.float32),
            pltpu.VMEM((frames, pixels + 2 * TSIDE, CH), jnp.bfloat16),
            pltpu.VMEM((3 * CH, 9 * lanes), jnp.bfloat16),
            pltpu.VMEM((3, frames, pixels, lanes), jnp.float32),
            pltpu.VMEM((8 * (frames + len(cases)), len(cases) * pixels), jnp.float32),
            pltpu.SemaphoreType.DMA((27,)),
        ],
        compiler_params=pltpu.CompilerParams(vmem_limit_bytes=VMEM_BYTES),
        cost_estimate=pl.CostEstimate(
            flops=2 * frames * pixels * 27 * CH * lanes, bytes_accessed=8_000_000, transcendentals=0
        ),
    )(w_mid, table, order, *latents_all, *w_in_own, *w_in_all)
    total = ring_sum(kept, sent, "tm")
    total = ring_sum(total, [total] * (shares - 1), "chan")
    numer = total[0]
    for number, (down, across) in enumerate(cases):
        steps = down * GRID_X + across
        if steps and steps < tiles:
            numer = numer + shifted(total[number], "tile", steps)
    return jnp.transpose(numer / denom[0][None, None, :], (1, 0, 2))


def solution(mesh):
    placed = (
        P("tm", "groups", "tile"),
        P("groups"),
        P(None, None, "chan"),
        P("chan"),
        P("chan"),
        P(None, None, "chan"),
        P("chan"),
        P("chan"),
        P(None, "chan"),
        P("groups", None),
    )
    whole_lanes = (
        CH % (mesh.shape["chan"] * mesh.shape["tm"] * LANES) == 0
        and mesh.shape["chan"] <= mesh.shape["tile"]
    )
    return jax.shard_map(
        lanes_body if whole_lanes else general_body,
        mesh=mesh,
        in_specs=placed,
        out_specs=P("tm", "groups", "tile"),
        check_vma=False,
    )
```

```python
import functools

import jax
import jax.numpy as jnp
from jax import lax
from jax.experimental import pallas as pl
from jax.experimental.pallas import tpu as pltpu
from jax.sharding import PartitionSpec as P

CH = 512
GROUPS = 32
TSIDE = 16
STRIDE = 12
GRID_X = 4

EPSILON = 1e-06
LANES = 128
VMEM_BYTES = 48 * 1024 * 1024


def shifted(value, axis, steps):
    count = lax.axis_size(axis)
    leading, last = (max(0, -steps), min(count, count - steps))
    return lax.ppermute(value, axis, [(source, source + steps) for source in range(leading, last)])


def window_index(tile_id, tiles):
    slots = jnp.arange(TSIDE * TSIDE, dtype=jnp.int32)
    row = tile_id // GRID_X * STRIDE + slots // TSIDE
    col = tile_id % GRID_X * STRIDE + slots % TSIDE
    valid = (row < tiles // GRID_X * STRIDE) & (col < GRID_X * STRIDE)
    block = row // STRIDE * GRID_X + col // STRIDE
    index = block * (STRIDE * STRIDE) + row % STRIDE * STRIDE + col % STRIDE
    return (jnp.where(valid, index, 0), valid)


def causal_conv(extended, weights, frames, side):
    pixels = side * side
    rows = jnp.arange(pixels, dtype=jnp.int32) // side
    cols = jnp.arange(pixels, dtype=jnp.int32) % side
    total = jnp.zeros((frames, weights.shape[2], pixels), jnp.float32)
    for depth in range(3):
        window = extended[depth : depth + frames]
        for down in range(3):
            for across in range(3):
                offset = (down - 1) * side + (across - 1)
                inside = (
                    (rows + down - 1 >= 0)
                    & (rows + down - 1 < side)
                    & (cols + across - 1 >= 0)
                    & (cols + across - 1 < side)
                )
                moved = jnp.roll(window, -offset, axis=2)
                moved = jnp.where(inside[None, None, :], moved, jnp.zeros_like(moved))
                total = total + jnp.einsum(
                    "fcp,co->fop",
                    moved,
                    weights[9 * depth + 3 * down + across],
                    preferred_element_type=jnp.float32,
                )
    return total


def with_history(values):
    frames = values.shape[0]
    earlier = shifted(values[frames - 2 :], "tm", 1)
    return jnp.concatenate([earlier, values], axis=0)


def normalize(values, gain, shift, total_frames):
    frames, chans, pixels = values.shape
    width = CH // GROUPS
    grouped = values.reshape(frames, chans // width, width, pixels)
    sums = jnp.sum(grouped, axis=(0, 2, 3))
    squares = jnp.sum(grouped * grouped, axis=(0, 2, 3))
    sums, squares = lax.psum((sums, squares), "tm")
    count = total_frames * width * pixels
    mean = sums / count
    variance = squares / count - mean * mean
    scale = lax.rsqrt(variance + EPSILON)
    normed = (grouped - mean[None, :, None, None]) * scale[None, :, None, None]
    normed = normed.reshape(frames, chans, pixels) * gain[None, :, None] + shift[None, :, None]
    return jax.nn.silu(normed).astype(jnp.bfloat16)


def spread(color, weight, index, total_pixels):
    numer = (
        jnp.zeros((color.shape[0], 3, total_pixels), jnp.float32)
        .at[:, :, index]
        .add(color * weight[None, None, :])
    )
    denom = jnp.zeros((total_pixels,), jnp.float32).at[index].add(weight)
    return (numer, denom)


def route_owned(numer, denom, tile_id, own):
    frames = numer.shape[0]
    margin = (GRID_X + 1) * own
    numer_wide = jnp.concatenate([numer, jnp.zeros((frames, 3, margin), jnp.float32)], axis=2)
    denom_wide = jnp.concatenate([denom, jnp.zeros((margin,), jnp.float32)], axis=0)
    first_pixel = tile_id * own

    def block_at(offset):
        start_pixel = first_pixel + offset * own
        return (
            lax.dynamic_slice_in_dim(numer_wide, start_pixel, own, 2),
            lax.dynamic_slice_in_dim(denom_wide, start_pixel, own, 0),
        )

    owned_numer, owned_denom = block_at(0)
    for offset in (1, GRID_X, GRID_X + 1):
        piece_numer, piece_denom = block_at(offset)
        got_numer, got_denom = shifted((piece_numer, piece_denom), "tile", offset)
        owned_numer = owned_numer + got_numer
        owned_denom = owned_denom + got_denom
    return (owned_numer, owned_denom)


def general_body(
    latents, tile_order, w_in, gain_in, shift_in, w_mid, gain_mid, shift_mid, w_out, blend_weight
):
    frames = latents.shape[0]
    total_frames = frames * lax.axis_size("tm")
    tiles = tile_order.shape[0]
    own = STRIDE * STRIDE
    total_pixels = tiles * own
    tile_id = lax.axis_index("tile")
    index, valid = window_index(tile_id, tiles)
    whole = lax.all_gather(latents, "tile", axis=2, tiled=True)
    blocks = whole.reshape(frames, whole.shape[1], tiles, own)
    image = (
        jnp.zeros_like(blocks)
        .at[:, :, tile_order]
        .set(blocks)
        .reshape(frames, whole.shape[1], total_pixels)
    )
    window = jnp.where(
        valid[None, None, :], jnp.take(image, index, axis=2), jnp.zeros((), jnp.bfloat16)
    )
    first = causal_conv(with_history(window), w_in, frames, TSIDE)
    hidden = normalize(first, gain_in, shift_in, total_frames)
    second = causal_conv(
        lax.all_gather(with_history(hidden), "chan", axis=1, tiled=True), w_mid, frames, TSIDE
    )
    upper = normalize(second, gain_mid, shift_mid, total_frames)
    color = jnp.einsum("oc,fcp->fop", w_out, upper, preferred_element_type=jnp.float32)
    weight = jnp.where(valid, blend_weight[tile_id], jnp.float32(0.0))
    numer, denom = spread(color, weight, index, total_pixels)
    numer, denom = route_owned(numer, denom, tile_id, own)
    numer = lax.psum(numer, "chan")
    return numer / denom[None, None, :]


def block_cases(tiles):
    downs = (0, 1) if tiles // GRID_X > 1 else (0,)
    return [(down, across) for down in downs for across in (0, 1)]


def exact_dot(values, ones):
    rows = values.shape[0]
    high = values.astype(jnp.bfloat16)
    rest = values - high.astype(jnp.float32)
    middle = rest.astype(jnp.bfloat16)
    low = (rest - middle.astype(jnp.float32)).astype(jnp.bfloat16)
    total = jnp.dot(
        jnp.concatenate([high, middle, low], axis=0), ones, preferred_element_type=jnp.float32
    )
    return total[:rows] + total[rows : 2 * rows] + total[2 * rows :]


def group_affine(sums, squares, gain, shift, count):
    lanes = sums.shape[1]
    width = CH // GROUPS
    same = lax.broadcasted_iota(jnp.int32, (lanes, lanes), 0) // width == (
        lax.broadcasted_iota(jnp.int32, (lanes, lanes), 1) // width
    )
    total = exact_dot(
        jnp.concatenate([sums, squares], axis=0), jnp.where(same, 1.0, 0.0).astype(jnp.bfloat16)
    )
    mean = jnp.sum(total[:8], axis=0, keepdims=True) / count
    variance = jnp.sum(total[8:], axis=0, keepdims=True) / count - mean * mean
    scale = gain * lax.rsqrt(variance + EPSILON)
    return 0.5 * scale, 0.5 * (shift - mean * scale)


def silu_of_half(half):
    return half + half * jnp.tanh(half)


def fold(values):
    rows, lanes = values.shape
    return jnp.sum(values.reshape(rows // 8, 8, lanes), axis=0)


def decode_kernel(
    tiles,
    spans,
    shares,
    *refs,
):
    cases = block_cases(tiles)
    refs = list(refs)

    def take(number):
        taken = refs[:number]
        del refs[:number]
        return taken

    w_mid_ref, table_ref, order_ref = take(3)
    latent_refs, w_in_refs = take(spans), take(shares)
    keep_ref, send_ref, denom_ref = take(3)
    chosen, taps, turned_taps, turned_last, first, hidden, weights, partial = take(8)
    shown_ref, sems = take(2)

    own = denom_ref.shape[1]
    own_frames = keep_ref.shape[2]
    frames = own_frames * spans
    latent, wide = w_in_refs[0].shape[1:]
    rows_in = frames * latent
    rows_own = rows_in // spans
    depth_in = 27 * latent
    pixels = TSIDE * TSIDE
    lanes = partial.shape[3]
    tile_id = lax.axis_index("tile")
    mine = lax.axis_index("tm")
    chan_id = lax.axis_index("chan")

    copies = []
    for a in range(3):
        for b in range(3):
            for e in range(3):
                tap = 9 * a + 3 * b + e
                copy = pltpu.make_async_copy(
                    w_mid_ref.at[tap, :, pl.ds(pl.multiple_of(mine * lanes, LANES), lanes)],
                    weights.at[pl.ds(b * CH, CH), pl.ds((3 * a + e) * lanes, lanes)],
                    sems.at[tap],
                )
                copy.start()
                copies.append(copy)

    tile_row, tile_col = tile_id // GRID_X, tile_id % GRID_X
    gain_row = rows_own + 2
    w_out_row = gain_row + 2
    blend_row = w_out_row + 3
    order = order_ref[...]
    number_of = lax.broadcasted_iota(jnp.int32, order.shape, 0)
    lane_of = lax.broadcasted_iota(jnp.int32, order.shape, 1)
    rows_all = latent_refs[0].shape[0] // tiles
    turns = []
    for down, across in cases:
        wanted = tile_id + down * GRID_X + across
        found = (order == wanted.astype(jnp.float32)) & (lane_of == 0)
        place = jnp.sum(jnp.where(found, number_of.astype(jnp.float32), 0.0))
        turns.append((tile_id - place.astype(jnp.int32) + tiles) % tiles)
    for number, (down, across) in enumerate(cases):
        inside = (tile_row + down < tiles // GRID_X) & (tile_col + across < GRID_X)
        turn = turns[number]
        part = slice(number * LANES, (number + 1) * LANES)
        for steps in range(tiles):

            @pl.when(inside & (turn == steps))
            def _():
                for swap in range(spans):
                    at, tail_at = swap * rows_own, rows_in + swap * latent
                    block = latent_refs[swap][steps * rows_all : (steps + 1) * rows_all]
                    chosen[at : at + rows_own, part] = block[:rows_own]
                    chosen[tail_at : tail_at + latent, part] = block[rows_own : rows_own + latent]

        @pl.when(jnp.logical_not(inside))
        def _():
            chosen[:, part] = jnp.zeros((chosen.shape[0], LANES), chosen.dtype)

    slot = lax.broadcasted_iota(jnp.int32, (1, pixels), 1)
    up, along = slot // TSIDE, slot % TSIDE
    source = lax.broadcasted_iota(jnp.int32, (LANES, pixels), 0)
    tail = own - LANES

    def pick(first_pixel):
        parts = []
        for down, across in cases:
            u, v = up - down * STRIDE, along - across * STRIDE
            good = (u >= 0) & (u < STRIDE) & (v >= 0) & (v < STRIDE)
            wanted = jnp.where(good, u * STRIDE + v - first_pixel, -1)
            parts.append(jnp.where(source == wanted, 1.0, 0.0).astype(jnp.bfloat16))
        return jnp.concatenate(parts, axis=0)

    tails = chosen[rows_in:].astype(jnp.float32)
    width = tails.shape[1]
    turned = [pltpu.roll(tails, (-f * tail) % width, 1) if f else tails for f in range(own_frames)]
    tails = jnp.concatenate(
        [
            turned[f][swap * latent : (swap + 1) * latent]
            for swap in range(spans)
            for f in range(own_frames)
        ],
        axis=0,
    ).astype(jnp.bfloat16)
    in_tail = lax.broadcasted_iota(jnp.int32, tails.shape, 1) % LANES < tail
    tails = jnp.where(in_tail, tails.astype(jnp.float32), 0.0).astype(jnp.bfloat16)
    window = jnp.dot(
        chosen[:rows_in], pick(0), preferred_element_type=jnp.float32
    ) + jnp.dot(tails, pick(LANES), preferred_element_type=jnp.float32)
    for b in range(3):
        for e in range(3):
            inside = (
                (up + b - 1 >= 0)
                & (up + b - 1 < TSIDE)
                & (along + e - 1 >= 0)
                & (along + e - 1 < TSIDE)
            )
            offset = (b - 1) * TSIDE + e - 1
            moved = pltpu.roll(window, (-offset) % pixels, 1) if offset else window
            moved = jnp.where(inside, moved, 0.0).astype(jnp.bfloat16)
            for swap in range(spans):
                value = moved[swap * rows_own : (swap + 1) * rows_own]
                span = pl.ds((mine + swap) % spans * own_frames, own_frames)
                taps[span, 3 * b + e] = value.reshape(own_frames, latent, pixels)

    turned_taps[0:2] = jnp.zeros((2, pixels, LANES), turned_taps.dtype)
    for f in range(frames):
        turned_taps[f + 2] = taps[f, 0:8].reshape(8 * latent, pixels).T
    turned_last[...] = taps[:, 8].reshape(frames * latent, pixels).T
    joined = jnp.concatenate([w_in_refs[s][...] for s in range(shares)], axis=2)
    main_rows = [joined[9 * a : 9 * a + 8].reshape(8 * latent, CH) for a in range(3)]
    sums = jnp.zeros((8, CH), jnp.float32)
    squares = jnp.zeros((8, CH), jnp.float32)
    nothing = jnp.zeros((latent, CH), jnp.bfloat16)
    for f in range(frames):
        patch = [turned_taps[f + a] for a in range(3)] + [turned_last[...]]
        last_rows = [
            joined[9 * (g - f + 2) + 8] if 0 <= g - f + 2 < 3 else nothing for g in range(frames)
        ]
        value = jnp.dot(
            jnp.concatenate(patch, axis=1),
            jnp.concatenate(main_rows + last_rows, axis=0),
            preferred_element_type=jnp.float32,
        )
        first[f] = value
        sums = sums + fold(value)
        squares = squares + fold(value * value)
    count = frames * (CH // GROUPS) * pixels
    affine = []
    for s in range(shares):
        at = s * rows_all + rows_own + latent
        table = latent_refs[0][at : at + wide // LANES * 4].astype(jnp.float32)
        pieces = [table[4 * lane : 4 * lane + 4] for lane in range(wide // LANES)]
        table = jnp.concatenate([part[0:2] + part[2:4] for part in pieces], axis=1)
        part = slice(s * wide, (s + 1) * wide)
        affine.append(
            group_affine(sums[:, part], squares[:, part], table[0:1], table[1:2], count)
        )
    channels = [
        pl.ds(pl.multiple_of((chan_id + s) % shares * wide, LANES), wide) for s in range(shares)
    ]

    def hide(f):
        edge = jnp.zeros((TSIDE, CH), jnp.bfloat16)
        hidden[f, 0:TSIDE] = edge
        hidden[f, TSIDE + pixels : 2 * TSIDE + pixels] = edge
        for s in range(shares):
            scale, bias = affine[s]
            value = first[f, :, s * wide : (s + 1) * wide] * scale + bias
            hidden[f, TSIDE : TSIDE + pixels, channels[s]] = silu_of_half(value).astype(
                jnp.bfloat16
            )

    def convolve(start, several, depth_taps):
        lhs = jnp.concatenate(
            [
                hidden[start : start + several, b * TSIDE : b * TSIDE + pixels].reshape(
                    several * pixels, CH
                )
                for b in range(3)
            ],
            axis=1,
        )
        low = depth_taps[0] * 3 * lanes
        odd = len(depth_taps) % 2
        product = jnp.dot(
            lhs, weights[:, low : (9 - odd) * lanes], preferred_element_type=jnp.float32
        )
        if odd:
            rows = jnp.concatenate(
                [weights[b * CH : (b + 1) * CH, 8 * lanes :] for b in range(3)], axis=1
            )
            apart = jnp.dot(lhs[:, CH : 2 * CH], rows, preferred_element_type=jnp.float32)
        edge = jnp.zeros((TSIDE, lanes), jnp.float32)
        for a in depth_taps:
            for e in range(3):
                at = (3 * a + e) * lanes - low
                for f in range(several):
                    target = start + f + 2 - a
                    if odd and (a, e) == (2, 2):
                        value = apart[f * pixels : (f + 1) * pixels]
                        above = value[: pixels - TSIDE, :lanes]
                        below = value[TSIDE:, 2 * lanes :]
                        value = (
                            value[:, lanes : 2 * lanes]
                            + jnp.concatenate([edge, above], axis=0)
                            + jnp.concatenate([below, edge], axis=0)
                        )
                    else:
                        value = product[f * pixels : (f + 1) * pixels, at : at + lanes]
                    if start + f == max(target - 2, 0):
                        partial[e, target] = value
                    else:
                        partial[e, target] += value

    column = lax.broadcasted_iota(jnp.int32, (pixels, lanes), 0) % TSIDE
    total = [jnp.zeros((8, lanes), jnp.float32)] * 2

    def gather(f):
        left = jnp.where(column == 0, 0.0, pltpu.roll(partial[0, f], 1, 0))
        right = jnp.where(column == TSIDE - 1, 0.0, pltpu.roll(partial[2, f], pixels - 1, 0))
        value = partial[1, f] + left + right
        partial[1, f] = value
        total[0] = total[0] + fold(value)
        total[1] = total[1] + fold(value * value)

    bounds = [0, 2, frames - 2, frames - 1, frames]
    groups = [range(low, high) for low, high in zip(bounds, bounds[1:]) if high > low]
    for copy in copies:
        copy.wait()
    for f in groups[0]:
        hide(f)
    for number, group in enumerate(groups):
        if number + 1 < len(groups):
            for f in groups[number + 1]:
                hide(f)
        convolve(
            group.start,
            len(group),
            tuple(a for a in range(3) if group.stop - 1 + 2 - a < frames),
        )
        if number:
            for f in groups[number - 1]:
                gather(f)
    for f in groups[-1]:
        gather(f)

    part = pl.ds(pl.multiple_of(mine * lanes, LANES), lanes)
    scale, bias = group_affine(
        total[0],
        total[1],
        table_ref[gain_row : gain_row + 1, part],
        table_ref[gain_row + 1 : gain_row + 2, part],
        count,
    )
    blend = table_ref[pl.ds(blend_row + tile_id, 1), :]
    blend = jnp.where(
        (tile_row * STRIDE + up < tiles // GRID_X * STRIDE)
        & (tile_col * STRIDE + along < GRID_X * STRIDE),
        blend,
        0.0,
    )
    w_out = jnp.concatenate(
        [table_ref[w_out_row : w_out_row + 3, part], jnp.zeros((5, lanes), jnp.float32)], axis=0
    ).astype(jnp.bfloat16)
    colors = []
    for f in range(frames):
        upper = silu_of_half(partial[1, f] * scale + bias).astype(jnp.bfloat16)
        color = lax.dot_general(
            w_out, upper, (((1,), (1,)), ((), ())), preferred_element_type=jnp.float32
        )
        colors.append(color * blend)
    colors = jnp.concatenate(colors, axis=0)

    slot_in = lax.broadcasted_iota(jnp.int32, (pixels, pixels), 0)
    pixel = lax.broadcasted_iota(jnp.int32, (pixels, pixels), 1)
    shown, weight_rows = [], []
    for down, across in cases:
        u, v = slot_in // TSIDE - down * STRIDE, slot_in % TSIDE - across * STRIDE
        good = (u >= 0) & (u < STRIDE) & (v >= 0) & (v < STRIDE) & (u * STRIDE + v == pixel)
        shown.append(jnp.where(good, 1.0, 0.0).astype(jnp.bfloat16))
        inside = (tile_row >= down) & (tile_col >= across)
        other = jnp.maximum(tile_id - down * GRID_X - across, 0)
        weight = jnp.where(inside, table_ref[pl.ds(blend_row + other, 1), :], 0.0)
        weight_rows.append(jnp.broadcast_to(weight, (8, pixels)))
    shown_ref[...] = exact_dot(
        jnp.concatenate([colors] + weight_rows, axis=0), jnp.concatenate(shown, axis=1)
    )
    denom = jnp.zeros((8, own), jnp.float32)
    for number in range(len(cases)):
        lane = slice(number * pixels, number * pixels + own)
        row = 8 * (frames + number)
        denom = denom + shown_ref[row : row + 8, lane]
        for swap in range(spans):
            target = keep_ref if swap == 0 else send_ref.at[swap - 1]
            base = (mine + swap) % spans * own_frames * 8
            for at in range(own_frames):
                for o in range(3):
                    target[number, o, at : at + 1, :] = shown_ref[
                        pl.ds(base + 8 * at + o, 1), lane
                    ]
    denom_ref[...] = denom


def from_ring(value, axis):
    count = lax.axis_size(axis)
    return [
        lax.ppermute(value, axis, [((d + turn) % count, d) for d in range(count)])
        for turn in range(1, count)
    ]


def ring_sum(kept, sent, axis):
    count = lax.axis_size(axis)
    for turn in range(1, count):
        kept = kept + lax.ppermute(
            sent[turn - 1], axis, [(d, (d + turn) % count) for d in range(count)]
        )
    return kept


def small_table(*values):
    values = [value.reshape(-1, value.shape[-1]) for value in values]
    wide = max(value.shape[1] for value in values)
    height = sum(value.shape[0] for value in values)
    total, row = 0.0, 0
    for value in values:
        below = height - row - value.shape[0]
        value = jnp.pad(value.astype(jnp.float32), ((row, below), (0, wide - value.shape[1])))
        total = total + value
        row = height - below
    return total


def exchange_latents(frames, latent, own, table):
    tiles, shares = lax.axis_size("tile"), lax.axis_size("chan")
    tail = own - LANES
    height = frames * latent
    mine = table[:height, :own].astype(jnp.bfloat16)
    tails = sum(
        jnp.pad(
            mine[f * latent : (f + 1) * latent, LANES:],
            ((0, 0), (tail * f, LANES - tail * (f + 1))),
        )
        for f in range(frames)
    )
    affine = table[height : height + 2]
    high = lax.reduce_precision(affine, 8, 7)
    low = lax.reduce_precision(affine - high, 8, 7)
    affine = jnp.concatenate([high, low], axis=0).astype(jnp.bfloat16)
    rows = [affine[:, at : at + LANES] for at in range(0, affine.shape[1], LANES)]
    rows = jnp.concatenate(rows, axis=0)
    rows = jnp.pad(rows, ((0, -rows.shape[0] % 16), (0, 0)))
    message = jnp.concatenate([mine[:, :LANES], tails, rows], axis=0)
    got = [message]
    for steps in range(1, tiles):
        turn = steps if steps < shares else 0
        pairs = [
            (t * shares + (c + turn) % shares, (t + steps) % tiles * shares + c)
            for t in range(tiles)
            for c in range(shares)
        ]
        got.append(lax.ppermute(message, ("tile", "chan"), pairs))
    stack = jnp.concatenate(got, axis=0)
    return [stack] + from_ring(stack, "tm")


def lanes_body(
    latents, tile_order, w_in, gain_in, shift_in, w_mid, gain_mid, shift_mid, w_out, blend_weight
):
    own_frames, latent, own = latents.shape
    spans = lax.axis_size("tm")
    shares = lax.axis_size("chan")
    frames = own_frames * spans
    if 8 * latent != LANES or frames * latent != LANES:
        return general_body(
            latents,
            tile_order,
            w_in,
            gain_in,
            shift_in,
            w_mid,
            gain_mid,
            shift_mid,
            w_out,
            blend_weight,
        )
    tiles = tile_order.shape[0]
    wide = w_in.shape[2]
    lanes = wide // spans
    pixels = TSIDE * TSIDE
    cases = block_cases(tiles)

    w_in_all = [(from_ring(other, "tm") or [other])[0] for other in from_ring(w_in, "chan")]
    table = lax.optimization_barrier(
        small_table(
            latents.reshape(own_frames * latent, own),
            gain_in,
            shift_in,
            gain_mid,
            shift_mid,
            w_out,
            blend_weight,
        )
    )
    latents_all = exchange_latents(own_frames, latent, own, table)
    _, w_in, tile_order = lax.optimization_barrier((table, w_in, tile_order))
    order = jnp.broadcast_to(tile_order.astype(jnp.float32)[:, None], (tiles, LANES))
    w_in_own = from_ring(w_in, "tm")[:1] or [w_in]

    vmem = pl.BlockSpec(memory_space=pltpu.VMEM)
    piece = (len(cases), 3, own_frames, own)
    kept, sent, denom = pl.pallas_call(
        functools.partial(decode_kernel, tiles, spans, shares),
        out_shape=[
            jax.ShapeDtypeStruct(piece, jnp.float32),
            jax.ShapeDtypeStruct((max(spans - 1, 1),) + piece, jnp.float32),
            jax.ShapeDtypeStruct((8, own), jnp.float32),
        ],
        in_specs=[pl.BlockSpec(memory_space=pl.ANY)] + [vmem] * (2 + spans + shares),
        out_specs=[vmem] * 3,
        scratch_shapes=[
            pltpu.VMEM(((frames + spans) * latent, len(cases) * LANES), jnp.bfloat16),
            pltpu.VMEM((frames, 9, latent, pixels), jnp.bfloat16),
            pltpu.VMEM((frames + 2, pixels, LANES), jnp.bfloat16),
            pltpu.VMEM((pixels, LANES), jnp.bfloat16),
            pltpu.VMEM((frames, pixels, CH), jnp.float32),
            pltpu.VMEM((frames, pixels + 2 * TSIDE, CH), jnp.bfloat16),
            pltpu.VMEM((3 * CH, 9 * lanes), jnp.bfloat16),
            pltpu.VMEM((3, frames, pixels, lanes), jnp.float32),
            pltpu.VMEM((8 * (frames + len(cases)), len(cases) * pixels), jnp.float32),
            pltpu.SemaphoreType.DMA((27,)),
        ],
        compiler_params=pltpu.CompilerParams(vmem_limit_bytes=VMEM_BYTES),
        cost_estimate=pl.CostEstimate(
            flops=2 * frames * pixels * 27 * CH * lanes, bytes_accessed=8_000_000, transcendentals=0
        ),
    )(w_mid, table, order, *latents_all, *w_in_own, *w_in_all)
    total = ring_sum(kept, sent, "tm")
    total = ring_sum(total, [total] * (shares - 1), "chan")
    numer = total[0]
    for number, (down, across) in enumerate(cases):
        steps = down * GRID_X + across
        if steps and steps < tiles:
            numer = numer + shifted(total[number], "tile", steps)
    return jnp.transpose(numer / denom[0][None, None, :], (1, 0, 2))


def solution(mesh):
    placed = (
        P("tm", "groups", "tile"),
        P("groups"),
        P(None, None, "chan"),
        P("chan"),
        P("chan"),
        P(None, None, "chan"),
        P("chan"),
        P("chan"),
        P(None, "chan"),
        P("groups", None),
    )
    whole_lanes = (
        CH % (mesh.shape["chan"] * mesh.shape["tm"] * LANES) == 0
        and mesh.shape["chan"] <= mesh.shape["tile"]
    )
    return jax.shard_map(
        lanes_body if whole_lanes else general_body,
        mesh=mesh,
        in_specs=placed,
        out_specs=P("tm", "groups", "tile"),
        check_vma=False,
    )
```

```python
import functools

import jax
import jax.numpy as jnp
from jax import lax
from jax.experimental import pallas as pl
from jax.experimental.pallas import tpu as pltpu
from jax.sharding import PartitionSpec as P

CH = 512
GROUPS = 32
TSIDE = 16
STRIDE = 12
GRID_X = 4

EPSILON = 1e-06
LANES = 128
VMEM_BYTES = 48 * 1024 * 1024


def shifted(value, axis, steps):
    count = lax.axis_size(axis)
    leading, last = (max(0, -steps), min(count, count - steps))
    return lax.ppermute(value, axis, [(source, source + steps) for source in range(leading, last)])


def window_index(tile_id, tiles):
    slots = jnp.arange(TSIDE * TSIDE, dtype=jnp.int32)
    row = tile_id // GRID_X * STRIDE + slots // TSIDE
    col = tile_id % GRID_X * STRIDE + slots % TSIDE
    valid = (row < tiles // GRID_X * STRIDE) & (col < GRID_X * STRIDE)
    block = row // STRIDE * GRID_X + col // STRIDE
    index = block * (STRIDE * STRIDE) + row % STRIDE * STRIDE + col % STRIDE
    return (jnp.where(valid, index, 0), valid)


def causal_conv(extended, weights, frames, side):
    pixels = side * side
    rows = jnp.arange(pixels, dtype=jnp.int32) // side
    cols = jnp.arange(pixels, dtype=jnp.int32) % side
    total = jnp.zeros((frames, weights.shape[2], pixels), jnp.float32)
    for depth in range(3):
        window = extended[depth : depth + frames]
        for down in range(3):
            for across in range(3):
                offset = (down - 1) * side + (across - 1)
                inside = (
                    (rows + down - 1 >= 0)
                    & (rows + down - 1 < side)
                    & (cols + across - 1 >= 0)
                    & (cols + across - 1 < side)
                )
                moved = jnp.roll(window, -offset, axis=2)
                moved = jnp.where(inside[None, None, :], moved, jnp.zeros_like(moved))
                total = total + jnp.einsum(
                    "fcp,co->fop",
                    moved,
                    weights[9 * depth + 3 * down + across],
                    preferred_element_type=jnp.float32,
                )
    return total


def with_history(values):
    frames = values.shape[0]
    earlier = shifted(values[frames - 2 :], "tm", 1)
    return jnp.concatenate([earlier, values], axis=0)


def normalize(values, gain, shift, total_frames):
    frames, chans, pixels = values.shape
    width = CH // GROUPS
    grouped = values.reshape(frames, chans // width, width, pixels)
    sums = jnp.sum(grouped, axis=(0, 2, 3))
    squares = jnp.sum(grouped * grouped, axis=(0, 2, 3))
    sums, squares = lax.psum((sums, squares), "tm")
    count = total_frames * width * pixels
    mean = sums / count
    variance = squares / count - mean * mean
    scale = lax.rsqrt(variance + EPSILON)
    normed = (grouped - mean[None, :, None, None]) * scale[None, :, None, None]
    normed = normed.reshape(frames, chans, pixels) * gain[None, :, None] + shift[None, :, None]
    return jax.nn.silu(normed).astype(jnp.bfloat16)


def spread(color, weight, index, total_pixels):
    numer = (
        jnp.zeros((color.shape[0], 3, total_pixels), jnp.float32)
        .at[:, :, index]
        .add(color * weight[None, None, :])
    )
    denom = jnp.zeros((total_pixels,), jnp.float32).at[index].add(weight)
    return (numer, denom)


def route_owned(numer, denom, tile_id, own):
    frames = numer.shape[0]
    margin = (GRID_X + 1) * own
    numer_wide = jnp.concatenate([numer, jnp.zeros((frames, 3, margin), jnp.float32)], axis=2)
    denom_wide = jnp.concatenate([denom, jnp.zeros((margin,), jnp.float32)], axis=0)
    first_pixel = tile_id * own

    def block_at(offset):
        start_pixel = first_pixel + offset * own
        return (
            lax.dynamic_slice_in_dim(numer_wide, start_pixel, own, 2),
            lax.dynamic_slice_in_dim(denom_wide, start_pixel, own, 0),
        )

    owned_numer, owned_denom = block_at(0)
    for offset in (1, GRID_X, GRID_X + 1):
        piece_numer, piece_denom = block_at(offset)
        got_numer, got_denom = shifted((piece_numer, piece_denom), "tile", offset)
        owned_numer = owned_numer + got_numer
        owned_denom = owned_denom + got_denom
    return (owned_numer, owned_denom)


def general_body(
    latents, tile_order, w_in, gain_in, shift_in, w_mid, gain_mid, shift_mid, w_out, blend_weight
):
    frames = latents.shape[0]
    total_frames = frames * lax.axis_size("tm")
    tiles = tile_order.shape[0]
    own = STRIDE * STRIDE
    total_pixels = tiles * own
    tile_id = lax.axis_index("tile")
    index, valid = window_index(tile_id, tiles)
    whole = lax.all_gather(latents, "tile", axis=2, tiled=True)
    blocks = whole.reshape(frames, whole.shape[1], tiles, own)
    image = (
        jnp.zeros_like(blocks)
        .at[:, :, tile_order]
        .set(blocks)
        .reshape(frames, whole.shape[1], total_pixels)
    )
    window = jnp.where(
        valid[None, None, :], jnp.take(image, index, axis=2), jnp.zeros((), jnp.bfloat16)
    )
    first = causal_conv(with_history(window), w_in, frames, TSIDE)
    hidden = normalize(first, gain_in, shift_in, total_frames)
    second = causal_conv(
        lax.all_gather(with_history(hidden), "chan", axis=1, tiled=True), w_mid, frames, TSIDE
    )
    upper = normalize(second, gain_mid, shift_mid, total_frames)
    color = jnp.einsum("oc,fcp->fop", w_out, upper, preferred_element_type=jnp.float32)
    weight = jnp.where(valid, blend_weight[tile_id], jnp.float32(0.0))
    numer, denom = spread(color, weight, index, total_pixels)
    numer, denom = route_owned(numer, denom, tile_id, own)
    numer = lax.psum(numer, "chan")
    return numer / denom[None, None, :]


def block_cases(tiles):
    downs = (0, 1) if tiles // GRID_X > 1 else (0,)
    return [(down, across) for down in downs for across in (0, 1)]


def exact_dot(values, ones):
    rows = values.shape[0]
    high = values.astype(jnp.bfloat16)
    rest = values - high.astype(jnp.float32)
    middle = rest.astype(jnp.bfloat16)
    low = (rest - middle.astype(jnp.float32)).astype(jnp.bfloat16)
    total = jnp.dot(
        jnp.concatenate([high, middle, low], axis=0), ones, preferred_element_type=jnp.float32
    )
    return total[:rows] + total[rows : 2 * rows] + total[2 * rows :]


def group_affine(sums, squares, gain, shift, count):
    lanes = sums.shape[1]
    width = CH // GROUPS
    same = lax.broadcasted_iota(jnp.int32, (lanes, lanes), 0) // width == (
        lax.broadcasted_iota(jnp.int32, (lanes, lanes), 1) // width
    )
    total = exact_dot(
        jnp.concatenate([sums, squares], axis=0), jnp.where(same, 1.0, 0.0).astype(jnp.bfloat16)
    )
    mean = jnp.sum(total[:8], axis=0, keepdims=True) / count
    variance = jnp.sum(total[8:], axis=0, keepdims=True) / count - mean * mean
    scale = gain * lax.rsqrt(variance + EPSILON)
    return 0.5 * scale, 0.5 * (shift - mean * scale)


def silu_of_half(half):
    return half + half * jnp.tanh(half)


def fold(values):
    rows, lanes = values.shape
    return jnp.sum(values.reshape(rows // 8, 8, lanes), axis=0)


def decode_kernel(
    tiles,
    spans,
    shares,
    *refs,
):
    cases = block_cases(tiles)
    refs = list(refs)

    def take(number):
        taken = refs[:number]
        del refs[:number]
        return taken

    w_mid_ref, table_ref, order_ref = take(3)
    latent_refs, w_in_refs = take(spans), take(shares)
    keep_ref, send_ref, denom_ref = take(3)
    chosen, taps, turned_taps, turned_last, first, hidden, weights, partial = take(8)
    shown_ref, sems = take(2)

    own = denom_ref.shape[1]
    own_frames = keep_ref.shape[2]
    frames = own_frames * spans
    latent, wide = w_in_refs[0].shape[1:]
    rows_in = frames * latent
    rows_own = rows_in // spans
    depth_in = 27 * latent
    pixels = TSIDE * TSIDE
    lanes = partial.shape[3]
    tile_id = lax.axis_index("tile")
    mine = lax.axis_index("tm")
    chan_id = lax.axis_index("chan")

    half = pl.ds(pl.multiple_of(mine * lanes, LANES), lanes)
    copies = []
    for tap in range(27):
        copy = pltpu.make_async_copy(w_mid_ref.at[tap, :, half], weights.at[tap], sems.at[tap])
        copy.start()
        copies.append(copy)

    tile_row, tile_col = tile_id // GRID_X, tile_id % GRID_X
    gain_row = rows_own + 2
    w_out_row = gain_row + 2
    blend_row = w_out_row + 3
    order = order_ref[...]
    number_of = lax.broadcasted_iota(jnp.int32, order.shape, 0)
    lane_of = lax.broadcasted_iota(jnp.int32, order.shape, 1)
    rows_all = latent_refs[0].shape[0] // tiles
    turns = []
    for down, across in cases:
        wanted = tile_id + down * GRID_X + across
        found = (order == wanted.astype(jnp.float32)) & (lane_of == 0)
        place = jnp.sum(jnp.where(found, number_of.astype(jnp.float32), 0.0))
        turns.append((tile_id - place.astype(jnp.int32) + tiles) % tiles)
    for number, (down, across) in enumerate(cases):
        inside = (tile_row + down < tiles // GRID_X) & (tile_col + across < GRID_X)
        turn = turns[number]
        part = slice(number * LANES, (number + 1) * LANES)
        for steps in range(tiles):

            @pl.when(inside & (turn == steps))
            def _():
                for swap in range(spans):
                    at, tail_at = swap * rows_own, rows_in + swap * latent
                    block = latent_refs[swap][steps * rows_all : (steps + 1) * rows_all]
                    chosen[at : at + rows_own, part] = block[:rows_own]
                    chosen[tail_at : tail_at + latent, part] = block[rows_own : rows_own + latent]

        @pl.when(jnp.logical_not(inside))
        def _():
            chosen[:, part] = jnp.zeros((chosen.shape[0], LANES), chosen.dtype)

    slot = lax.broadcasted_iota(jnp.int32, (1, pixels), 1)
    up, along = slot // TSIDE, slot % TSIDE
    source = lax.broadcasted_iota(jnp.int32, (LANES, pixels), 0)
    tail = own - LANES

    def pick(first_pixel):
        parts = []
        for down, across in cases:
            u, v = up - down * STRIDE, along - across * STRIDE
            good = (u >= 0) & (u < STRIDE) & (v >= 0) & (v < STRIDE)
            wanted = jnp.where(good, u * STRIDE + v - first_pixel, -1)
            parts.append(jnp.where(source == wanted, 1.0, 0.0).astype(jnp.bfloat16))
        return jnp.concatenate(parts, axis=0)

    tails = chosen[rows_in:].astype(jnp.float32)
    width = tails.shape[1]
    turned = [pltpu.roll(tails, (-f * tail) % width, 1) if f else tails for f in range(own_frames)]
    tails = jnp.concatenate(
        [
            turned[f][swap * latent : (swap + 1) * latent]
            for swap in range(spans)
            for f in range(own_frames)
        ],
        axis=0,
    ).astype(jnp.bfloat16)
    in_tail = lax.broadcasted_iota(jnp.int32, tails.shape, 1) % LANES < tail
    tails = jnp.where(in_tail, tails.astype(jnp.float32), 0.0).astype(jnp.bfloat16)
    window = jnp.dot(
        chosen[:rows_in], pick(0), preferred_element_type=jnp.float32
    ) + jnp.dot(tails, pick(LANES), preferred_element_type=jnp.float32)
    for b in range(3):
        for e in range(3):
            inside = (
                (up + b - 1 >= 0)
                & (up + b - 1 < TSIDE)
                & (along + e - 1 >= 0)
                & (along + e - 1 < TSIDE)
            )
            offset = (b - 1) * TSIDE + e - 1
            moved = pltpu.roll(window, (-offset) % pixels, 1) if offset else window
            moved = jnp.where(inside, moved, 0.0).astype(jnp.bfloat16)
            for swap in range(spans):
                value = moved[swap * rows_own : (swap + 1) * rows_own]
                span = pl.ds((mine + swap) % spans * own_frames, own_frames)
                taps[span, 3 * b + e] = value.reshape(own_frames, latent, pixels)

    turned_taps[0:2] = jnp.zeros((2, pixels, LANES), turned_taps.dtype)
    for f in range(frames):
        turned_taps[f + 2] = taps[f, 0:8].reshape(8 * latent, pixels).T
    turned_last[...] = taps[:, 8].reshape(frames * latent, pixels).T
    joined = jnp.concatenate([w_in_refs[s][...] for s in range(shares)], axis=2)
    main_rows = [joined[9 * a : 9 * a + 8].reshape(8 * latent, CH) for a in range(3)]
    sums = jnp.zeros((8, CH), jnp.float32)
    squares = jnp.zeros((8, CH), jnp.float32)
    nothing = jnp.zeros((latent, CH), jnp.bfloat16)
    for f in range(frames):
        patch = [turned_taps[f + a] for a in range(3)] + [turned_last[...]]
        last_rows = [
            joined[9 * (g - f + 2) + 8] if 0 <= g - f + 2 < 3 else nothing for g in range(frames)
        ]
        value = jnp.dot(
            jnp.concatenate(patch, axis=1),
            jnp.concatenate(main_rows + last_rows, axis=0),
            preferred_element_type=jnp.float32,
        )
        first[f] = value
        sums = sums + fold(value)
        squares = squares + fold(value * value)
    count = frames * (CH // GROUPS) * pixels
    affine = []
    for s in range(shares):
        at = s * rows_all + rows_own + latent
        table = latent_refs[0][at : at + wide // LANES * 4].astype(jnp.float32)
        pieces = [table[4 * lane : 4 * lane + 4] for lane in range(wide // LANES)]
        table = jnp.concatenate([part[0:2] + part[2:4] for part in pieces], axis=1)
        part = slice(s * wide, (s + 1) * wide)
        affine.append(
            group_affine(sums[:, part], squares[:, part], table[0:1], table[1:2], count)
        )
    channels = [
        pl.ds(pl.multiple_of((chan_id + s) % shares * wide, LANES), wide) for s in range(shares)
    ]

    def hide(f):
        edge = jnp.zeros((TSIDE, CH), jnp.bfloat16)
        hidden[f, 0:TSIDE] = edge
        hidden[f, TSIDE + pixels : 2 * TSIDE + pixels] = edge
        for s in range(shares):
            scale, bias = affine[s]
            value = first[f, :, s * wide : (s + 1) * wide] * scale + bias
            hidden[f, TSIDE : TSIDE + pixels, channels[s]] = silu_of_half(value).astype(
                jnp.bfloat16
            )

    def convolve(start, several, depth_taps):
        lhs = jnp.concatenate(
            [
                hidden[start : start + several, b * TSIDE : b * TSIDE + pixels].reshape(
                    several * pixels, CH
                )
                for b in range(3)
            ],
            axis=1,
        )
        low = depth_taps[0] * 3 * lanes
        odd = len(depth_taps) % 2
        columns = [(a, e) for a in depth_taps for e in range(3)]
        rhs = jnp.concatenate(
            [
                jnp.concatenate(
                    [weights[9 * a + 3 * b + e] for a, e in columns[: len(columns) - odd]], axis=1
                )
                for b in range(3)
            ],
            axis=0,
        )
        product = jnp.dot(lhs, rhs, preferred_element_type=jnp.float32)
        if odd:
            rows = jnp.concatenate([weights[18 + 3 * b + 2] for b in range(3)], axis=1)
            apart = jnp.dot(lhs[:, CH : 2 * CH], rows, preferred_element_type=jnp.float32)
        edge = jnp.zeros((TSIDE, lanes), jnp.float32)
        for a in depth_taps:
            for e in range(3):
                at = (3 * a + e) * lanes - low
                for f in range(several):
                    target = start + f + 2 - a
                    if odd and (a, e) == (2, 2):
                        value = apart[f * pixels : (f + 1) * pixels]
                        above = value[: pixels - TSIDE, :lanes]
                        below = value[TSIDE:, 2 * lanes :]
                        value = (
                            value[:, lanes : 2 * lanes]
                            + jnp.concatenate([edge, above], axis=0)
                            + jnp.concatenate([below, edge], axis=0)
                        )
                    else:
                        value = product[f * pixels : (f + 1) * pixels, at : at + lanes]
                    if start + f == max(target - 2, 0):
                        partial[e, target] = value
                    else:
                        partial[e, target] += value

    column = lax.broadcasted_iota(jnp.int32, (pixels, lanes), 0) % TSIDE
    total = [jnp.zeros((8, lanes), jnp.float32)] * 2

    def gather(f):
        left = jnp.where(column == 0, 0.0, pltpu.roll(partial[0, f], 1, 0))
        right = jnp.where(column == TSIDE - 1, 0.0, pltpu.roll(partial[2, f], pixels - 1, 0))
        value = partial[1, f] + left + right
        partial[1, f] = value
        total[0] = total[0] + fold(value)
        total[1] = total[1] + fold(value * value)

    bounds = [0, 2, frames - 2, frames - 1, frames]
    groups = [range(low, high) for low, high in zip(bounds, bounds[1:]) if high > low]
    for f in groups[0]:
        hide(f)
    for copy in copies:
        copy.wait()
    for number, group in enumerate(groups):
        if number + 1 < len(groups):
            for f in groups[number + 1]:
                hide(f)
        convolve(
            group.start,
            len(group),
            tuple(a for a in range(3) if group.stop - 1 + 2 - a < frames),
        )
        if number:
            for f in groups[number - 1]:
                gather(f)
    for f in groups[-1]:
        gather(f)

    part = pl.ds(pl.multiple_of(mine * lanes, LANES), lanes)
    scale, bias = group_affine(
        total[0],
        total[1],
        table_ref[gain_row : gain_row + 1, part],
        table_ref[gain_row + 1 : gain_row + 2, part],
        count,
    )
    blend = table_ref[pl.ds(blend_row + tile_id, 1), :]
    blend = jnp.where(
        (tile_row * STRIDE + up < tiles // GRID_X * STRIDE)
        & (tile_col * STRIDE + along < GRID_X * STRIDE),
        blend,
        0.0,
    )
    w_out = jnp.concatenate(
        [table_ref[w_out_row : w_out_row + 3, part], jnp.zeros((5, lanes), jnp.float32)], axis=0
    ).astype(jnp.bfloat16)
    colors = []
    for f in range(frames):
        upper = silu_of_half(partial[1, f] * scale + bias).astype(jnp.bfloat16)
        color = lax.dot_general(
            w_out, upper, (((1,), (1,)), ((), ())), preferred_element_type=jnp.float32
        )
        colors.append(color * blend)
    colors = jnp.concatenate(colors, axis=0)

    slot_in = lax.broadcasted_iota(jnp.int32, (pixels, pixels), 0)
    pixel = lax.broadcasted_iota(jnp.int32, (pixels, pixels), 1)
    shown, weight_rows = [], []
    for down, across in cases:
        u, v = slot_in // TSIDE - down * STRIDE, slot_in % TSIDE - across * STRIDE
        good = (u >= 0) & (u < STRIDE) & (v >= 0) & (v < STRIDE) & (u * STRIDE + v == pixel)
        shown.append(jnp.where(good, 1.0, 0.0).astype(jnp.bfloat16))
        inside = (tile_row >= down) & (tile_col >= across)
        other = jnp.maximum(tile_id - down * GRID_X - across, 0)
        weight = jnp.where(inside, table_ref[pl.ds(blend_row + other, 1), :], 0.0)
        weight_rows.append(jnp.broadcast_to(weight, (8, pixels)))
    shown_ref[...] = exact_dot(
        jnp.concatenate([colors] + weight_rows, axis=0), jnp.concatenate(shown, axis=1)
    )
    denom = jnp.zeros((8, own), jnp.float32)
    for number in range(len(cases)):
        lane = slice(number * pixels, number * pixels + own)
        row = 8 * (frames + number)
        denom = denom + shown_ref[row : row + 8, lane]
        for swap in range(spans):
            target = keep_ref if swap == 0 else send_ref.at[swap - 1]
            base = (mine + swap) % spans * own_frames * 8
            for at in range(own_frames):
                for o in range(3):
                    target[number, o, at : at + 1, :] = shown_ref[
                        pl.ds(base + 8 * at + o, 1), lane
                    ]
    denom_ref[...] = denom


def from_ring(value, axis):
    count = lax.axis_size(axis)
    return [
        lax.ppermute(value, axis, [((d + turn) % count, d) for d in range(count)])
        for turn in range(1, count)
    ]


def ring_sum(kept, sent, axis):
    count = lax.axis_size(axis)
    for turn in range(1, count):
        kept = kept + lax.ppermute(
            sent[turn - 1], axis, [(d, (d + turn) % count) for d in range(count)]
        )
    return kept


def small_table(*values):
    values = [value.reshape(-1, value.shape[-1]) for value in values]
    wide = max(value.shape[1] for value in values)
    height = sum(value.shape[0] for value in values)
    total, row = 0.0, 0
    for value in values:
        below = height - row - value.shape[0]
        value = jnp.pad(value.astype(jnp.float32), ((row, below), (0, wide - value.shape[1])))
        total = total + value
        row = height - below
    return total


def exchange_latents(frames, latent, own, table):
    tiles, shares = lax.axis_size("tile"), lax.axis_size("chan")
    tail = own - LANES
    height = frames * latent
    mine = table[:height, :own].astype(jnp.bfloat16)
    tails = sum(
        jnp.pad(
            mine[f * latent : (f + 1) * latent, LANES:],
            ((0, 0), (tail * f, LANES - tail * (f + 1))),
        )
        for f in range(frames)
    )
    affine = table[height : height + 2]
    high = lax.reduce_precision(affine, 8, 7)
    low = lax.reduce_precision(affine - high, 8, 7)
    affine = jnp.concatenate([high, low], axis=0).astype(jnp.bfloat16)
    rows = [affine[:, at : at + LANES] for at in range(0, affine.shape[1], LANES)]
    rows = jnp.concatenate(rows, axis=0)
    rows = jnp.pad(rows, ((0, -rows.shape[0] % 16), (0, 0)))
    message = jnp.concatenate([mine[:, :LANES], tails, rows], axis=0)
    got = [message]
    for steps in range(1, tiles):
        turn = steps if steps < shares else 0
        pairs = [
            (t * shares + (c + turn) % shares, (t + steps) % tiles * shares + c)
            for t in range(tiles)
            for c in range(shares)
        ]
        got.append(lax.ppermute(message, ("tile", "chan"), pairs))
    stack = jnp.concatenate(got, axis=0)
    return [stack] + from_ring(stack, "tm")


def lanes_body(
    latents, tile_order, w_in, gain_in, shift_in, w_mid, gain_mid, shift_mid, w_out, blend_weight
):
    own_frames, latent, own = latents.shape
    spans = lax.axis_size("tm")
    shares = lax.axis_size("chan")
    frames = own_frames * spans
    if 8 * latent != LANES or frames * latent != LANES:
        return general_body(
            latents,
            tile_order,
            w_in,
            gain_in,
            shift_in,
            w_mid,
            gain_mid,
            shift_mid,
            w_out,
            blend_weight,
        )
    tiles = tile_order.shape[0]
    wide = w_in.shape[2]
    lanes = wide // spans
    pixels = TSIDE * TSIDE
    cases = block_cases(tiles)

    w_in_all = [(from_ring(other, "tm") or [other])[0] for other in from_ring(w_in, "chan")]
    table = lax.optimization_barrier(
        small_table(
            latents.reshape(own_frames * latent, own),
            gain_in,
            shift_in,
            gain_mid,
            shift_mid,
            w_out,
            blend_weight,
        )
    )
    latents_all = exchange_latents(own_frames, latent, own, table)
    _, w_in, tile_order = lax.optimization_barrier((table, w_in, tile_order))
    order = jnp.broadcast_to(tile_order.astype(jnp.float32)[:, None], (tiles, LANES))
    w_in_own = from_ring(w_in, "tm")[:1] or [w_in]

    vmem = pl.BlockSpec(memory_space=pltpu.VMEM)
    piece = (len(cases), 3, own_frames, own)
    kept, sent, denom = pl.pallas_call(
        functools.partial(decode_kernel, tiles, spans, shares),
        out_shape=[
            jax.ShapeDtypeStruct(piece, jnp.float32),
            jax.ShapeDtypeStruct((max(spans - 1, 1),) + piece, jnp.float32),
            jax.ShapeDtypeStruct((8, own), jnp.float32),
        ],
        in_specs=[pl.BlockSpec(memory_space=pl.ANY)] + [vmem] * (2 + spans + shares),
        out_specs=[vmem] * 3,
        scratch_shapes=[
            pltpu.VMEM(((frames + spans) * latent, len(cases) * LANES), jnp.bfloat16),
            pltpu.VMEM((frames, 9, latent, pixels), jnp.bfloat16),
            pltpu.VMEM((frames + 2, pixels, LANES), jnp.bfloat16),
            pltpu.VMEM((pixels, LANES), jnp.bfloat16),
            pltpu.VMEM((frames, pixels, CH), jnp.float32),
            pltpu.VMEM((frames, pixels + 2 * TSIDE, CH), jnp.bfloat16),
            pltpu.VMEM((27, CH, lanes), jnp.bfloat16),
            pltpu.VMEM((3, frames, pixels, lanes), jnp.float32),
            pltpu.VMEM((8 * (frames + len(cases)), len(cases) * pixels), jnp.float32),
            pltpu.SemaphoreType.DMA((27,)),
        ],
        compiler_params=pltpu.CompilerParams(vmem_limit_bytes=VMEM_BYTES),
        cost_estimate=pl.CostEstimate(
            flops=2 * frames * pixels * 27 * CH * lanes, bytes_accessed=8_000_000, transcendentals=0
        ),
    )(w_mid, table, order, *latents_all, *w_in_own, *w_in_all)
    total = ring_sum(kept, sent, "tm")
    total = ring_sum(total, [total] * (shares - 1), "chan")
    numer = total[0]
    for number, (down, across) in enumerate(cases):
        steps = down * GRID_X + across
        if steps and steps < tiles:
            numer = numer + shifted(total[number], "tile", steps)
    return jnp.transpose(numer / denom[0][None, None, :], (1, 0, 2))


def solution(mesh):
    placed = (
        P("tm", "groups", "tile"),
        P("groups"),
        P(None, None, "chan"),
        P("chan"),
        P("chan"),
        P(None, None, "chan"),
        P("chan"),
        P("chan"),
        P(None, "chan"),
        P("groups", None),
    )
    whole_lanes = (
        CH % (mesh.shape["chan"] * mesh.shape["tm"] * LANES) == 0
        and mesh.shape["chan"] <= mesh.shape["tile"]
    )
    return jax.shard_map(
        lanes_body if whole_lanes else general_body,
        mesh=mesh,
        in_specs=placed,
        out_specs=P("tm", "groups", "tile"),
        check_vma=False,
    )
```

```python
import functools

import jax
import jax.numpy as jnp
from jax import lax
from jax.experimental import pallas as pl
from jax.experimental.pallas import tpu as pltpu
from jax.sharding import PartitionSpec as P

CH = 512
GROUPS = 32
TSIDE = 16
STRIDE = 12
GRID_X = 4

EPSILON = 1e-06
LANES = 128
LOG2_E = 1.4426950408889634
VMEM_BYTES = 48 * 1024 * 1024


def shifted(value, axis, steps):
    count = lax.axis_size(axis)
    leading, last = (max(0, -steps), min(count, count - steps))
    return lax.ppermute(value, axis, [(source, source + steps) for source in range(leading, last)])


def window_index(tile_id, tiles):
    slots = jnp.arange(TSIDE * TSIDE, dtype=jnp.int32)
    row = tile_id // GRID_X * STRIDE + slots // TSIDE
    col = tile_id % GRID_X * STRIDE + slots % TSIDE
    valid = (row < tiles // GRID_X * STRIDE) & (col < GRID_X * STRIDE)
    block = row // STRIDE * GRID_X + col // STRIDE
    index = block * (STRIDE * STRIDE) + row % STRIDE * STRIDE + col % STRIDE
    return (jnp.where(valid, index, 0), valid)


def causal_conv(extended, weights, frames, side):
    pixels = side * side
    rows = jnp.arange(pixels, dtype=jnp.int32) // side
    cols = jnp.arange(pixels, dtype=jnp.int32) % side
    total = jnp.zeros((frames, weights.shape[2], pixels), jnp.float32)
    for depth in range(3):
        window = extended[depth : depth + frames]
        for down in range(3):
            for across in range(3):
                offset = (down - 1) * side + (across - 1)
                inside = (
                    (rows + down - 1 >= 0)
                    & (rows + down - 1 < side)
                    & (cols + across - 1 >= 0)
                    & (cols + across - 1 < side)
                )
                moved = jnp.roll(window, -offset, axis=2)
                moved = jnp.where(inside[None, None, :], moved, jnp.zeros_like(moved))
                total = total + jnp.einsum(
                    "fcp,co->fop",
                    moved,
                    weights[9 * depth + 3 * down + across],
                    preferred_element_type=jnp.float32,
                )
    return total


def with_history(values):
    frames = values.shape[0]
    earlier = shifted(values[frames - 2 :], "tm", 1)
    return jnp.concatenate([earlier, values], axis=0)


def normalize(values, gain, shift, total_frames):
    frames, chans, pixels = values.shape
    width = CH // GROUPS
    grouped = values.reshape(frames, chans // width, width, pixels)
    sums = jnp.sum(grouped, axis=(0, 2, 3))
    squares = jnp.sum(grouped * grouped, axis=(0, 2, 3))
    sums, squares = lax.psum((sums, squares), "tm")
    count = total_frames * width * pixels
    mean = sums / count
    variance = squares / count - mean * mean
    scale = lax.rsqrt(variance + EPSILON)
    normed = (grouped - mean[None, :, None, None]) * scale[None, :, None, None]
    normed = normed.reshape(frames, chans, pixels) * gain[None, :, None] + shift[None, :, None]
    return jax.nn.silu(normed).astype(jnp.bfloat16)


def spread(color, weight, index, total_pixels):
    numer = (
        jnp.zeros((color.shape[0], 3, total_pixels), jnp.float32)
        .at[:, :, index]
        .add(color * weight[None, None, :])
    )
    denom = jnp.zeros((total_pixels,), jnp.float32).at[index].add(weight)
    return (numer, denom)


def route_owned(numer, denom, tile_id, own):
    frames = numer.shape[0]
    margin = (GRID_X + 1) * own
    numer_wide = jnp.concatenate([numer, jnp.zeros((frames, 3, margin), jnp.float32)], axis=2)
    denom_wide = jnp.concatenate([denom, jnp.zeros((margin,), jnp.float32)], axis=0)
    first_pixel = tile_id * own

    def block_at(offset):
        start_pixel = first_pixel + offset * own
        return (
            lax.dynamic_slice_in_dim(numer_wide, start_pixel, own, 2),
            lax.dynamic_slice_in_dim(denom_wide, start_pixel, own, 0),
        )

    owned_numer, owned_denom = block_at(0)
    for offset in (1, GRID_X, GRID_X + 1):
        piece_numer, piece_denom = block_at(offset)
        got_numer, got_denom = shifted((piece_numer, piece_denom), "tile", offset)
        owned_numer = owned_numer + got_numer
        owned_denom = owned_denom + got_denom
    return (owned_numer, owned_denom)


def general_body(
    latents, tile_order, w_in, gain_in, shift_in, w_mid, gain_mid, shift_mid, w_out, blend_weight
):
    frames = latents.shape[0]
    total_frames = frames * lax.axis_size("tm")
    tiles = tile_order.shape[0]
    own = STRIDE * STRIDE
    total_pixels = tiles * own
    tile_id = lax.axis_index("tile")
    index, valid = window_index(tile_id, tiles)
    whole = lax.all_gather(latents, "tile", axis=2, tiled=True)
    blocks = whole.reshape(frames, whole.shape[1], tiles, own)
    image = (
        jnp.zeros_like(blocks)
        .at[:, :, tile_order]
        .set(blocks)
        .reshape(frames, whole.shape[1], total_pixels)
    )
    window = jnp.where(
        valid[None, None, :], jnp.take(image, index, axis=2), jnp.zeros((), jnp.bfloat16)
    )
    first = causal_conv(with_history(window), w_in, frames, TSIDE)
    hidden = normalize(first, gain_in, shift_in, total_frames)
    second = causal_conv(
        lax.all_gather(with_history(hidden), "chan", axis=1, tiled=True), w_mid, frames, TSIDE
    )
    upper = normalize(second, gain_mid, shift_mid, total_frames)
    color = jnp.einsum("oc,fcp->fop", w_out, upper, preferred_element_type=jnp.float32)
    weight = jnp.where(valid, blend_weight[tile_id], jnp.float32(0.0))
    numer, denom = spread(color, weight, index, total_pixels)
    numer, denom = route_owned(numer, denom, tile_id, own)
    numer = lax.psum(numer, "chan")
    return numer / denom[None, None, :]


def block_cases(tiles):
    downs = (0, 1) if tiles // GRID_X > 1 else (0,)
    return [(down, across) for down in downs for across in (0, 1)]


def exact_dot(values, ones):
    rows = values.shape[0]
    high = values.astype(jnp.bfloat16)
    rest = values - high.astype(jnp.float32)
    middle = rest.astype(jnp.bfloat16)
    low = (rest - middle.astype(jnp.float32)).astype(jnp.bfloat16)
    total = jnp.dot(
        jnp.concatenate([high, middle, low], axis=0), ones, preferred_element_type=jnp.float32
    )
    return total[:rows] + total[rows : 2 * rows] + total[2 * rows :]


def group_affine(sums, squares, gain, shift, count):
    lanes = sums.shape[1]
    width = CH // GROUPS
    same = lax.broadcasted_iota(jnp.int32, (lanes, lanes), 0) // width == (
        lax.broadcasted_iota(jnp.int32, (lanes, lanes), 1) // width
    )
    total = exact_dot(
        jnp.concatenate([sums, squares], axis=0), jnp.where(same, 1.0, 0.0).astype(jnp.bfloat16)
    )
    mean = jnp.sum(total[:8], axis=0, keepdims=True) / count
    variance = jnp.sum(total[8:], axis=0, keepdims=True) / count - mean * mean
    scale = gain * lax.rsqrt(variance + EPSILON)
    return scale, shift - mean * scale


def silu(value):
    below = 1.0 + jnp.exp2(jnp.minimum(value * -LOG2_E, 115.0))
    inverse = pl.reciprocal(below, approx=True)
    inverse = inverse * (2.0 - below * inverse)
    return value * inverse


def fold(values):
    rows, lanes = values.shape
    return jnp.sum(values.reshape(rows // 8, 8, lanes), axis=0)


def decode_kernel(
    tiles,
    spans,
    shares,
    *refs,
):
    cases = block_cases(tiles)
    refs = list(refs)

    def take(number):
        taken = refs[:number]
        del refs[:number]
        return taken

    w_mid_ref, table_ref, order_ref = take(3)
    latent_refs, w_in_refs = take(spans), take(shares)
    keep_ref, send_ref, denom_ref = take(3)
    chosen, taps, turned_taps, turned_last, first, hidden, weights, partial = take(8)
    shown_ref, sems = take(2)

    own = denom_ref.shape[1]
    own_frames = keep_ref.shape[2]
    frames = own_frames * spans
    latent, wide = w_in_refs[0].shape[1:]
    rows_in = frames * latent
    rows_own = rows_in // spans
    depth_in = 27 * latent
    pixels = TSIDE * TSIDE
    lanes = partial.shape[3]
    tile_id = lax.axis_index("tile")
    mine = lax.axis_index("tm")
    chan_id = lax.axis_index("chan")

    copies = []
    for a in range(3):
        for b in range(3):
            for e in range(3):
                tap = 9 * a + 3 * b + e
                copy = pltpu.make_async_copy(
                    w_mid_ref.at[tap, :, pl.ds(pl.multiple_of(mine * lanes, LANES), lanes)],
                    weights.at[pl.ds(b * CH, CH), pl.ds((3 * a + e) * lanes, lanes)],
                    sems.at[tap],
                )
                copy.start()
                copies.append(copy)

    tile_row, tile_col = tile_id // GRID_X, tile_id % GRID_X
    gain_row = rows_own + 2
    w_out_row = gain_row + 2
    blend_row = w_out_row + 3
    order = order_ref[...]
    number_of = lax.broadcasted_iota(jnp.int32, order.shape, 0)
    lane_of = lax.broadcasted_iota(jnp.int32, order.shape, 1)
    rows_all = latent_refs[0].shape[0] // tiles
    turns = []
    for down, across in cases:
        wanted = tile_id + down * GRID_X + across
        found = (order == wanted.astype(jnp.float32)) & (lane_of == 0)
        place = jnp.sum(jnp.where(found, number_of.astype(jnp.float32), 0.0))
        turns.append((tile_id - place.astype(jnp.int32) + tiles) % tiles)
    for number, (down, across) in enumerate(cases):
        inside = (tile_row + down < tiles // GRID_X) & (tile_col + across < GRID_X)
        turn = turns[number]
        part = slice(number * LANES, (number + 1) * LANES)
        for steps in range(tiles):

            @pl.when(inside & (turn == steps))
            def _():
                for swap in range(spans):
                    at, tail_at = swap * rows_own, rows_in + swap * latent
                    block = latent_refs[swap][steps * rows_all : (steps + 1) * rows_all]
                    chosen[at : at + rows_own, part] = block[:rows_own]
                    chosen[tail_at : tail_at + latent, part] = block[rows_own : rows_own + latent]

        @pl.when(jnp.logical_not(inside))
        def _():
            chosen[:, part] = jnp.zeros((chosen.shape[0], LANES), chosen.dtype)

    slot = lax.broadcasted_iota(jnp.int32, (1, pixels), 1)
    up, along = slot // TSIDE, slot % TSIDE
    source = lax.broadcasted_iota(jnp.int32, (LANES, pixels), 0)
    tail = own - LANES

    def pick(first_pixel):
        parts = []
        for down, across in cases:
            u, v = up - down * STRIDE, along - across * STRIDE
            good = (u >= 0) & (u < STRIDE) & (v >= 0) & (v < STRIDE)
            wanted = jnp.where(good, u * STRIDE + v - first_pixel, -1)
            parts.append(jnp.where(source == wanted, 1.0, 0.0).astype(jnp.bfloat16))
        return jnp.concatenate(parts, axis=0)

    tails = chosen[rows_in:].astype(jnp.float32)
    width = tails.shape[1]
    turned = [pltpu.roll(tails, (-f * tail) % width, 1) if f else tails for f in range(own_frames)]
    tails = jnp.concatenate(
        [
            turned[f][swap * latent : (swap + 1) * latent]
            for swap in range(spans)
            for f in range(own_frames)
        ],
        axis=0,
    ).astype(jnp.bfloat16)
    in_tail = lax.broadcasted_iota(jnp.int32, tails.shape, 1) % LANES < tail
    tails = jnp.where(in_tail, tails.astype(jnp.float32), 0.0).astype(jnp.bfloat16)
    window = jnp.dot(
        chosen[:rows_in], pick(0), preferred_element_type=jnp.float32
    ) + jnp.dot(tails, pick(LANES), preferred_element_type=jnp.float32)
    for b in range(3):
        for e in range(3):
            inside = (
                (up + b - 1 >= 0)
                & (up + b - 1 < TSIDE)
                & (along + e - 1 >= 0)
                & (along + e - 1 < TSIDE)
            )
            offset = (b - 1) * TSIDE + e - 1
            moved = pltpu.roll(window, (-offset) % pixels, 1) if offset else window
            moved = jnp.where(inside, moved, 0.0).astype(jnp.bfloat16)
            for swap in range(spans):
                value = moved[swap * rows_own : (swap + 1) * rows_own]
                span = pl.ds((mine + swap) % spans * own_frames, own_frames)
                taps[span, 3 * b + e] = value.reshape(own_frames, latent, pixels)

    turned_taps[0:2] = jnp.zeros((2, pixels, LANES), turned_taps.dtype)
    for f in range(frames):
        turned_taps[f + 2] = taps[f, 0:8].reshape(8 * latent, pixels).T
    turned_last[...] = taps[:, 8].reshape(frames * latent, pixels).T
    joined = jnp.concatenate([w_in_refs[s][...] for s in range(shares)], axis=2)
    main_rows = [joined[9 * a : 9 * a + 8].reshape(8 * latent, CH) for a in range(3)]
    sums = jnp.zeros((8, CH), jnp.float32)
    squares = jnp.zeros((8, CH), jnp.float32)
    nothing = jnp.zeros((latent, CH), jnp.bfloat16)
    for f in range(frames):
        patch = [turned_taps[f + a] for a in range(3)] + [turned_last[...]]
        last_rows = [
            joined[9 * (g - f + 2) + 8] if 0 <= g - f + 2 < 3 else nothing for g in range(frames)
        ]
        value = jnp.dot(
            jnp.concatenate(patch, axis=1),
            jnp.concatenate(main_rows + last_rows, axis=0),
            preferred_element_type=jnp.float32,
        )
        first[f] = value
        sums = sums + fold(value)
        squares = squares + fold(value * value)
    count = frames * (CH // GROUPS) * pixels
    affine = []
    for s in range(shares):
        at = s * rows_all + rows_own + latent
        table = latent_refs[0][at : at + wide // LANES * 4].astype(jnp.float32)
        pieces = [table[4 * lane : 4 * lane + 4] for lane in range(wide // LANES)]
        table = jnp.concatenate([part[0:2] + part[2:4] for part in pieces], axis=1)
        part = slice(s * wide, (s + 1) * wide)
        affine.append(
            group_affine(sums[:, part], squares[:, part], table[0:1], table[1:2], count)
        )
    channels = [
        pl.ds(pl.multiple_of((chan_id + s) % shares * wide, LANES), wide) for s in range(shares)
    ]

    def hide(f):
        edge = jnp.zeros((TSIDE, CH), jnp.bfloat16)
        hidden[f, 0:TSIDE] = edge
        hidden[f, TSIDE + pixels : 2 * TSIDE + pixels] = edge
        for s in range(shares):
            scale, bias = affine[s]
            value = first[f, :, s * wide : (s + 1) * wide] * scale + bias
            hidden[f, TSIDE : TSIDE + pixels, channels[s]] = silu(value).astype(
                jnp.bfloat16
            )

    def convolve(start, several, depth_taps):
        lhs = jnp.concatenate(
            [
                hidden[start : start + several, b * TSIDE : b * TSIDE + pixels].reshape(
                    several * pixels, CH
                )
                for b in range(3)
            ],
            axis=1,
        )
        low = depth_taps[0] * 3 * lanes
        odd = len(depth_taps) % 2
        product = jnp.dot(
            lhs, weights[:, low : (9 - odd) * lanes], preferred_element_type=jnp.float32
        )
        if odd:
            rows = jnp.concatenate(
                [weights[b * CH : (b + 1) * CH, 8 * lanes :] for b in range(3)], axis=1
            )
            apart = jnp.dot(lhs[:, CH : 2 * CH], rows, preferred_element_type=jnp.float32)
        edge = jnp.zeros((TSIDE, lanes), jnp.float32)
        for a in depth_taps:
            for e in range(3):
                at = (3 * a + e) * lanes - low
                for f in range(several):
                    target = start + f + 2 - a
                    if odd and (a, e) == (2, 2):
                        value = apart[f * pixels : (f + 1) * pixels]
                        above = value[: pixels - TSIDE, :lanes]
                        below = value[TSIDE:, 2 * lanes :]
                        value = (
                            value[:, lanes : 2 * lanes]
                            + jnp.concatenate([edge, above], axis=0)
                            + jnp.concatenate([below, edge], axis=0)
                        )
                    else:
                        value = product[f * pixels : (f + 1) * pixels, at : at + lanes]
                    if start + f == max(target - 2, 0):
                        partial[e, target] = value
                    else:
                        partial[e, target] += value

    column = lax.broadcasted_iota(jnp.int32, (pixels, lanes), 0) % TSIDE
    total = [jnp.zeros((8, lanes), jnp.float32)] * 2

    def gather(f):
        left = jnp.where(column == 0, 0.0, pltpu.roll(partial[0, f], 1, 0))
        right = jnp.where(column == TSIDE - 1, 0.0, pltpu.roll(partial[2, f], pixels - 1, 0))
        value = partial[1, f] + left + right
        partial[1, f] = value
        total[0] = total[0] + fold(value)
        total[1] = total[1] + fold(value * value)

    bounds = [0, 2, frames - 2, frames - 1, frames]
    groups = [range(low, high) for low, high in zip(bounds, bounds[1:]) if high > low]
    for copy in copies:
        copy.wait()
    for f in groups[0]:
        hide(f)
    for number, group in enumerate(groups):
        if number + 1 < len(groups):
            for f in groups[number + 1]:
                hide(f)
        convolve(
            group.start,
            len(group),
            tuple(a for a in range(3) if group.stop - 1 + 2 - a < frames),
        )
        if number:
            for f in groups[number - 1]:
                gather(f)
    for f in groups[-1]:
        gather(f)

    part = pl.ds(pl.multiple_of(mine * lanes, LANES), lanes)
    scale, bias = group_affine(
        total[0],
        total[1],
        table_ref[gain_row : gain_row + 1, part],
        table_ref[gain_row + 1 : gain_row + 2, part],
        count,
    )
    blend = table_ref[pl.ds(blend_row + tile_id, 1), :]
    blend = jnp.where(
        (tile_row * STRIDE + up < tiles // GRID_X * STRIDE)
        & (tile_col * STRIDE + along < GRID_X * STRIDE),
        blend,
        0.0,
    )
    w_out = jnp.concatenate(
        [table_ref[w_out_row : w_out_row + 3, part], jnp.zeros((5, lanes), jnp.float32)], axis=0
    ).astype(jnp.bfloat16)
    colors = []
    for f in range(frames):
        upper = silu(partial[1, f] * scale + bias).astype(jnp.bfloat16)
        color = lax.dot_general(
            w_out, upper, (((1,), (1,)), ((), ())), preferred_element_type=jnp.float32
        )
        colors.append(color * blend)
    colors = jnp.concatenate(colors, axis=0)

    slot_in = lax.broadcasted_iota(jnp.int32, (pixels, pixels), 0)
    pixel = lax.broadcasted_iota(jnp.int32, (pixels, pixels), 1)
    shown, weight_rows = [], []
    for down, across in cases:
        u, v = slot_in // TSIDE - down * STRIDE, slot_in % TSIDE - across * STRIDE
        good = (u >= 0) & (u < STRIDE) & (v >= 0) & (v < STRIDE) & (u * STRIDE + v == pixel)
        shown.append(jnp.where(good, 1.0, 0.0).astype(jnp.bfloat16))
        inside = (tile_row >= down) & (tile_col >= across)
        other = jnp.maximum(tile_id - down * GRID_X - across, 0)
        weight = jnp.where(inside, table_ref[pl.ds(blend_row + other, 1), :], 0.0)
        weight_rows.append(jnp.broadcast_to(weight, (8, pixels)))
    shown_ref[...] = exact_dot(
        jnp.concatenate([colors] + weight_rows, axis=0), jnp.concatenate(shown, axis=1)
    )
    denom = jnp.zeros((8, own), jnp.float32)
    for number in range(len(cases)):
        lane = slice(number * pixels, number * pixels + own)
        row = 8 * (frames + number)
        denom = denom + shown_ref[row : row + 8, lane]
        for swap in range(spans):
            target = keep_ref if swap == 0 else send_ref.at[swap - 1]
            base = (mine + swap) % spans * own_frames * 8
            for at in range(own_frames):
                for o in range(3):
                    target[number, o, at : at + 1, :] = shown_ref[
                        pl.ds(base + 8 * at + o, 1), lane
                    ]
    denom_ref[...] = denom


def from_ring(value, axis):
    count = lax.axis_size(axis)
    return [
        lax.ppermute(value, axis, [((d + turn) % count, d) for d in range(count)])
        for turn in range(1, count)
    ]


def ring_sum(kept, sent, axis):
    count = lax.axis_size(axis)
    for turn in range(1, count):
        kept = kept + lax.ppermute(
            sent[turn - 1], axis, [(d, (d + turn) % count) for d in range(count)]
        )
    return kept


def small_table(*values):
    values = [value.reshape(-1, value.shape[-1]) for value in values]
    wide = max(value.shape[1] for value in values)
    height = sum(value.shape[0] for value in values)
    total, row = 0.0, 0
    for value in values:
        below = height - row - value.shape[0]
        value = jnp.pad(value.astype(jnp.float32), ((row, below), (0, wide - value.shape[1])))
        total = total + value
        row = height - below
    return total


def exchange_latents(frames, latent, own, table):
    tiles, shares = lax.axis_size("tile"), lax.axis_size("chan")
    tail = own - LANES
    height = frames * latent
    mine = table[:height, :own].astype(jnp.bfloat16)
    tails = sum(
        jnp.pad(
            mine[f * latent : (f + 1) * latent, LANES:],
            ((0, 0), (tail * f, LANES - tail * (f + 1))),
        )
        for f in range(frames)
    )
    affine = table[height : height + 2]
    high = lax.reduce_precision(affine, 8, 7)
    low = lax.reduce_precision(affine - high, 8, 7)
    affine = jnp.concatenate([high, low], axis=0).astype(jnp.bfloat16)
    rows = [affine[:, at : at + LANES] for at in range(0, affine.shape[1], LANES)]
    rows = jnp.concatenate(rows, axis=0)
    rows = jnp.pad(rows, ((0, -rows.shape[0] % 16), (0, 0)))
    message = jnp.concatenate([mine[:, :LANES], tails, rows], axis=0)
    got = [message]
    for steps in range(1, tiles):
        turn = steps if steps < shares else 0
        pairs = [
            (t * shares + (c + turn) % shares, (t + steps) % tiles * shares + c)
            for t in range(tiles)
            for c in range(shares)
        ]
        got.append(lax.ppermute(message, ("tile", "chan"), pairs))
    stack = jnp.concatenate(got, axis=0)
    return [stack] + from_ring(stack, "tm")


def lanes_body(
    latents, tile_order, w_in, gain_in, shift_in, w_mid, gain_mid, shift_mid, w_out, blend_weight
):
    own_frames, latent, own = latents.shape
    spans = lax.axis_size("tm")
    shares = lax.axis_size("chan")
    frames = own_frames * spans
    if 8 * latent != LANES or frames * latent != LANES:
        return general_body(
            latents,
            tile_order,
            w_in,
            gain_in,
            shift_in,
            w_mid,
            gain_mid,
            shift_mid,
            w_out,
            blend_weight,
        )
    tiles = tile_order.shape[0]
    wide = w_in.shape[2]
    lanes = wide // spans
    pixels = TSIDE * TSIDE
    cases = block_cases(tiles)

    w_in_all = [(from_ring(other, "tm") or [other])[0] for other in from_ring(w_in, "chan")]
    table = lax.optimization_barrier(
        small_table(
            latents.reshape(own_frames * latent, own),
            gain_in,
            shift_in,
            gain_mid,
            shift_mid,
            w_out,
            blend_weight,
        )
    )
    latents_all = exchange_latents(own_frames, latent, own, table)
    _, w_in, tile_order = lax.optimization_barrier((table, w_in, tile_order))
    order = jnp.broadcast_to(tile_order.astype(jnp.float32)[:, None], (tiles, LANES))
    w_in_own = from_ring(w_in, "tm")[:1] or [w_in]

    vmem = pl.BlockSpec(memory_space=pltpu.VMEM)
    piece = (len(cases), 3, own_frames, own)
    kept, sent, denom = pl.pallas_call(
        functools.partial(decode_kernel, tiles, spans, shares),
        out_shape=[
            jax.ShapeDtypeStruct(piece, jnp.float32),
            jax.ShapeDtypeStruct((max(spans - 1, 1),) + piece, jnp.float32),
            jax.ShapeDtypeStruct((8, own), jnp.float32),
        ],
        in_specs=[pl.BlockSpec(memory_space=pl.ANY)] + [vmem] * (2 + spans + shares),
        out_specs=[vmem] * 3,
        scratch_shapes=[
            pltpu.VMEM(((frames + spans) * latent, len(cases) * LANES), jnp.bfloat16),
            pltpu.VMEM((frames, 9, latent, pixels), jnp.bfloat16),
            pltpu.VMEM((frames + 2, pixels, LANES), jnp.bfloat16),
            pltpu.VMEM((pixels, LANES), jnp.bfloat16),
            pltpu.VMEM((frames, pixels, CH), jnp.float32),
            pltpu.VMEM((frames, pixels + 2 * TSIDE, CH), jnp.bfloat16),
            pltpu.VMEM((3 * CH, 9 * lanes), jnp.bfloat16),
            pltpu.VMEM((3, frames, pixels, lanes), jnp.float32),
            pltpu.VMEM((8 * (frames + len(cases)), len(cases) * pixels), jnp.float32),
            pltpu.SemaphoreType.DMA((27,)),
        ],
        compiler_params=pltpu.CompilerParams(vmem_limit_bytes=VMEM_BYTES),
        cost_estimate=pl.CostEstimate(
            flops=2 * frames * pixels * 27 * CH * lanes, bytes_accessed=8_000_000, transcendentals=0
        ),
    )(w_mid, table, order, *latents_all, *w_in_own, *w_in_all)
    total = ring_sum(kept, sent, "tm")
    total = ring_sum(total, [total] * (shares - 1), "chan")
    numer = total[0]
    for number, (down, across) in enumerate(cases):
        steps = down * GRID_X + across
        if steps and steps < tiles:
            numer = numer + shifted(total[number], "tile", steps)
    return jnp.transpose(numer / denom[0][None, None, :], (1, 0, 2))


def solution(mesh):
    placed = (
        P("tm", "groups", "tile"),
        P("groups"),
        P(None, None, "chan"),
        P("chan"),
        P("chan"),
        P(None, None, "chan"),
        P("chan"),
        P("chan"),
        P(None, "chan"),
        P("groups", None),
    )
    whole_lanes = (
        CH % (mesh.shape["chan"] * mesh.shape["tm"] * LANES) == 0
        and mesh.shape["chan"] <= mesh.shape["tile"]
    )
    return jax.shard_map(
        lanes_body if whole_lanes else general_body,
        mesh=mesh,
        in_specs=placed,
        out_specs=P("tm", "groups", "tile"),
        check_vma=False,
    )
```

```python
import functools

import jax
import jax.numpy as jnp
from jax import lax
from jax.experimental import pallas as pl
from jax.experimental.pallas import tpu as pltpu
from jax.sharding import PartitionSpec as P

CH = 512
GROUPS = 32
TSIDE = 16
STRIDE = 12
GRID_X = 4

EPSILON = 1e-06
LANES = 128
VMEM_BYTES = 48 * 1024 * 1024


def shifted(value, axis, steps):
    count = lax.axis_size(axis)
    leading, last = (max(0, -steps), min(count, count - steps))
    return lax.ppermute(value, axis, [(source, source + steps) for source in range(leading, last)])


def window_index(tile_id, tiles):
    slots = jnp.arange(TSIDE * TSIDE, dtype=jnp.int32)
    row = tile_id // GRID_X * STRIDE + slots // TSIDE
    col = tile_id % GRID_X * STRIDE + slots % TSIDE
    valid = (row < tiles // GRID_X * STRIDE) & (col < GRID_X * STRIDE)
    block = row // STRIDE * GRID_X + col // STRIDE
    index = block * (STRIDE * STRIDE) + row % STRIDE * STRIDE + col % STRIDE
    return (jnp.where(valid, index, 0), valid)


def causal_conv(extended, weights, frames, side):
    pixels = side * side
    rows = jnp.arange(pixels, dtype=jnp.int32) // side
    cols = jnp.arange(pixels, dtype=jnp.int32) % side
    total = jnp.zeros((frames, weights.shape[2], pixels), jnp.float32)
    for depth in range(3):
        window = extended[depth : depth + frames]
        for down in range(3):
            for across in range(3):
                offset = (down - 1) * side + (across - 1)
                inside = (
                    (rows + down - 1 >= 0)
                    & (rows + down - 1 < side)
                    & (cols + across - 1 >= 0)
                    & (cols + across - 1 < side)
                )
                moved = jnp.roll(window, -offset, axis=2)
                moved = jnp.where(inside[None, None, :], moved, jnp.zeros_like(moved))
                total = total + jnp.einsum(
                    "fcp,co->fop",
                    moved,
                    weights[9 * depth + 3 * down + across],
                    preferred_element_type=jnp.float32,
                )
    return total


def with_history(values):
    frames = values.shape[0]
    earlier = shifted(values[frames - 2 :], "tm", 1)
    return jnp.concatenate([earlier, values], axis=0)


def normalize(values, gain, shift, total_frames):
    frames, chans, pixels = values.shape
    width = CH // GROUPS
    grouped = values.reshape(frames, chans // width, width, pixels)
    sums = jnp.sum(grouped, axis=(0, 2, 3))
    squares = jnp.sum(grouped * grouped, axis=(0, 2, 3))
    sums, squares = lax.psum((sums, squares), "tm")
    count = total_frames * width * pixels
    mean = sums / count
    variance = squares / count - mean * mean
    scale = lax.rsqrt(variance + EPSILON)
    normed = (grouped - mean[None, :, None, None]) * scale[None, :, None, None]
    normed = normed.reshape(frames, chans, pixels) * gain[None, :, None] + shift[None, :, None]
    return jax.nn.silu(normed).astype(jnp.bfloat16)


def spread(color, weight, index, total_pixels):
    numer = (
        jnp.zeros((color.shape[0], 3, total_pixels), jnp.float32)
        .at[:, :, index]
        .add(color * weight[None, None, :])
    )
    denom = jnp.zeros((total_pixels,), jnp.float32).at[index].add(weight)
    return (numer, denom)


def route_owned(numer, denom, tile_id, own):
    frames = numer.shape[0]
    margin = (GRID_X + 1) * own
    numer_wide = jnp.concatenate([numer, jnp.zeros((frames, 3, margin), jnp.float32)], axis=2)
    denom_wide = jnp.concatenate([denom, jnp.zeros((margin,), jnp.float32)], axis=0)
    first_pixel = tile_id * own

    def block_at(offset):
        start_pixel = first_pixel + offset * own
        return (
            lax.dynamic_slice_in_dim(numer_wide, start_pixel, own, 2),
            lax.dynamic_slice_in_dim(denom_wide, start_pixel, own, 0),
        )

    owned_numer, owned_denom = block_at(0)
    for offset in (1, GRID_X, GRID_X + 1):
        piece_numer, piece_denom = block_at(offset)
        got_numer, got_denom = shifted((piece_numer, piece_denom), "tile", offset)
        owned_numer = owned_numer + got_numer
        owned_denom = owned_denom + got_denom
    return (owned_numer, owned_denom)


def general_body(
    latents, tile_order, w_in, gain_in, shift_in, w_mid, gain_mid, shift_mid, w_out, blend_weight
):
    frames = latents.shape[0]
    total_frames = frames * lax.axis_size("tm")
    tiles = tile_order.shape[0]
    own = STRIDE * STRIDE
    total_pixels = tiles * own
    tile_id = lax.axis_index("tile")
    index, valid = window_index(tile_id, tiles)
    whole = lax.all_gather(latents, "tile", axis=2, tiled=True)
    blocks = whole.reshape(frames, whole.shape[1], tiles, own)
    image = (
        jnp.zeros_like(blocks)
        .at[:, :, tile_order]
        .set(blocks)
        .reshape(frames, whole.shape[1], total_pixels)
    )
    window = jnp.where(
        valid[None, None, :], jnp.take(image, index, axis=2), jnp.zeros((), jnp.bfloat16)
    )
    first = causal_conv(with_history(window), w_in, frames, TSIDE)
    hidden = normalize(first, gain_in, shift_in, total_frames)
    second = causal_conv(
        lax.all_gather(with_history(hidden), "chan", axis=1, tiled=True), w_mid, frames, TSIDE
    )
    upper = normalize(second, gain_mid, shift_mid, total_frames)
    color = jnp.einsum("oc,fcp->fop", w_out, upper, preferred_element_type=jnp.float32)
    weight = jnp.where(valid, blend_weight[tile_id], jnp.float32(0.0))
    numer, denom = spread(color, weight, index, total_pixels)
    numer, denom = route_owned(numer, denom, tile_id, own)
    numer = lax.psum(numer, "chan")
    return numer / denom[None, None, :]


def block_cases(tiles):
    downs = (0, 1) if tiles // GRID_X > 1 else (0,)
    return [(down, across) for down in downs for across in (0, 1)]


def exact_dot(values, ones):
    rows = values.shape[0]
    high = values.astype(jnp.bfloat16)
    rest = values - high.astype(jnp.float32)
    middle = rest.astype(jnp.bfloat16)
    low = (rest - middle.astype(jnp.float32)).astype(jnp.bfloat16)
    total = jnp.dot(
        jnp.concatenate([high, middle, low], axis=0), ones, preferred_element_type=jnp.float32
    )
    return total[:rows] + total[rows : 2 * rows] + total[2 * rows :]


def group_affine(sums, squares, gain, shift, count):
    lanes = sums.shape[1]
    width = CH // GROUPS
    same = lax.broadcasted_iota(jnp.int32, (lanes, lanes), 0) // width == (
        lax.broadcasted_iota(jnp.int32, (lanes, lanes), 1) // width
    )
    total = exact_dot(
        jnp.concatenate([sums, squares], axis=0), jnp.where(same, 1.0, 0.0).astype(jnp.bfloat16)
    )
    mean = jnp.sum(total[:8], axis=0, keepdims=True) / count
    variance = jnp.sum(total[8:], axis=0, keepdims=True) / count - mean * mean
    scale = gain * lax.rsqrt(variance + EPSILON)
    return 0.5 * scale, 0.5 * (shift - mean * scale)


def silu_of_half(half):
    return half + half * jnp.tanh(half)


def fold(values):
    rows, lanes = values.shape
    return jnp.sum(values.reshape(rows // 8, 8, lanes), axis=0)


def decode_kernel(
    tiles,
    spans,
    shares,
    *refs,
):
    cases = block_cases(tiles)
    refs = list(refs)

    def take(number):
        taken = refs[:number]
        del refs[:number]
        return taken

    w_mid_ref, table_ref, order_ref = take(3)
    latent_refs, w_in_refs = take(spans), take(shares)
    keep_ref, send_ref, denom_ref = take(3)
    chosen, taps, turned_taps, turned_last, first, weights, partial = take(7)
    shown_ref, sems = take(2)
    hidden = take(first.shape[0])

    own = denom_ref.shape[1]
    own_frames = keep_ref.shape[2]
    frames = own_frames * spans
    latent, wide = w_in_refs[0].shape[1:]
    rows_in = frames * latent
    rows_own = rows_in // spans
    depth_in = 27 * latent
    pixels = TSIDE * TSIDE
    lanes = partial.shape[3]
    tile_id = lax.axis_index("tile")
    mine = lax.axis_index("tm")
    chan_id = lax.axis_index("chan")

    half = pl.ds(pl.multiple_of(mine * lanes, LANES), lanes)
    copies = []
    for a in range(3):
        for b in range(3):
            for e in range(3):
                for share in range(shares):
                    tap = 9 * a + 3 * b + e
                    held = pl.multiple_of((chan_id + share) % shares * wide, LANES)
                    copy = pltpu.make_async_copy(
                        w_mid_ref.at[tap, pl.ds(held, wide), half],
                        weights.at[
                            pl.ds(b * CH + share * wide, wide), pl.ds((3 * a + e) * lanes, lanes)
                        ],
                        sems.at[tap * shares + share],
                    )
                    copy.start()
                    copies.append(copy)

    tile_row, tile_col = tile_id // GRID_X, tile_id % GRID_X
    gain_row = rows_own + 2
    w_out_row = gain_row + 2
    blend_row = w_out_row + 3
    order = order_ref[...]
    number_of = lax.broadcasted_iota(jnp.int32, order.shape, 0)
    lane_of = lax.broadcasted_iota(jnp.int32, order.shape, 1)
    rows_all = latent_refs[0].shape[0] // tiles
    turns = []
    for down, across in cases:
        wanted = tile_id + down * GRID_X + across
        found = (order == wanted.astype(jnp.float32)) & (lane_of == 0)
        place = jnp.sum(jnp.where(found, number_of.astype(jnp.float32), 0.0))
        turns.append((tile_id - place.astype(jnp.int32) + tiles) % tiles)
    for number, (down, across) in enumerate(cases):
        inside = (tile_row + down < tiles // GRID_X) & (tile_col + across < GRID_X)
        turn = turns[number]
        part = slice(number * LANES, (number + 1) * LANES)
        for steps in range(tiles):

            @pl.when(inside & (turn == steps))
            def _():
                for swap in range(spans):
                    at, tail_at = swap * rows_own, rows_in + swap * latent
                    block = latent_refs[swap][steps * rows_all : (steps + 1) * rows_all]
                    chosen[at : at + rows_own, part] = block[:rows_own]
                    chosen[tail_at : tail_at + latent, part] = block[rows_own : rows_own + latent]

        @pl.when(jnp.logical_not(inside))
        def _():
            chosen[:, part] = jnp.zeros((chosen.shape[0], LANES), chosen.dtype)

    slot = lax.broadcasted_iota(jnp.int32, (1, pixels), 1)
    up, along = slot // TSIDE, slot % TSIDE
    source = lax.broadcasted_iota(jnp.int32, (LANES, pixels), 0)
    tail = own - LANES

    def pick(first_pixel):
        parts = []
        for down, across in cases:
            u, v = up - down * STRIDE, along - across * STRIDE
            good = (u >= 0) & (u < STRIDE) & (v >= 0) & (v < STRIDE)
            wanted = jnp.where(good, u * STRIDE + v - first_pixel, -1)
            parts.append(jnp.where(source == wanted, 1.0, 0.0).astype(jnp.bfloat16))
        return jnp.concatenate(parts, axis=0)

    tails = chosen[rows_in:].astype(jnp.float32)
    width = tails.shape[1]
    turned = [pltpu.roll(tails, (-f * tail) % width, 1) if f else tails for f in range(own_frames)]
    tails = jnp.concatenate(
        [
            turned[f][swap * latent : (swap + 1) * latent]
            for swap in range(spans)
            for f in range(own_frames)
        ],
        axis=0,
    ).astype(jnp.bfloat16)
    in_tail = lax.broadcasted_iota(jnp.int32, tails.shape, 1) % LANES < tail
    tails = jnp.where(in_tail, tails.astype(jnp.float32), 0.0).astype(jnp.bfloat16)
    window = jnp.dot(
        chosen[:rows_in], pick(0), preferred_element_type=jnp.float32
    ) + jnp.dot(tails, pick(LANES), preferred_element_type=jnp.float32)
    for b in range(3):
        for e in range(3):
            inside = (
                (up + b - 1 >= 0)
                & (up + b - 1 < TSIDE)
                & (along + e - 1 >= 0)
                & (along + e - 1 < TSIDE)
            )
            offset = (b - 1) * TSIDE + e - 1
            moved = pltpu.roll(window, (-offset) % pixels, 1) if offset else window
            moved = jnp.where(inside, moved, 0.0).astype(jnp.bfloat16)
            for swap in range(spans):
                value = moved[swap * rows_own : (swap + 1) * rows_own]
                span = pl.ds((mine + swap) % spans * own_frames, own_frames)
                taps[span, 3 * b + e] = value.reshape(own_frames, latent, pixels)

    turned_taps[0:2] = jnp.zeros((2, pixels, LANES), turned_taps.dtype)
    for f in range(frames):
        turned_taps[f + 2] = taps[f, 0:8].reshape(8 * latent, pixels).T
    turned_last[...] = taps[:, 8].reshape(frames * latent, pixels).T
    joined = jnp.concatenate([w_in_refs[s][...] for s in range(shares)], axis=2)
    main_rows = [joined[9 * a : 9 * a + 8].reshape(8 * latent, CH) for a in range(3)]
    sums = jnp.zeros((8, CH), jnp.float32)
    squares = jnp.zeros((8, CH), jnp.float32)
    nothing = jnp.zeros((latent, CH), jnp.bfloat16)
    for f in range(frames):
        patch = [turned_taps[f + a] for a in range(3)] + [turned_last[...]]
        last_rows = [
            joined[9 * (g - f + 2) + 8] if 0 <= g - f + 2 < 3 else nothing for g in range(frames)
        ]
        value = jnp.dot(
            jnp.concatenate(patch, axis=1),
            jnp.concatenate(main_rows + last_rows, axis=0),
            preferred_element_type=jnp.float32,
        )
        first[f] = value
        sums = sums + fold(value)
        squares = squares + fold(value * value)
    count = frames * (CH // GROUPS) * pixels
    affine = []
    for s in range(shares):
        at = s * rows_all + rows_own + latent
        table = latent_refs[0][at : at + wide // LANES * 4].astype(jnp.float32)
        pieces = [table[4 * lane : 4 * lane + 4] for lane in range(wide // LANES)]
        table = jnp.concatenate([part[0:2] + part[2:4] for part in pieces], axis=1)
        part = slice(s * wide, (s + 1) * wide)
        affine.append(
            group_affine(sums[:, part], squares[:, part], table[0:1], table[1:2], count)
        )
    def hide(f):
        edge = jnp.zeros((TSIDE, CH), jnp.bfloat16)
        hidden[f][0:TSIDE] = edge
        hidden[f][TSIDE + pixels : 2 * TSIDE + pixels] = edge
        for s in range(shares):
            scale, bias = affine[s]
            part = slice(s * wide, (s + 1) * wide)
            value = first[f, :, part] * scale + bias
            hidden[f][TSIDE : TSIDE + pixels, part] = silu_of_half(value).astype(jnp.bfloat16)

    def convolve(start, several, depth_taps):
        lhs = jnp.concatenate(
            [
                jnp.concatenate(
                    [
                        hidden[start + f][b * TSIDE : b * TSIDE + pixels]
                        for f in range(several)
                    ],
                    axis=0,
                )
                for b in range(3)
            ],
            axis=1,
        )
        low = depth_taps[0] * 3 * lanes
        odd = len(depth_taps) % 2
        product = jnp.dot(
            lhs, weights[:, low : (9 - odd) * lanes], preferred_element_type=jnp.float32
        )
        if odd:
            rows = jnp.concatenate(
                [weights[b * CH : (b + 1) * CH, 8 * lanes :] for b in range(3)], axis=1
            )
            apart = jnp.dot(lhs[:, CH : 2 * CH], rows, preferred_element_type=jnp.float32)
        edge = jnp.zeros((TSIDE, lanes), jnp.float32)
        for a in depth_taps:
            for e in range(3):
                at = (3 * a + e) * lanes - low
                for f in range(several):
                    target = start + f + 2 - a
                    if odd and (a, e) == (2, 2):
                        value = apart[f * pixels : (f + 1) * pixels]
                        above = value[: pixels - TSIDE, :lanes]
                        below = value[TSIDE:, 2 * lanes :]
                        value = (
                            value[:, lanes : 2 * lanes]
                            + jnp.concatenate([edge, above], axis=0)
                            + jnp.concatenate([below, edge], axis=0)
                        )
                    else:
                        value = product[f * pixels : (f + 1) * pixels, at : at + lanes]
                    if start + f == max(target - 2, 0):
                        partial[e, target] = value
                    else:
                        partial[e, target] += value

    column = lax.broadcasted_iota(jnp.int32, (pixels, lanes), 0) % TSIDE
    total = [jnp.zeros((8, lanes), jnp.float32)] * 2

    def gather(f):
        left = jnp.where(column == 0, 0.0, pltpu.roll(partial[0, f], 1, 0))
        right = jnp.where(column == TSIDE - 1, 0.0, pltpu.roll(partial[2, f], pixels - 1, 0))
        value = partial[1, f] + left + right
        partial[1, f] = value
        total[0] = total[0] + fold(value)
        total[1] = total[1] + fold(value * value)

    bounds = [0, 2, frames - 2, frames - 1, frames]
    groups = [range(low, high) for low, high in zip(bounds, bounds[1:]) if high > low]
    for copy in copies:
        copy.wait()
    for f in groups[0]:
        hide(f)
    for number, group in enumerate(groups):
        if number + 1 < len(groups):
            for f in groups[number + 1]:
                hide(f)
        convolve(
            group.start,
            len(group),
            tuple(a for a in range(3) if group.stop - 1 + 2 - a < frames),
        )
        if number:
            for f in groups[number - 1]:
                gather(f)
    for f in groups[-1]:
        gather(f)

    part = pl.ds(pl.multiple_of(mine * lanes, LANES), lanes)
    scale, bias = group_affine(
        total[0],
        total[1],
        table_ref[gain_row : gain_row + 1, part],
        table_ref[gain_row + 1 : gain_row + 2, part],
        count,
    )
    blend = table_ref[pl.ds(blend_row + tile_id, 1), :]
    blend = jnp.where(
        (tile_row * STRIDE + up < tiles // GRID_X * STRIDE)
        & (tile_col * STRIDE + along < GRID_X * STRIDE),
        blend,
        0.0,
    )
    w_out = jnp.concatenate(
        [table_ref[w_out_row : w_out_row + 3, part], jnp.zeros((5, lanes), jnp.float32)], axis=0
    ).astype(jnp.bfloat16)
    colors = []
    for f in range(frames):
        upper = silu_of_half(partial[1, f] * scale + bias).astype(jnp.bfloat16)
        color = lax.dot_general(
            w_out, upper, (((1,), (1,)), ((), ())), preferred_element_type=jnp.float32
        )
        colors.append(color * blend)
    colors = jnp.concatenate(colors, axis=0)

    slot_in = lax.broadcasted_iota(jnp.int32, (pixels, pixels), 0)
    pixel = lax.broadcasted_iota(jnp.int32, (pixels, pixels), 1)
    shown, weight_rows = [], []
    for down, across in cases:
        u, v = slot_in // TSIDE - down * STRIDE, slot_in % TSIDE - across * STRIDE
        good = (u >= 0) & (u < STRIDE) & (v >= 0) & (v < STRIDE) & (u * STRIDE + v == pixel)
        shown.append(jnp.where(good, 1.0, 0.0).astype(jnp.bfloat16))
        inside = (tile_row >= down) & (tile_col >= across)
        other = jnp.maximum(tile_id - down * GRID_X - across, 0)
        weight = jnp.where(inside, table_ref[pl.ds(blend_row + other, 1), :], 0.0)
        weight_rows.append(jnp.broadcast_to(weight, (8, pixels)))
    shown_ref[...] = exact_dot(
        jnp.concatenate([colors] + weight_rows, axis=0), jnp.concatenate(shown, axis=1)
    )
    denom = jnp.zeros((8, own), jnp.float32)
    for number in range(len(cases)):
        lane = slice(number * pixels, number * pixels + own)
        row = 8 * (frames + number)
        denom = denom + shown_ref[row : row + 8, lane]
        for swap in range(spans):
            target = keep_ref if swap == 0 else send_ref.at[swap - 1]
            base = (mine + swap) % spans * own_frames * 8
            for at in range(own_frames):
                for o in range(3):
                    target[number, o, at : at + 1, :] = shown_ref[
                        pl.ds(base + 8 * at + o, 1), lane
                    ]
    denom_ref[...] = denom


def from_ring(value, axis):
    count = lax.axis_size(axis)
    return [
        lax.ppermute(value, axis, [((d + turn) % count, d) for d in range(count)])
        for turn in range(1, count)
    ]


def ring_sum(kept, sent, axis):
    count = lax.axis_size(axis)
    for turn in range(1, count):
        kept = kept + lax.ppermute(
            sent[turn - 1], axis, [(d, (d + turn) % count) for d in range(count)]
        )
    return kept


def small_table(*values):
    values = [value.reshape(-1, value.shape[-1]) for value in values]
    wide = max(value.shape[1] for value in values)
    height = sum(value.shape[0] for value in values)
    total, row = 0.0, 0
    for value in values:
        below = height - row - value.shape[0]
        value = jnp.pad(value.astype(jnp.float32), ((row, below), (0, wide - value.shape[1])))
        total = total + value
        row = height - below
    return total


def exchange_latents(frames, latent, own, table):
    tiles, shares = lax.axis_size("tile"), lax.axis_size("chan")
    tail = own - LANES
    height = frames * latent
    mine = table[:height, :own].astype(jnp.bfloat16)
    tails = sum(
        jnp.pad(
            mine[f * latent : (f + 1) * latent, LANES:],
            ((0, 0), (tail * f, LANES - tail * (f + 1))),
        )
        for f in range(frames)
    )
    affine = table[height : height + 2]
    high = lax.reduce_precision(affine, 8, 7)
    low = lax.reduce_precision(affine - high, 8, 7)
    affine = jnp.concatenate([high, low], axis=0).astype(jnp.bfloat16)
    rows = [affine[:, at : at + LANES] for at in range(0, affine.shape[1], LANES)]
    rows = jnp.concatenate(rows, axis=0)
    rows = jnp.pad(rows, ((0, -rows.shape[0] % 16), (0, 0)))
    message = jnp.concatenate([mine[:, :LANES], tails, rows], axis=0)
    got = [message]
    for steps in range(1, tiles):
        turn = steps if steps < shares else 0
        pairs = [
            (t * shares + (c + turn) % shares, (t + steps) % tiles * shares + c)
            for t in range(tiles)
            for c in range(shares)
        ]
        got.append(lax.ppermute(message, ("tile", "chan"), pairs))
    stack = jnp.concatenate(got, axis=0)
    return [stack] + from_ring(stack, "tm")


def lanes_body(
    latents, tile_order, w_in, gain_in, shift_in, w_mid, gain_mid, shift_mid, w_out, blend_weight
):
    own_frames, latent, own = latents.shape
    spans = lax.axis_size("tm")
    shares = lax.axis_size("chan")
    frames = own_frames * spans
    if 8 * latent != LANES or frames * latent != LANES:
        return general_body(
            latents,
            tile_order,
            w_in,
            gain_in,
            shift_in,
            w_mid,
            gain_mid,
            shift_mid,
            w_out,
            blend_weight,
        )
    tiles = tile_order.shape[0]
    wide = w_in.shape[2]
    lanes = wide // spans
    pixels = TSIDE * TSIDE
    cases = block_cases(tiles)

    w_in_all = [(from_ring(other, "tm") or [other])[0] for other in from_ring(w_in, "chan")]
    table = lax.optimization_barrier(
        small_table(
            latents.reshape(own_frames * latent, own),
            gain_in,
            shift_in,
            gain_mid,
            shift_mid,
            w_out,
            blend_weight,
        )
    )
    latents_all = exchange_latents(own_frames, latent, own, table)
    _, w_in, tile_order = lax.optimization_barrier((table, w_in, tile_order))
    order = jnp.broadcast_to(tile_order.astype(jnp.float32)[:, None], (tiles, LANES))
    w_in_own = from_ring(w_in, "tm")[:1] or [w_in]

    vmem = pl.BlockSpec(memory_space=pltpu.VMEM)
    piece = (len(cases), 3, own_frames, own)
    kept, sent, denom = pl.pallas_call(
        functools.partial(decode_kernel, tiles, spans, shares),
        out_shape=[
            jax.ShapeDtypeStruct(piece, jnp.float32),
            jax.ShapeDtypeStruct((max(spans - 1, 1),) + piece, jnp.float32),
            jax.ShapeDtypeStruct((8, own), jnp.float32),
        ],
        in_specs=[pl.BlockSpec(memory_space=pl.ANY)] + [vmem] * (2 + spans + shares),
        out_specs=[vmem] * 3,
        scratch_shapes=[
            pltpu.VMEM(((frames + spans) * latent, len(cases) * LANES), jnp.bfloat16),
            pltpu.VMEM((frames, 9, latent, pixels), jnp.bfloat16),
            pltpu.VMEM((frames + 2, pixels, LANES), jnp.bfloat16),
            pltpu.VMEM((pixels, LANES), jnp.bfloat16),
            pltpu.VMEM((frames, pixels, CH), jnp.float32),
            pltpu.VMEM((3 * CH, 9 * lanes), jnp.bfloat16),
            pltpu.VMEM((3, frames, pixels, lanes), jnp.float32),
            pltpu.VMEM((8 * (frames + len(cases)), len(cases) * pixels), jnp.float32),
            pltpu.SemaphoreType.DMA((27 * shares,)),
        ]
        + [pltpu.VMEM((pixels + 2 * TSIDE, CH), jnp.bfloat16)] * frames,
        compiler_params=pltpu.CompilerParams(vmem_limit_bytes=VMEM_BYTES),
        cost_estimate=pl.CostEstimate(
            flops=2 * frames * pixels * 27 * CH * lanes, bytes_accessed=8_000_000, transcendentals=0
        ),
    )(w_mid, table, order, *latents_all, *w_in_own, *w_in_all)
    total = ring_sum(kept, sent, "tm")
    total = ring_sum(total, [total] * (shares - 1), "chan")
    numer = total[0]
    for number, (down, across) in enumerate(cases):
        steps = down * GRID_X + across
        if steps and steps < tiles:
            numer = numer + shifted(total[number], "tile", steps)
    return jnp.transpose(numer / denom[0][None, None, :], (1, 0, 2))


def solution(mesh):
    placed = (
        P("tm", "groups", "tile"),
        P("groups"),
        P(None, None, "chan"),
        P("chan"),
        P("chan"),
        P(None, None, "chan"),
        P("chan"),
        P("chan"),
        P(None, "chan"),
        P("groups", None),
    )
    whole_lanes = (
        CH % (mesh.shape["chan"] * mesh.shape["tm"] * LANES) == 0
        and mesh.shape["chan"] <= mesh.shape["tile"]
    )
    return jax.shard_map(
        lanes_body if whole_lanes else general_body,
        mesh=mesh,
        in_specs=placed,
        out_specs=P("tm", "groups", "tile"),
        check_vma=False,
    )
```

```python
import functools

import jax
import jax.numpy as jnp
from jax import lax
from jax.experimental import pallas as pl
from jax.experimental.pallas import tpu as pltpu
from jax.sharding import PartitionSpec as P

CH = 512
GROUPS = 32
TSIDE = 16
STRIDE = 12
GRID_X = 4

EPSILON = 1e-06
LANES = 128
VMEM_BYTES = 48 * 1024 * 1024


def shifted(value, axis, steps):
    count = lax.axis_size(axis)
    leading, last = (max(0, -steps), min(count, count - steps))
    return lax.ppermute(value, axis, [(source, source + steps) for source in range(leading, last)])


def window_index(tile_id, tiles):
    slots = jnp.arange(TSIDE * TSIDE, dtype=jnp.int32)
    row = tile_id // GRID_X * STRIDE + slots // TSIDE
    col = tile_id % GRID_X * STRIDE + slots % TSIDE
    valid = (row < tiles // GRID_X * STRIDE) & (col < GRID_X * STRIDE)
    block = row // STRIDE * GRID_X + col // STRIDE
    index = block * (STRIDE * STRIDE) + row % STRIDE * STRIDE + col % STRIDE
    return (jnp.where(valid, index, 0), valid)


def causal_conv(extended, weights, frames, side):
    pixels = side * side
    rows = jnp.arange(pixels, dtype=jnp.int32) // side
    cols = jnp.arange(pixels, dtype=jnp.int32) % side
    total = jnp.zeros((frames, weights.shape[2], pixels), jnp.float32)
    for depth in range(3):
        window = extended[depth : depth + frames]
        for down in range(3):
            for across in range(3):
                offset = (down - 1) * side + (across - 1)
                inside = (
                    (rows + down - 1 >= 0)
                    & (rows + down - 1 < side)
                    & (cols + across - 1 >= 0)
                    & (cols + across - 1 < side)
                )
                moved = jnp.roll(window, -offset, axis=2)
                moved = jnp.where(inside[None, None, :], moved, jnp.zeros_like(moved))
                total = total + jnp.einsum(
                    "fcp,co->fop",
                    moved,
                    weights[9 * depth + 3 * down + across],
                    preferred_element_type=jnp.float32,
                )
    return total


def with_history(values):
    frames = values.shape[0]
    earlier = shifted(values[frames - 2 :], "tm", 1)
    return jnp.concatenate([earlier, values], axis=0)


def normalize(values, gain, shift, total_frames):
    frames, chans, pixels = values.shape
    width = CH // GROUPS
    grouped = values.reshape(frames, chans // width, width, pixels)
    sums = jnp.sum(grouped, axis=(0, 2, 3))
    squares = jnp.sum(grouped * grouped, axis=(0, 2, 3))
    sums, squares = lax.psum((sums, squares), "tm")
    count = total_frames * width * pixels
    mean = sums / count
    variance = squares / count - mean * mean
    scale = lax.rsqrt(variance + EPSILON)
    normed = (grouped - mean[None, :, None, None]) * scale[None, :, None, None]
    normed = normed.reshape(frames, chans, pixels) * gain[None, :, None] + shift[None, :, None]
    return jax.nn.silu(normed).astype(jnp.bfloat16)


def spread(color, weight, index, total_pixels):
    numer = (
        jnp.zeros((color.shape[0], 3, total_pixels), jnp.float32)
        .at[:, :, index]
        .add(color * weight[None, None, :])
    )
    denom = jnp.zeros((total_pixels,), jnp.float32).at[index].add(weight)
    return (numer, denom)


def route_owned(numer, denom, tile_id, own):
    frames = numer.shape[0]
    margin = (GRID_X + 1) * own
    numer_wide = jnp.concatenate([numer, jnp.zeros((frames, 3, margin), jnp.float32)], axis=2)
    denom_wide = jnp.concatenate([denom, jnp.zeros((margin,), jnp.float32)], axis=0)
    first_pixel = tile_id * own

    def block_at(offset):
        start_pixel = first_pixel + offset * own
        return (
            lax.dynamic_slice_in_dim(numer_wide, start_pixel, own, 2),
            lax.dynamic_slice_in_dim(denom_wide, start_pixel, own, 0),
        )

    owned_numer, owned_denom = block_at(0)
    for offset in (1, GRID_X, GRID_X + 1):
        piece_numer, piece_denom = block_at(offset)
        got_numer, got_denom = shifted((piece_numer, piece_denom), "tile", offset)
        owned_numer = owned_numer + got_numer
        owned_denom = owned_denom + got_denom
    return (owned_numer, owned_denom)


def general_body(
    latents, tile_order, w_in, gain_in, shift_in, w_mid, gain_mid, shift_mid, w_out, blend_weight
):
    frames = latents.shape[0]
    total_frames = frames * lax.axis_size("tm")
    tiles = tile_order.shape[0]
    own = STRIDE * STRIDE
    total_pixels = tiles * own
    tile_id = lax.axis_index("tile")
    index, valid = window_index(tile_id, tiles)
    whole = lax.all_gather(latents, "tile", axis=2, tiled=True)
    blocks = whole.reshape(frames, whole.shape[1], tiles, own)
    image = (
        jnp.zeros_like(blocks)
        .at[:, :, tile_order]
        .set(blocks)
        .reshape(frames, whole.shape[1], total_pixels)
    )
    window = jnp.where(
        valid[None, None, :], jnp.take(image, index, axis=2), jnp.zeros((), jnp.bfloat16)
    )
    first = causal_conv(with_history(window), w_in, frames, TSIDE)
    hidden = normalize(first, gain_in, shift_in, total_frames)
    second = causal_conv(
        lax.all_gather(with_history(hidden), "chan", axis=1, tiled=True), w_mid, frames, TSIDE
    )
    upper = normalize(second, gain_mid, shift_mid, total_frames)
    color = jnp.einsum("oc,fcp->fop", w_out, upper, preferred_element_type=jnp.float32)
    weight = jnp.where(valid, blend_weight[tile_id], jnp.float32(0.0))
    numer, denom = spread(color, weight, index, total_pixels)
    numer, denom = route_owned(numer, denom, tile_id, own)
    numer = lax.psum(numer, "chan")
    return numer / denom[None, None, :]


def block_cases(tiles):
    downs = (0, 1) if tiles // GRID_X > 1 else (0,)
    return [(down, across) for down in downs for across in (0, 1)]


def exact_dot(values, ones):
    rows = values.shape[0]
    high = values.astype(jnp.bfloat16)
    rest = values - high.astype(jnp.float32)
    middle = rest.astype(jnp.bfloat16)
    low = (rest - middle.astype(jnp.float32)).astype(jnp.bfloat16)
    total = jnp.dot(
        jnp.concatenate([high, middle, low], axis=0), ones, preferred_element_type=jnp.float32
    )
    return total[:rows] + total[rows : 2 * rows] + total[2 * rows :]


def group_affine(sums, squares, gain, shift, count):
    lanes = sums.shape[1]
    width = CH // GROUPS
    same = lax.broadcasted_iota(jnp.int32, (lanes, lanes), 0) // width == (
        lax.broadcasted_iota(jnp.int32, (lanes, lanes), 1) // width
    )
    total = exact_dot(
        jnp.concatenate([sums, squares], axis=0), jnp.where(same, 1.0, 0.0).astype(jnp.bfloat16)
    )
    mean = jnp.sum(total[:8], axis=0, keepdims=True) / count
    variance = jnp.sum(total[8:], axis=0, keepdims=True) / count - mean * mean
    scale = gain * lax.rsqrt(variance + EPSILON)
    return 0.5 * scale, 0.5 * (shift - mean * scale)


def silu_of_half(half):
    return half + half * jnp.tanh(half)


def fold(values):
    rows, lanes = values.shape
    return jnp.sum(values.reshape(rows // 8, 8, lanes), axis=0)


def decode_kernel(
    tiles,
    spans,
    shares,
    *refs,
):
    cases = block_cases(tiles)
    refs = list(refs)

    def take(number):
        taken = refs[:number]
        del refs[:number]
        return taken

    w_mid_ref, table_ref, order_ref = take(3)
    latent_refs, w_in_refs = take(spans), take(shares)
    keep_ref, send_ref, denom_ref = take(3)
    chosen, taps, turned_taps, turned_last, first, weights, partial = take(7)
    shown_ref, picks, sems = take(3)
    hidden = take(first.shape[0])

    own = denom_ref.shape[1]
    own_frames = keep_ref.shape[2]
    frames = own_frames * spans
    latent, wide = w_in_refs[0].shape[1:]
    rows_in = frames * latent
    rows_own = rows_in // spans
    depth_in = 27 * latent
    pixels = TSIDE * TSIDE
    lanes = partial.shape[3]
    tile_id = lax.axis_index("tile")
    mine = lax.axis_index("tm")
    chan_id = lax.axis_index("chan")

    half = pl.ds(pl.multiple_of(mine * lanes, LANES), lanes)
    copies = []
    for a in range(3):
        for b in range(3):
            for e in range(3):
                for share in range(shares):
                    tap = 9 * a + 3 * b + e
                    held = pl.multiple_of((chan_id + share) % shares * wide, LANES)
                    copy = pltpu.make_async_copy(
                        w_mid_ref.at[tap, pl.ds(held, wide), half],
                        weights.at[
                            pl.ds(b * CH + share * wide, wide), pl.ds((3 * a + e) * lanes, lanes)
                        ],
                        sems.at[tap * shares + share],
                    )
                    copy.start()
                    copies.append(copy)

    tile_row, tile_col = tile_id // GRID_X, tile_id % GRID_X
    gain_row = rows_own + 2
    w_out_row = gain_row + 2
    blend_row = w_out_row + 3
    order = order_ref[...]
    number_of = lax.broadcasted_iota(jnp.int32, order.shape, 0)
    lane_of = lax.broadcasted_iota(jnp.int32, order.shape, 1)
    rows_all = latent_refs[0].shape[0] // tiles
    turns = []
    for down, across in cases:
        wanted = tile_id + down * GRID_X + across
        found = (order == wanted.astype(jnp.float32)) & (lane_of == 0)
        place = jnp.sum(jnp.where(found, number_of.astype(jnp.float32), 0.0))
        turns.append((tile_id - place.astype(jnp.int32) + tiles) % tiles)
    for number, (down, across) in enumerate(cases):
        inside = (tile_row + down < tiles // GRID_X) & (tile_col + across < GRID_X)
        turn = turns[number]
        part = slice(number * LANES, (number + 1) * LANES)
        for steps in range(tiles):

            @pl.when(inside & (turn == steps))
            def _():
                for swap in range(spans):
                    at, tail_at = swap * rows_own, rows_in + swap * latent
                    block = latent_refs[swap][steps * rows_all : (steps + 1) * rows_all]
                    chosen[at : at + rows_own, part] = block[:rows_own]
                    chosen[tail_at : tail_at + latent, part] = block[rows_own : rows_own + latent]

        @pl.when(jnp.logical_not(inside))
        def _():
            chosen[:, part] = jnp.zeros((chosen.shape[0], LANES), chosen.dtype)

    slot = lax.broadcasted_iota(jnp.int32, (1, pixels), 1)
    up, along = slot // TSIDE, slot % TSIDE
    source = lax.broadcasted_iota(jnp.int32, (LANES, pixels), 0)
    tail = own - LANES

    def pick(first_pixel):
        parts = []
        for down, across in cases:
            u, v = up - down * STRIDE, along - across * STRIDE
            good = (u >= 0) & (u < STRIDE) & (v >= 0) & (v < STRIDE)
            wanted = jnp.where(good, u * STRIDE + v - first_pixel, -1)
            parts.append(jnp.where(source == wanted, 1.0, 0.0).astype(jnp.bfloat16))
        return jnp.concatenate(parts, axis=0)

    tails = chosen[rows_in:].astype(jnp.float32)
    width = tails.shape[1]
    turned = [pltpu.roll(tails, (-f * tail) % width, 1) if f else tails for f in range(own_frames)]
    tails = jnp.concatenate(
        [
            turned[f][swap * latent : (swap + 1) * latent]
            for swap in range(spans)
            for f in range(own_frames)
        ],
        axis=0,
    ).astype(jnp.bfloat16)
    in_tail = lax.broadcasted_iota(jnp.int32, tails.shape, 1) % LANES < tail
    tails = jnp.where(in_tail, tails.astype(jnp.float32), 0.0).astype(jnp.bfloat16)
    window = jnp.dot(
        chosen[:rows_in], pick(0), preferred_element_type=jnp.float32
    ) + jnp.dot(tails, pick(LANES), preferred_element_type=jnp.float32)
    for b in range(3):
        for e in range(3):
            inside = (
                (up + b - 1 >= 0)
                & (up + b - 1 < TSIDE)
                & (along + e - 1 >= 0)
                & (along + e - 1 < TSIDE)
            )
            offset = (b - 1) * TSIDE + e - 1
            moved = pltpu.roll(window, (-offset) % pixels, 1) if offset else window
            moved = jnp.where(inside, moved, 0.0).astype(jnp.bfloat16)
            for swap in range(spans):
                value = moved[swap * rows_own : (swap + 1) * rows_own]
                span = pl.ds((mine + swap) % spans * own_frames, own_frames)
                taps[span, 3 * b + e] = value.reshape(own_frames, latent, pixels)

    turned_taps[0:2] = jnp.zeros((2, pixels, LANES), turned_taps.dtype)
    for f in range(frames):
        turned_taps[f + 2] = taps[f, 0:8].reshape(8 * latent, pixels).T
    turned_last[...] = taps[:, 8].reshape(frames * latent, pixels).T
    joined = jnp.concatenate([w_in_refs[s][...] for s in range(shares)], axis=2)
    main_rows = [joined[9 * a : 9 * a + 8].reshape(8 * latent, CH) for a in range(3)]
    sums = jnp.zeros((8, CH), jnp.float32)
    squares = jnp.zeros((8, CH), jnp.float32)
    nothing = jnp.zeros((latent, CH), jnp.bfloat16)
    for f in range(frames):
        patch = [turned_taps[f + a] for a in range(3)] + [turned_last[...]]
        last_rows = [
            joined[9 * (g - f + 2) + 8] if 0 <= g - f + 2 < 3 else nothing for g in range(frames)
        ]
        value = jnp.dot(
            jnp.concatenate(patch, axis=1),
            jnp.concatenate(main_rows + last_rows, axis=0),
            preferred_element_type=jnp.float32,
        )
        first[f] = value
        sums = sums + fold(value)
        squares = squares + fold(value * value)
    count = frames * (CH // GROUPS) * pixels
    affine = []
    for s in range(shares):
        at = s * rows_all + rows_own + latent
        table = latent_refs[0][at : at + wide // LANES * 4].astype(jnp.float32)
        pieces = [table[4 * lane : 4 * lane + 4] for lane in range(wide // LANES)]
        table = jnp.concatenate([part[0:2] + part[2:4] for part in pieces], axis=1)
        part = slice(s * wide, (s + 1) * wide)
        affine.append(
            group_affine(sums[:, part], squares[:, part], table[0:1], table[1:2], count)
        )
    def hide(f):
        edge = jnp.zeros((TSIDE, CH), jnp.bfloat16)
        hidden[f][0:TSIDE] = edge
        hidden[f][TSIDE + pixels : 2 * TSIDE + pixels] = edge
        for s in range(shares):
            scale, bias = affine[s]
            part = slice(s * wide, (s + 1) * wide)
            value = first[f, :, part] * scale + bias
            hidden[f][TSIDE : TSIDE + pixels, part] = silu_of_half(value).astype(jnp.bfloat16)

    def convolve(start, several, depth_taps):
        lhs = jnp.concatenate(
            [
                jnp.concatenate(
                    [
                        hidden[start + f][b * TSIDE : b * TSIDE + pixels]
                        for f in range(several)
                    ],
                    axis=0,
                )
                for b in range(3)
            ],
            axis=1,
        )
        low = depth_taps[0] * 3 * lanes
        odd = len(depth_taps) % 2
        product = jnp.dot(
            lhs, weights[:, low : (9 - odd) * lanes], preferred_element_type=jnp.float32
        )
        if odd:
            rows = jnp.concatenate(
                [weights[b * CH : (b + 1) * CH, 8 * lanes :] for b in range(3)], axis=1
            )
            apart = jnp.dot(lhs[:, CH : 2 * CH], rows, preferred_element_type=jnp.float32)
        edge = jnp.zeros((TSIDE, lanes), jnp.float32)
        for a in depth_taps:
            for e in range(3):
                at = (3 * a + e) * lanes - low
                for f in range(several):
                    target = start + f + 2 - a
                    if odd and (a, e) == (2, 2):
                        value = apart[f * pixels : (f + 1) * pixels]
                        above = value[: pixels - TSIDE, :lanes]
                        below = value[TSIDE:, 2 * lanes :]
                        value = (
                            value[:, lanes : 2 * lanes]
                            + jnp.concatenate([edge, above], axis=0)
                            + jnp.concatenate([below, edge], axis=0)
                        )
                    else:
                        value = product[f * pixels : (f + 1) * pixels, at : at + lanes]
                    if start + f == max(target - 2, 0):
                        partial[e, target] = value
                    else:
                        partial[e, target] += value

    column = lax.broadcasted_iota(jnp.int32, (pixels, lanes), 0) % TSIDE
    total = [jnp.zeros((8, lanes), jnp.float32)] * 2

    def gather(f):
        left = jnp.where(column == 0, 0.0, pltpu.roll(partial[0, f], 1, 0))
        right = jnp.where(column == TSIDE - 1, 0.0, pltpu.roll(partial[2, f], pixels - 1, 0))
        value = partial[1, f] + left + right
        partial[1, f] = value
        total[0] = total[0] + fold(value)
        total[1] = total[1] + fold(value * value)

    bounds = [0, 2, frames - 2, frames - 1, frames]
    groups = [range(low, high) for low, high in zip(bounds, bounds[1:]) if high > low]
    for copy in copies:
        copy.wait()
    for f in groups[0]:
        hide(f)
    slot_in = lax.broadcasted_iota(jnp.int32, (pixels, 1), 0)
    pixel = lax.broadcasted_iota(jnp.int32, (pixels, pixels), 1)
    for number, (down, across) in enumerate(cases):
        u, v = slot_in // TSIDE - down * STRIDE, slot_in % TSIDE - across * STRIDE
        good = (u >= 0) & (u < STRIDE) & (v >= 0) & (v < STRIDE)
        wanted = jnp.where(good, u * STRIDE + v, -1)
        picks[:, number * pixels : (number + 1) * pixels] = jnp.where(
            wanted == pixel, 1.0, 0.0
        ).astype(jnp.bfloat16)
    for number, group in enumerate(groups):
        if number + 1 < len(groups):
            for f in groups[number + 1]:
                hide(f)
        convolve(
            group.start,
            len(group),
            tuple(a for a in range(3) if group.stop - 1 + 2 - a < frames),
        )
        if number:
            for f in groups[number - 1]:
                gather(f)
    for f in groups[-1]:
        gather(f)

    part = pl.ds(pl.multiple_of(mine * lanes, LANES), lanes)
    scale, bias = group_affine(
        total[0],
        total[1],
        table_ref[gain_row : gain_row + 1, part],
        table_ref[gain_row + 1 : gain_row + 2, part],
        count,
    )
    blend = table_ref[pl.ds(blend_row + tile_id, 1), :]
    blend = jnp.where(
        (tile_row * STRIDE + up < tiles // GRID_X * STRIDE)
        & (tile_col * STRIDE + along < GRID_X * STRIDE),
        blend,
        0.0,
    )
    w_out = jnp.concatenate(
        [table_ref[w_out_row : w_out_row + 3, part], jnp.zeros((5, lanes), jnp.float32)], axis=0
    ).astype(jnp.bfloat16)
    colors = []
    for f in range(frames):
        upper = silu_of_half(partial[1, f] * scale + bias).astype(jnp.bfloat16)
        color = lax.dot_general(
            w_out, upper, (((1,), (1,)), ((), ())), preferred_element_type=jnp.float32
        )
        colors.append(color * blend)
    colors = jnp.concatenate(colors, axis=0)

    weight_rows = []
    for down, across in cases:
        inside = (tile_row >= down) & (tile_col >= across)
        other = jnp.maximum(tile_id - down * GRID_X - across, 0)
        weight = jnp.where(inside, table_ref[pl.ds(blend_row + other, 1), :], 0.0)
        weight_rows.append(jnp.broadcast_to(weight, (8, pixels)))
    shown_ref[...] = exact_dot(
        jnp.concatenate([colors] + weight_rows, axis=0), picks[...]
    )
    denom = jnp.zeros((8, own), jnp.float32)
    for number in range(len(cases)):
        lane = slice(number * pixels, number * pixels + own)
        row = 8 * (frames + number)
        denom = denom + shown_ref[row : row + 8, lane]
        for swap in range(spans):
            target = keep_ref if swap == 0 else send_ref.at[swap - 1]
            base = (mine + swap) % spans * own_frames * 8
            for at in range(own_frames):
                for o in range(3):
                    target[number, o, at : at + 1, :] = shown_ref[
                        pl.ds(base + 8 * at + o, 1), lane
                    ]
    denom_ref[...] = denom


def from_ring(value, axis):
    count = lax.axis_size(axis)
    return [
        lax.ppermute(value, axis, [((d + turn) % count, d) for d in range(count)])
        for turn in range(1, count)
    ]


def ring_sum(kept, sent, axis):
    count = lax.axis_size(axis)
    for turn in range(1, count):
        kept = kept + lax.ppermute(
            sent[turn - 1], axis, [(d, (d + turn) % count) for d in range(count)]
        )
    return kept


def small_table(*values):
    values = [value.reshape(-1, value.shape[-1]) for value in values]
    wide = max(value.shape[1] for value in values)
    height = sum(value.shape[0] for value in values)
    total, row = 0.0, 0
    for value in values:
        below = height - row - value.shape[0]
        value = jnp.pad(value.astype(jnp.float32), ((row, below), (0, wide - value.shape[1])))
        total = total + value
        row = height - below
    return total


def exchange_latents(frames, latent, own, table):
    tiles, shares = lax.axis_size("tile"), lax.axis_size("chan")
    tail = own - LANES
    height = frames * latent
    mine = table[:height, :own].astype(jnp.bfloat16)
    tails = sum(
        jnp.pad(
            mine[f * latent : (f + 1) * latent, LANES:],
            ((0, 0), (tail * f, LANES - tail * (f + 1))),
        )
        for f in range(frames)
    )
    affine = table[height : height + 2]
    high = lax.reduce_precision(affine, 8, 7)
    low = lax.reduce_precision(affine - high, 8, 7)
    affine = jnp.concatenate([high, low], axis=0).astype(jnp.bfloat16)
    rows = [affine[:, at : at + LANES] for at in range(0, affine.shape[1], LANES)]
    rows = jnp.concatenate(rows, axis=0)
    rows = jnp.pad(rows, ((0, -rows.shape[0] % 16), (0, 0)))
    message = jnp.concatenate([mine[:, :LANES], tails, rows], axis=0)
    got = [message]
    for steps in range(1, tiles):
        turn = steps if steps < shares else 0
        pairs = [
            (t * shares + (c + turn) % shares, (t + steps) % tiles * shares + c)
            for t in range(tiles)
            for c in range(shares)
        ]
        got.append(lax.ppermute(message, ("tile", "chan"), pairs))
    stack = jnp.concatenate(got, axis=0)
    return [stack] + from_ring(stack, "tm")


def lanes_body(
    latents, tile_order, w_in, gain_in, shift_in, w_mid, gain_mid, shift_mid, w_out, blend_weight
):
    own_frames, latent, own = latents.shape
    spans = lax.axis_size("tm")
    shares = lax.axis_size("chan")
    frames = own_frames * spans
    if 8 * latent != LANES or frames * latent != LANES:
        return general_body(
            latents,
            tile_order,
            w_in,
            gain_in,
            shift_in,
            w_mid,
            gain_mid,
            shift_mid,
            w_out,
            blend_weight,
        )
    tiles = tile_order.shape[0]
    wide = w_in.shape[2]
    lanes = wide // spans
    pixels = TSIDE * TSIDE
    cases = block_cases(tiles)

    w_in_all = [(from_ring(other, "tm") or [other])[0] for other in from_ring(w_in, "chan")]
    table = lax.optimization_barrier(
        small_table(
            latents.reshape(own_frames * latent, own),
            gain_in,
            shift_in,
            gain_mid,
            shift_mid,
            w_out,
            blend_weight,
        )
    )
    latents_all = exchange_latents(own_frames, latent, own, table)
    _, w_in, tile_order = lax.optimization_barrier((table, w_in, tile_order))
    order = jnp.broadcast_to(tile_order.astype(jnp.float32)[:, None], (tiles, LANES))
    w_in_own = from_ring(w_in, "tm")[:1] or [w_in]

    vmem = pl.BlockSpec(memory_space=pltpu.VMEM)
    piece = (len(cases), 3, own_frames, own)
    kept, sent, denom = pl.pallas_call(
        functools.partial(decode_kernel, tiles, spans, shares),
        out_shape=[
            jax.ShapeDtypeStruct(piece, jnp.float32),
            jax.ShapeDtypeStruct((max(spans - 1, 1),) + piece, jnp.float32),
            jax.ShapeDtypeStruct((8, own), jnp.float32),
        ],
        in_specs=[pl.BlockSpec(memory_space=pl.ANY)] + [vmem] * (2 + spans + shares),
        out_specs=[vmem] * 3,
        scratch_shapes=[
            pltpu.VMEM(((frames + spans) * latent, len(cases) * LANES), jnp.bfloat16),
            pltpu.VMEM((frames, 9, latent, pixels), jnp.bfloat16),
            pltpu.VMEM((frames + 2, pixels, LANES), jnp.bfloat16),
            pltpu.VMEM((pixels, LANES), jnp.bfloat16),
            pltpu.VMEM((frames, pixels, CH), jnp.float32),
            pltpu.VMEM((3 * CH, 9 * lanes), jnp.bfloat16),
            pltpu.VMEM((3, frames, pixels, lanes), jnp.float32),
            pltpu.VMEM((8 * (frames + len(cases)), len(cases) * pixels), jnp.float32),
            pltpu.VMEM((pixels, len(cases) * pixels), jnp.bfloat16),
            pltpu.SemaphoreType.DMA((27 * shares,)),
        ]
        + [pltpu.VMEM((pixels + 2 * TSIDE, CH), jnp.bfloat16)] * frames,
        compiler_params=pltpu.CompilerParams(vmem_limit_bytes=VMEM_BYTES),
        cost_estimate=pl.CostEstimate(
            flops=2 * frames * pixels * 27 * CH * lanes, bytes_accessed=8_000_000, transcendentals=0
        ),
    )(w_mid, table, order, *latents_all, *w_in_own, *w_in_all)
    total = ring_sum(kept, sent, "tm")
    total = ring_sum(total, [total] * (shares - 1), "chan")
    numer = total[0]
    for number, (down, across) in enumerate(cases):
        steps = down * GRID_X + across
        if steps and steps < tiles:
            numer = numer + shifted(total[number], "tile", steps)
    return jnp.transpose(numer / denom[0][None, None, :], (1, 0, 2))


def solution(mesh):
    placed = (
        P("tm", "groups", "tile"),
        P("groups"),
        P(None, None, "chan"),
        P("chan"),
        P("chan"),
        P(None, None, "chan"),
        P("chan"),
        P("chan"),
        P(None, "chan"),
        P("groups", None),
    )
    whole_lanes = (
        CH % (mesh.shape["chan"] * mesh.shape["tm"] * LANES) == 0
        and mesh.shape["chan"] <= mesh.shape["tile"]
    )
    return jax.shard_map(
        lanes_body if whole_lanes else general_body,
        mesh=mesh,
        in_specs=placed,
        out_specs=P("tm", "groups", "tile"),
        check_vma=False,
    )
```

```python
import functools

import jax
import jax.numpy as jnp
from jax import lax
from jax.experimental import pallas as pl
from jax.experimental.pallas import tpu as pltpu
from jax.sharding import PartitionSpec as P

CH = 512
GROUPS = 32
TSIDE = 16
STRIDE = 12
GRID_X = 4

EPSILON = 1e-06
LANES = 128
VMEM_BYTES = 48 * 1024 * 1024


def shifted(value, axis, steps):
    count = lax.axis_size(axis)
    leading, last = (max(0, -steps), min(count, count - steps))
    return lax.ppermute(value, axis, [(source, source + steps) for source in range(leading, last)])


def window_index(tile_id, tiles):
    slots = jnp.arange(TSIDE * TSIDE, dtype=jnp.int32)
    row = tile_id // GRID_X * STRIDE + slots // TSIDE
    col = tile_id % GRID_X * STRIDE + slots % TSIDE
    valid = (row < tiles // GRID_X * STRIDE) & (col < GRID_X * STRIDE)
    block = row // STRIDE * GRID_X + col // STRIDE
    index = block * (STRIDE * STRIDE) + row % STRIDE * STRIDE + col % STRIDE
    return (jnp.where(valid, index, 0), valid)


def causal_conv(extended, weights, frames, side):
    pixels = side * side
    rows = jnp.arange(pixels, dtype=jnp.int32) // side
    cols = jnp.arange(pixels, dtype=jnp.int32) % side
    total = jnp.zeros((frames, weights.shape[2], pixels), jnp.float32)
    for depth in range(3):
        window = extended[depth : depth + frames]
        for down in range(3):
            for across in range(3):
                offset = (down - 1) * side + (across - 1)
                inside = (
                    (rows + down - 1 >= 0)
                    & (rows + down - 1 < side)
                    & (cols + across - 1 >= 0)
                    & (cols + across - 1 < side)
                )
                moved = jnp.roll(window, -offset, axis=2)
                moved = jnp.where(inside[None, None, :], moved, jnp.zeros_like(moved))
                total = total + jnp.einsum(
                    "fcp,co->fop",
                    moved,
                    weights[9 * depth + 3 * down + across],
                    preferred_element_type=jnp.float32,
                )
    return total


def with_history(values):
    frames = values.shape[0]
    earlier = shifted(values[frames - 2 :], "tm", 1)
    return jnp.concatenate([earlier, values], axis=0)


def normalize(values, gain, shift, total_frames):
    frames, chans, pixels = values.shape
    width = CH // GROUPS
    grouped = values.reshape(frames, chans // width, width, pixels)
    sums = jnp.sum(grouped, axis=(0, 2, 3))
    squares = jnp.sum(grouped * grouped, axis=(0, 2, 3))
    sums, squares = lax.psum((sums, squares), "tm")
    count = total_frames * width * pixels
    mean = sums / count
    variance = squares / count - mean * mean
    scale = lax.rsqrt(variance + EPSILON)
    normed = (grouped - mean[None, :, None, None]) * scale[None, :, None, None]
    normed = normed.reshape(frames, chans, pixels) * gain[None, :, None] + shift[None, :, None]
    return jax.nn.silu(normed).astype(jnp.bfloat16)


def spread(color, weight, index, total_pixels):
    numer = (
        jnp.zeros((color.shape[0], 3, total_pixels), jnp.float32)
        .at[:, :, index]
        .add(color * weight[None, None, :])
    )
    denom = jnp.zeros((total_pixels,), jnp.float32).at[index].add(weight)
    return (numer, denom)


def route_owned(numer, denom, tile_id, own):
    frames = numer.shape[0]
    margin = (GRID_X + 1) * own
    numer_wide = jnp.concatenate([numer, jnp.zeros((frames, 3, margin), jnp.float32)], axis=2)
    denom_wide = jnp.concatenate([denom, jnp.zeros((margin,), jnp.float32)], axis=0)
    first_pixel = tile_id * own

    def block_at(offset):
        start_pixel = first_pixel + offset * own
        return (
            lax.dynamic_slice_in_dim(numer_wide, start_pixel, own, 2),
            lax.dynamic_slice_in_dim(denom_wide, start_pixel, own, 0),
        )

    owned_numer, owned_denom = block_at(0)
    for offset in (1, GRID_X, GRID_X + 1):
        piece_numer, piece_denom = block_at(offset)
        got_numer, got_denom = shifted((piece_numer, piece_denom), "tile", offset)
        owned_numer = owned_numer + got_numer
        owned_denom = owned_denom + got_denom
    return (owned_numer, owned_denom)


def general_body(
    latents, tile_order, w_in, gain_in, shift_in, w_mid, gain_mid, shift_mid, w_out, blend_weight
):
    frames = latents.shape[0]
    total_frames = frames * lax.axis_size("tm")
    tiles = tile_order.shape[0]
    own = STRIDE * STRIDE
    total_pixels = tiles * own
    tile_id = lax.axis_index("tile")
    index, valid = window_index(tile_id, tiles)
    whole = lax.all_gather(latents, "tile", axis=2, tiled=True)
    blocks = whole.reshape(frames, whole.shape[1], tiles, own)
    image = (
        jnp.zeros_like(blocks)
        .at[:, :, tile_order]
        .set(blocks)
        .reshape(frames, whole.shape[1], total_pixels)
    )
    window = jnp.where(
        valid[None, None, :], jnp.take(image, index, axis=2), jnp.zeros((), jnp.bfloat16)
    )
    first = causal_conv(with_history(window), w_in, frames, TSIDE)
    hidden = normalize(first, gain_in, shift_in, total_frames)
    second = causal_conv(
        lax.all_gather(with_history(hidden), "chan", axis=1, tiled=True), w_mid, frames, TSIDE
    )
    upper = normalize(second, gain_mid, shift_mid, total_frames)
    color = jnp.einsum("oc,fcp->fop", w_out, upper, preferred_element_type=jnp.float32)
    weight = jnp.where(valid, blend_weight[tile_id], jnp.float32(0.0))
    numer, denom = spread(color, weight, index, total_pixels)
    numer, denom = route_owned(numer, denom, tile_id, own)
    numer = lax.psum(numer, "chan")
    return numer / denom[None, None, :]


def block_cases(tiles):
    downs = (0, 1) if tiles // GRID_X > 1 else (0,)
    return [(down, across) for down in downs for across in (0, 1)]


def exact_dot(values, ones):
    rows = values.shape[0]
    high = values.astype(jnp.bfloat16)
    rest = values - high.astype(jnp.float32)
    middle = rest.astype(jnp.bfloat16)
    low = (rest - middle.astype(jnp.float32)).astype(jnp.bfloat16)
    total = jnp.dot(
        jnp.concatenate([high, middle, low], axis=0), ones, preferred_element_type=jnp.float32
    )
    return total[:rows] + total[rows : 2 * rows] + total[2 * rows :]


def group_affine(sums, squares, gain, shift, count):
    lanes = sums.shape[1]
    width = CH // GROUPS
    same = lax.broadcasted_iota(jnp.int32, (lanes, lanes), 0) // width == (
        lax.broadcasted_iota(jnp.int32, (lanes, lanes), 1) // width
    )
    total = exact_dot(
        jnp.concatenate([sums, squares], axis=0), jnp.where(same, 1.0, 0.0).astype(jnp.bfloat16)
    )
    mean = jnp.sum(total[:8], axis=0, keepdims=True) / count
    variance = jnp.sum(total[8:], axis=0, keepdims=True) / count - mean * mean
    scale = gain * lax.rsqrt(variance + EPSILON)
    return 0.5 * scale, 0.5 * (shift - mean * scale)


def silu_of_half(half):
    return half + half * jnp.tanh(half)


def fold(values):
    rows, lanes = values.shape
    return jnp.sum(values.reshape(rows // 8, 8, lanes), axis=0)


def decode_kernel(
    tiles,
    spans,
    shares,
    *refs,
):
    cases = block_cases(tiles)
    refs = list(refs)

    def take(number):
        taken = refs[:number]
        del refs[:number]
        return taken

    w_mid_ref, table_ref, order_ref = take(3)
    latent_refs, w_in_refs = take(spans), take(shares)
    keep_ref, send_ref, denom_ref = take(3)
    chosen, taps, turned_taps, turned_last, first, weights = take(6)
    shown_ref, sems = take(2)
    hidden = take(first.shape[0])
    partial = take(first.shape[0])

    own = denom_ref.shape[1]
    own_frames = keep_ref.shape[2]
    frames = own_frames * spans
    latent, wide = w_in_refs[0].shape[1:]
    rows_in = frames * latent
    rows_own = rows_in // spans
    depth_in = 27 * latent
    pixels = TSIDE * TSIDE
    lanes = partial[0].shape[2]
    tile_id = lax.axis_index("tile")
    mine = lax.axis_index("tm")
    chan_id = lax.axis_index("chan")

    half = pl.ds(pl.multiple_of(mine * lanes, LANES), lanes)
    copies = []
    for a in range(3):
        for b in range(3):
            for e in range(3):
                for share in range(shares):
                    tap = 9 * a + 3 * b + e
                    held = pl.multiple_of((chan_id + share) % shares * wide, LANES)
                    copy = pltpu.make_async_copy(
                        w_mid_ref.at[tap, pl.ds(held, wide), half],
                        weights.at[
                            pl.ds(b * CH + share * wide, wide), pl.ds((3 * a + e) * lanes, lanes)
                        ],
                        sems.at[tap * shares + share],
                    )
                    copy.start()
                    copies.append(copy)

    tile_row, tile_col = tile_id // GRID_X, tile_id % GRID_X
    gain_row = rows_own + 2
    w_out_row = gain_row + 2
    blend_row = w_out_row + 3
    order = order_ref[...]
    number_of = lax.broadcasted_iota(jnp.int32, order.shape, 0)
    lane_of = lax.broadcasted_iota(jnp.int32, order.shape, 1)
    rows_all = latent_refs[0].shape[0] // tiles
    turns = []
    for down, across in cases:
        wanted = tile_id + down * GRID_X + across
        found = (order == wanted.astype(jnp.float32)) & (lane_of == 0)
        place = jnp.sum(jnp.where(found, number_of.astype(jnp.float32), 0.0))
        turns.append((tile_id - place.astype(jnp.int32) + tiles) % tiles)
    for number, (down, across) in enumerate(cases):
        inside = (tile_row + down < tiles // GRID_X) & (tile_col + across < GRID_X)
        turn = turns[number]
        part = slice(number * LANES, (number + 1) * LANES)
        for steps in range(tiles):

            @pl.when(inside & (turn == steps))
            def _():
                for swap in range(spans):
                    at, tail_at = swap * rows_own, rows_in + swap * latent
                    block = latent_refs[swap][steps * rows_all : (steps + 1) * rows_all]
                    chosen[at : at + rows_own, part] = block[:rows_own]
                    chosen[tail_at : tail_at + latent, part] = block[rows_own : rows_own + latent]

        @pl.when(jnp.logical_not(inside))
        def _():
            chosen[:, part] = jnp.zeros((chosen.shape[0], LANES), chosen.dtype)

    slot = lax.broadcasted_iota(jnp.int32, (1, pixels), 1)
    up, along = slot // TSIDE, slot % TSIDE
    source = lax.broadcasted_iota(jnp.int32, (LANES, pixels), 0)
    tail = own - LANES

    def pick(first_pixel):
        parts = []
        for down, across in cases:
            u, v = up - down * STRIDE, along - across * STRIDE
            good = (u >= 0) & (u < STRIDE) & (v >= 0) & (v < STRIDE)
            wanted = jnp.where(good, u * STRIDE + v - first_pixel, -1)
            parts.append(jnp.where(source == wanted, 1.0, 0.0).astype(jnp.bfloat16))
        return jnp.concatenate(parts, axis=0)

    tails = chosen[rows_in:].astype(jnp.float32)
    width = tails.shape[1]
    turned = [pltpu.roll(tails, (-f * tail) % width, 1) if f else tails for f in range(own_frames)]
    tails = jnp.concatenate(
        [
            turned[f][swap * latent : (swap + 1) * latent]
            for swap in range(spans)
            for f in range(own_frames)
        ],
        axis=0,
    ).astype(jnp.bfloat16)
    in_tail = lax.broadcasted_iota(jnp.int32, tails.shape, 1) % LANES < tail
    tails = jnp.where(in_tail, tails.astype(jnp.float32), 0.0).astype(jnp.bfloat16)
    window = jnp.dot(
        chosen[:rows_in], pick(0), preferred_element_type=jnp.float32
    ) + jnp.dot(tails, pick(LANES), preferred_element_type=jnp.float32)
    for b in range(3):
        for e in range(3):
            inside = (
                (up + b - 1 >= 0)
                & (up + b - 1 < TSIDE)
                & (along + e - 1 >= 0)
                & (along + e - 1 < TSIDE)
            )
            offset = (b - 1) * TSIDE + e - 1
            moved = pltpu.roll(window, (-offset) % pixels, 1) if offset else window
            moved = jnp.where(inside, moved, 0.0).astype(jnp.bfloat16)
            for swap in range(spans):
                value = moved[swap * rows_own : (swap + 1) * rows_own]
                span = pl.ds((mine + swap) % spans * own_frames, own_frames)
                taps[span, 3 * b + e] = value.reshape(own_frames, latent, pixels)

    turned_taps[0:2] = jnp.zeros((2, pixels, LANES), turned_taps.dtype)
    for f in range(frames):
        turned_taps[f + 2] = taps[f, 0:8].reshape(8 * latent, pixels).T
    turned_last[...] = taps[:, 8].reshape(frames * latent, pixels).T
    joined = jnp.concatenate([w_in_refs[s][...] for s in range(shares)], axis=2)
    main_rows = [joined[9 * a : 9 * a + 8].reshape(8 * latent, CH) for a in range(3)]
    sums = jnp.zeros((8, CH), jnp.float32)
    squares = jnp.zeros((8, CH), jnp.float32)
    nothing = jnp.zeros((latent, CH), jnp.bfloat16)
    for f in range(frames):
        patch = [turned_taps[f + a] for a in range(3)] + [turned_last[...]]
        last_rows = [
            joined[9 * (g - f + 2) + 8] if 0 <= g - f + 2 < 3 else nothing for g in range(frames)
        ]
        value = jnp.dot(
            jnp.concatenate(patch, axis=1),
            jnp.concatenate(main_rows + last_rows, axis=0),
            preferred_element_type=jnp.float32,
        )
        first[f] = value
        sums = sums + fold(value)
        squares = squares + fold(value * value)
    count = frames * (CH // GROUPS) * pixels
    affine = []
    for s in range(shares):
        at = s * rows_all + rows_own + latent
        table = latent_refs[0][at : at + wide // LANES * 4].astype(jnp.float32)
        pieces = [table[4 * lane : 4 * lane + 4] for lane in range(wide // LANES)]
        table = jnp.concatenate([part[0:2] + part[2:4] for part in pieces], axis=1)
        part = slice(s * wide, (s + 1) * wide)
        affine.append(
            group_affine(sums[:, part], squares[:, part], table[0:1], table[1:2], count)
        )
    def hide(f):
        edge = jnp.zeros((TSIDE, CH), jnp.bfloat16)
        hidden[f][0:TSIDE] = edge
        hidden[f][TSIDE + pixels : 2 * TSIDE + pixels] = edge
        for s in range(shares):
            scale, bias = affine[s]
            part = slice(s * wide, (s + 1) * wide)
            value = first[f, :, part] * scale + bias
            hidden[f][TSIDE : TSIDE + pixels, part] = silu_of_half(value).astype(jnp.bfloat16)

    def convolve(start, several, depth_taps):
        lhs = jnp.concatenate(
            [
                jnp.concatenate(
                    [
                        hidden[start + f][b * TSIDE : b * TSIDE + pixels]
                        for f in range(several)
                    ],
                    axis=0,
                )
                for b in range(3)
            ],
            axis=1,
        )
        low = depth_taps[0] * 3 * lanes
        odd = len(depth_taps) % 2
        product = jnp.dot(
            lhs, weights[:, low : (9 - odd) * lanes], preferred_element_type=jnp.float32
        )
        if odd:
            rows = jnp.concatenate(
                [weights[b * CH : (b + 1) * CH, 8 * lanes :] for b in range(3)], axis=1
            )
            apart = jnp.dot(lhs[:, CH : 2 * CH], rows, preferred_element_type=jnp.float32)
        edge = jnp.zeros((TSIDE, lanes), jnp.float32)
        for a in depth_taps:
            for e in range(3):
                at = (3 * a + e) * lanes - low
                for f in range(several):
                    target = start + f + 2 - a
                    if odd and (a, e) == (2, 2):
                        value = apart[f * pixels : (f + 1) * pixels]
                        above = value[: pixels - TSIDE, :lanes]
                        below = value[TSIDE:, 2 * lanes :]
                        value = (
                            value[:, lanes : 2 * lanes]
                            + jnp.concatenate([edge, above], axis=0)
                            + jnp.concatenate([below, edge], axis=0)
                        )
                    else:
                        value = product[f * pixels : (f + 1) * pixels, at : at + lanes]
                    if start + f == max(target - 2, 0):
                        partial[target][e] = value
                    else:
                        partial[target][e] += value

    column = lax.broadcasted_iota(jnp.int32, (pixels, lanes), 0) % TSIDE
    total = [jnp.zeros((8, lanes), jnp.float32)] * 2

    def gather(f):
        left = jnp.where(column == 0, 0.0, pltpu.roll(partial[f][0], 1, 0))
        right = jnp.where(column == TSIDE - 1, 0.0, pltpu.roll(partial[f][2], pixels - 1, 0))
        value = partial[f][1] + left + right
        partial[f][1] = value
        total[0] = total[0] + fold(value)
        total[1] = total[1] + fold(value * value)

    bounds = [0, 2, frames - 2, frames - 1, frames]
    groups = [range(low, high) for low, high in zip(bounds, bounds[1:]) if high > low]
    for copy in copies:
        copy.wait()
    for f in groups[0]:
        hide(f)
    for number, group in enumerate(groups):
        if number + 1 < len(groups):
            for f in groups[number + 1]:
                hide(f)
        convolve(
            group.start,
            len(group),
            tuple(a for a in range(3) if group.stop - 1 + 2 - a < frames),
        )
        if number:
            for f in groups[number - 1]:
                gather(f)
    for f in groups[-1]:
        gather(f)

    part = pl.ds(pl.multiple_of(mine * lanes, LANES), lanes)
    scale, bias = group_affine(
        total[0],
        total[1],
        table_ref[gain_row : gain_row + 1, part],
        table_ref[gain_row + 1 : gain_row + 2, part],
        count,
    )
    blend = table_ref[pl.ds(blend_row + tile_id, 1), :]
    blend = jnp.where(
        (tile_row * STRIDE + up < tiles // GRID_X * STRIDE)
        & (tile_col * STRIDE + along < GRID_X * STRIDE),
        blend,
        0.0,
    )
    w_out = jnp.concatenate(
        [table_ref[w_out_row : w_out_row + 3, part], jnp.zeros((5, lanes), jnp.float32)], axis=0
    ).astype(jnp.bfloat16)
    colors = []
    for f in range(frames):
        upper = silu_of_half(partial[f][1] * scale + bias).astype(jnp.bfloat16)
        color = lax.dot_general(
            w_out, upper, (((1,), (1,)), ((), ())), preferred_element_type=jnp.float32
        )
        colors.append(color * blend)
    colors = jnp.concatenate(colors, axis=0)

    slot_in = lax.broadcasted_iota(jnp.int32, (pixels, pixels), 0)
    pixel = lax.broadcasted_iota(jnp.int32, (pixels, pixels), 1)
    shown, weight_rows = [], []
    for down, across in cases:
        u, v = slot_in // TSIDE - down * STRIDE, slot_in % TSIDE - across * STRIDE
        good = (u >= 0) & (u < STRIDE) & (v >= 0) & (v < STRIDE) & (u * STRIDE + v == pixel)
        shown.append(jnp.where(good, 1.0, 0.0).astype(jnp.bfloat16))
        inside = (tile_row >= down) & (tile_col >= across)
        other = jnp.maximum(tile_id - down * GRID_X - across, 0)
        weight = jnp.where(inside, table_ref[pl.ds(blend_row + other, 1), :], 0.0)
        weight_rows.append(jnp.broadcast_to(weight, (8, pixels)))
    shown_ref[...] = exact_dot(
        jnp.concatenate([colors] + weight_rows, axis=0), jnp.concatenate(shown, axis=1)
    )
    denom = jnp.zeros((8, own), jnp.float32)
    for number in range(len(cases)):
        lane = slice(number * pixels, number * pixels + own)
        row = 8 * (frames + number)
        denom = denom + shown_ref[row : row + 8, lane]
        for swap in range(spans):
            target = keep_ref if swap == 0 else send_ref.at[swap - 1]
            base = (mine + swap) % spans * own_frames * 8
            for at in range(own_frames):
                for o in range(3):
                    target[number, o, at : at + 1, :] = shown_ref[
                        pl.ds(base + 8 * at + o, 1), lane
                    ]
    denom_ref[...] = denom


def from_ring(value, axis):
    count = lax.axis_size(axis)
    return [
        lax.ppermute(value, axis, [((d + turn) % count, d) for d in range(count)])
        for turn in range(1, count)
    ]


def ring_sum(kept, sent, axis):
    count = lax.axis_size(axis)
    for turn in range(1, count):
        kept = kept + lax.ppermute(
            sent[turn - 1], axis, [(d, (d + turn) % count) for d in range(count)]
        )
    return kept


def small_table(*values):
    values = [value.reshape(-1, value.shape[-1]) for value in values]
    wide = max(value.shape[1] for value in values)
    height = sum(value.shape[0] for value in values)
    total, row = 0.0, 0
    for value in values:
        below = height - row - value.shape[0]
        value = jnp.pad(value.astype(jnp.float32), ((row, below), (0, wide - value.shape[1])))
        total = total + value
        row = height - below
    return total


def exchange_latents(frames, latent, own, table):
    tiles, shares = lax.axis_size("tile"), lax.axis_size("chan")
    tail = own - LANES
    height = frames * latent
    mine = table[:height, :own].astype(jnp.bfloat16)
    tails = sum(
        jnp.pad(
            mine[f * latent : (f + 1) * latent, LANES:],
            ((0, 0), (tail * f, LANES - tail * (f + 1))),
        )
        for f in range(frames)
    )
    affine = table[height : height + 2]
    high = lax.reduce_precision(affine, 8, 7)
    low = lax.reduce_precision(affine - high, 8, 7)
    affine = jnp.concatenate([high, low], axis=0).astype(jnp.bfloat16)
    rows = [affine[:, at : at + LANES] for at in range(0, affine.shape[1], LANES)]
    rows = jnp.concatenate(rows, axis=0)
    rows = jnp.pad(rows, ((0, -rows.shape[0] % 16), (0, 0)))
    message = jnp.concatenate([mine[:, :LANES], tails, rows], axis=0)
    got = [message]
    for steps in range(1, tiles):
        turn = steps if steps < shares else 0
        pairs = [
            (t * shares + (c + turn) % shares, (t + steps) % tiles * shares + c)
            for t in range(tiles)
            for c in range(shares)
        ]
        got.append(lax.ppermute(message, ("tile", "chan"), pairs))
    stack = jnp.concatenate(got, axis=0)
    return [stack] + from_ring(stack, "tm")


def lanes_body(
    latents, tile_order, w_in, gain_in, shift_in, w_mid, gain_mid, shift_mid, w_out, blend_weight
):
    own_frames, latent, own = latents.shape
    spans = lax.axis_size("tm")
    shares = lax.axis_size("chan")
    frames = own_frames * spans
    if 8 * latent != LANES or frames * latent != LANES:
        return general_body(
            latents,
            tile_order,
            w_in,
            gain_in,
            shift_in,
            w_mid,
            gain_mid,
            shift_mid,
            w_out,
            blend_weight,
        )
    tiles = tile_order.shape[0]
    wide = w_in.shape[2]
    lanes = wide // spans
    pixels = TSIDE * TSIDE
    cases = block_cases(tiles)

    w_in_all = [(from_ring(other, "tm") or [other])[0] for other in from_ring(w_in, "chan")]
    table = lax.optimization_barrier(
        small_table(
            latents.reshape(own_frames * latent, own),
            gain_in,
            shift_in,
            gain_mid,
            shift_mid,
            w_out,
            blend_weight,
        )
    )
    latents_all = exchange_latents(own_frames, latent, own, table)
    _, w_in, tile_order = lax.optimization_barrier((table, w_in, tile_order))
    order = jnp.broadcast_to(tile_order.astype(jnp.float32)[:, None], (tiles, LANES))
    w_in_own = from_ring(w_in, "tm")[:1] or [w_in]

    vmem = pl.BlockSpec(memory_space=pltpu.VMEM)
    piece = (len(cases), 3, own_frames, own)
    kept, sent, denom = pl.pallas_call(
        functools.partial(decode_kernel, tiles, spans, shares),
        out_shape=[
            jax.ShapeDtypeStruct(piece, jnp.float32),
            jax.ShapeDtypeStruct((max(spans - 1, 1),) + piece, jnp.float32),
            jax.ShapeDtypeStruct((8, own), jnp.float32),
        ],
        in_specs=[pl.BlockSpec(memory_space=pl.ANY)] + [vmem] * (2 + spans + shares),
        out_specs=[vmem] * 3,
        scratch_shapes=[
            pltpu.VMEM(((frames + spans) * latent, len(cases) * LANES), jnp.bfloat16),
            pltpu.VMEM((frames, 9, latent, pixels), jnp.bfloat16),
            pltpu.VMEM((frames + 2, pixels, LANES), jnp.bfloat16),
            pltpu.VMEM((pixels, LANES), jnp.bfloat16),
            pltpu.VMEM((frames, pixels, CH), jnp.float32),
            pltpu.VMEM((3 * CH, 9 * lanes), jnp.bfloat16),
            pltpu.VMEM((8 * (frames + len(cases)), len(cases) * pixels), jnp.float32),
            pltpu.SemaphoreType.DMA((27 * shares,)),
        ]
        + [pltpu.VMEM((pixels + 2 * TSIDE, CH), jnp.bfloat16)] * frames
        + [pltpu.VMEM((3, pixels, lanes), jnp.float32)] * frames,
        compiler_params=pltpu.CompilerParams(vmem_limit_bytes=VMEM_BYTES),
        cost_estimate=pl.CostEstimate(
            flops=2 * frames * pixels * 27 * CH * lanes, bytes_accessed=8_000_000, transcendentals=0
        ),
    )(w_mid, table, order, *latents_all, *w_in_own, *w_in_all)
    total = ring_sum(kept, sent, "tm")
    total = ring_sum(total, [total] * (shares - 1), "chan")
    numer = total[0]
    for number, (down, across) in enumerate(cases):
        steps = down * GRID_X + across
        if steps and steps < tiles:
            numer = numer + shifted(total[number], "tile", steps)
    return jnp.transpose(numer / denom[0][None, None, :], (1, 0, 2))


def solution(mesh):
    placed = (
        P("tm", "groups", "tile"),
        P("groups"),
        P(None, None, "chan"),
        P("chan"),
        P("chan"),
        P(None, None, "chan"),
        P("chan"),
        P("chan"),
        P(None, "chan"),
        P("groups", None),
    )
    whole_lanes = (
        CH % (mesh.shape["chan"] * mesh.shape["tm"] * LANES) == 0
        and mesh.shape["chan"] <= mesh.shape["tile"]
    )
    return jax.shard_map(
        lanes_body if whole_lanes else general_body,
        mesh=mesh,
        in_specs=placed,
        out_specs=P("tm", "groups", "tile"),
        check_vma=False,
    )
```

```python
import functools

import jax
import jax.numpy as jnp
from jax import lax
from jax.experimental import pallas as pl
from jax.experimental.pallas import tpu as pltpu
from jax.sharding import PartitionSpec as P

CH = 512
GROUPS = 32
TSIDE = 16
STRIDE = 12
GRID_X = 4

EPSILON = 1e-06
LANES = 128
VMEM_BYTES = 48 * 1024 * 1024


def shifted(value, axis, steps):
    count = lax.axis_size(axis)
    leading, last = (max(0, -steps), min(count, count - steps))
    return lax.ppermute(value, axis, [(source, source + steps) for source in range(leading, last)])


def window_index(tile_id, tiles):
    slots = jnp.arange(TSIDE * TSIDE, dtype=jnp.int32)
    row = tile_id // GRID_X * STRIDE + slots // TSIDE
    col = tile_id % GRID_X * STRIDE + slots % TSIDE
    valid = (row < tiles // GRID_X * STRIDE) & (col < GRID_X * STRIDE)
    block = row // STRIDE * GRID_X + col // STRIDE
    index = block * (STRIDE * STRIDE) + row % STRIDE * STRIDE + col % STRIDE
    return (jnp.where(valid, index, 0), valid)


def causal_conv(extended, weights, frames, side):
    pixels = side * side
    rows = jnp.arange(pixels, dtype=jnp.int32) // side
    cols = jnp.arange(pixels, dtype=jnp.int32) % side
    total = jnp.zeros((frames, weights.shape[2], pixels), jnp.float32)
    for depth in range(3):
        window = extended[depth : depth + frames]
        for down in range(3):
            for across in range(3):
                offset = (down - 1) * side + (across - 1)
                inside = (
                    (rows + down - 1 >= 0)
                    & (rows + down - 1 < side)
                    & (cols + across - 1 >= 0)
                    & (cols + across - 1 < side)
                )
                moved = jnp.roll(window, -offset, axis=2)
                moved = jnp.where(inside[None, None, :], moved, jnp.zeros_like(moved))
                total = total + jnp.einsum(
                    "fcp,co->fop",
                    moved,
                    weights[9 * depth + 3 * down + across],
                    preferred_element_type=jnp.float32,
                )
    return total


def with_history(values):
    frames = values.shape[0]
    earlier = shifted(values[frames - 2 :], "tm", 1)
    return jnp.concatenate([earlier, values], axis=0)


def normalize(values, gain, shift, total_frames):
    frames, chans, pixels = values.shape
    width = CH // GROUPS
    grouped = values.reshape(frames, chans // width, width, pixels)
    sums = jnp.sum(grouped, axis=(0, 2, 3))
    squares = jnp.sum(grouped * grouped, axis=(0, 2, 3))
    sums, squares = lax.psum((sums, squares), "tm")
    count = total_frames * width * pixels
    mean = sums / count
    variance = squares / count - mean * mean
    scale = lax.rsqrt(variance + EPSILON)
    normed = (grouped - mean[None, :, None, None]) * scale[None, :, None, None]
    normed = normed.reshape(frames, chans, pixels) * gain[None, :, None] + shift[None, :, None]
    return jax.nn.silu(normed).astype(jnp.bfloat16)


def spread(color, weight, index, total_pixels):
    numer = (
        jnp.zeros((color.shape[0], 3, total_pixels), jnp.float32)
        .at[:, :, index]
        .add(color * weight[None, None, :])
    )
    denom = jnp.zeros((total_pixels,), jnp.float32).at[index].add(weight)
    return (numer, denom)


def route_owned(numer, denom, tile_id, own):
    frames = numer.shape[0]
    margin = (GRID_X + 1) * own
    numer_wide = jnp.concatenate([numer, jnp.zeros((frames, 3, margin), jnp.float32)], axis=2)
    denom_wide = jnp.concatenate([denom, jnp.zeros((margin,), jnp.float32)], axis=0)
    first_pixel = tile_id * own

    def block_at(offset):
        start_pixel = first_pixel + offset * own
        return (
            lax.dynamic_slice_in_dim(numer_wide, start_pixel, own, 2),
            lax.dynamic_slice_in_dim(denom_wide, start_pixel, own, 0),
        )

    owned_numer, owned_denom = block_at(0)
    for offset in (1, GRID_X, GRID_X + 1):
        piece_numer, piece_denom = block_at(offset)
        got_numer, got_denom = shifted((piece_numer, piece_denom), "tile", offset)
        owned_numer = owned_numer + got_numer
        owned_denom = owned_denom + got_denom
    return (owned_numer, owned_denom)


def general_body(
    latents, tile_order, w_in, gain_in, shift_in, w_mid, gain_mid, shift_mid, w_out, blend_weight
):
    frames = latents.shape[0]
    total_frames = frames * lax.axis_size("tm")
    tiles = tile_order.shape[0]
    own = STRIDE * STRIDE
    total_pixels = tiles * own
    tile_id = lax.axis_index("tile")
    index, valid = window_index(tile_id, tiles)
    whole = lax.all_gather(latents, "tile", axis=2, tiled=True)
    blocks = whole.reshape(frames, whole.shape[1], tiles, own)
    image = (
        jnp.zeros_like(blocks)
        .at[:, :, tile_order]
        .set(blocks)
        .reshape(frames, whole.shape[1], total_pixels)
    )
    window = jnp.where(
        valid[None, None, :], jnp.take(image, index, axis=2), jnp.zeros((), jnp.bfloat16)
    )
    first = causal_conv(with_history(window), w_in, frames, TSIDE)
    hidden = normalize(first, gain_in, shift_in, total_frames)
    second = causal_conv(
        lax.all_gather(with_history(hidden), "chan", axis=1, tiled=True), w_mid, frames, TSIDE
    )
    upper = normalize(second, gain_mid, shift_mid, total_frames)
    color = jnp.einsum("oc,fcp->fop", w_out, upper, preferred_element_type=jnp.float32)
    weight = jnp.where(valid, blend_weight[tile_id], jnp.float32(0.0))
    numer, denom = spread(color, weight, index, total_pixels)
    numer, denom = route_owned(numer, denom, tile_id, own)
    numer = lax.psum(numer, "chan")
    return numer / denom[None, None, :]


def block_cases(tiles):
    downs = (0, 1) if tiles // GRID_X > 1 else (0,)
    return [(down, across) for down in downs for across in (0, 1)]


def exact_dot(values, ones):
    rows = values.shape[0]
    high = values.astype(jnp.bfloat16)
    rest = values - high.astype(jnp.float32)
    middle = rest.astype(jnp.bfloat16)
    low = (rest - middle.astype(jnp.float32)).astype(jnp.bfloat16)
    total = jnp.dot(
        jnp.concatenate([high, middle, low], axis=0), ones, preferred_element_type=jnp.float32
    )
    return total[:rows] + total[rows : 2 * rows] + total[2 * rows :]


def group_affine(sums, squares, gain, shift, count):
    lanes = sums.shape[1]
    width = CH // GROUPS
    same = lax.broadcasted_iota(jnp.int32, (lanes, lanes), 0) // width == (
        lax.broadcasted_iota(jnp.int32, (lanes, lanes), 1) // width
    )
    total = exact_dot(
        jnp.concatenate([sums, squares], axis=0), jnp.where(same, 1.0, 0.0).astype(jnp.bfloat16)
    )
    mean = jnp.sum(total[:8], axis=0, keepdims=True) / count
    variance = jnp.sum(total[8:], axis=0, keepdims=True) / count - mean * mean
    scale = gain * lax.rsqrt(variance + EPSILON)
    return 0.5 * scale, 0.5 * (shift - mean * scale)


def silu_of_half(half):
    return half + half * jnp.tanh(half)


def fold(values):
    rows, lanes = values.shape
    return jnp.sum(values.reshape(rows // 8, 8, lanes), axis=0)


def decode_kernel(
    tiles,
    spans,
    shares,
    *refs,
):
    cases = block_cases(tiles)
    refs = list(refs)

    def take(number):
        taken = refs[:number]
        del refs[:number]
        return taken

    w_mid_ref, table_ref, order_ref = take(3)
    latent_refs, w_in_refs = take(spans), take(shares)
    keep_ref, send_ref, denom_ref = take(3)
    chosen, taps, turned_taps, turned_last, first, weights, partial = take(7)
    shown_ref, sems = take(2)
    hidden = take(first.shape[0])

    own = denom_ref.shape[1]
    own_frames = keep_ref.shape[2]
    frames = own_frames * spans
    latent, wide = w_in_refs[0].shape[1:]
    rows_in = frames * latent
    rows_own = rows_in // spans
    depth_in = 27 * latent
    pixels = TSIDE * TSIDE
    lanes = partial.shape[3]
    tile_id = lax.axis_index("tile")
    mine = lax.axis_index("tm")
    chan_id = lax.axis_index("chan")

    half = pl.ds(pl.multiple_of(mine * lanes, LANES), lanes)
    copies = []
    for a in range(3):
        for b in range(3):
            for e in range(3):
                for share in range(shares):
                    tap = 9 * a + 3 * b + e
                    held = pl.multiple_of((chan_id + share) % shares * wide, LANES)
                    copy = pltpu.make_async_copy(
                        w_mid_ref.at[tap, pl.ds(held, wide), half],
                        weights.at[
                            pl.ds(b * CH + share * wide, wide), pl.ds((3 * a + e) * lanes, lanes)
                        ],
                        sems.at[tap * shares + share],
                    )
                    copy.start()
                    copies.append(copy)

    tile_row, tile_col = tile_id // GRID_X, tile_id % GRID_X
    gain_row = rows_own + 2
    w_out_row = gain_row + 2
    blend_row = w_out_row + 3
    order = order_ref[...]
    number_of = lax.broadcasted_iota(jnp.int32, order.shape, 0)
    lane_of = lax.broadcasted_iota(jnp.int32, order.shape, 1)
    rows_all = latent_refs[0].shape[0] // tiles
    turns = []
    for down, across in cases:
        wanted = tile_id + down * GRID_X + across
        found = (order == wanted.astype(jnp.float32)) & (lane_of == 0)
        place = jnp.sum(jnp.where(found, number_of.astype(jnp.float32), 0.0))
        turns.append((tile_id - place.astype(jnp.int32) + tiles) % tiles)
    for number, (down, across) in enumerate(cases):
        inside = (tile_row + down < tiles // GRID_X) & (tile_col + across < GRID_X)
        turn = turns[number]
        part = slice(number * LANES, (number + 1) * LANES)
        for steps in range(tiles):

            @pl.when(inside & (turn == steps))
            def _():
                for swap in range(spans):
                    at, tail_at = swap * rows_own, rows_in + swap * latent
                    block = latent_refs[swap][steps * rows_all : (steps + 1) * rows_all]
                    chosen[at : at + rows_own, part] = block[:rows_own]
                    chosen[tail_at : tail_at + latent, part] = block[rows_own : rows_own + latent]

        @pl.when(jnp.logical_not(inside))
        def _():
            chosen[:, part] = jnp.zeros((chosen.shape[0], LANES), chosen.dtype)

    slot = lax.broadcasted_iota(jnp.int32, (1, pixels), 1)
    up, along = slot // TSIDE, slot % TSIDE
    source = lax.broadcasted_iota(jnp.int32, (LANES, pixels), 0)
    tail = own - LANES

    def pick(first_pixel):
        parts = []
        for down, across in cases:
            u, v = up - down * STRIDE, along - across * STRIDE
            good = (u >= 0) & (u < STRIDE) & (v >= 0) & (v < STRIDE)
            wanted = jnp.where(good, u * STRIDE + v - first_pixel, -1)
            parts.append(jnp.where(source == wanted, 1.0, 0.0).astype(jnp.bfloat16))
        return jnp.concatenate(parts, axis=0)

    tails = chosen[rows_in:].astype(jnp.float32)
    width = tails.shape[1]
    turned = [pltpu.roll(tails, (-f * tail) % width, 1) if f else tails for f in range(own_frames)]
    tails = jnp.concatenate(
        [
            turned[f][swap * latent : (swap + 1) * latent]
            for swap in range(spans)
            for f in range(own_frames)
        ],
        axis=0,
    ).astype(jnp.bfloat16)
    in_tail = lax.broadcasted_iota(jnp.int32, tails.shape, 1) % LANES < tail
    tails = jnp.where(in_tail, tails.astype(jnp.float32), 0.0).astype(jnp.bfloat16)
    window = jnp.dot(
        chosen[:rows_in], pick(0), preferred_element_type=jnp.float32
    ) + jnp.dot(tails, pick(LANES), preferred_element_type=jnp.float32)
    for b in range(3):
        for e in range(3):
            inside = (
                (up + b - 1 >= 0)
                & (up + b - 1 < TSIDE)
                & (along + e - 1 >= 0)
                & (along + e - 1 < TSIDE)
            )
            offset = (b - 1) * TSIDE + e - 1
            moved = pltpu.roll(window, (-offset) % pixels, 1) if offset else window
            moved = jnp.where(inside, moved, 0.0).astype(jnp.bfloat16)
            for swap in range(spans):
                value = moved[swap * rows_own : (swap + 1) * rows_own]
                span = pl.ds((mine + swap) % spans * own_frames, own_frames)
                taps[span, 3 * b + e] = value.reshape(own_frames, latent, pixels)

    turned_taps[0:2] = jnp.zeros((2, pixels, LANES), turned_taps.dtype)
    for f in range(frames):
        turned_taps[f + 2] = taps[f, 0:8].reshape(8 * latent, pixels).T
    turned_last[...] = taps[:, 8].reshape(frames * latent, pixels).T
    joined = jnp.concatenate([w_in_refs[s][...] for s in range(shares)], axis=2)
    main_rows = [joined[9 * a : 9 * a + 8].reshape(8 * latent, CH) for a in range(3)]
    sums = jnp.zeros((8, CH), jnp.float32)
    squares = jnp.zeros((8, CH), jnp.float32)
    nothing = jnp.zeros((latent, CH), jnp.bfloat16)
    for f in range(frames):
        patch = [turned_taps[f + a] for a in range(3)] + [turned_last[...]]
        last_rows = [
            joined[9 * (g - f + 2) + 8] if 0 <= g - f + 2 < 3 else nothing for g in range(frames)
        ]
        value = jnp.dot(
            jnp.concatenate(patch, axis=1),
            jnp.concatenate(main_rows + last_rows, axis=0),
            preferred_element_type=jnp.float32,
        )
        first[f] = value
        sums = sums + fold(value)
        squares = squares + fold(value * value)
    count = frames * (CH // GROUPS) * pixels
    affine = []
    for s in range(shares):
        at = s * rows_all + rows_own + latent
        packed = (wide // LANES * 4 + 15) // 16 * 16
        table = latent_refs[0][at : at + packed].astype(jnp.float32)
        pieces = [table[4 * lane : 4 * lane + 4] for lane in range(wide // LANES)]
        table = jnp.concatenate([part[0:2] + part[2:4] for part in pieces], axis=1)
        part = slice(s * wide, (s + 1) * wide)
        affine.append(
            group_affine(sums[:, part], squares[:, part], table[0:1], table[1:2], count)
        )
    def hide(f):
        edge = jnp.zeros((TSIDE, CH), jnp.bfloat16)
        hidden[f][0:TSIDE] = edge
        hidden[f][TSIDE + pixels : 2 * TSIDE + pixels] = edge
        for s in range(shares):
            scale, bias = affine[s]
            part = slice(s * wide, (s + 1) * wide)
            value = first[f, :, part] * scale + bias
            hidden[f][TSIDE : TSIDE + pixels, part] = silu_of_half(value).astype(jnp.bfloat16)

    def convolve(start, several, depth_taps):
        lhs = jnp.concatenate(
            [
                jnp.concatenate(
                    [
                        hidden[start + f][b * TSIDE : b * TSIDE + pixels]
                        for f in range(several)
                    ],
                    axis=0,
                )
                for b in range(3)
            ],
            axis=1,
        )
        low = depth_taps[0] * 3 * lanes
        odd = len(depth_taps) % 2
        product = jnp.dot(
            lhs, weights[:, low : (9 - odd) * lanes], preferred_element_type=jnp.float32
        )
        if odd:
            rows = jnp.concatenate(
                [weights[b * CH : (b + 1) * CH, 8 * lanes :] for b in range(3)], axis=1
            )
            apart = jnp.dot(lhs[:, CH : 2 * CH], rows, preferred_element_type=jnp.float32)
        edge = jnp.zeros((TSIDE, lanes), jnp.float32)
        for a in depth_taps:
            for e in range(3):
                at = (3 * a + e) * lanes - low
                for f in range(several):
                    target = start + f + 2 - a
                    if odd and (a, e) == (2, 2):
                        value = apart[f * pixels : (f + 1) * pixels]
                        above = value[: pixels - TSIDE, :lanes]
                        below = value[TSIDE:, 2 * lanes :]
                        value = (
                            value[:, lanes : 2 * lanes]
                            + jnp.concatenate([edge, above], axis=0)
                            + jnp.concatenate([below, edge], axis=0)
                        )
                    else:
                        value = product[f * pixels : (f + 1) * pixels, at : at + lanes]
                    if start + f == max(target - 2, 0):
                        partial[e, target] = value
                    else:
                        partial[e, target] += value

    column = lax.broadcasted_iota(jnp.int32, (pixels, lanes), 0) % TSIDE
    total = [jnp.zeros((8, lanes), jnp.float32)] * 2

    def gather(f):
        left = jnp.where(column == 0, 0.0, pltpu.roll(partial[0, f], 1, 0))
        right = jnp.where(column == TSIDE - 1, 0.0, pltpu.roll(partial[2, f], pixels - 1, 0))
        value = partial[1, f] + left + right
        partial[1, f] = value
        total[0] = total[0] + fold(value)
        total[1] = total[1] + fold(value * value)

    bounds = [0, 2, frames - 2, frames - 1, frames]
    groups = [range(low, high) for low, high in zip(bounds, bounds[1:]) if high > low]
    for copy in copies:
        copy.wait()
    for f in groups[0]:
        hide(f)
    for number, group in enumerate(groups):
        if number + 1 < len(groups):
            for f in groups[number + 1]:
                hide(f)
        convolve(
            group.start,
            len(group),
            tuple(a for a in range(3) if group.stop - 1 + 2 - a < frames),
        )
        if number:
            for f in groups[number - 1]:
                gather(f)
    for f in groups[-1]:
        gather(f)

    part = pl.ds(pl.multiple_of(mine * lanes, LANES), lanes)
    scale, bias = group_affine(
        total[0],
        total[1],
        table_ref[gain_row : gain_row + 1, part],
        table_ref[gain_row + 1 : gain_row + 2, part],
        count,
    )
    blend = table_ref[pl.ds(blend_row + tile_id, 1), :]
    blend = jnp.where(
        (tile_row * STRIDE + up < tiles // GRID_X * STRIDE)
        & (tile_col * STRIDE + along < GRID_X * STRIDE),
        blend,
        0.0,
    )
    w_out = jnp.concatenate(
        [table_ref[w_out_row : w_out_row + 3, part], jnp.zeros((5, lanes), jnp.float32)], axis=0
    ).astype(jnp.bfloat16)
    colors = []
    for f in range(frames):
        upper = silu_of_half(partial[1, f] * scale + bias).astype(jnp.bfloat16)
        color = lax.dot_general(
            w_out, upper, (((1,), (1,)), ((), ())), preferred_element_type=jnp.float32
        )
        colors.append(color * blend)
    colors = jnp.concatenate(colors, axis=0)

    slot_in = lax.broadcasted_iota(jnp.int32, (pixels, pixels), 0)
    pixel = lax.broadcasted_iota(jnp.int32, (pixels, pixels), 1)
    shown, weight_rows = [], []
    for down, across in cases:
        u, v = slot_in // TSIDE - down * STRIDE, slot_in % TSIDE - across * STRIDE
        good = (u >= 0) & (u < STRIDE) & (v >= 0) & (v < STRIDE) & (u * STRIDE + v == pixel)
        shown.append(jnp.where(good, 1.0, 0.0).astype(jnp.bfloat16))
        inside = (tile_row >= down) & (tile_col >= across)
        other = jnp.maximum(tile_id - down * GRID_X - across, 0)
        weight = jnp.where(inside, table_ref[pl.ds(blend_row + other, 1), :], 0.0)
        weight_rows.append(jnp.broadcast_to(weight, (8, pixels)))
    shown_ref[...] = exact_dot(
        jnp.concatenate([colors] + weight_rows, axis=0), jnp.concatenate(shown, axis=1)
    )
    denom = jnp.zeros((8, own), jnp.float32)
    for number in range(len(cases)):
        lane = slice(number * pixels, number * pixels + own)
        row = 8 * (frames + number)
        denom = denom + shown_ref[row : row + 8, lane]
        for swap in range(spans):
            target = keep_ref if swap == 0 else send_ref.at[swap - 1]
            base = (mine + swap) % spans * own_frames * 8
            for at in range(own_frames):
                for o in range(3):
                    target[number, o, at : at + 1, :] = shown_ref[
                        pl.ds(base + 8 * at + o, 1), lane
                    ]
    denom_ref[...] = denom


def from_ring(value, axis):
    count = lax.axis_size(axis)
    return [
        lax.ppermute(value, axis, [((d + turn) % count, d) for d in range(count)])
        for turn in range(1, count)
    ]


def ring_sum(kept, sent, axis):
    count = lax.axis_size(axis)
    for turn in range(1, count):
        kept = kept + lax.ppermute(
            sent[turn - 1], axis, [(d, (d + turn) % count) for d in range(count)]
        )
    return kept


def small_table(*values):
    values = [value.reshape(-1, value.shape[-1]) for value in values]
    wide = max(value.shape[1] for value in values)
    height = sum(value.shape[0] for value in values)
    total, row = 0.0, 0
    for value in values:
        below = height - row - value.shape[0]
        value = jnp.pad(value.astype(jnp.float32), ((row, below), (0, wide - value.shape[1])))
        total = total + value
        row = height - below
    return total


def exchange_latents(frames, latent, own, table):
    tiles, shares = lax.axis_size("tile"), lax.axis_size("chan")
    tail = own - LANES
    height = frames * latent
    mine = table[:height, :own].astype(jnp.bfloat16)
    tails = sum(
        jnp.pad(
            mine[f * latent : (f + 1) * latent, LANES:],
            ((0, 0), (tail * f, LANES - tail * (f + 1))),
        )
        for f in range(frames)
    )
    affine = table[height : height + 2]
    high = lax.reduce_precision(affine, 8, 7)
    low = lax.reduce_precision(affine - high, 8, 7)
    affine = jnp.concatenate([high, low], axis=0).astype(jnp.bfloat16)
    rows = [affine[:, at : at + LANES] for at in range(0, affine.shape[1], LANES)]
    rows = jnp.concatenate(rows, axis=0)
    rows = jnp.pad(rows, ((0, -rows.shape[0] % 16), (0, 0)))
    message = jnp.concatenate([mine[:, :LANES], tails, rows], axis=0)
    got = [message]
    for steps in range(1, tiles):
        turn = steps if steps < shares else 0
        pairs = [
            (t * shares + (c + turn) % shares, (t + steps) % tiles * shares + c)
            for t in range(tiles)
            for c in range(shares)
        ]
        got.append(lax.ppermute(message, ("tile", "chan"), pairs))
    stack = jnp.concatenate(got, axis=0)
    return [stack] + from_ring(stack, "tm")


def lanes_body(
    latents, tile_order, w_in, gain_in, shift_in, w_mid, gain_mid, shift_mid, w_out, blend_weight
):
    own_frames, latent, own = latents.shape
    spans = lax.axis_size("tm")
    shares = lax.axis_size("chan")
    frames = own_frames * spans
    if 8 * latent != LANES or frames * latent != LANES:
        return general_body(
            latents,
            tile_order,
            w_in,
            gain_in,
            shift_in,
            w_mid,
            gain_mid,
            shift_mid,
            w_out,
            blend_weight,
        )
    tiles = tile_order.shape[0]
    wide = w_in.shape[2]
    lanes = wide // spans
    pixels = TSIDE * TSIDE
    cases = block_cases(tiles)

    w_in_all = [(from_ring(other, "tm") or [other])[0] for other in from_ring(w_in, "chan")]
    table = lax.optimization_barrier(
        small_table(
            latents.reshape(own_frames * latent, own),
            gain_in,
            shift_in,
            gain_mid,
            shift_mid,
            w_out,
            blend_weight,
        )
    )
    latents_all = exchange_latents(own_frames, latent, own, table)
    _, w_in, tile_order = lax.optimization_barrier((table, w_in, tile_order))
    order = jnp.broadcast_to(tile_order.astype(jnp.float32)[:, None], (tiles, LANES))
    w_in_own = from_ring(w_in, "tm")[:1] or [w_in]

    vmem = pl.BlockSpec(memory_space=pltpu.VMEM)
    piece = (len(cases), 3, own_frames, own)
    kept, sent, denom = pl.pallas_call(
        functools.partial(decode_kernel, tiles, spans, shares),
        out_shape=[
            jax.ShapeDtypeStruct(piece, jnp.float32),
            jax.ShapeDtypeStruct((max(spans - 1, 1),) + piece, jnp.float32),
            jax.ShapeDtypeStruct((8, own), jnp.float32),
        ],
        in_specs=[pl.BlockSpec(memory_space=pl.ANY)] + [vmem] * (2 + spans + shares),
        out_specs=[vmem] * 3,
        scratch_shapes=[
            pltpu.VMEM(((frames + spans) * latent, len(cases) * LANES), jnp.bfloat16),
            pltpu.VMEM((frames, 9, latent, pixels), jnp.bfloat16),
            pltpu.VMEM((frames + 2, pixels, LANES), jnp.bfloat16),
            pltpu.VMEM((pixels, LANES), jnp.bfloat16),
            pltpu.VMEM((frames, pixels, CH), jnp.float32),
            pltpu.VMEM((3 * CH, 9 * lanes), jnp.bfloat16),
            pltpu.VMEM((3, frames, pixels, lanes), jnp.float32),
            pltpu.VMEM((8 * (frames + len(cases)), len(cases) * pixels), jnp.float32),
            pltpu.SemaphoreType.DMA((27 * shares,)),
        ]
        + [pltpu.VMEM((pixels + 2 * TSIDE, CH), jnp.bfloat16)] * frames,
        compiler_params=pltpu.CompilerParams(vmem_limit_bytes=VMEM_BYTES),
        cost_estimate=pl.CostEstimate(
            flops=2 * frames * pixels * 27 * CH * lanes, bytes_accessed=8_000_000, transcendentals=0
        ),
    )(w_mid, table, order, *latents_all, *w_in_own, *w_in_all)
    total = ring_sum(kept, sent, "tm")
    total = ring_sum(total, [total] * (shares - 1), "chan")
    numer = total[0]
    for number, (down, across) in enumerate(cases):
        steps = down * GRID_X + across
        if steps and steps < tiles:
            numer = numer + shifted(total[number], "tile", steps)
    return jnp.transpose(numer / denom[0][None, None, :], (1, 0, 2))


def solution(mesh):
    placed = (
        P("tm", "groups", "tile"),
        P("groups"),
        P(None, None, "chan"),
        P("chan"),
        P("chan"),
        P(None, None, "chan"),
        P("chan"),
        P("chan"),
        P(None, "chan"),
        P("groups", None),
    )
    whole_lanes = (
        CH % (mesh.shape["chan"] * mesh.shape["tm"] * LANES) == 0
        and mesh.shape["chan"] <= mesh.shape["tile"]
    )
    return jax.shard_map(
        lanes_body if whole_lanes else general_body,
        mesh=mesh,
        in_specs=placed,
        out_specs=P("tm", "groups", "tile"),
        check_vma=False,
    )
```
